32 devices in a mesh: rep: 4 (over y, x), shard: 8 (over z, core).
Axes of the slice: x: 2, y: 2, z: 4, core: 2. Of those that a mesh axis runs over, the one named last changes fastest.
Arguments:
- tokens: bfloat16 [8192, 1152], P(('rep', 'shard')), may hold values from -6 to 6
- cotangent: bfloat16 [8192, 1152], P(('rep', 'shard')), may hold values from -6 to 6
- lengths: int32 [32, 8], P(('rep', 'shard')), may hold values from 0 to 256, as said below
- deal: int32 [8192], replicated, may hold values from 0 to 8191, as said below
- w_qkv: float32 [1152, 1536], P('shard'), may hold values from -0.3125 to 0.3125
- w_out: float32 [1024, 1152], P('shard'), may hold values from -0.75 to 0.75
- w_gu: float32 [2, 6912, 1152], P(None, 'shard'), may hold values from -0.1875 to 0.1875
- w_down: float32 [6912, 1152], P('shard'), may hold values from -0.078125 to 0.078125
- gains: float32 [4, 1152], P(None, 'shard'), may hold values from 0.5 to 1.5
- first_qkv: float32 [1152, 1536], P('shard'), may hold values from -256 to 256
- first_out: float32 [1024, 1152], P('shard'), may hold values from -128 to 128
- first_gu: float32 [2, 6912, 1152], P(None, 'shard'), may hold values from -256 to 256
- first_down: float32 [6912, 1152], P('shard'), may hold values from -256 to 256
- first_gains: float32 [4, 1152], P(None, 'shard'), may hold values from -512 to 512
- second_qkv: float32 [1152, 1536], P('shard'), may hold values from 2048 to 8192
- second_out: float32 [1024, 1152], P('shard'), may hold values from 512 to 2048
- second_gu: float32 [2, 6912, 1152], P(None, 'shard'), may hold values from 2048 to 8192
- second_down: float32 [6912, 1152], P('shard'), may hold values from 2048 to 8192
- second_gains: float32 [4, 1152], P(None, 'shard'), may hold values from 8192 to 32768
Outputs:
- output: bfloat16 [8192, 1152], P(('rep', 'shard'))
- input_grad: bfloat16 [8192, 1152], P(('rep', 'shard'))
- new_qkv: float32 [1152, 1536], P('shard')
- new_out: float32 [1024, 1152], P('shard')
- new_gu: float32 [2, 6912, 1152], P(None, 'shard')
- new_down: float32 [6912, 1152], P('shard')
- new_gains: float32 [4, 1152], P(None, 'shard')
- moment_qkv: float32 [1152, 1536], P('shard')
- moment_out: float32 [1024, 1152], P('shard')
- moment_gu: float32 [2, 6912, 1152], P(None, 'shard')
- moment_down: float32 [6912, 1152], P('shard')
- moment_gains: float32 [4, 1152], P(None, 'shard')
- square_qkv: float32 [1152, 1536], P('shard')
- square_out: float32 [1024, 1152], P('shard')
- square_gu: float32 [2, 6912, 1152], P(None, 'shard')
- square_down: float32 [6912, 1152], P('shard')
- square_gains: float32 [4, 1152], P(None, 'shard')
- grad_qkv: float32 [1152, 1536], P('shard')
- grad_out: float32 [1024, 1152], P('shard')
- grad_gu: float32 [2, 6912, 1152], P(None, 'shard')
- grad_down: float32 [6912, 1152], P('shard')
- grad_gains: float32 [4, 1152], P(None, 'shard')
- copy_qkv: bfloat16 [1152, 1536], P('shard')
- copy_out: bfloat16 [1024, 1152], P('shard')
- copy_gu: bfloat16 [2, 6912, 1152], P(None, 'shard')
- copy_down: bfloat16 [6912, 1152], P('shard')
- copy_gains: bfloat16 [4, 1152], P(None, 'shard')
The draws below stay inside these ranges and needn't reach their ends.
Inputs may be any that keep to these rules, and one draw needn't show every extreme that they name: `lengths`: each row sums to 256; in every draw one row holds a single sequence of 256 tokens, the rest zeros. `deal`: a permutation of the slots; each device's input rows go to every device, exactly 8 to each.
All inputs are finite; a program needn't handle non-finite values.
Results may differ from the reference program's by a relative error of at most 0.028.
The reference program's roundings to bfloat16 on the way count: a program that leaves them out, or rounds other values in their place, can miss the bound.
Values may be sent and summed in bfloat16 or wider, within the bound.
A program may use at most 384 MiB of HBM per device.

```python
import math
import jax
import jax.numpy as jnp
from jax import lax

D = 1152
FF = 6912
H = 4
KV = 1
HD = 256
TOK_DEV = 256
DOCS = 8
STEP = 10
TOKENS = 8192
PEER_ROWS = 8
DEVICES = 32


def shuffle_rows(sub_key):
    return jax.random.permutation(sub_key, TOK_DEV)


def draw_lengths(key, part):
    key = jax.random.fold_in(key, 11)
    cut_key, whole_key = jax.random.split(key)
    cut_points = jnp.sort(jax.random.randint(cut_key, (DEVICES, DOCS - 1), 0, TOK_DEV + 1), axis=1)
    edges = jnp.concatenate([jnp.zeros((DEVICES, 1), jnp.int32), cut_points.astype(jnp.int32), jnp.full((DEVICES, 1), TOK_DEV, jnp.int32)], axis=1)
    counts = edges[:, 1:] - edges[:, :-1]
    single = jax.random.randint(whole_key, (), 0, DEVICES)
    whole_row = jnp.where(jnp.arange(DOCS) == 0, TOK_DEV, 0).astype(jnp.int32)
    picked = (jnp.arange(DEVICES) == single)[:, None]
    return jnp.where(picked, whole_row[None, :], counts).astype(jnp.int32)


def draw_deal(key, part):
    key = jax.random.fold_in(key, 23)
    slot_key, row_key = jax.random.split(key)
    slot_perm = jax.vmap(shuffle_rows)(jax.random.split(slot_key, DEVICES))
    blocks = slot_perm.reshape(DEVICES, DEVICES, PEER_ROWS)
    slots = jnp.transpose(blocks, (1, 0, 2)) + (jnp.arange(DEVICES) * TOK_DEV)[None, :, None]
    slots = slots.reshape(DEVICES, TOK_DEV)
    row_perm = jax.vmap(shuffle_rows)(jax.random.split(row_key, DEVICES))
    inverse = jnp.argsort(row_perm, axis=1)
    return jnp.take_along_axis(slots, inverse, axis=1).reshape(TOKENS).astype(jnp.int32)


def shard_levels(rng, dims, cuts, low, top_value):
    def one(axis_at, blocks):
        draws = jax.random.uniform(jax.random.fold_in(jax.random.fold_in(rng, 6), axis_at), (blocks,), jnp.float32, low / len(cuts), top_value / len(cuts))
        return jnp.repeat(jnp.exp(draws), dims[axis_at] // blocks).reshape((-1,) + (1,) * (len(dims) - axis_at - 1))

    level = one(*cuts[0])
    for cut in cuts[1:]:
        level = level * one(*cut)
    return level


def noise(key, extent, width, limit, shards=(), dtype=jnp.bfloat16):
    values = jax.random.normal(key, extent, jnp.float32) * width
    if len(shards) > 0:
        values = shard_levels(key, extent, shards, -0.22, 0.18) * values
    return jnp.clip(values, min=-limit, max=limit).astype(dtype)


def setup_inputs(seed: int = 0) -> dict:
    arg_keys = jax.random.split(jax.random.key(seed), 20)
    tokens = noise(arg_keys[0], (TOKENS, D), 1.0, 6.0, ((0, 32),))
    cotangent = noise(arg_keys[1], (TOKENS, D), 1.0, 6.0, ((0, 32),))
    lengths = draw_lengths(jax.random.fold_in(arg_keys[19], 71), 0)
    deal = draw_deal(jax.random.fold_in(arg_keys[19], 71), 0)
    w_qkv = noise(arg_keys[4], (D, (H + 2 * KV) * HD), (D // 3) ** -0.5, 0.3125, ((0, 8),), jnp.float32)
    w_out = noise(arg_keys[5], (H * HD, D), (H * HD // 16) ** -0.5, 0.75, ((0, 8),), jnp.float32)
    w_gu = noise(arg_keys[6], (2, FF, D), D ** -0.5, 0.1875, ((1, 8),), jnp.float32)
    w_down = noise(arg_keys[7], (FF, D), FF ** -0.5, 0.078125, ((0, 8),), jnp.float32)
    gains = jnp.clip(1.0 + 0.1 * jax.random.normal(arg_keys[8], (4, D), jnp.float32), 0.5, 1.5)
    first_qkv = noise(arg_keys[9], (D, (H + 2 * KV) * HD), (0.5 * TOKENS ** 0.5), 256.0, ((0, 8),), jnp.float32)
    first_out = noise(arg_keys[10], (H * HD, D), (0.25 * TOKENS ** 0.5), 128.0, ((0, 8),), jnp.float32)
    first_gu = noise(arg_keys[11], (2, FF, D), (0.5 * TOKENS ** 0.5), 256.0, ((1, 8),), jnp.float32)
    first_down = noise(arg_keys[12], (FF, D), (0.5 * TOKENS ** 0.5), 256.0, ((0, 8),), jnp.float32)
    first_gains = noise(arg_keys[13], (4, D), (TOKENS ** 0.5), 512.0, ((1, 8),), jnp.float32)
    second_qkv = jnp.clip(jnp.exp(math.log(8192.0) - 1.3862944 * jax.random.uniform(arg_keys[14], (D, (H + 2 * KV) * HD), jnp.float32) ** shard_levels(arg_keys[14], (D, (H + 2 * KV) * HD), ((0, 8),), -0.2, 0.2)), 2048.0, 8192.0)
    second_out = jnp.clip(jnp.exp(math.log(2048.0) - 1.3862944 * jax.random.uniform(arg_keys[15], (H * HD, D), jnp.float32) ** shard_levels(arg_keys[15], (H * HD, D), ((0, 8),), -0.2, 0.2)), 512.0, 2048.0)
    second_gu = jnp.clip(jnp.exp(math.log(8192.0) - 1.3862944 * jax.random.uniform(arg_keys[16], (2, FF, D), jnp.float32) ** shard_levels(arg_keys[16], (2, FF, D), ((1, 8),), -0.2, 0.2)), 2048.0, 8192.0)
    second_down = jnp.clip(jnp.exp(math.log(8192.0) - 1.3862944 * jax.random.uniform(arg_keys[17], (FF, D), jnp.float32) ** shard_levels(arg_keys[17], (FF, D), ((0, 8),), -0.2, 0.2)), 2048.0, 8192.0)
    second_gains = jnp.clip(jnp.exp(math.log(32768.0) - 1.3862944 * jax.random.uniform(arg_keys[18], (4, D), jnp.float32) ** shard_levels(arg_keys[18], (4, D), ((1, 8),), -0.2, 0.2)), 8192.0, 32768.0)
    return dict(tokens=tokens, cotangent=cotangent, lengths=lengths, deal=deal, w_qkv=w_qkv, w_out=w_out, w_gu=w_gu, w_down=w_down, gains=gains, first_qkv=first_qkv, first_out=first_out, first_gu=first_gu, first_down=first_down, first_gains=first_gains, second_qkv=second_qkv, second_out=second_out, second_gu=second_gu, second_down=second_down, second_gains=second_gains)


CAP_LIMIT = 50.0
NORM_EPS = 1e-06
ROPE_BASE = 10000.0
MASKED_SCORE = -1e+30
BETA_FIRST = 0.5
BETA_SECOND = 0.5
ADAM_EPS = 1e-08
LEARN_RATES = (0.05, 0.1, 0.03, 0.012, 0.4)
DECAY_RATES = (0.1, 0.1, 0.1, 0.1, 0.0)

@jax.custom_vjp
def low(v):
    return lax.optimization_barrier(v.astype(jnp.bfloat16)).astype(jnp.float32)

@jax.custom_vjp
def low_back(v):
    return v

def low_keep(v):
    return (low(v), None)

def low_pass(kept, grad):
    return (grad,)

def back_keep(v):
    return (v, None)

def back_low(kept, grad):
    return (low(grad),)
low.defvjp(low_keep, low_pass)
low_back.defvjp(back_keep, back_low)

def exact_product(leading, trailing):
    return jnp.dot(leading, trailing, precision=lax.Precision.HIGHEST, preferred_element_type=jnp.float32)

def rms_norm(values, gain_row):
    inverse_rms = lax.rsqrt(lax.optimization_barrier(jnp.mean(values * values, axis=-1, keepdims=True)) + NORM_EPS)
    return values * inverse_rms * gain_row

def pack_layout(length_row):
    seq_ends = jnp.cumsum(length_row)
    starts = seq_ends - length_row
    slot_ids = jnp.arange(TOK_DEV)
    document = lax.optimization_barrier(jnp.sum((slot_ids[:, None] >= seq_ends[None, :]).astype(jnp.int32), axis=1))
    chosen = document[:, None] == jnp.arange(DOCS)[None, :]
    begins = lax.optimization_barrier(jnp.sum(jnp.where(chosen, starts[None, :], 0), axis=1))
    position = (slot_ids - begins).astype(jnp.float32)
    allowed = (document[:, None] == document[None, :]) & (slot_ids[None, :] <= slot_ids[:, None])
    return (position, allowed)

def angle_tables(position):
    exponent = jnp.arange(HD // 2).astype(jnp.float32) * (-2.0 / HD)
    frequency = ROPE_BASE ** exponent
    angles = position[..., None] * frequency
    return (jnp.cos(angles), jnp.sin(angles))

def rotate_pairs(values, cosine_table, sine_table):
    half_width = values.shape[-1] // 2
    front_half = values[..., :half_width]
    back_half = values[..., half_width:]
    return jnp.concatenate([front_half * cosine_table - back_half * sine_table, back_half * cosine_table + front_half * sine_table], axis=-1)

def group_forward(params, token_group, position, allowed):
    w_qkv, w_out, w_gu, w_down, gains = params
    packs = token_group.shape[0]
    row_count = packs * TOK_DEV
    inputs = token_group.reshape(row_count, D)
    normed_one = low(rms_norm(inputs, gains[0]))
    projected = low_back(exact_product(normed_one, w_qkv))
    cosine_table, sine_table = angle_tables(position)
    queries = projected[:, :H * HD].reshape(packs, TOK_DEV, H, HD)
    queries = low(rotate_pairs(queries, cosine_table[:, :, None, :], sine_table[:, :, None, :]))
    key_rows = projected[:, H * HD:(H + KV) * HD].reshape(packs, TOK_DEV, HD)
    key_rows = low(rotate_pairs(key_rows, cosine_table, sine_table))
    value_rows = low(projected[:, (H + KV) * HD:].reshape(packs, TOK_DEV, HD))
    raw_scores = low_back(jnp.einsum('gqhd,gkd->ghqk', queries, key_rows, precision=lax.Precision.HIGHEST))
    capped = CAP_LIMIT * jnp.tanh(raw_scores * HD ** (-0.5) / CAP_LIMIT)
    capped = jnp.where(allowed[:, None], capped, MASKED_SCORE)
    softmax_weights = jax.nn.softmax(capped, axis=-1)
    attended = jnp.einsum('ghqk,gkd->gqhd', low(softmax_weights), value_rows, precision=lax.Precision.HIGHEST)
    attended = low(low_back(attended.reshape(row_count, H * HD)))
    branch = low_back(exact_product(attended, w_out))
    middle = inputs + rms_norm(branch, gains[1])
    normed_two = low(rms_norm(middle, gains[2]))
    gate_pre = low_back(exact_product(normed_two, w_gu[0].T))
    upper = low_back(exact_product(normed_two, w_gu[1].T))
    hidden = low(jax.nn.gelu(gate_pre, approximate=True) * upper)
    feed_out = low_back(exact_product(hidden, w_down))
    return (middle + rms_norm(feed_out, gains[3])).reshape(packs, TOK_DEV, D)

def adamw_step(master, gradient, first_moment, second_moment, rate, decay):
    moment = BETA_FIRST * first_moment + (1.0 - BETA_FIRST) * gradient
    square = BETA_SECOND * second_moment + (1.0 - BETA_SECOND) * gradient * gradient
    moment_hat = moment / (1.0 - BETA_FIRST ** STEP)
    square_hat = square / (1.0 - BETA_SECOND ** STEP)
    updated = master - rate * (moment_hat / (jnp.sqrt(square_hat) + ADAM_EPS) + decay * master)
    return (updated, moment, square)

def reference(tokens, cotangent, lengths, deal, w_qkv, w_out, w_gu, w_down, gains, first_qkv, first_out, first_gu, first_down, first_gains, second_qkv, second_out, second_gu, second_down, second_gains):
    masters = (w_qkv, w_out, w_gu, w_down, gains)
    firsts = (first_qkv, first_out, first_gu, first_down, first_gains)
    seconds = (second_qkv, second_out, second_gu, second_down, second_gains)
    rounded = tuple((lax.optimization_barrier(master.astype(jnp.bfloat16)).astype(jnp.float32) for master in masters))
    source_rows = jnp.argsort(deal)
    work_tokens = tokens.astype(jnp.float32)[source_rows].reshape(DEVICES, TOK_DEV, D)
    work_upstream = cotangent.astype(jnp.float32)[source_rows].reshape(DEVICES, TOK_DEV, D)
    position, allowed = jax.vmap(pack_layout)(lengths)
    group_size = math.gcd(DEVICES, max(1, 4096 // TOK_DEV))
    group_count = DEVICES // group_size
    layered = jax.checkpoint(group_forward)

    def regroup(array_in):
        return array_in.reshape((group_count, group_size) + array_in.shape[1:])

    def forward(params, token_packs):

        def one_group(items):
            return layered(params, items[0], items[1], items[2])
        stacked = lax.map(one_group, (regroup(token_packs), regroup(position), regroup(allowed)))
        return stacked.reshape(DEVICES, TOK_DEV, D)
    result, pullback = jax.vjp(forward, rounded, work_tokens)
    weight_grads, input_grads = pullback(work_upstream)
    output = result.reshape(TOKENS, D)[deal].astype(jnp.bfloat16)
    input_grad = input_grads.reshape(TOKENS, D)[deal].astype(jnp.bfloat16)
    updates = [adamw_step(masters[member], weight_grads[member], firsts[member], seconds[member], LEARN_RATES[member], DECAY_RATES[member]) for member in range(5)]
    return (output, input_grad, updates[0][0], updates[1][0], updates[2][0], updates[3][0], updates[4][0], updates[0][1], updates[1][1], updates[2][1], updates[3][1], updates[4][1], updates[0][2], updates[1][2], updates[2][2], updates[3][2], updates[4][2], weight_grads[0], weight_grads[1], weight_grads[2], weight_grads[3], weight_grads[4], updates[0][0].astype(jnp.bfloat16), updates[1][0].astype(jnp.bfloat16), updates[2][0].astype(jnp.bfloat16), updates[3][0].astype(jnp.bfloat16), updates[4][0].astype(jnp.bfloat16))
```

```python
import functools

import jax
import jax.numpy as jnp
import numpy as np
from jax import lax
from jax.experimental import pallas as pl
from jax.experimental.pallas import tpu as pltpu
from jax.sharding import PartitionSpec as P

H = 4
KV = 1
HD = 256
STEP = 10


CAP_LIMIT = 50.0
NORM_EPS = 1e-06
ROPE_BASE = 10000.0
MASKED_SCORE = -1e30
BETA_FIRST = 0.5
BETA_SECOND = 0.5
ADAM_EPS = 1e-08
LEARN_RATES = (0.05, 0.1, 0.03, 0.012, 0.4)
DECAY_RATES = (0.1, 0.1, 0.1, 0.1, 0.0)
GELU_COEF = 0.7978845608028654
GELU_CUBIC = 0.044715


def rms_scale(values):
    return lax.rsqrt(jnp.mean(values * values, axis=-1, keepdims=True) + NORM_EPS)


def norm_backward(grad_out, values, inverse_rms, gain_row):
    scaled = grad_out * gain_row
    inner = jnp.mean(scaled * values, axis=-1, keepdims=True)
    grad_in = inverse_rms * scaled - values * inverse_rms * inverse_rms * inverse_rms * inner
    grad_gain = jnp.sum(grad_out * values * inverse_rms, axis=0)
    return (grad_in, grad_gain)


def cross_rows(leading, trailing):
    return lax.dot_general(
        leading, trailing, (((0,), (0,)), ((), ())), preferred_element_type=jnp.float32
    )


def against_cols(leading, trailing):
    return lax.dot_general(
        leading, trailing, (((1,), (1,)), ((), ())), preferred_element_type=jnp.float32
    )


def adamw_step(master, gradient, first_moment, second_moment, rate, decay):
    moment = BETA_FIRST * first_moment + (1.0 - BETA_FIRST) * gradient
    square = BETA_SECOND * second_moment + (1.0 - BETA_SECOND) * gradient * gradient
    moment_hat = moment / (1.0 - BETA_FIRST**STEP)
    square_hat = square / (1.0 - BETA_SECOND**STEP)
    updated = master - rate * (moment_hat / (jnp.sqrt(square_hat) + ADAM_EPS) + decay * master)
    return (updated, moment, square)


LANES = 128
UNIT_TILE = 256
MESH = pl.DeviceIdType.MESH


def round_up(count, step):
    return -(-count // step) * step


def partner_of(index, bit):
    value = lax.rem(lax.div(index, 1 << bit), 2)
    return index + (1 - 2 * value) * (1 << bit), value


EARLY = 2


def deal_row(deal_ref, device, rows):
    lines = rows // LANES
    return jnp.concatenate(
        [deal_ref[pl.ds(device * lines + at, 1), :] for at in range(lines)], axis=1
    )


def halving_spans(rep, bits, part, part_rows):
    spans = []
    first = part * part_rows
    size = part_rows
    for bit in range(bits) if part == 0 else range(bits - 1, -1, -1):
        size //= 2
        partner, value = partner_of(rep, bit)
        spans.append((partner, first + value * size, first + (1 - value) * size, size))
        first = first + value * size
    return spans


def at_rows(first, size):
    return pl.ds(pl.multiple_of(first, 16), size)


def feed_kernel(
    line,
    replicas,
    own_rows,
    middle_ref,
    upstream_ref,
    gain_ref,
    weights_hbm,
    out_ref,
    gain_grad_ref,
    back_ref,
    grads_ref,
    weights,
    blocks,
    acts,
    partial,
    chain,
    sibling_out,
    sibling_in,
    landing,
    load_sems,
    store_sems,
    gather_send,
    gather_recv,
    chain_send,
    chain_recv,
    sibling_send,
    sibling_recv,
    half_send,
    half_recv,
):
    rep = lax.axis_index("rep")
    shard = lax.axis_index("shard")
    core = lax.rem(shard, 2)
    place = lax.div(shard, 2)
    sibling = (rep, shard + 1 - 2 * core)
    left = (rep, shard - 2)
    right = (rep, shard + 2)
    has_left = place > 0
    has_right = place < line - 1
    rows = own_rows.shape[0] // 2
    width = own_rows.shape[1]
    half = weights.shape[1] // 2
    tiles = 2 * half // UNIT_TILE

    load = pltpu.make_async_copy(weights_hbm, weights, load_sems.at[0])
    load.start()

    barrier = pltpu.get_barrier_semaphore()
    pl.semaphore_signal(barrier, inc=1, device_id=sibling, device_id_type=MESH)

    @pl.when(has_left)
    def _():
        pl.semaphore_signal(barrier, inc=1, device_id=left, device_id_type=MESH)

    @pl.when(has_right)
    def _():
        pl.semaphore_signal(barrier, inc=1, device_id=right, device_id_type=MESH)

    bits = replicas.bit_length() - 1
    greeted = sorted({0, bits - 1})
    for bit in greeted:
        partner, _ = partner_of(rep, bit)
        pl.semaphore_signal(barrier, inc=1, device_id=(partner, shard), device_id_type=MESH)

    def block_span(block):
        return pl.ds(pl.multiple_of(block * rows, rows), rows)

    for part in range(2):
        blocks[0, part, block_span(place), :] = own_rows[part * rows : (part + 1) * rows, :]

    pl.semaphore_wait(
        barrier,
        1 + len(greeted) + has_left.astype(jnp.int32) + has_right.astype(jnp.int32),
    )

    def gather_copy(phase, part, way, step, block):
        return pltpu.make_async_remote_copy(
            src_ref=blocks.at[phase, part, block_span(block)],
            dst_ref=blocks.at[phase, part, block_span(block)],
            send_sem=gather_send.at[phase, part, way, step],
            recv_sem=gather_recv.at[phase, part, way, step],
            device_id=left if way else right,
            device_id_type=MESH,
        )

    def gather_start(phase, part, step):
        @pl.when(has_right & (place - step >= 0))
        def _():
            gather_copy(phase, part, 0, step, place - step).start()

        @pl.when(has_left & (place + step <= line - 1))
        def _():
            gather_copy(phase, part, 1, step, place + step).start()

    def gather_arrive(phase, part, step):
        @pl.when(place - 1 - step >= 0)
        def _():
            gather_copy(phase, part, 0, step, place - 1 - step).wait_recv()

        @pl.when(place + 1 + step <= line - 1)
        def _():
            gather_copy(phase, part, 1, step, place + 1 + step).wait_recv()

    def gather_drain(phase, part):
        @pl.loop(0, line - 1)
        def _(step):
            @pl.when(has_right & (place - step >= 0))
            def _():
                gather_copy(phase, part, 0, step, place - step).wait_send()

            @pl.when(has_left & (place + step <= line - 1))
            def _():
                gather_copy(phase, part, 1, step, place + step).wait_send()

    def chain_copy(phase, part, way, packet, block):
        return pltpu.make_async_remote_copy(
            src_ref=partial.at[part, block_span(block)],
            dst_ref=chain.at[part, way, packet],
            send_sem=chain_send.at[phase, part, way, packet],
            recv_sem=chain_recv.at[phase, part, way, packet],
            device_id=left if way else right,
            device_id_type=MESH,
        )

    def chain_add(phase, part, way, packet, block):
        chain_copy(phase, part, way, packet, block).wait_recv()
        span = block_span(block)
        partial[part, span, :] = (
            partial[part, span, :].astype(jnp.float32) + chain[part, way, packet].astype(jnp.float32)
        ).astype(partial.dtype)

    def chain_turn(phase, part, turn):
        outward = turn - place

        @pl.when(outward >= 0)
        def _():
            @pl.when(has_left)
            def _():
                chain_add(phase, part, 0, outward, line - 1 - outward)

            chain_copy(phase, part, 0, outward, line - 1 - outward).start()

        inward = turn - (line - 1 - place)

        @pl.when(inward >= 0)
        def _():
            @pl.when(has_right)
            def _():
                chain_add(phase, part, 1, inward, inward)

            chain_copy(phase, part, 1, inward, inward).start()

    def chain_finish(phase, part):
        out = slice(part * rows, (part + 1) * rows)
        back_ref[out, :] = partial[part, block_span(place), :].astype(jnp.float32)

        @pl.when(has_left)
        def _():
            last = line - 1 - place
            chain_copy(phase, part, 0, last, place).wait_recv()
            back_ref[out, :] += chain[part, 0, last].astype(jnp.float32)

        @pl.when(has_right)
        def _():
            chain_copy(phase, part, 1, place, place).wait_recv()
            back_ref[out, :] += chain[part, 1, place].astype(jnp.float32)

    def chain_drain(phase, part):
        @pl.loop(0, line - 1)
        def _(packet):
            @pl.when(line - 1 - packet > place)
            def _():
                chain_copy(phase, part, 0, packet, line - 1 - packet).wait_send()

            @pl.when(packet < place)
            def _():
                chain_copy(phase, part, 1, packet, packet).wait_send()

    def sweep(phase, part, work, reduce=None, last=None, beside=None):
        @pl.loop(1, line)
        def _(turn):
            gather_arrive(phase, part, turn - 1)

            @pl.when(turn < line - 1)
            def _():
                gather_start(phase, part, turn)
                if reduce is not None:
                    chain_turn(*reduce, turn)

            if last is not None:

                @pl.when(turn == line - 1)
                def _():
                    last()

            @pl.loop(0, line // 2)
            def _(pair):
                ready = jnp.maximum(jnp.abs(2 * pair - place), jnp.abs(2 * pair + 1 - place))

                @pl.when(ready == turn)
                def _():
                    work(part, pair)

            if beside is not None:
                beside(turn)

    def pair_span(pair):
        return pl.ds(pl.multiple_of(pair * 2 * rows, 2 * rows), 2 * rows)

    def token_span(part, pair):
        first = part * line * rows
        return pl.ds(pl.multiple_of(first + pair * 2 * rows, 2 * rows), 2 * rows)

    def unit_span(tile):
        return pl.ds(pl.multiple_of(tile * UNIT_TILE, UNIT_TILE), UNIT_TILE)

    def forward(part, pair):
        span = token_span(part, pair)

        @pl.loop(0, tiles)
        def _(tile):
            cols = unit_span(tile)
            rows_in = blocks[0, part, pair_span(pair), :]
            gate = against_cols(rows_in, weights[1, cols, :])
            upper = against_cols(rows_in, weights[2, cols, :])
            tanh_inner = jnp.tanh(GELU_COEF * (gate + GELU_CUBIC * gate * gate * gate))
            lifted = 0.5 * (1.0 + tanh_inner)
            activated = gate * lifted
            slope = lifted + 0.5 * gate * (1.0 - tanh_inner * tanh_inner) * GELU_COEF * (
                1.0 + 3.0 * GELU_CUBIC * gate * gate
            )
            acts[0, span, cols] = (activated * upper).astype(acts.dtype)
            acts[1, span, cols] = (upper * slope).astype(acts.dtype)
            acts[2, span, cols] = activated.astype(acts.dtype)

        partial[part, pair_span(pair), :] = jnp.dot(
            acts[0, span, :], weights[0], preferred_element_type=jnp.float32
        ).astype(partial.dtype)

    def backward(part, pair):
        span = token_span(part, pair)

        @pl.loop(0, tiles)
        def _(tile):
            cols = unit_span(tile)
            grad_hidden = against_cols(blocks[1, part, pair_span(pair), :], weights[0, cols, :])
            for member in (1, 2):
                acts[member, span, cols] = (
                    grad_hidden * acts[member, span, cols].astype(jnp.float32)
                ).astype(acts.dtype)

        partial[part, pair_span(pair), :] = (
            jnp.dot(acts[1, span, :], weights[1], preferred_element_type=jnp.float32)
            + jnp.dot(acts[2, span, :], weights[2], preferred_element_type=jnp.float32)
        ).astype(partial.dtype)

    def output_half(part):
        out = slice(part * rows, (part + 1) * rows)
        feed = back_ref[out, :]
        upstream = upstream_ref[out, :].astype(jnp.float32)
        gain = gain_ref[3:4, :]
        inverse = lax.rsqrt(jnp.mean(feed * feed, axis=-1, keepdims=True) + NORM_EPS)
        scaled = upstream * gain
        inner = jnp.mean(scaled * feed, axis=-1, keepdims=True)
        blocks[1, part, block_span(place), :] = (
            inverse * scaled - feed * inverse * inverse * inverse * inner
        ).astype(blocks.dtype)
        gather_start(1, part, 0)
        gain_grad = jnp.sum(upstream * feed * inverse, axis=0, keepdims=True)
        if part == 0:
            gain_grad_ref[...] = gain_grad
        else:
            gain_grad_ref[...] += gain_grad
        out_ref[out, :] = (middle_ref[out, :] + feed * inverse * gain).astype(out_ref.dtype)

    def sibling_copy(member):
        return pltpu.make_async_remote_copy(
            src_ref=sibling_out.at[member],
            dst_ref=sibling_in.at[member],
            send_sem=sibling_send.at[member],
            recv_sem=sibling_recv.at[member],
            device_id=sibling,
            device_id_type=MESH,
        )

    def store_copy(member):
        return pltpu.make_async_copy(
            sibling_in.at[member], grads_ref.at[member], store_sems.at[member]
        )

    cuts = [(start, min(512, half - start)) for start in range(0, half, 512)]

    def far_grad(part, member):
        tokens = line * rows
        trailing = jnp.where(member == 0, 1, 0)
        for start, size in cuts:
            span = slice(start, start + size)
            piece = cross_rows(
                acts[member, part * tokens : (part + 1) * tokens, half + start : half + start + size],
                blocks[trailing, part],
            )
            if part == 1:
                piece = piece + sibling_out[member, span, :].astype(jnp.float32)
            sibling_out[member, span, :] = piece.astype(sibling_out.dtype)
        if part == 1:
            sibling_copy(member).start()

    first_spans = [halving_spans(rep, bits, part, half // 2)[0] for part in range(2)]

    def halve(member, part):
        partner, keep, give, size = first_spans[part]
        return pltpu.make_async_remote_copy(
            src_ref=sibling_in.at[member, at_rows(give, size)],
            dst_ref=landing.at[member, part],
            send_sem=half_send.at[member, part],
            recv_sem=half_recv.at[member, part],
            device_id=(partner, shard),
            device_id_type=MESH,
        )

    def near_grad(member):
        trailing = jnp.where(member == 0, 1, 0)
        sibling_copy(member).wait_recv()
        for start, size in cuts:
            span = slice(start, start + size)
            piece = cross_rows(
                acts[member, :, span], blocks[trailing].reshape(2 * line * rows, width)
            )
            sibling_in[member, span, :] = (
                sibling_in[member, span, :].astype(jnp.float32) + piece
            ).astype(sibling_in.dtype)

        @pl.when(member < EARLY)
        def _():
            for part in range(2):
                halve(member, part).start()

        @pl.when(member >= EARLY)
        def _():
            store_copy(member).start()

    def share(turn, count, turns):
        return lax.div(turn * count, turns), lax.div((turn + 1) * count, turns)

    def first_grads(turn):
        @pl.when(turn < line - 1)
        def _():
            @pl.loop(*share(turn - 1, 3, line - 2))
            def _(member):
                far_grad(0, member)

    def last_grads(turn):
        @pl.loop(*share(turn, 6, line - 1))
        def _(unit):
            @pl.when(unit < 3)
            def _():
                far_grad(1, unit)

            @pl.when(unit >= 3)
            def _():
                near_grad(unit - 3)

    def turn_around(part):
        chain_finish(0, part)
        output_half(part)

    gather_start(0, 0, 0)
    load.wait()
    sweep(0, 0, forward, last=lambda: gather_start(0, 1, 0))
    chain_turn(0, 0, 0)
    sweep(0, 1, forward, reduce=(0, 0), last=lambda: turn_around(0))
    chain_turn(0, 1, 0)
    chain_drain(0, 0)
    sweep(1, 0, backward, reduce=(0, 1), last=lambda: turn_around(1))
    chain_turn(1, 0, 0)
    chain_drain(0, 1)
    sweep(1, 1, backward, reduce=(1, 0), beside=first_grads)
    chain_turn(1, 1, 0)
    chain_finish(1, 0)

    @pl.loop(0, line - 1)
    def _(turn):
        @pl.when(turn > 0)
        def _():
            chain_turn(1, 1, turn)

        last_grads(turn)

    chain_finish(1, 1)
    for member in range(EARLY):
        for part in range(2):
            halve(member, part).wait_recv()
            partner, keep, give, size = first_spans[part]
            kept = at_rows(keep, size)
            sibling_in[member, kept, :] = (
                sibling_in[member, kept, :].astype(jnp.float32)
                + landing[member, part].astype(jnp.float32)
            ).astype(sibling_in.dtype)
        store_copy(member).start()
    for part in range(2):
        for phase in range(2):
            gather_drain(phase, part)
        chain_drain(1, part)
        for member in range(EARLY):
            halve(member, part).wait_send()
    for member in range(3):
        sibling_copy(member).wait_send()
        store_copy(member).wait()


def feed_forward(line, replicas, normed, middle, upstream, gains, weights):
    rows, width = normed.shape
    half = weights.shape[1] // 2
    low = jnp.bfloat16
    full = jnp.float32
    vmem = pl.BlockSpec(memory_space=pltpu.VMEM)
    hbm = pl.BlockSpec(memory_space=pl.ANY)
    tokens = line * rows
    return pl.pallas_call(
        functools.partial(feed_kernel, line, replicas),
        out_shape=(
            jax.ShapeDtypeStruct((rows, width), low),
            jax.ShapeDtypeStruct((1, width), full),
            jax.ShapeDtypeStruct((rows, width), full),
            jax.ShapeDtypeStruct((3, half, width), low),
        ),
        in_specs=[vmem, vmem, vmem, vmem, hbm],
        out_specs=(vmem, vmem, vmem, hbm),
        scratch_shapes=[
            pltpu.VMEM((3, 2 * half, width), low),
            pltpu.VMEM((2, 2, tokens // 2, width), low),
            pltpu.VMEM((3, tokens, 2 * half), low),
            pltpu.VMEM((2, tokens // 2, width), low),
            pltpu.VMEM((2, 2, line - 1, rows // 2, width), low),
            pltpu.VMEM((3, half, width), low),
            pltpu.VMEM((3, half, width), low),
            pltpu.VMEM((EARLY, 2, half // 4, width), low),
            pltpu.SemaphoreType.DMA((1,)),
            pltpu.SemaphoreType.DMA((3,)),
            pltpu.SemaphoreType.DMA((2, 2, 2, line - 1)),
            pltpu.SemaphoreType.DMA((2, 2, 2, line - 1)),
            pltpu.SemaphoreType.DMA((2, 2, 2, line - 1)),
            pltpu.SemaphoreType.DMA((2, 2, 2, line - 1)),
            pltpu.SemaphoreType.DMA((3,)),
            pltpu.SemaphoreType.DMA((3,)),
            pltpu.SemaphoreType.DMA((EARLY, 2)),
            pltpu.SemaphoreType.DMA((EARLY, 2)),
        ],
        compiler_params=pltpu.CompilerParams(
            collective_id=0, has_side_effects=True, vmem_limit_bytes=63 * 1024 * 1024
        ),
        cost_estimate=pl.CostEstimate(
            flops=18 * tokens * 2 * half * width,
            bytes_accessed=9 * half * width * 2,
            transcendentals=tokens * 2 * half,
        ),
    )(normed, middle, upstream, gains, weights)


def back_kernel(
    line,
    replicas,
    back_hbm,
    middle_hbm,
    upstream_hbm,
    branch_hbm,
    inputs_hbm,
    normed_hbm,
    attended_hbm,
    queries_hbm,
    keys_hbm,
    values_hbm,
    cosine_hbm,
    sine_hbm,
    doc_col_ref,
    doc_row_ref,
    gains_ref,
    last_gain_ref,
    out_rows_ref,
    deal_ref,
    first_hbm,
    out_hbm,
    grads_hbm,
    first_half_hbm,
    second_half_hbm,
    qkv_hbm,
    outw_hbm,
    output_ref,
    input_grad_ref,
    w_qkv,
    w_out,
    acc,
    total,
    landing,
    late_landing,
    qkv_parts,
    qkv_pair,
    qkv_chain,
    qkv_steps,
    qkv_land,
    out_parts,
    out_pair,
    out_chain,
    out_steps,
    out_land,
    grad_rows,
    grad_keys,
    grad_values,
    pack_rows,
    send_rows,
    recv_rows,
    held,
    operand_sems,
    load_sems,
    store_sems,
    half_send,
    half_recv,
    pair_send,
    pair_recv,
    chain_send,
    chain_recv,
    step_send,
    step_recv,
    row_send,
    row_recv,
):
    rep = lax.axis_index("rep")
    shard = lax.axis_index("shard")
    shards = 2 * line
    devices = replicas * shards
    me = rep * shards + shard
    core = lax.rem(shard, 2)
    place = lax.div(shard, 2)
    sibling = (rep, shard + 1 - 2 * core)
    left = (rep, shard - 2)
    right = (rep, shard + 2)
    has_left = place > 0
    has_right = place < line - 1
    bits = replicas.bit_length() - 1
    full = jnp.float32
    rows, width = inputs_hbm.shape
    key_width = keys_hbm.shape[1]
    query_width = queries_hbm.shape[1]
    heads = query_width // key_width
    members, half_rows = acc.shape[0], acc.shape[1]
    part_rows = half_rows // 2
    peer_rows = rows // devices
    block_rows = send_rows.shape[2]
    packed = devices * block_rows
    qkv_rows = first_hbm.shape[0] // shards
    out_rows = out_hbm.shape[0] // shards

    load_qkv = pltpu.make_async_copy(first_hbm, w_qkv, load_sems.at[0])
    load_out = pltpu.make_async_copy(out_hbm, w_out, load_sems.at[1])
    load_acc = pltpu.make_async_copy(grads_hbm, acc, load_sems.at[2])
    operands = (
        back_hbm,
        middle_hbm,
        upstream_hbm,
        branch_hbm,
        inputs_hbm,
        normed_hbm,
        attended_hbm,
        queries_hbm,
        keys_hbm,
        values_hbm,
        cosine_hbm,
        sine_hbm,
    )
    operand_loads = [
        pltpu.make_async_copy(source, target, operand_sems.at[at])
        for at, (source, target) in enumerate(zip(operands, held))
    ]
    (
        back_ref,
        middle_ref,
        upstream_ref,
        branch_ref,
        inputs_ref,
        normed_ref,
        attended_ref,
        queries_ref,
        keys_ref,
        values_ref,
        cosine_ref,
        sine_ref,
    ) = held
    load_acc.start()
    for load in operand_loads:
        load.start()
    load_out.start()
    load_qkv.start()

    barrier = pltpu.get_barrier_semaphore()

    @pl.loop(1, devices)
    def _(hop):
        peer = lax.rem(me + hop, devices)
        pl.semaphore_signal(
            barrier,
            inc=1,
            device_id=(lax.div(peer, shards), lax.rem(peer, shards)),
            device_id_type=MESH,
        )

    pl.semaphore_wait(barrier, devices - 1)

    spans = [halving_spans(rep, bits, part, part_rows) for part in range(2)]

    def first_stage(member):
        return 1 if member < EARLY else 0

    def landed(member, part, stage):
        if stage == 0:
            return landing.at[member - EARLY, part]
        size = part_rows >> (stage + 1)
        return late_landing.at[member, part, pl.ds(part_rows // 2 - 2 * size, size)]

    def halve(member, part, stage):
        partner, keep, give, size = spans[part][stage]
        source = grads_hbm if stage == first_stage(member) else acc
        return pltpu.make_async_remote_copy(
            src_ref=source.at[member, at_rows(give, size)],
            dst_ref=landed(member, part, stage),
            send_sem=half_send.at[0, member, part, stage],
            recv_sem=half_recv.at[0, member, part, stage],
            device_id=(partner, shard),
            device_id_type=MESH,
        )

    def halve_add(member, part, stage):
        partner, keep, give, size = spans[part][stage]
        halve(member, part, stage).wait_recv()
        target = total if stage == bits - 1 else acc
        target[member, at_rows(keep, size), :] = (
            acc[member, at_rows(keep, size), :].astype(full)
            + landed(member, part, stage)[...].astype(full)
        ).astype(acc.dtype)

    def double(member, part, stage):
        partner, keep, give, size = spans[part][stage]
        return pltpu.make_async_remote_copy(
            src_ref=total.at[member, at_rows(keep, size)],
            dst_ref=total.at[member, at_rows(keep, size)],
            send_sem=half_send.at[1, member, part, stage],
            recv_sem=half_recv.at[1, member, part, stage],
            device_id=(partner, shard),
            device_id_type=MESH,
        )

    def double_arrive(member, part, stage):
        partner, keep, give, size = spans[part][stage]
        pltpu.make_async_remote_copy(
            src_ref=total.at[member, at_rows(give, size)],
            dst_ref=total.at[member, at_rows(give, size)],
            send_sem=half_send.at[1, member, part, stage],
            recv_sem=half_recv.at[1, member, part, stage],
            device_id=(partner, shard),
            device_id_type=MESH,
        ).wait_recv()

    def each(work):
        for member in range(members):
            for part in range(2):
                work(member, part)

    for part in range(2):
        halve(members - 1, part, first_stage(members - 1)).start()
    for member in range(members - 1):
        for part in range(2):
            halve(member, part, first_stage(member)).start()
    load_acc.wait()

    down_ids = lax.broadcasted_iota(jnp.int32, (rows, rows), 0)
    along_ids = lax.broadcasted_iota(jnp.int32, (rows, rows), 1)
    own_slots = down_ids + me * rows

    def find(source, found):
        return found + jnp.where(deal_row(deal_ref, source, rows) == own_slots, source, 0)

    found = lax.fori_loop(0, devices, find, jnp.zeros((rows, rows), jnp.int32))
    origin = jnp.sum(found, axis=1, keepdims=True)
    origin_row = jnp.sum(jnp.where(down_ids == along_ids, origin, 0), axis=0, keepdims=True)
    before = (origin_row == origin) & (down_ids < along_ids)
    back_place = origin_row * block_rows + jnp.sum(
        before.astype(jnp.int32), axis=0, keepdims=True
    )
    pack_rows[...] = (
        lax.broadcasted_iota(jnp.int32, (packed, rows), 0) == back_place
    ).astype(pack_rows.dtype)

    def row_copy(kind, hop, peer, source):
        return pltpu.make_async_remote_copy(
            src_ref=send_rows.at[kind, peer],
            dst_ref=recv_rows.at[kind, source],
            send_sem=row_send.at[kind, hop],
            recv_sem=row_recv.at[kind, hop],
            device_id=(lax.div(peer, shards), lax.rem(peer, shards)),
            device_id_type=MESH,
        )

    def send_back(kind, values):
        send_rows[kind] = (
            jnp.dot(pack_rows[...], values, preferred_element_type=full)
            .reshape(devices, block_rows, width)
            .astype(send_rows.dtype)
        )
        recv_rows[kind, me] = send_rows[kind, me]

        @pl.loop(1, devices)
        def _(hop):
            row_copy(kind, hop, lax.rem(me + hop, devices), me).start()

    send_back(0, out_rows_ref[...])

    def pair_copy(kind, parts, pair):
        return pltpu.make_async_remote_copy(
            src_ref=parts.at[1 - core],
            dst_ref=pair,
            send_sem=pair_send.at[kind],
            recv_sem=pair_recv.at[kind],
            device_id=sibling,
            device_id_type=MESH,
        )

    kinds = (
        (out_parts, out_pair, out_chain, out_steps, out_land),
        (qkv_parts, qkv_pair, qkv_chain, qkv_steps, qkv_land),
    )

    def pair_add(kind):
        parts, pair = kinds[kind][:2]
        pair_copy(kind, parts, pair).wait_recv()

        @pl.loop(0, line)
        def _(block):
            parts[core, block] = (
                parts[core, block].astype(full) + pair[block].astype(full)
            ).astype(parts.dtype)

    def chain_copy(kind, way, step, block):
        parts, _, chain = kinds[kind][:3]
        return pltpu.make_async_remote_copy(
            src_ref=parts.at[core, block],
            dst_ref=chain.at[way, step],
            send_sem=chain_send.at[kind, way, step],
            recv_sem=chain_recv.at[kind, way, step],
            device_id=left if way else right,
            device_id_type=MESH,
        )

    def chain_add(kind, way, step, block):
        parts, _, chain = kinds[kind][:3]
        chain_copy(kind, way, step, block).wait_recv()
        parts[core, block] = (
            parts[core, block].astype(full) + chain[way, step].astype(full)
        ).astype(parts.dtype)

    def chain_step(kind, turn):
        outward = turn - place

        @pl.when(outward >= 0)
        def _():
            @pl.when(has_left)
            def _():
                chain_add(kind, 0, outward, line - 1 - outward)

            chain_copy(kind, 0, outward, line - 1 - outward).start()

        inward = turn - (line - 1 - place)

        @pl.when(inward >= 0)
        def _():
            @pl.when(has_right)
            def _():
                chain_add(kind, 1, inward, inward)

            chain_copy(kind, 1, inward, inward).start()

    def chain_finish(kind):
        parts, _, _, steps, _ = kinds[kind]

        @pl.when(has_left)
        def _():
            chain_add(kind, 0, line - 1 - place, place)

        @pl.when(has_right)
        def _():
            chain_add(kind, 1, place, place)

        steps[0] = parts[core, place]

    def step_copy(kind, stage):
        steps, land = kinds[kind][3:]
        bit = stage if kind else bits - 1 - stage
        partner, _ = partner_of(rep, bit)
        return pltpu.make_async_remote_copy(
            src_ref=steps.at[stage],
            dst_ref=land.at[stage],
            send_sem=step_send.at[kind, stage],
            recv_sem=step_recv.at[kind, stage],
            device_id=(partner, shard),
            device_id_type=MESH,
        )

    def step_add(kind, stage):
        steps, land = kinds[kind][3:]
        step_copy(kind, stage).wait_recv()
        steps[stage + 1] = (steps[stage].astype(full) + land[stage].astype(full)).astype(
            steps.dtype
        )

    served = {0: 0}

    def chain_to(kind, end):
        for step in range(served[kind], end):
            chain_step(kind, step)
        served[kind] = max(end, served[kind])

    def advance(member, stage):
        for part in range(2):
            halve_add(member, part, stage)
            if stage + 1 < bits:
                halve(member, part, stage + 1).start()
            else:
                double(member, part, stage).start()

    def redouble(member, stage):
        for part in range(2):
            double_arrive(member, part, stage)
            if stage > 1:
                double(member, part, stage - 1).start()
            else:
                store_half(member, part).start()

    def store_half(member, part):
        _, keep, _, size = spans[part][0]
        return pltpu.make_async_copy(
            total.at[member, at_rows(keep, size)],
            (first_half_hbm, second_half_hbm)[part].at[member],
            store_sems.at[2 + 2 * member + part],
        )

    todo = [
        [functools.partial(advance, member, stage) for stage in range(first_stage(member), bits)]
        + [functools.partial(redouble, member, stage) for stage in range(bits - 1, 0, -1)]
        for member in range(members)
    ]

    def serve(*chosen):
        for member in chosen:
            if todo[member]:
                todo[member].pop(0)()

    for load in operand_loads:
        load.wait()
    middle = middle_ref[...]
    upstream = upstream_ref[...].astype(full)
    scale_two = rms_scale(middle)
    grad_middle_norm, gain_two = norm_backward(
        back_ref[...], middle, scale_two, gains_ref[2:3, :]
    )
    back_ref[...] = upstream + grad_middle_norm
    branch = branch_ref[...]
    grad_branch, gain_one = norm_backward(
        back_ref[...], branch, rms_scale(branch), gains_ref[1:2, :]
    )
    grad_branch = grad_branch.astype(jnp.bfloat16)
    half_query = query_width // 2
    half_shards = shards // 2
    for group in range(2):
        grad_out = cross_rows(
            attended_ref[:, group * half_query : (group + 1) * half_query], grad_branch
        )
        for offset in range(half_shards):
            member = group * half_shards + offset
            out_parts[member % 2, member // 2, 0:out_rows, :] = grad_out[
                offset * out_rows : (offset + 1) * out_rows
            ].astype(out_parts.dtype)

    pair_copy(0, out_parts, out_pair).start()
    load_out.wait()
    grad_rows[:, 0:query_width] = against_cols(grad_branch, w_out[...]).astype(grad_rows.dtype)
    grad_keys[...] = jnp.zeros_like(grad_keys)
    grad_values[...] = jnp.zeros_like(grad_values)
    half_key = key_width // 2
    pair_add(0)
    chain_to(0, 1)

    for head in range(heads):
        start = head * key_width
        cols = pl.ds(start, key_width)
        query = queries_ref[:, cols]
        key = keys_ref[...]
        allowed = (doc_col_ref[...] == doc_row_ref[...]) & (
            lax.broadcasted_iota(jnp.int32, (rows, rows), 0)
            >= lax.broadcasted_iota(jnp.int32, (rows, rows), 1)
        )
        tanh_scores = jnp.tanh(against_cols(query, key) * (HD ** (-0.5) / CAP_LIMIT))
        capped = jnp.where(allowed, CAP_LIMIT * tanh_scores, MASKED_SCORE)
        powers = jnp.exp(capped - jnp.max(capped, axis=-1, keepdims=True))
        probs = powers / jnp.sum(powers, axis=-1, keepdims=True)
        grad_att = grad_rows[:, cols]
        grad_values[...] += cross_rows(probs.astype(jnp.bfloat16), grad_att)
        grad_probs = against_cols(grad_att, values_ref[...])
        grad_capped = probs * (grad_probs - jnp.sum(probs * grad_probs, axis=-1, keepdims=True))
        grad_raw = (
            grad_capped * (1.0 - tanh_scores * tanh_scores) * HD ** (-0.5)
        ).astype(jnp.bfloat16)
        grad_keys[...] += cross_rows(grad_raw, query)
        grad_query = jnp.dot(grad_raw, key, preferred_element_type=full)
        front = grad_query[:, :half_key]
        back = grad_query[:, half_key:]
        cosine, sine = cosine_ref[...], sine_ref[...]
        grad_rows[:, pl.ds(start, half_key)] = (front * cosine + back * sine).astype(
            grad_rows.dtype
        )
        grad_rows[:, pl.ds(start + half_key, half_key)] = (
            back * cosine - front * sine
        ).astype(grad_rows.dtype)

    serve(members - 1, 0)
    chain_to(0, min(2, line - 1))
    front = grad_keys[:, :half_key]
    back = grad_keys[:, half_key:]
    cosine, sine = cosine_ref[...], sine_ref[...]
    grad_rows[:, query_width : query_width + half_key] = (
        front * cosine + back * sine
    ).astype(grad_rows.dtype)
    grad_rows[:, query_width + half_key : query_width + key_width] = (
        back * cosine - front * sine
    ).astype(grad_rows.dtype)
    grad_rows[:, query_width + key_width :] = grad_values[...].astype(grad_rows.dtype)

    load_qkv.wait()
    grad_normed = against_cols(grad_rows[...], w_qkv[...])
    inputs = inputs_ref[...].astype(full)
    grad_norm, gain_zero = norm_backward(
        grad_normed, inputs, rms_scale(inputs), gains_ref[0:1, :]
    )
    grad_inputs = (back_ref[...] + grad_norm).astype(jnp.bfloat16)
    gain_rows = jnp.concatenate(
        [
            jnp.stack([gain_zero, gain_one, gain_two, last_gain_ref[0]]),
            jnp.zeros((12, width), full),
        ]
    ).astype(jnp.bfloat16)
    for first in range(0, grad_rows.shape[1], 512):
        cols = slice(first, first + 512)
        grad_qkv = cross_rows(normed_ref[...], grad_rows[:, cols])
        for member in range(shards):
            qkv_parts[member % 2, member // 2, 0:qkv_rows, cols] = grad_qkv[
                member * qkv_rows : (member + 1) * qkv_rows
            ].astype(qkv_parts.dtype)
    for member in range(shards):
        gain_at = qkv_parts.shape[2] - 16
        qkv_parts[member % 2, member // 2, gain_at:, 0:width] = gain_rows
        qkv_parts[member % 2, member // 2, gain_at:, width:] = jnp.zeros(
            (16, qkv_parts.shape[3] - width), qkv_parts.dtype
        )
    pair_copy(1, qkv_parts, qkv_pair).start()

    send_back(1, grad_inputs)
    serve(1, members - 1)

    pair_add(1)
    chain_step(1, 0)
    chain_to(0, line - 1)
    chain_finish(0)
    step_copy(0, 0).start()
    serve(0)
    if line > 2:
        chain_step(1, 1)
    serve(1, members - 1)
    for step in range(2, line - 1):
        chain_step(1, step)
        serve(*range(members))
    chain_finish(1)
    step_copy(1, 0).start()
    while any(todo):
        serve(*range(members))
    for stage in range(bits):
        for kind in range(2):
            step_add(kind, stage)
            if stage + 1 < bits:
                step_copy(kind, stage + 1).start()
    store_small = (
        pltpu.make_async_copy(out_steps.at[bits], outw_hbm, store_sems.at[0]),
        pltpu.make_async_copy(qkv_steps.at[bits], qkv_hbm, store_sems.at[1]),
    )
    for store in store_small:
        store.start()
    own_deal = deal_row(deal_ref, me, rows)
    own_column = jnp.sum(jnp.where(down_ids == along_ids, own_deal, 0), axis=1, keepdims=True)
    send_place = jnp.sum((own_deal < own_column).astype(jnp.int32), axis=1, keepdims=True)
    target = lax.div(send_place, peer_rows) * block_rows + lax.rem(send_place, peer_rows)
    placer = (
        lax.broadcasted_iota(jnp.int32, (rows, packed), 1) == target
    ).astype(jnp.bfloat16)
    for kind, result in enumerate((output_ref, input_grad_ref)):

        @pl.loop(1, devices)
        def _(hop, kind=kind):
            source = lax.rem(me + devices - hop, devices)
            row_copy(kind, hop, source, source).wait_recv()

        stacked = recv_rows[kind].astype(full).reshape(packed, width).astype(jnp.bfloat16)
        result[...] = jnp.dot(placer, stacked, preferred_element_type=full).astype(result.dtype)

    for kind in range(2):

        @pl.loop(1, devices)
        def _(hop, kind=kind):
            row_copy(kind, hop, lax.rem(me + hop, devices), me).wait_send()

    def sent(member, part):
        for stage in range(bits):
            if stage >= first_stage(member):
                halve(member, part, stage).wait_send()
            if stage > 0:
                double(member, part, stage).wait_send()

    each(sent)
    for kind in range(2):
        parts, pair = kinds[kind][:2]
        pair_copy(kind, parts, pair).wait_send()
        for stage in range(bits):
            step_copy(kind, stage).wait_send()

        @pl.loop(0, line - 1)
        def _(step, kind=kind):
            far = line - 1 - step

            @pl.when(far > place)
            def _():
                chain_copy(kind, 0, step, far).wait_send()

            @pl.when(step < place)
            def _():
                chain_copy(kind, 1, step, step).wait_send()

    for store in store_small:
        store.wait()
    each(lambda member, part: store_half(member, part).wait())


def back_and_reduce(line, replicas, small, first_full, out_full, ff_grads):
    inputs, normed, queries, keys = small[4], small[5], small[7], small[8]
    held = 12
    rows, width = inputs.shape
    shards = 2 * line
    devices = replicas * shards
    vmem_limit = (60 if devices <= 32 else 63) * 1024 * 1024
    block_rows = round_up(rows // devices, 8)
    bits = replicas.bit_length() - 1
    qkv_width = queries.shape[1] + 2 * keys.shape[1]
    qkv_rows = round_up(width // shards, 16) + 16
    out_rows = round_up(out_full.shape[0] // shards, 16)
    members, half_rows = ff_grads.shape[:2]
    low = jnp.bfloat16
    full = jnp.float32
    vmem = pl.BlockSpec(memory_space=pltpu.VMEM)
    hbm = pl.BlockSpec(memory_space=pl.ANY)
    dma = pltpu.SemaphoreType.DMA

    def chain_scratch(count, cols):
        return [
            pltpu.VMEM((2, line, count, cols), low),
            pltpu.VMEM((line, count, cols), low),
            pltpu.VMEM((2, line - 1, count, cols), low),
            pltpu.VMEM((bits + 1, count, cols), low),
            pltpu.VMEM((bits, count, cols), low),
        ]

    return pl.pallas_call(
        functools.partial(back_kernel, line, replicas),
        out_shape=(
            jax.ShapeDtypeStruct((members, half_rows // 4, width), low),
            jax.ShapeDtypeStruct((members, half_rows // 4, width), low),
            jax.ShapeDtypeStruct((qkv_rows, qkv_width), low),
            jax.ShapeDtypeStruct((out_rows, width), low),
            jax.ShapeDtypeStruct((rows, width), low),
            jax.ShapeDtypeStruct((rows, width), low),
        ),
        in_specs=[hbm] * held + [vmem] * (len(small) - held) + [hbm] * 3,
        out_specs=(hbm,) * 4 + (vmem,) * 2,
        scratch_shapes=[
            pltpu.VMEM((width, qkv_width), low),
            pltpu.VMEM(out_full.shape, low),
            pltpu.VMEM(ff_grads.shape, low),
            pltpu.VMEM(ff_grads.shape, low),
            pltpu.VMEM((members - EARLY, 2, half_rows // 4, width), low),
            pltpu.VMEM(
                (members, 2, half_rows // 4 - half_rows // (2 * replicas), width), low
            ),
            *chain_scratch(qkv_rows, qkv_width),
            *chain_scratch(out_rows, width),
            pltpu.VMEM((rows, qkv_width), low),
            pltpu.VMEM((rows, keys.shape[1]), full),
            pltpu.VMEM((rows, keys.shape[1]), full),
            pltpu.VMEM((devices * block_rows, rows), low),
            pltpu.VMEM((2, devices, block_rows, width), low),
            pltpu.VMEM((2, devices, block_rows, width), low),
            [pltpu.VMEM(operand.shape, operand.dtype) for operand in small[:held]],
            dma((held,)),
            dma((3,)),
            dma((2 + 2 * members,)),
            dma((2, members, 2, bits)),
            dma((2, members, 2, bits)),
            dma((2,)),
            dma((2,)),
            dma((2, 2, line - 1)),
            dma((2, 2, line - 1)),
            dma((2, bits)),
            dma((2, bits)),
            dma((2, devices)),
            dma((2, devices)),
        ],
        compiler_params=pltpu.CompilerParams(
            collective_id=1, has_side_effects=True, vmem_limit_bytes=vmem_limit
        ),
        cost_estimate=pl.CostEstimate(
            flops=16 * rows * width * qkv_width,
            bytes_accessed=4 * members * half_rows * width,
            transcendentals=2 * rows * rows * 4,
        ),
    )(*small, first_full, out_full, ff_grads)


def bring_kernel(
    line,
    replicas,
    near_weights,
    tokens_ref,
    cotangent_ref,
    deal_ref,
    gains_in,
    qkv_in,
    out_in,
    lengths_ref,
    frequency_ref,
    gu_hbm,
    down_hbm,
    inputs_ref,
    upstream_ref,
    normed_ref,
    queries_ref,
    keys_ref,
    values_ref,
    attended_ref,
    branch_ref,
    middle_ref,
    normed_two_ref,
    gains_ref,
    cosine_ref,
    sine_ref,
    doc_col_ref,
    doc_row_ref,
    qkv_hbm,
    outw_hbm,
    weights_hbm,
    w_qkv,
    w_out,
    gain_blocks,
    weights,
    tiles,
    sent,
    arrived,
    projected,
    load_sems,
    store_sems,
    row_send,
    row_recv,
    line_send,
    line_recv,
    rep_send,
    rep_recv,
    pair_send,
    pair_recv,
    gain_send,
    gain_recv,
    sibling_send,
    sibling_recv,
):
    rep = lax.axis_index("rep")
    shard = lax.axis_index("shard")
    shards = 2 * line
    devices = replicas * shards
    me = rep * shards + shard
    core = lax.rem(shard, 2)
    place = lax.div(shard, 2)
    sibling = (rep, shard + 1 - 2 * core)
    share = min(4, replicas)
    quarter = lax.rem(rep, share)
    full = jnp.float32
    low = jnp.bfloat16
    rows, width = tokens_ref.shape
    peer_rows = rows // devices
    block_rows = sent.shape[2]
    units = gu_hbm.shape[1]
    half = weights.shape[1] // 2
    tile_rows = tiles.shape[1]
    tile_count = units // tile_rows
    depth = tiles.shape[0]
    key_width = keys_ref.shape[1]
    query_width = queries_ref.shape[1]
    heads = query_width // key_width
    half_key = key_width // 2

    def tile_load(turn):
        member, at = turn // tile_count, turn % tile_count * tile_rows
        source = down_hbm if member == 0 else gu_hbm.at[member - 1]
        return pltpu.make_async_copy(
            source.at[pl.ds(at, tile_rows)], tiles.at[turn % depth], load_sems.at[turn % depth]
        )

    for turn in range(min(depth, 3 * tile_count)):
        tile_load(turn).start()

    barrier = pltpu.get_barrier_semaphore()

    @pl.loop(1, devices)
    def _(hop):
        peer = lax.rem(me + hop, devices)
        pl.semaphore_signal(
            barrier,
            inc=1,
            device_id=(lax.div(peer, shards), lax.rem(peer, shards)),
            device_id_type=MESH,
        )

    if near_weights:
        w_qkv[shard] = qkv_in[...].astype(low)

    down_ids = lax.broadcasted_iota(jnp.int32, (rows, rows), 0)
    along_ids = lax.broadcasted_iota(jnp.int32, (rows, rows), 1)
    eye = down_ids == along_ids

    def to_column(row):
        return jnp.sum(jnp.where(eye, row, 0), axis=1, keepdims=True)

    def to_row(column):
        return jnp.sum(jnp.where(eye, column, 0), axis=0, keepdims=True)

    def spread(places):
        return lax.div(places, peer_rows) * block_rows + lax.rem(places, peer_rows)

    own_deal = deal_row(deal_ref, me, rows)
    send_place = jnp.sum((to_column(own_deal) < own_deal).astype(jnp.int32), axis=0, keepdims=True)
    packed = devices * block_rows
    picker = (
        lax.broadcasted_iota(jnp.int32, (packed, rows), 0) == spread(send_place)
    ).astype(low)

    def pack(kind, source):
        sent[kind] = (
            jnp.dot(picker, source[...], preferred_element_type=full)
            .reshape(devices, block_rows, width)
            .astype(low)
        )
        arrived[kind, me] = sent[kind, me]

    pack(0, tokens_ref)
    pl.semaphore_wait(barrier, devices - 1)

    def row_copy(kind, hop, peer, source):
        return pltpu.make_async_remote_copy(
            src_ref=sent.at[kind, peer],
            dst_ref=arrived.at[kind, source],
            send_sem=row_send.at[kind, hop],
            recv_sem=row_recv.at[kind, hop],
            device_id=(lax.div(peer, shards), lax.rem(peer, shards)),
            device_id_type=MESH,
        )

    def rows_start(kind):
        @pl.loop(1, devices)
        def _(hop):
            row_copy(kind, hop, lax.rem(me + hop, devices), me).start()

    def rows_arrive(kind):
        @pl.loop(1, devices)
        def _(hop):
            source = lax.rem(me + devices - hop, devices)
            row_copy(kind, hop, source, source).wait_recv()

    gathered = (w_qkv, w_out)

    def part_of(kind, member, portion):
        buffer = gathered[kind]
        if kind == 0:
            size = buffer.shape[2] // share
            return buffer.at[member, :, pl.ds(pl.multiple_of(portion * size, LANES), size)]
        size = buffer.shape[1] // share
        return buffer.at[member, pl.ds(pl.multiple_of(portion * size, 16), size)]

    def line_copy(kind, target, source):
        part = part_of(kind, 2 * source + core, quarter)
        return pltpu.make_async_remote_copy(
            src_ref=part,
            dst_ref=part,
            send_sem=line_send.at[kind, target],
            recv_sem=line_recv.at[kind, source],
            device_id=(rep, 2 * target + core),
            device_id_type=MESH,
        )

    def rep_copy(kind, block, hop, portion):
        part = part_of(kind, 2 * block + core, portion)
        return pltpu.make_async_remote_copy(
            src_ref=part,
            dst_ref=part,
            send_sem=rep_send.at[kind, block, hop],
            recv_sem=rep_recv.at[kind, block, portion],
            device_id=(rep - quarter + lax.rem(quarter + hop, share), shard),
            device_id_type=MESH,
        )

    def pair_copy(kind, block, side):
        buffer = gathered[kind]
        return pltpu.make_async_remote_copy(
            src_ref=buffer.at[2 * block + side],
            dst_ref=buffer.at[2 * block + side],
            send_sem=pair_send.at[kind, block],
            recv_sem=pair_recv.at[kind, block],
            device_id=sibling,
            device_id_type=MESH,
        )

    def gain_copy(hop, source):
        return pltpu.make_async_remote_copy(
            src_ref=gain_blocks.at[source],
            dst_ref=gain_blocks.at[source],
            send_sem=gain_send.at[hop],
            recv_sem=gain_recv.at[hop],
            device_id=(rep, lax.rem(shard + hop, shards)),
            device_id_type=MESH,
        )

    def others():
        return [lax.rem(place + hop, line) for hop in range(1, line)]

    def line_start(kind):
        for target in others():
            line_copy(kind, target, place).start()
        pair_copy(kind, place, core).start()

    def line_pass(kind):
        for source in others():
            line_copy(kind, source, source).wait_recv()
            for hop in range(1, share):
                rep_copy(kind, source, hop, quarter).start()

    def rep_pass(kind):
        for block in others():
            for hop in range(1, share):
                rep_copy(kind, block, hop, lax.rem(quarter + hop, share)).wait_recv()
            pair_copy(kind, block, core).start()

    def pair_arrive(kind):
        for block in range(line):
            pair_copy(kind, block, 1 - core).wait_recv()

    if near_weights:
        line_start(0)
    rows_start(0)
    if near_weights:
        w_out[shard] = out_in[...].astype(low)
        line_start(1)
        gain_blocks[shard] = jnp.zeros(gain_blocks.shape[1:], low)
        gain_blocks[shard, : gains_in.shape[0], : gains_in.shape[1]] = gains_in[...].astype(low)
        for hop in range(1, shards):
            gain_copy(hop, shard).start()

    def sibling_copy(member):
        return pltpu.make_async_remote_copy(
            src_ref=weights.at[member, pl.ds(0, half)],
            dst_ref=weights.at[member, pl.ds(half, half)],
            send_sem=sibling_send.at[member],
            recv_sem=sibling_recv.at[member],
            device_id=sibling,
            device_id_type=MESH,
        )

    def cast(begin, end):
        for turn in range(begin, end):
            member, at = turn // tile_count, turn % tile_count * tile_rows
            tile_load(turn).wait()
            weights[member, at : at + tile_rows, :] = tiles[turn % depth].astype(low)
            if turn + depth < 3 * tile_count:
                tile_load(turn + depth).start()

    if half > units:
        for member in range(3):
            weights[member, units:half, :] = jnp.zeros((half - units, width), low)

    own_slots = lax.broadcasted_iota(jnp.int32, (rows, rows), 0) + me * rows

    def find(source, total):
        return total + jnp.where(deal_row(deal_ref, source, rows) == own_slots, source, 0)

    found = lax.fori_loop(0, devices, find, jnp.zeros((rows, rows), jnp.int32))
    source = jnp.sum(found, axis=1, keepdims=True)
    earlier = (to_row(source) == source) & (along_ids < down_ids)
    recv_place = source * peer_rows + jnp.sum(earlier.astype(jnp.int32), axis=1, keepdims=True)
    placer = (
        lax.broadcasted_iota(jnp.int32, (rows, packed), 1) == spread(recv_place)
    ).astype(low)

    if near_weights:
        line_pass(0)
    pack(1, cotangent_ref)
    if near_weights:
        line_pass(1)
    rows_start(1)

    ids = lax.broadcasted_iota(jnp.int32, (rows, 1), 0)
    end = jnp.int32(0)
    document = jnp.zeros((rows, 1), jnp.int32)
    begin = jnp.zeros((rows, 1), jnp.int32)
    for member in range(lengths_ref.shape[1]):
        end = end + lengths_ref[0, member]
        passed = ids >= end
        document = document + passed.astype(jnp.int32)
        begin = jnp.where(passed, end, begin)
    doc_col_ref[...] = document
    doc_row_ref[...] = to_row(document)
    angles = (ids - begin).astype(full) * frequency_ref[...]
    cosine_ref[...] = jnp.cos(angles)
    sine_ref[...] = jnp.sin(angles)
    cast(0, tile_count)
    if near_weights:
        rep_pass(0)
    sibling_copy(0).start()
    cast(tile_count, 2 * tile_count)
    sibling_copy(1).start()
    if near_weights:
        rep_pass(1)
    cast(2 * tile_count, 3 * tile_count)
    sibling_copy(2).start()
    near_stores = [
        pltpu.make_async_copy(
            weights.at[member, pl.ds(0, half)],
            weights_hbm.at[member, pl.ds(0, half)],
            store_sems.at[2 + member],
        )
        for member in range(3)
    ]
    for store in near_stores:
        store.start()

    def placed(kind):
        stacked = arrived[kind].astype(full).reshape(packed, width).astype(low)
        return jnp.dot(placer, stacked, preferred_element_type=full)

    if near_weights:
        for hop in range(1, shards):
            gain_copy(hop, lax.rem(shard + shards - hop, shards)).wait_recv()
        span = gains_in.shape[1]
        line_ids = lax.broadcasted_iota(jnp.int32, (gain_blocks.shape[2], width), 0)
        lane_ids = lax.broadcasted_iota(jnp.int32, (gain_blocks.shape[2], width), 1)
        joined = jnp.zeros((gain_blocks.shape[1], width), full)
        for member in range(shards):
            move = ((lane_ids - member * span == line_ids) & (line_ids < span)).astype(low)
            joined = joined + jnp.dot(gain_blocks[member], move, preferred_element_type=full)
        gains_ref[...] = joined[: gains_ref.shape[0]]
    else:
        gains_ref[...] = gains_in[...]
    rows_arrive(0)
    inputs = placed(0)
    inputs_ref[...] = inputs.astype(low)
    normed_ref[...] = (inputs * rms_scale(inputs) * gains_ref[0:1, :]).astype(low)
    if near_weights:
        pair_arrive(0)
        qkv_matrix = w_qkv[...].reshape(width, w_qkv.shape[2])
    else:
        qkv_matrix = qkv_in[...]
    projected[...] = jnp.dot(normed_ref[...], qkv_matrix, preferred_element_type=full)
    def turned(start):
        front = projected[:, pl.ds(start, half_key)]
        back = projected[:, pl.ds(start + half_key, half_key)]
        cosine, sine = cosine_ref[...], sine_ref[...]
        return (
            (front * cosine - back * sine).astype(low),
            (back * cosine + front * sine).astype(low),
        )

    keys_ref[:, :half_key], keys_ref[:, half_key:] = turned(query_width)
    values_ref[...] = projected[:, query_width + key_width :].astype(low)

    for head in range(heads):
        start = head * key_width
        cols = pl.ds(start, key_width)
        front, back = turned(start)
        queries_ref[:, pl.ds(start, half_key)] = front
        queries_ref[:, pl.ds(start + half_key, half_key)] = back
        allowed = (doc_col_ref[...] == doc_row_ref[...]) & (
            lax.broadcasted_iota(jnp.int32, (rows, rows), 0)
            >= lax.broadcasted_iota(jnp.int32, (rows, rows), 1)
        )
        scores = against_cols(queries_ref[:, cols], keys_ref[...]) * (HD ** (-0.5) / CAP_LIMIT)
        capped = jnp.where(allowed, CAP_LIMIT * jnp.tanh(scores), MASKED_SCORE)
        powers = jnp.exp(capped - jnp.max(capped, axis=-1, keepdims=True))
        probs = powers / jnp.sum(powers, axis=-1, keepdims=True)
        attended_ref[:, cols] = jnp.dot(
            probs.astype(low), values_ref[...], preferred_element_type=full
        ).astype(low)

    if near_weights:
        pair_arrive(1)
        out_matrix = w_out[...].reshape(query_width, width)
    else:
        out_matrix = out_in[...]
    stores = []
    if near_weights:
        stores.append(pltpu.make_async_copy(w_qkv, qkv_hbm, store_sems.at[0]))
        stores.append(pltpu.make_async_copy(w_out, outw_hbm, store_sems.at[1]))
    else:
        stores.append(pltpu.make_async_copy(qkv_in, qkv_hbm, store_sems.at[0]))
        stores.append(pltpu.make_async_copy(out_in, outw_hbm, store_sems.at[1]))
    for store in stores:
        store.start()
    for member in range(3):
        sibling_copy(member).wait_recv()
        store = pltpu.make_async_copy(
            weights.at[member, pl.ds(half, half)],
            weights_hbm.at[member, pl.ds(half, half)],
            store_sems.at[5 + member],
        )
        store.start()
        stores.append(store)
    branch = jnp.dot(attended_ref[...], out_matrix, preferred_element_type=full)
    branch_ref[...] = branch
    middle = inputs_ref[...].astype(full) + branch * rms_scale(branch) * gains_ref[1:2, :]
    middle_ref[...] = middle
    normed_two_ref[...] = (middle * rms_scale(middle) * gains_ref[2:3, :]).astype(low)
    rows_arrive(1)
    upstream_ref[...] = placed(1).astype(low)
    stores.extend(near_stores)

    for kind in range(2):

        @pl.loop(1, devices)
        def _(hop, kind=kind):
            row_copy(kind, hop, lax.rem(me + hop, devices), me).wait_send()

        if near_weights:
            for block in others():
                line_copy(kind, block, place).wait_send()
                for hop in range(1, share):
                    rep_copy(kind, block, hop, quarter).wait_send()
            for block in range(line):
                pair_copy(kind, block, core).wait_send()
    if near_weights:
        for hop in range(1, shards):
            gain_copy(hop, shard).wait_send()
    for member in range(3):
        sibling_copy(member).wait_send()
    for store in stores:
        store.wait()


def bring_and_attend(
    line, replicas, near_weights, tokens, cotangent, deal, small, gu, down, key_width
):
    gains_in, qkv_in, out_in = small[:3]
    rows, width = tokens.shape
    shards = 2 * line
    devices = replicas * shards
    share = min(4, replicas)
    block_rows = round_up(rows // devices, 8)
    units = down.shape[0]
    half = round_up(units, LANES)
    low = jnp.bfloat16
    full = jnp.float32
    vmem = pl.BlockSpec(memory_space=pltpu.VMEM)
    hbm = pl.BlockSpec(memory_space=pl.ANY)
    dma = pltpu.SemaphoreType.DMA
    qkv_width = qkv_in.shape[1]
    query_width = qkv_width - 2 * key_width
    if near_weights:
        qkv_shape = (shards, *qkv_in.shape)
        out_shape = (shards, *out_in.shape)
    else:
        qkv_shape = qkv_in.shape
        out_shape = out_in.shape
    tile_rows = max(size for size in range(16, 145, 16) if units % size == 0)
    hold = near_weights
    qkv_scratch = qkv_shape if hold else (shards, 16, LANES)
    out_scratch = out_shape if hold else (shards, 16, LANES)
    gain_lanes = round_up(width // shards, LANES) if hold else LANES

    def array(shape, dtype):
        return jax.ShapeDtypeStruct(shape, dtype)

    return pl.pallas_call(
        functools.partial(bring_kernel, line, replicas, near_weights),
        out_shape=(
            array((rows, width), low),
            array((rows, width), low),
            array((rows, width), low),
            array((rows, query_width), low),
            array((rows, key_width), low),
            array((rows, key_width), low),
            array((rows, query_width), low),
            array((rows, width), full),
            array((rows, width), full),
            array((rows, width), low),
            array((4, width), full),
            array((rows, key_width // 2), full),
            array((rows, key_width // 2), full),
            array((rows, 1), jnp.int32),
            array((1, rows), jnp.int32),
            array(qkv_shape, low),
            array(out_shape, low),
            array((3, 2 * half, width), low),
        ),
        in_specs=[vmem] * 6
        + [pl.BlockSpec(memory_space=pltpu.SMEM), vmem]
        + [hbm] * 2,
        out_specs=(vmem,) * 15 + (hbm,) * 3,
        scratch_shapes=[
            pltpu.VMEM(qkv_scratch, low),
            pltpu.VMEM(out_scratch, low),
            pltpu.VMEM((shards, 16, gain_lanes), low),
            pltpu.VMEM((3, 2 * half, width), low),
            pltpu.VMEM((4, tile_rows, width), full),
            pltpu.VMEM((2, devices, block_rows, width), low),
            pltpu.VMEM((2, devices, block_rows, width), low),
            pltpu.VMEM((rows, qkv_width), full),
            dma((4,)),
            dma((8,)),
            dma((2, devices)),
            dma((2, devices)),
            dma((2, line)),
            dma((2, line)),
            dma((2, line, share)),
            dma((2, line, share)),
            dma((2, line)),
            dma((2, line)),
            dma((shards,)),
            dma((shards,)),
            dma((3,)),
            dma((3,)),
        ],
        compiler_params=pltpu.CompilerParams(
            collective_id=2, has_side_effects=True, vmem_limit_bytes=63 * 1024 * 1024
        ),
        cost_estimate=pl.CostEstimate(
            flops=6 * rows * width * qkv_width,
            bytes_accessed=3 * units * width * 8,
            transcendentals=2 * rows * rows * 4,
        ),
    )(tokens, cotangent, deal, *small, gu, down)


def adam_half_kernel(which, first_half, second_half, *refs):
    del which
    inputs, results = refs[:6], refs[-10:]
    part, member = pl.program_id(0), pl.program_id(1)
    gradient = jnp.where(part == 0, first_half[0], second_half[0]).astype(jnp.float32)

    def step(rows_in, rows_out, rate, decay):
        master, first, second = (ref[...].reshape(gradient.shape) for ref in rows_in)
        updated, moment, square = adamw_step(master, gradient, first, second, rate, decay)
        for ref, value in zip(rows_out, (updated, moment, square, gradient, updated)):
            ref[...] = value.astype(ref.dtype).reshape(ref.shape)

    @pl.when(member == 0)
    def _():
        step(inputs[:3], results[:5], LEARN_RATES[3], DECAY_RATES[3])

    @pl.when(member > 0)
    def _():
        step(inputs[3:], results[5:], LEARN_RATES[2], DECAY_RATES[2])


def adam_half(which, halves, arrays, begun=()):
    members, half_rows, width = halves[0].shape
    tile = half_rows // 2
    down, gu = arrays[0], arrays[3]

    def down_at(part, member, sub, chosen):
        return (part * 4 + chosen[part] * 2 + jnp.where(member == 0, sub, 1), 0)

    def gu_at(part, member, sub, chosen):
        row = part * 4 + chosen[part] * 2 + jnp.where(member == 0, 0, sub)
        return (jnp.maximum(member - 1, 0), row, 0)

    def first_at(part, member, sub, chosen):
        return (jnp.where(part == 0, member, members - 1), jnp.where(part == 0, sub, 1), 0)

    def second_at(part, member, sub, chosen):
        return (jnp.where(part == 0, 0, member), jnp.where(part == 0, 0, sub), 0)

    down_block = pl.BlockSpec((tile, width), down_at)
    gu_block = pl.BlockSpec((1, tile, width), gu_at)
    half_block = (1, tile, width)
    hbm = pl.BlockSpec(memory_space=pl.ANY)
    shapes = []
    for like in (down, gu):
        shapes.extend([jax.ShapeDtypeStruct(like.shape, jnp.float32)] * 4)
        shapes.append(jax.ShapeDtypeStruct(like.shape, jnp.bfloat16))
    count = members * half_rows * width * 2
    return pl.pallas_call(
        adam_half_kernel,
        out_shape=tuple(shapes),
        grid_spec=pltpu.PrefetchScalarGridSpec(
            num_scalar_prefetch=1,
            grid=(2, members, 2),
            in_specs=[
                pl.BlockSpec(half_block, first_at),
                pl.BlockSpec(half_block, second_at),
                *[down_block] * 3,
                *[gu_block] * 3,
                *[hbm] * len(begun),
            ],
            out_specs=(*[down_block] * 5, *[gu_block] * 5),
        ),
        input_output_aliases={9 + at: at for at in range(len(begun))},
        compiler_params=pltpu.CompilerParams(vmem_limit_bytes=60 * 1024 * 1024),
        cost_estimate=pl.CostEstimate(
            flops=16 * count, bytes_accessed=32 * count, transcendentals=2 * count
        ),
    )(which, *halves, *arrays, *begun)


def local(
    tokens,
    cotangent,
    lengths,
    deal,
    w_qkv,
    w_out,
    w_gu,
    w_down,
    gains,
    first_qkv,
    first_out,
    first_gu,
    first_down,
    first_gains,
    second_qkv,
    second_out,
    second_gu,
    second_down,
    second_gains,
):
    row_count, width = tokens.shape
    shards = lax.axis_size("shard")
    replicas = lax.axis_size("rep")
    line = shards // 2
    devices = replicas * shards
    deal_blocks = deal.reshape(deal.shape[0] // LANES, LANES)
    exponent = np.arange(HD // 2, dtype=np.float32) * np.float32(-2.0 / HD)
    frequency = jnp.asarray((np.float32(ROPE_BASE) ** exponent)[None, :])
    near_weights = w_qkv.shape[0] % 16 == 0
    if near_weights:
        first_weights = (gains, w_qkv, w_out)
    else:
        first_weights = (
            lax.all_gather(gains.astype(jnp.bfloat16), "shard", axis=1, tiled=True).astype(
                jnp.float32
            ),
            lax.all_gather(w_qkv.astype(jnp.bfloat16), "shard", axis=0, tiled=True),
            lax.all_gather(w_out.astype(jnp.bfloat16), "shard", axis=0, tiled=True),
        )
    (
        inputs,
        upstream,
        normed_one,
        queries,
        key_rows,
        value_rows,
        attended,
        branch,
        middle,
        normed_two,
        gain_values,
        cosine_table,
        sine_table,
        doc_col,
        doc_row,
        full_qkv,
        full_out,
        ff_weights,
    ) = bring_and_attend(
        line,
        replicas,
        near_weights,
        tokens,
        cotangent,
        deal_blocks,
        (*first_weights, lengths, frequency),
        w_gu,
        w_down,
        HD,
    )
    full_qkv = full_qkv.reshape(width, w_qkv.shape[1])
    full_out = full_out.reshape(H * HD, width)
    output_rows, last_gain_grad, grad_normed_two, ff_grads = feed_forward(
        line,
        replicas,
        normed_two,
        middle,
        upstream,
        gain_values,
        ff_weights,
    )
    first_half, second_half, qkv_sums, out_sums, output, input_grad = back_and_reduce(
        line,
        replicas,
        (
            grad_normed_two,
            middle,
            upstream,
            branch,
            inputs,
            normed_one,
            attended,
            queries,
            key_rows,
            value_rows,
            cosine_table,
            sine_table,
            doc_col,
            doc_row,
            gain_values,
            last_gain_grad,
            output_rows,
            deal_blocks,
        ),
        full_qkv,
        full_out,
        ff_grads,
    )
    bits = replicas.bit_length() - 1
    flips = (1, 1 << (bits - 1))
    other_halves = tuple(
        lax.ppermute(half, "rep", [(member, member ^ flip) for member in range(replicas)])
        for half, flip in zip((first_half, second_half), flips)
    )
    rep = lax.axis_index("rep")
    held = jnp.stack([lax.rem(lax.div(rep, flip), 2) for flip in flips]).astype(jnp.int32)
    ff_arrays = (w_down, first_down, second_down, w_gu, first_gu, second_gu)
    begun = adam_half(held, (first_half, second_half), ff_arrays)
    (
        new_down,
        moment_down,
        square_down,
        summed_down,
        copy_down,
        new_gu,
        moment_gu,
        square_gu,
        summed_gu,
        copy_gu,
    ) = adam_half(1 - held, other_halves, ff_arrays, begun)
    summed_qkv = qkv_sums[: w_qkv.shape[0]].astype(jnp.float32)
    summed_out = out_sums[: w_out.shape[0]].astype(jnp.float32)
    gain_span = gains.shape[1]
    summed_gains = lax.dynamic_slice(
        qkv_sums,
        (qkv_sums.shape[0] - 16, lax.axis_index("shard") * gain_span),
        (gains.shape[0], gain_span),
    ).astype(jnp.float32)
    new_qkv, moment_qkv, square_qkv = adamw_step(
        w_qkv, summed_qkv, first_qkv, second_qkv, LEARN_RATES[0], DECAY_RATES[0]
    )
    new_out, moment_out, square_out = adamw_step(
        w_out, summed_out, first_out, second_out, LEARN_RATES[1], DECAY_RATES[1]
    )
    new_gains, moment_gains, square_gains = adamw_step(
        gains, summed_gains, first_gains, second_gains, LEARN_RATES[4], DECAY_RATES[4]
    )
    return (
        output,
        input_grad,
        new_qkv,
        new_out,
        new_gu,
        new_down,
        new_gains,
        moment_qkv,
        moment_out,
        moment_gu,
        moment_down,
        moment_gains,
        square_qkv,
        square_out,
        square_gu,
        square_down,
        square_gains,
        summed_qkv,
        summed_out,
        summed_gu,
        summed_down,
        summed_gains,
        new_qkv.astype(jnp.bfloat16),
        new_out.astype(jnp.bfloat16),
        copy_gu,
        copy_down,
        new_gains.astype(jnp.bfloat16),
    )


def solution(mesh):
    placed = (
        P(("rep", "shard"), None),
        P(("rep", "shard"), None),
        P(("rep", "shard"), None),
        P(),
        P("shard", None),
        P("shard", None),
        P(None, "shard", None),
        P("shard", None),
        P(None, "shard"),
        P("shard", None),
        P("shard", None),
        P(None, "shard", None),
        P("shard", None),
        P(None, "shard"),
        P("shard", None),
        P("shard", None),
        P(None, "shard", None),
        P("shard", None),
        P(None, "shard"),
    )
    return jax.shard_map(
        local,
        mesh=mesh,
        in_specs=placed,
        out_specs=(
            P(("rep", "shard"), None),
            P(("rep", "shard"), None),
            P("shard", None),
            P("shard", None),
            P(None, "shard", None),
            P("shard", None),
            P(None, "shard"),
            P("shard", None),
            P("shard", None),
            P(None, "shard", None),
            P("shard", None),
            P(None, "shard"),
            P("shard", None),
            P("shard", None),
            P(None, "shard", None),
            P("shard", None),
            P(None, "shard"),
            P("shard", None),
            P("shard", None),
            P(None, "shard", None),
            P("shard", None),
            P(None, "shard"),
            P("shard", None),
            P("shard", None),
            P(None, "shard", None),
            P("shard", None),
            P(None, "shard"),
        ),
        check_vma=False,
    )
```

```python
import functools

import jax
import jax.numpy as jnp
import numpy as np
from jax import lax
from jax.experimental import pallas as pl
from jax.experimental.pallas import tpu as pltpu
from jax.sharding import PartitionSpec as P

H = 4
KV = 1
HD = 256
STEP = 10


CAP_LIMIT = 50.0
NORM_EPS = 1e-06
ROPE_BASE = 10000.0
MASKED_SCORE = -1e30
BETA_FIRST = 0.5
BETA_SECOND = 0.5
ADAM_EPS = 1e-08
LEARN_RATES = (0.05, 0.1, 0.03, 0.012, 0.4)
DECAY_RATES = (0.1, 0.1, 0.1, 0.1, 0.0)
GELU_COEF = 0.7978845608028654
GELU_CUBIC = 0.044715


def rms_scale(values):
    return lax.rsqrt(jnp.mean(values * values, axis=-1, keepdims=True) + NORM_EPS)


def norm_backward(grad_out, values, inverse_rms, gain_row):
    scaled = grad_out * gain_row
    inner = jnp.mean(scaled * values, axis=-1, keepdims=True)
    grad_in = inverse_rms * scaled - values * inverse_rms * inverse_rms * inverse_rms * inner
    grad_gain = jnp.sum(grad_out * values * inverse_rms, axis=0)
    return (grad_in, grad_gain)


def cross_rows(leading, trailing):
    return lax.dot_general(
        leading, trailing, (((0,), (0,)), ((), ())), preferred_element_type=jnp.float32
    )


def against_cols(leading, trailing):
    return lax.dot_general(
        leading, trailing, (((1,), (1,)), ((), ())), preferred_element_type=jnp.float32
    )


def adamw_step(master, gradient, first_moment, second_moment, rate, decay):
    moment = BETA_FIRST * first_moment + (1.0 - BETA_FIRST) * gradient
    square = BETA_SECOND * second_moment + (1.0 - BETA_SECOND) * gradient * gradient
    moment_hat = moment / (1.0 - BETA_FIRST**STEP)
    square_hat = square / (1.0 - BETA_SECOND**STEP)
    updated = master - rate * (moment_hat / (jnp.sqrt(square_hat) + ADAM_EPS) + decay * master)
    return (updated, moment, square)


LANES = 128
UNIT_TILE = 256
MESH = pl.DeviceIdType.MESH


def round_up(count, step):
    return -(-count // step) * step


def partner_of(index, bit):
    value = lax.rem(lax.div(index, 1 << bit), 2)
    return index + (1 - 2 * value) * (1 << bit), value


EARLY = 2


def deal_row(deal_ref, device, rows):
    lines = rows // LANES
    return jnp.concatenate(
        [deal_ref[pl.ds(device * lines + at, 1), :] for at in range(lines)], axis=1
    )


def halving_spans(rep, bits, part, part_rows):
    spans = []
    first = part * part_rows
    size = part_rows
    for bit in range(bits) if part == 0 else range(bits - 1, -1, -1):
        size //= 2
        partner, value = partner_of(rep, bit)
        spans.append((partner, first + value * size, first + (1 - value) * size, size))
        first = first + value * size
    return spans


def at_rows(first, size):
    return pl.ds(pl.multiple_of(first, 16), size)


def feed_kernel(
    line,
    replicas,
    own_rows,
    middle_ref,
    upstream_ref,
    gain_ref,
    weights_hbm,
    out_ref,
    gain_grad_ref,
    back_ref,
    grads_ref,
    weights,
    blocks,
    acts,
    partial,
    chain,
    sibling_out,
    sibling_in,
    landing,
    load_sems,
    store_sems,
    gather_send,
    gather_recv,
    chain_send,
    chain_recv,
    sibling_send,
    sibling_recv,
    half_send,
    half_recv,
):
    rep = lax.axis_index("rep")
    shard = lax.axis_index("shard")
    core = lax.rem(shard, 2)
    place = lax.div(shard, 2)
    sibling = (rep, shard + 1 - 2 * core)
    left = (rep, shard - 2)
    right = (rep, shard + 2)
    has_left = place > 0
    has_right = place < line - 1
    rows = own_rows.shape[0] // 2
    width = own_rows.shape[1]
    half = weights.shape[1] // 2
    tiles = 2 * half // UNIT_TILE

    load = pltpu.make_async_copy(weights_hbm, weights, load_sems.at[0])
    load.start()

    barrier = pltpu.get_barrier_semaphore()
    pl.semaphore_signal(barrier, inc=1, device_id=sibling, device_id_type=MESH)

    @pl.when(has_left)
    def _():
        pl.semaphore_signal(barrier, inc=1, device_id=left, device_id_type=MESH)

    @pl.when(has_right)
    def _():
        pl.semaphore_signal(barrier, inc=1, device_id=right, device_id_type=MESH)

    bits = replicas.bit_length() - 1
    greeted = sorted({0, bits - 1})
    for bit in greeted:
        partner, _ = partner_of(rep, bit)
        pl.semaphore_signal(barrier, inc=1, device_id=(partner, shard), device_id_type=MESH)

    def block_span(block):
        return pl.ds(pl.multiple_of(block * rows, rows), rows)

    for part in range(2):
        blocks[0, part, block_span(place), :] = own_rows[part * rows : (part + 1) * rows, :]

    pl.semaphore_wait(
        barrier,
        1 + len(greeted) + has_left.astype(jnp.int32) + has_right.astype(jnp.int32),
    )

    def gather_copy(phase, part, way, step, block):
        return pltpu.make_async_remote_copy(
            src_ref=blocks.at[phase, part, block_span(block)],
            dst_ref=blocks.at[phase, part, block_span(block)],
            send_sem=gather_send.at[phase, part, way, step],
            recv_sem=gather_recv.at[phase, part, way, step],
            device_id=left if way else right,
            device_id_type=MESH,
        )

    def gather_start(phase, part, step):
        @pl.when(has_right & (place - step >= 0))
        def _():
            gather_copy(phase, part, 0, step, place - step).start()

        @pl.when(has_left & (place + step <= line - 1))
        def _():
            gather_copy(phase, part, 1, step, place + step).start()

    def gather_arrive(phase, part, step):
        @pl.when(place - 1 - step >= 0)
        def _():
            gather_copy(phase, part, 0, step, place - 1 - step).wait_recv()

        @pl.when(place + 1 + step <= line - 1)
        def _():
            gather_copy(phase, part, 1, step, place + 1 + step).wait_recv()

    def gather_drain(phase, part):
        @pl.loop(0, line - 1)
        def _(step):
            @pl.when(has_right & (place - step >= 0))
            def _():
                gather_copy(phase, part, 0, step, place - step).wait_send()

            @pl.when(has_left & (place + step <= line - 1))
            def _():
                gather_copy(phase, part, 1, step, place + step).wait_send()

    def chain_copy(phase, part, way, packet, block):
        return pltpu.make_async_remote_copy(
            src_ref=partial.at[part, block_span(block)],
            dst_ref=chain.at[part, way, packet],
            send_sem=chain_send.at[phase, part, way, packet],
            recv_sem=chain_recv.at[phase, part, way, packet],
            device_id=left if way else right,
            device_id_type=MESH,
        )

    def chain_add(phase, part, way, packet, block):
        chain_copy(phase, part, way, packet, block).wait_recv()
        span = block_span(block)
        partial[part, span, :] = (
            partial[part, span, :].astype(jnp.float32) + chain[part, way, packet].astype(jnp.float32)
        ).astype(partial.dtype)

    def chain_turn(phase, part, turn):
        outward = turn - place

        @pl.when(outward >= 0)
        def _():
            @pl.when(has_left)
            def _():
                chain_add(phase, part, 0, outward, line - 1 - outward)

            chain_copy(phase, part, 0, outward, line - 1 - outward).start()

        inward = turn - (line - 1 - place)

        @pl.when(inward >= 0)
        def _():
            @pl.when(has_right)
            def _():
                chain_add(phase, part, 1, inward, inward)

            chain_copy(phase, part, 1, inward, inward).start()

    def chain_finish(phase, part):
        out = slice(part * rows, (part + 1) * rows)
        back_ref[out, :] = partial[part, block_span(place), :].astype(jnp.float32)

        @pl.when(has_left)
        def _():
            last = line - 1 - place
            chain_copy(phase, part, 0, last, place).wait_recv()
            back_ref[out, :] += chain[part, 0, last].astype(jnp.float32)

        @pl.when(has_right)
        def _():
            chain_copy(phase, part, 1, place, place).wait_recv()
            back_ref[out, :] += chain[part, 1, place].astype(jnp.float32)

    def chain_drain(phase, part):
        @pl.loop(0, line - 1)
        def _(packet):
            @pl.when(line - 1 - packet > place)
            def _():
                chain_copy(phase, part, 0, packet, line - 1 - packet).wait_send()

            @pl.when(packet < place)
            def _():
                chain_copy(phase, part, 1, packet, packet).wait_send()

    def sweep(phase, part, work, reduce=None, last=None, beside=None):
        @pl.loop(1, line)
        def _(turn):
            gather_arrive(phase, part, turn - 1)

            @pl.when(turn < line - 1)
            def _():
                gather_start(phase, part, turn)
                if reduce is not None:
                    chain_turn(*reduce, turn)

            if last is not None:

                @pl.when(turn == line - 1)
                def _():
                    last()

            @pl.loop(0, line // 2)
            def _(pair):
                ready = jnp.maximum(jnp.abs(2 * pair - place), jnp.abs(2 * pair + 1 - place))

                @pl.when(ready == turn)
                def _():
                    work(part, pair)

            if beside is not None:
                beside(turn)

    def pair_span(pair):
        return pl.ds(pl.multiple_of(pair * 2 * rows, 2 * rows), 2 * rows)

    def token_span(part, pair):
        first = part * line * rows
        return pl.ds(pl.multiple_of(first + pair * 2 * rows, 2 * rows), 2 * rows)

    def unit_span(tile):
        return pl.ds(pl.multiple_of(tile * UNIT_TILE, UNIT_TILE), UNIT_TILE)

    def forward(part, pair):
        span = token_span(part, pair)

        @pl.loop(0, tiles)
        def _(tile):
            cols = unit_span(tile)
            rows_in = blocks[0, part, pair_span(pair), :]
            gate = against_cols(rows_in, weights[1, cols, :])
            upper = against_cols(rows_in, weights[2, cols, :])
            tanh_inner = jnp.tanh(GELU_COEF * (gate + GELU_CUBIC * gate * gate * gate))
            lifted = 0.5 * (1.0 + tanh_inner)
            activated = gate * lifted
            slope = lifted + 0.5 * gate * (1.0 - tanh_inner * tanh_inner) * GELU_COEF * (
                1.0 + 3.0 * GELU_CUBIC * gate * gate
            )
            acts[0, span, cols] = (activated * upper).astype(acts.dtype)
            acts[1, span, cols] = (upper * slope).astype(acts.dtype)
            acts[2, span, cols] = activated.astype(acts.dtype)

        partial[part, pair_span(pair), :] = jnp.dot(
            acts[0, span, :], weights[0], preferred_element_type=jnp.float32
        ).astype(partial.dtype)

    def backward(part, pair):
        span = token_span(part, pair)

        @pl.loop(0, tiles)
        def _(tile):
            cols = unit_span(tile)
            grad_hidden = against_cols(blocks[1, part, pair_span(pair), :], weights[0, cols, :])
            for member in (1, 2):
                acts[member, span, cols] = (
                    grad_hidden * acts[member, span, cols].astype(jnp.float32)
                ).astype(acts.dtype)

        partial[part, pair_span(pair), :] = (
            jnp.dot(acts[1, span, :], weights[1], preferred_element_type=jnp.float32)
            + jnp.dot(acts[2, span, :], weights[2], preferred_element_type=jnp.float32)
        ).astype(partial.dtype)

    def output_half(part):
        out = slice(part * rows, (part + 1) * rows)
        feed = back_ref[out, :]
        upstream = upstream_ref[out, :].astype(jnp.float32)
        gain = gain_ref[3:4, :]
        inverse = lax.rsqrt(jnp.mean(feed * feed, axis=-1, keepdims=True) + NORM_EPS)
        scaled = upstream * gain
        inner = jnp.mean(scaled * feed, axis=-1, keepdims=True)
        blocks[1, part, block_span(place), :] = (
            inverse * scaled - feed * inverse * inverse * inverse * inner
        ).astype(blocks.dtype)
        gather_start(1, part, 0)
        gain_grad = jnp.sum(upstream * feed * inverse, axis=0, keepdims=True)
        if part == 0:
            gain_grad_ref[...] = gain_grad
        else:
            gain_grad_ref[...] += gain_grad
        out_ref[out, :] = (middle_ref[out, :] + feed * inverse * gain).astype(out_ref.dtype)

    def sibling_copy(member):
        return pltpu.make_async_remote_copy(
            src_ref=sibling_out.at[member],
            dst_ref=sibling_in.at[member],
            send_sem=sibling_send.at[member],
            recv_sem=sibling_recv.at[member],
            device_id=sibling,
            device_id_type=MESH,
        )

    def store_copy(member):
        return pltpu.make_async_copy(
            sibling_in.at[member], grads_ref.at[member], store_sems.at[member]
        )

    cuts = [(start, min(512, half - start)) for start in range(0, half, 512)]

    def far_grad(part, member):
        tokens = line * rows
        trailing = jnp.where(member == 0, 1, 0)
        for start, size in cuts:
            span = slice(start, start + size)
            piece = cross_rows(
                acts[member, part * tokens : (part + 1) * tokens, half + start : half + start + size],
                blocks[trailing, part],
            )
            if part == 1:
                piece = piece + sibling_out[member, span, :].astype(jnp.float32)
            sibling_out[member, span, :] = piece.astype(sibling_out.dtype)
        if part == 1:
            sibling_copy(member).start()

    first_spans = [halving_spans(rep, bits, part, half // 2)[0] for part in range(2)]

    def halve(member, part):
        partner, keep, give, size = first_spans[part]
        return pltpu.make_async_remote_copy(
            src_ref=sibling_in.at[member, at_rows(give, size)],
            dst_ref=landing.at[member, part],
            send_sem=half_send.at[member, part],
            recv_sem=half_recv.at[member, part],
            device_id=(partner, shard),
            device_id_type=MESH,
        )

    def near_grad(member):
        trailing = jnp.where(member == 0, 1, 0)
        sibling_copy(member).wait_recv()
        for start, size in cuts:
            span = slice(start, start + size)
            piece = cross_rows(
                acts[member, :, span], blocks[trailing].reshape(2 * line * rows, width)
            )
            sibling_in[member, span, :] = (
                sibling_in[member, span, :].astype(jnp.float32) + piece
            ).astype(sibling_in.dtype)

        @pl.when(member < EARLY)
        def _():
            for part in range(2):
                halve(member, part).start()

        @pl.when(member >= EARLY)
        def _():
            store_copy(member).start()

    def share(turn, count, turns):
        return lax.div(turn * count, turns), lax.div((turn + 1) * count, turns)

    def first_grads(turn):
        @pl.when(turn < line - 1)
        def _():
            @pl.loop(*share(turn - 1, 3, line - 2))
            def _(member):
                far_grad(0, member)

    def last_grads(turn):
        @pl.loop(*share(turn, 6, line - 1))
        def _(unit):
            @pl.when(unit < 3)
            def _():
                far_grad(1, unit)

            @pl.when(unit >= 3)
            def _():
                near_grad(unit - 3)

    def turn_around(part):
        chain_finish(0, part)
        output_half(part)

    gather_start(0, 0, 0)
    load.wait()
    sweep(0, 0, forward, last=lambda: gather_start(0, 1, 0))
    chain_turn(0, 0, 0)
    sweep(0, 1, forward, reduce=(0, 0), last=lambda: turn_around(0))
    chain_turn(0, 1, 0)
    chain_drain(0, 0)
    sweep(1, 0, backward, reduce=(0, 1), last=lambda: turn_around(1))
    chain_turn(1, 0, 0)
    chain_drain(0, 1)
    sweep(1, 1, backward, reduce=(1, 0), beside=first_grads)
    chain_turn(1, 1, 0)
    chain_finish(1, 0)

    @pl.loop(0, line - 1)
    def _(turn):
        @pl.when(turn > 0)
        def _():
            chain_turn(1, 1, turn)

        last_grads(turn)

    chain_finish(1, 1)
    for member in range(EARLY):
        for part in range(2):
            halve(member, part).wait_recv()
            partner, keep, give, size = first_spans[part]
            kept = at_rows(keep, size)
            sibling_in[member, kept, :] = (
                sibling_in[member, kept, :].astype(jnp.float32)
                + landing[member, part].astype(jnp.float32)
            ).astype(sibling_in.dtype)
        store_copy(member).start()
    for part in range(2):
        for phase in range(2):
            gather_drain(phase, part)
        chain_drain(1, part)
        for member in range(EARLY):
            halve(member, part).wait_send()
    for member in range(3):
        sibling_copy(member).wait_send()
        store_copy(member).wait()


def feed_forward(line, replicas, normed, middle, upstream, gains, weights):
    rows, width = normed.shape
    half = weights.shape[1] // 2
    low = jnp.bfloat16
    full = jnp.float32
    vmem = pl.BlockSpec(memory_space=pltpu.VMEM)
    hbm = pl.BlockSpec(memory_space=pl.ANY)
    tokens = line * rows
    return pl.pallas_call(
        functools.partial(feed_kernel, line, replicas),
        out_shape=(
            jax.ShapeDtypeStruct((rows, width), low),
            jax.ShapeDtypeStruct((1, width), full),
            jax.ShapeDtypeStruct((rows, width), full),
            jax.ShapeDtypeStruct((3, half, width), low),
        ),
        in_specs=[vmem, vmem, vmem, vmem, hbm],
        out_specs=(vmem, vmem, vmem, hbm),
        scratch_shapes=[
            pltpu.VMEM((3, 2 * half, width), low),
            pltpu.VMEM((2, 2, tokens // 2, width), low),
            pltpu.VMEM((3, tokens, 2 * half), low),
            pltpu.VMEM((2, tokens // 2, width), low),
            pltpu.VMEM((2, 2, line - 1, rows // 2, width), low),
            pltpu.VMEM((3, half, width), low),
            pltpu.VMEM((3, half, width), low),
            pltpu.VMEM((EARLY, 2, half // 4, width), low),
            pltpu.SemaphoreType.DMA((1,)),
            pltpu.SemaphoreType.DMA((3,)),
            pltpu.SemaphoreType.DMA((2, 2, 2, line - 1)),
            pltpu.SemaphoreType.DMA((2, 2, 2, line - 1)),
            pltpu.SemaphoreType.DMA((2, 2, 2, line - 1)),
            pltpu.SemaphoreType.DMA((2, 2, 2, line - 1)),
            pltpu.SemaphoreType.DMA((3,)),
            pltpu.SemaphoreType.DMA((3,)),
            pltpu.SemaphoreType.DMA((EARLY, 2)),
            pltpu.SemaphoreType.DMA((EARLY, 2)),
        ],
        compiler_params=pltpu.CompilerParams(
            collective_id=0, has_side_effects=True, vmem_limit_bytes=63 * 1024 * 1024
        ),
        cost_estimate=pl.CostEstimate(
            flops=18 * tokens * 2 * half * width,
            bytes_accessed=9 * half * width * 2,
            transcendentals=tokens * 2 * half,
        ),
    )(normed, middle, upstream, gains, weights)


def back_kernel(
    line,
    replicas,
    back_hbm,
    middle_hbm,
    upstream_hbm,
    branch_hbm,
    inputs_hbm,
    normed_hbm,
    attended_hbm,
    queries_hbm,
    keys_hbm,
    values_hbm,
    cosine_hbm,
    sine_hbm,
    doc_col_ref,
    doc_row_ref,
    gains_ref,
    last_gain_ref,
    out_rows_ref,
    deal_ref,
    first_hbm,
    out_hbm,
    grads_hbm,
    first_half_hbm,
    second_half_hbm,
    qkv_hbm,
    outw_hbm,
    output_ref,
    input_grad_ref,
    w_qkv,
    w_out,
    acc,
    total,
    landing,
    late_landing,
    qkv_parts,
    qkv_pair,
    qkv_chain,
    qkv_steps,
    qkv_land,
    out_parts,
    out_pair,
    out_chain,
    out_steps,
    out_land,
    grad_rows,
    grad_keys,
    grad_values,
    pack_rows,
    send_rows,
    recv_rows,
    held,
    operand_sems,
    load_sems,
    store_sems,
    half_send,
    half_recv,
    pair_send,
    pair_recv,
    chain_send,
    chain_recv,
    step_send,
    step_recv,
    row_send,
    row_recv,
):
    rep = lax.axis_index("rep")
    shard = lax.axis_index("shard")
    shards = 2 * line
    devices = replicas * shards
    me = rep * shards + shard
    core = lax.rem(shard, 2)
    place = lax.div(shard, 2)
    sibling = (rep, shard + 1 - 2 * core)
    left = (rep, shard - 2)
    right = (rep, shard + 2)
    has_left = place > 0
    has_right = place < line - 1
    bits = replicas.bit_length() - 1
    full = jnp.float32
    rows, width = inputs_hbm.shape
    key_width = keys_hbm.shape[1]
    query_width = queries_hbm.shape[1]
    heads = query_width // key_width
    members, half_rows = acc.shape[0], acc.shape[1]
    part_rows = half_rows // 2
    peer_rows = rows // devices
    block_rows = send_rows.shape[2]
    packed = devices * block_rows
    qkv_rows = first_hbm.shape[0] // shards
    out_rows = out_hbm.shape[0] // shards

    load_qkv = pltpu.make_async_copy(first_hbm, w_qkv, load_sems.at[0])
    load_out = pltpu.make_async_copy(out_hbm, w_out, load_sems.at[1])
    load_acc = pltpu.make_async_copy(grads_hbm, acc, load_sems.at[2])
    operands = (
        back_hbm,
        middle_hbm,
        upstream_hbm,
        branch_hbm,
        inputs_hbm,
        normed_hbm,
        attended_hbm,
        queries_hbm,
        keys_hbm,
        values_hbm,
        cosine_hbm,
        sine_hbm,
    )
    operand_loads = [
        pltpu.make_async_copy(source, target, operand_sems.at[at])
        for at, (source, target) in enumerate(zip(operands, held))
    ]
    (
        back_ref,
        middle_ref,
        upstream_ref,
        branch_ref,
        inputs_ref,
        normed_ref,
        attended_ref,
        queries_ref,
        keys_ref,
        values_ref,
        cosine_ref,
        sine_ref,
    ) = held
    load_acc.start()
    for load in operand_loads:
        load.start()
    load_out.start()
    load_qkv.start()

    barrier = pltpu.get_barrier_semaphore()

    @pl.loop(1, devices)
    def _(hop):
        peer = lax.rem(me + hop, devices)
        pl.semaphore_signal(
            barrier,
            inc=1,
            device_id=(lax.div(peer, shards), lax.rem(peer, shards)),
            device_id_type=MESH,
        )

    pl.semaphore_wait(barrier, devices - 1)

    spans = [halving_spans(rep, bits, part, part_rows) for part in range(2)]

    def first_stage(member):
        return 1 if member < EARLY else 0

    def landed(member, part, stage):
        if stage == 0:
            return landing.at[member - EARLY, part]
        size = part_rows >> (stage + 1)
        return late_landing.at[member, part, pl.ds(part_rows // 2 - 2 * size, size)]

    def halve(member, part, stage):
        partner, keep, give, size = spans[part][stage]
        source = grads_hbm if stage == first_stage(member) else acc
        return pltpu.make_async_remote_copy(
            src_ref=source.at[member, at_rows(give, size)],
            dst_ref=landed(member, part, stage),
            send_sem=half_send.at[0, member, part, stage],
            recv_sem=half_recv.at[0, member, part, stage],
            device_id=(partner, shard),
            device_id_type=MESH,
        )

    def halve_add(member, part, stage):
        partner, keep, give, size = spans[part][stage]
        halve(member, part, stage).wait_recv()
        target = total if stage == bits - 1 else acc
        target[member, at_rows(keep, size), :] = (
            acc[member, at_rows(keep, size), :].astype(full)
            + landed(member, part, stage)[...].astype(full)
        ).astype(acc.dtype)

    def double(member, part, stage):
        partner, keep, give, size = spans[part][stage]
        return pltpu.make_async_remote_copy(
            src_ref=total.at[member, at_rows(keep, size)],
            dst_ref=total.at[member, at_rows(keep, size)],
            send_sem=half_send.at[1, member, part, stage],
            recv_sem=half_recv.at[1, member, part, stage],
            device_id=(partner, shard),
            device_id_type=MESH,
        )

    def double_arrive(member, part, stage):
        partner, keep, give, size = spans[part][stage]
        pltpu.make_async_remote_copy(
            src_ref=total.at[member, at_rows(give, size)],
            dst_ref=total.at[member, at_rows(give, size)],
            send_sem=half_send.at[1, member, part, stage],
            recv_sem=half_recv.at[1, member, part, stage],
            device_id=(partner, shard),
            device_id_type=MESH,
        ).wait_recv()

    def each(work):
        for member in range(members):
            for part in range(2):
                work(member, part)

    for part in range(2):
        halve(members - 1, part, first_stage(members - 1)).start()
    for member in range(members - 1):
        for part in range(2):
            halve(member, part, first_stage(member)).start()
    load_acc.wait()

    down_ids = lax.broadcasted_iota(jnp.int32, (rows, rows), 0)
    along_ids = lax.broadcasted_iota(jnp.int32, (rows, rows), 1)
    own_slots = down_ids + me * rows

    def find(source, found):
        return found + jnp.where(deal_row(deal_ref, source, rows) == own_slots, source, 0)

    found = lax.fori_loop(0, devices, find, jnp.zeros((rows, rows), jnp.int32))
    origin = jnp.sum(found, axis=1, keepdims=True)
    origin_row = jnp.sum(jnp.where(down_ids == along_ids, origin, 0), axis=0, keepdims=True)
    before = (origin_row == origin) & (down_ids < along_ids)
    back_place = origin_row * block_rows + jnp.sum(
        before.astype(jnp.int32), axis=0, keepdims=True
    )
    pack_rows[...] = (
        lax.broadcasted_iota(jnp.int32, (packed, rows), 0) == back_place
    ).astype(pack_rows.dtype)

    def row_copy(kind, hop, peer, source):
        return pltpu.make_async_remote_copy(
            src_ref=send_rows.at[kind, peer],
            dst_ref=recv_rows.at[kind, source],
            send_sem=row_send.at[kind, hop],
            recv_sem=row_recv.at[kind, hop],
            device_id=(lax.div(peer, shards), lax.rem(peer, shards)),
            device_id_type=MESH,
        )

    def send_back(kind, values):
        send_rows[kind] = (
            jnp.dot(pack_rows[...], values, preferred_element_type=full)
            .reshape(devices, block_rows, width)
            .astype(send_rows.dtype)
        )
        recv_rows[kind, me] = send_rows[kind, me]

        @pl.loop(1, devices)
        def _(hop):
            row_copy(kind, hop, lax.rem(me + hop, devices), me).start()

    send_back(0, out_rows_ref[...])

    def pair_copy(kind, parts, pair):
        return pltpu.make_async_remote_copy(
            src_ref=parts.at[1 - core],
            dst_ref=pair,
            send_sem=pair_send.at[kind],
            recv_sem=pair_recv.at[kind],
            device_id=sibling,
            device_id_type=MESH,
        )

    kinds = (
        (out_parts, out_pair, out_chain, out_steps, out_land),
        (qkv_parts, qkv_pair, qkv_chain, qkv_steps, qkv_land),
    )

    def pair_add(kind):
        parts, pair = kinds[kind][:2]
        pair_copy(kind, parts, pair).wait_recv()

        @pl.loop(0, line)
        def _(block):
            parts[core, block] = (
                parts[core, block].astype(full) + pair[block].astype(full)
            ).astype(parts.dtype)

    def chain_copy(kind, way, step, block):
        parts, _, chain = kinds[kind][:3]
        return pltpu.make_async_remote_copy(
            src_ref=parts.at[core, block],
            dst_ref=chain.at[way, step],
            send_sem=chain_send.at[kind, way, step],
            recv_sem=chain_recv.at[kind, way, step],
            device_id=left if way else right,
            device_id_type=MESH,
        )

    def chain_add(kind, way, step, block):
        parts, _, chain = kinds[kind][:3]
        chain_copy(kind, way, step, block).wait_recv()
        parts[core, block] = (
            parts[core, block].astype(full) + chain[way, step].astype(full)
        ).astype(parts.dtype)

    def chain_step(kind, turn):
        outward = turn - place

        @pl.when(outward >= 0)
        def _():
            @pl.when(has_left)
            def _():
                chain_add(kind, 0, outward, line - 1 - outward)

            chain_copy(kind, 0, outward, line - 1 - outward).start()

        inward = turn - (line - 1 - place)

        @pl.when(inward >= 0)
        def _():
            @pl.when(has_right)
            def _():
                chain_add(kind, 1, inward, inward)

            chain_copy(kind, 1, inward, inward).start()

    def chain_finish(kind):
        parts, _, _, steps, _ = kinds[kind]

        @pl.when(has_left)
        def _():
            chain_add(kind, 0, line - 1 - place, place)

        @pl.when(has_right)
        def _():
            chain_add(kind, 1, place, place)

        steps[0] = parts[core, place]

    lanes = {0: ((0, None),), 1: ((1, 0), (2, 1))}

    def columns(ref, piece):
        if piece is None:
            return ref
        size = ref.shape[1] // 2
        return ref.at[:, pl.ds(piece * size, size)]

    def step_copy(kind, stage, lane, piece):
        steps, land = kinds[kind][3:]
        partner, _ = partner_of(rep, stage if lane == 1 else bits - 1 - stage)
        return pltpu.make_async_remote_copy(
            src_ref=columns(steps.at[stage], piece),
            dst_ref=columns(land.at[stage], piece),
            send_sem=step_send.at[lane, stage],
            recv_sem=step_recv.at[lane, stage],
            device_id=(partner, shard),
            device_id_type=MESH,
        )

    def step_start(kind, stage):
        for lane, piece in lanes[kind]:
            step_copy(kind, stage, lane, piece).start()

    def step_add(kind, stage):
        steps, land = kinds[kind][3:]
        for lane, piece in lanes[kind]:
            step_copy(kind, stage, lane, piece).wait_recv()
            columns(steps.at[stage + 1], piece)[...] = (
                columns(steps.at[stage], piece)[...].astype(full)
                + columns(land.at[stage], piece)[...].astype(full)
            ).astype(steps.dtype)
            if stage + 1 < bits:
                step_copy(kind, stage + 1, lane, piece).start()

    served = {0: 0}

    def chain_to(kind, end):
        for step in range(served[kind], end):
            chain_step(kind, step)
        served[kind] = max(end, served[kind])

    def advance(member, stage):
        for part in range(2):
            halve_add(member, part, stage)
            if stage + 1 < bits:
                halve(member, part, stage + 1).start()
            else:
                double(member, part, stage).start()

    def redouble(member, stage):
        for part in range(2):
            double_arrive(member, part, stage)
            if stage > 1:
                double(member, part, stage - 1).start()
            else:
                store_half(member, part).start()

    def store_half(member, part):
        _, keep, _, size = spans[part][0]
        return pltpu.make_async_copy(
            total.at[member, at_rows(keep, size)],
            (first_half_hbm, second_half_hbm)[part].at[member],
            store_sems.at[2 + 2 * member + part],
        )

    todo = [
        [functools.partial(advance, member, stage) for stage in range(first_stage(member), bits)]
        + [functools.partial(redouble, member, stage) for stage in range(bits - 1, 0, -1)]
        for member in range(members)
    ]

    def serve(*chosen):
        for member in chosen:
            if todo[member]:
                todo[member].pop(0)()

    for load in operand_loads:
        load.wait()
    middle = middle_ref[...]
    upstream = upstream_ref[...].astype(full)
    scale_two = rms_scale(middle)
    grad_middle_norm, gain_two = norm_backward(
        back_ref[...], middle, scale_two, gains_ref[2:3, :]
    )
    back_ref[...] = upstream + grad_middle_norm
    branch = branch_ref[...]
    grad_branch, gain_one = norm_backward(
        back_ref[...], branch, rms_scale(branch), gains_ref[1:2, :]
    )
    grad_branch = grad_branch.astype(jnp.bfloat16)
    half_query = query_width // 2
    half_shards = shards // 2
    for group in range(2):
        grad_out = cross_rows(
            attended_ref[:, group * half_query : (group + 1) * half_query], grad_branch
        )
        for offset in range(half_shards):
            member = group * half_shards + offset
            out_parts[member % 2, member // 2, 0:out_rows, :] = grad_out[
                offset * out_rows : (offset + 1) * out_rows
            ].astype(out_parts.dtype)

    pair_copy(0, out_parts, out_pair).start()
    load_out.wait()
    grad_rows[:, 0:query_width] = against_cols(grad_branch, w_out[...]).astype(grad_rows.dtype)
    grad_keys[...] = jnp.zeros_like(grad_keys)
    grad_values[...] = jnp.zeros_like(grad_values)
    half_key = key_width // 2
    pair_add(0)
    chain_to(0, 1)

    for head in range(heads):
        start = head * key_width
        cols = pl.ds(start, key_width)
        query = queries_ref[:, cols]
        key = keys_ref[...]
        allowed = (doc_col_ref[...] == doc_row_ref[...]) & (
            lax.broadcasted_iota(jnp.int32, (rows, rows), 0)
            >= lax.broadcasted_iota(jnp.int32, (rows, rows), 1)
        )
        tanh_scores = jnp.tanh(against_cols(query, key) * (HD ** (-0.5) / CAP_LIMIT))
        capped = jnp.where(allowed, CAP_LIMIT * tanh_scores, MASKED_SCORE)
        powers = jnp.exp(capped - jnp.max(capped, axis=-1, keepdims=True))
        probs = powers / jnp.sum(powers, axis=-1, keepdims=True)
        grad_att = grad_rows[:, cols]
        grad_values[...] += cross_rows(probs.astype(jnp.bfloat16), grad_att)
        grad_probs = against_cols(grad_att, values_ref[...])
        grad_capped = probs * (grad_probs - jnp.sum(probs * grad_probs, axis=-1, keepdims=True))
        grad_raw = (
            grad_capped * (1.0 - tanh_scores * tanh_scores) * HD ** (-0.5)
        ).astype(jnp.bfloat16)
        grad_keys[...] += cross_rows(grad_raw, query)
        grad_query = jnp.dot(grad_raw, key, preferred_element_type=full)
        front = grad_query[:, :half_key]
        back = grad_query[:, half_key:]
        cosine, sine = cosine_ref[...], sine_ref[...]
        grad_rows[:, pl.ds(start, half_key)] = (front * cosine + back * sine).astype(
            grad_rows.dtype
        )
        grad_rows[:, pl.ds(start + half_key, half_key)] = (
            back * cosine - front * sine
        ).astype(grad_rows.dtype)

    serve(members - 1, 0)
    chain_to(0, min(2, line - 1))
    front = grad_keys[:, :half_key]
    back = grad_keys[:, half_key:]
    cosine, sine = cosine_ref[...], sine_ref[...]
    grad_rows[:, query_width : query_width + half_key] = (
        front * cosine + back * sine
    ).astype(grad_rows.dtype)
    grad_rows[:, query_width + half_key : query_width + key_width] = (
        back * cosine - front * sine
    ).astype(grad_rows.dtype)
    grad_rows[:, query_width + key_width :] = grad_values[...].astype(grad_rows.dtype)

    load_qkv.wait()
    grad_normed = against_cols(grad_rows[...], w_qkv[...])
    inputs = inputs_ref[...].astype(full)
    grad_norm, gain_zero = norm_backward(
        grad_normed, inputs, rms_scale(inputs), gains_ref[0:1, :]
    )
    grad_inputs = (back_ref[...] + grad_norm).astype(jnp.bfloat16)
    gain_rows = jnp.concatenate(
        [
            jnp.stack([gain_zero, gain_one, gain_two, last_gain_ref[0]]),
            jnp.zeros((12, width), full),
        ]
    ).astype(jnp.bfloat16)
    for first in range(0, grad_rows.shape[1], 512):
        cols = slice(first, first + 512)
        grad_qkv = cross_rows(normed_ref[...], grad_rows[:, cols])
        for member in range(shards):
            qkv_parts[member % 2, member // 2, 0:qkv_rows, cols] = grad_qkv[
                member * qkv_rows : (member + 1) * qkv_rows
            ].astype(qkv_parts.dtype)
    for member in range(shards):
        gain_at = qkv_parts.shape[2] - 16
        qkv_parts[member % 2, member // 2, gain_at:, 0:width] = gain_rows
        qkv_parts[member % 2, member // 2, gain_at:, width:] = jnp.zeros(
            (16, qkv_parts.shape[3] - width), qkv_parts.dtype
        )
    pair_copy(1, qkv_parts, qkv_pair).start()

    send_back(1, grad_inputs)
    serve(1, members - 1)

    pair_add(1)
    chain_step(1, 0)
    chain_to(0, line - 1)
    chain_finish(0)
    step_start(0, 0)
    serve(0)
    if line > 2:
        chain_step(1, 1)
    serve(1, members - 1)
    for step in range(2, line - 1):
        chain_step(1, step)
        serve(*range(members))
    chain_finish(1)
    step_start(1, 0)
    for stage in range(bits):
        serve(*range(members))
        for kind in range(2):
            step_add(kind, stage)
    while any(todo):
        serve(*range(members))
    store_small = (
        pltpu.make_async_copy(out_steps.at[bits], outw_hbm, store_sems.at[0]),
        pltpu.make_async_copy(qkv_steps.at[bits], qkv_hbm, store_sems.at[1]),
    )
    for store in store_small:
        store.start()
    own_deal = deal_row(deal_ref, me, rows)
    own_column = jnp.sum(jnp.where(down_ids == along_ids, own_deal, 0), axis=1, keepdims=True)
    send_place = jnp.sum((own_deal < own_column).astype(jnp.int32), axis=1, keepdims=True)
    target = lax.div(send_place, peer_rows) * block_rows + lax.rem(send_place, peer_rows)
    placer = (
        lax.broadcasted_iota(jnp.int32, (rows, packed), 1) == target
    ).astype(jnp.bfloat16)
    for kind, result in enumerate((output_ref, input_grad_ref)):

        @pl.loop(1, devices)
        def _(hop, kind=kind):
            source = lax.rem(me + devices - hop, devices)
            row_copy(kind, hop, source, source).wait_recv()

        stacked = recv_rows[kind].astype(full).reshape(packed, width).astype(jnp.bfloat16)
        result[...] = jnp.dot(placer, stacked, preferred_element_type=full).astype(result.dtype)

    for kind in range(2):

        @pl.loop(1, devices)
        def _(hop, kind=kind):
            row_copy(kind, hop, lax.rem(me + hop, devices), me).wait_send()

    def sent(member, part):
        for stage in range(bits):
            if stage >= first_stage(member):
                halve(member, part, stage).wait_send()
            if stage > 0:
                double(member, part, stage).wait_send()

    each(sent)
    for kind in range(2):
        parts, pair = kinds[kind][:2]
        pair_copy(kind, parts, pair).wait_send()
        for stage in range(bits):
            for lane, piece in lanes[kind]:
                step_copy(kind, stage, lane, piece).wait_send()

        @pl.loop(0, line - 1)
        def _(step, kind=kind):
            far = line - 1 - step

            @pl.when(far > place)
            def _():
                chain_copy(kind, 0, step, far).wait_send()

            @pl.when(step < place)
            def _():
                chain_copy(kind, 1, step, step).wait_send()

    for store in store_small:
        store.wait()
    each(lambda member, part: store_half(member, part).wait())


def back_and_reduce(line, replicas, small, first_full, out_full, ff_grads):
    inputs, normed, queries, keys = small[4], small[5], small[7], small[8]
    held = 12
    rows, width = inputs.shape
    shards = 2 * line
    devices = replicas * shards
    vmem_limit = (60 if devices <= 32 else 63) * 1024 * 1024
    block_rows = round_up(rows // devices, 8)
    bits = replicas.bit_length() - 1
    qkv_width = queries.shape[1] + 2 * keys.shape[1]
    qkv_rows = round_up(width // shards, 16) + 16
    out_rows = round_up(out_full.shape[0] // shards, 16)
    members, half_rows = ff_grads.shape[:2]
    low = jnp.bfloat16
    full = jnp.float32
    vmem = pl.BlockSpec(memory_space=pltpu.VMEM)
    hbm = pl.BlockSpec(memory_space=pl.ANY)
    dma = pltpu.SemaphoreType.DMA

    def chain_scratch(count, cols):
        return [
            pltpu.VMEM((2, line, count, cols), low),
            pltpu.VMEM((line, count, cols), low),
            pltpu.VMEM((2, line - 1, count, cols), low),
            pltpu.VMEM((bits + 1, count, cols), low),
            pltpu.VMEM((bits, count, cols), low),
        ]

    return pl.pallas_call(
        functools.partial(back_kernel, line, replicas),
        out_shape=(
            jax.ShapeDtypeStruct((members, half_rows // 4, width), low),
            jax.ShapeDtypeStruct((members, half_rows // 4, width), low),
            jax.ShapeDtypeStruct((qkv_rows, qkv_width), low),
            jax.ShapeDtypeStruct((out_rows, width), low),
            jax.ShapeDtypeStruct((rows, width), low),
            jax.ShapeDtypeStruct((rows, width), low),
        ),
        in_specs=[hbm] * held + [vmem] * (len(small) - held) + [hbm] * 3,
        out_specs=(hbm,) * 4 + (vmem,) * 2,
        scratch_shapes=[
            pltpu.VMEM((width, qkv_width), low),
            pltpu.VMEM(out_full.shape, low),
            pltpu.VMEM(ff_grads.shape, low),
            pltpu.VMEM(ff_grads.shape, low),
            pltpu.VMEM((members - EARLY, 2, half_rows // 4, width), low),
            pltpu.VMEM(
                (members, 2, half_rows // 4 - half_rows // (2 * replicas), width), low
            ),
            *chain_scratch(qkv_rows, qkv_width),
            *chain_scratch(out_rows, width),
            pltpu.VMEM((rows, qkv_width), low),
            pltpu.VMEM((rows, keys.shape[1]), full),
            pltpu.VMEM((rows, keys.shape[1]), full),
            pltpu.VMEM((devices * block_rows, rows), low),
            pltpu.VMEM((2, devices, block_rows, width), low),
            pltpu.VMEM((2, devices, block_rows, width), low),
            [pltpu.VMEM(operand.shape, operand.dtype) for operand in small[:held]],
            dma((held,)),
            dma((3,)),
            dma((2 + 2 * members,)),
            dma((2, members, 2, bits)),
            dma((2, members, 2, bits)),
            dma((2,)),
            dma((2,)),
            dma((2, 2, line - 1)),
            dma((2, 2, line - 1)),
            dma((3, bits)),
            dma((3, bits)),
            dma((2, devices)),
            dma((2, devices)),
        ],
        compiler_params=pltpu.CompilerParams(
            collective_id=1, has_side_effects=True, vmem_limit_bytes=vmem_limit
        ),
        cost_estimate=pl.CostEstimate(
            flops=16 * rows * width * qkv_width,
            bytes_accessed=4 * members * half_rows * width,
            transcendentals=2 * rows * rows * 4,
        ),
    )(*small, first_full, out_full, ff_grads)


def bring_kernel(
    line,
    replicas,
    near_weights,
    tokens_ref,
    cotangent_ref,
    deal_ref,
    gains_in,
    qkv_in,
    out_in,
    lengths_ref,
    frequency_ref,
    gu_hbm,
    down_hbm,
    inputs_ref,
    upstream_ref,
    normed_ref,
    queries_ref,
    keys_ref,
    values_ref,
    attended_ref,
    branch_ref,
    middle_ref,
    normed_two_ref,
    gains_ref,
    cosine_ref,
    sine_ref,
    doc_col_ref,
    doc_row_ref,
    qkv_hbm,
    outw_hbm,
    weights_hbm,
    w_qkv,
    w_out,
    gain_blocks,
    weights,
    tiles,
    sent,
    arrived,
    projected,
    load_sems,
    store_sems,
    row_send,
    row_recv,
    line_send,
    line_recv,
    rep_send,
    rep_recv,
    pair_send,
    pair_recv,
    gain_send,
    gain_recv,
    sibling_send,
    sibling_recv,
):
    rep = lax.axis_index("rep")
    shard = lax.axis_index("shard")
    shards = 2 * line
    devices = replicas * shards
    me = rep * shards + shard
    core = lax.rem(shard, 2)
    place = lax.div(shard, 2)
    sibling = (rep, shard + 1 - 2 * core)
    share = min(4, replicas)
    quarter = lax.rem(rep, share)
    full = jnp.float32
    low = jnp.bfloat16
    rows, width = tokens_ref.shape
    peer_rows = rows // devices
    block_rows = sent.shape[2]
    units = gu_hbm.shape[1]
    half = weights.shape[1] // 2
    tile_rows = tiles.shape[1]
    tile_count = units // tile_rows
    depth = tiles.shape[0]
    key_width = keys_ref.shape[1]
    query_width = queries_ref.shape[1]
    heads = query_width // key_width
    half_key = key_width // 2

    def tile_load(turn):
        member, at = turn // tile_count, turn % tile_count * tile_rows
        source = down_hbm if member == 0 else gu_hbm.at[member - 1]
        return pltpu.make_async_copy(
            source.at[pl.ds(at, tile_rows)], tiles.at[turn % depth], load_sems.at[turn % depth]
        )

    for turn in range(min(depth, 3 * tile_count)):
        tile_load(turn).start()

    barrier = pltpu.get_barrier_semaphore()

    @pl.loop(1, devices)
    def _(hop):
        peer = lax.rem(me + hop, devices)
        pl.semaphore_signal(
            barrier,
            inc=1,
            device_id=(lax.div(peer, shards), lax.rem(peer, shards)),
            device_id_type=MESH,
        )

    if near_weights:
        w_qkv[shard] = qkv_in[...].astype(low)

    down_ids = lax.broadcasted_iota(jnp.int32, (rows, rows), 0)
    along_ids = lax.broadcasted_iota(jnp.int32, (rows, rows), 1)
    eye = down_ids == along_ids

    def to_column(row):
        return jnp.sum(jnp.where(eye, row, 0), axis=1, keepdims=True)

    def to_row(column):
        return jnp.sum(jnp.where(eye, column, 0), axis=0, keepdims=True)

    def spread(places):
        return lax.div(places, peer_rows) * block_rows + lax.rem(places, peer_rows)

    own_deal = deal_row(deal_ref, me, rows)
    send_place = jnp.sum((to_column(own_deal) < own_deal).astype(jnp.int32), axis=0, keepdims=True)
    packed = devices * block_rows
    picker = (
        lax.broadcasted_iota(jnp.int32, (packed, rows), 0) == spread(send_place)
    ).astype(low)

    def pack(kind, source):
        sent[kind] = (
            jnp.dot(picker, source[...], preferred_element_type=full)
            .reshape(devices, block_rows, width)
            .astype(low)
        )
        arrived[kind, me] = sent[kind, me]

    pack(0, tokens_ref)
    pl.semaphore_wait(barrier, devices - 1)

    def row_copy(kind, hop, peer, source):
        return pltpu.make_async_remote_copy(
            src_ref=sent.at[kind, peer],
            dst_ref=arrived.at[kind, source],
            send_sem=row_send.at[kind, hop],
            recv_sem=row_recv.at[kind, hop],
            device_id=(lax.div(peer, shards), lax.rem(peer, shards)),
            device_id_type=MESH,
        )

    def rows_start(kind):
        @pl.loop(1, devices)
        def _(hop):
            row_copy(kind, hop, lax.rem(me + hop, devices), me).start()

    def rows_arrive(kind):
        @pl.loop(1, devices)
        def _(hop):
            source = lax.rem(me + devices - hop, devices)
            row_copy(kind, hop, source, source).wait_recv()

    gathered = (w_qkv, w_out)

    def part_of(kind, member, portion):
        buffer = gathered[kind]
        if kind == 0:
            size = buffer.shape[2] // share
            return buffer.at[member, :, pl.ds(pl.multiple_of(portion * size, LANES), size)]
        size = buffer.shape[1] // share
        return buffer.at[member, pl.ds(pl.multiple_of(portion * size, 16), size)]

    def line_copy(kind, target, source):
        part = part_of(kind, 2 * source + core, quarter)
        return pltpu.make_async_remote_copy(
            src_ref=part,
            dst_ref=part,
            send_sem=line_send.at[kind, target],
            recv_sem=line_recv.at[kind, source],
            device_id=(rep, 2 * target + core),
            device_id_type=MESH,
        )

    def rep_copy(kind, block, hop, portion):
        part = part_of(kind, 2 * block + core, portion)
        return pltpu.make_async_remote_copy(
            src_ref=part,
            dst_ref=part,
            send_sem=rep_send.at[kind, block, hop],
            recv_sem=rep_recv.at[kind, block, portion],
            device_id=(rep - quarter + lax.rem(quarter + hop, share), shard),
            device_id_type=MESH,
        )

    def pair_copy(kind, block, side):
        buffer = gathered[kind]
        return pltpu.make_async_remote_copy(
            src_ref=buffer.at[2 * block + side],
            dst_ref=buffer.at[2 * block + side],
            send_sem=pair_send.at[kind, block],
            recv_sem=pair_recv.at[kind, block],
            device_id=sibling,
            device_id_type=MESH,
        )

    def gain_copy(hop, source):
        return pltpu.make_async_remote_copy(
            src_ref=gain_blocks.at[source],
            dst_ref=gain_blocks.at[source],
            send_sem=gain_send.at[hop],
            recv_sem=gain_recv.at[hop],
            device_id=(rep, lax.rem(shard + hop, shards)),
            device_id_type=MESH,
        )

    def others():
        return [lax.rem(place + hop, line) for hop in range(1, line)]

    def line_start(kind):
        for target in others():
            line_copy(kind, target, place).start()
        pair_copy(kind, place, core).start()

    def line_pass(kind):
        for source in others():
            line_copy(kind, source, source).wait_recv()
            for hop in range(1, share):
                rep_copy(kind, source, hop, quarter).start()

    def rep_pass(kind):
        for block in others():
            for hop in range(1, share):
                rep_copy(kind, block, hop, lax.rem(quarter + hop, share)).wait_recv()
            pair_copy(kind, block, core).start()

    def pair_arrive(kind):
        for block in range(line):
            pair_copy(kind, block, 1 - core).wait_recv()

    if near_weights:
        line_start(0)
    rows_start(0)
    if near_weights:
        w_out[shard] = out_in[...].astype(low)
        line_start(1)
        gain_blocks[shard] = jnp.zeros(gain_blocks.shape[1:], low)
        gain_blocks[shard, : gains_in.shape[0], : gains_in.shape[1]] = gains_in[...].astype(low)
        for hop in range(1, shards):
            gain_copy(hop, shard).start()

    def sibling_copy(member):
        return pltpu.make_async_remote_copy(
            src_ref=weights.at[member, pl.ds(0, half)],
            dst_ref=weights.at[member, pl.ds(half, half)],
            send_sem=sibling_send.at[member],
            recv_sem=sibling_recv.at[member],
            device_id=sibling,
            device_id_type=MESH,
        )

    def cast(begin, end):
        for turn in range(begin, end):
            member, at = turn // tile_count, turn % tile_count * tile_rows
            tile_load(turn).wait()
            weights[member, at : at + tile_rows, :] = tiles[turn % depth].astype(low)
            if turn + depth < 3 * tile_count:
                tile_load(turn + depth).start()

    if half > units:
        for member in range(3):
            weights[member, units:half, :] = jnp.zeros((half - units, width), low)

    own_slots = lax.broadcasted_iota(jnp.int32, (rows, rows), 0) + me * rows

    def find(source, total):
        return total + jnp.where(deal_row(deal_ref, source, rows) == own_slots, source, 0)

    found = lax.fori_loop(0, devices, find, jnp.zeros((rows, rows), jnp.int32))
    source = jnp.sum(found, axis=1, keepdims=True)
    earlier = (to_row(source) == source) & (along_ids < down_ids)
    recv_place = source * peer_rows + jnp.sum(earlier.astype(jnp.int32), axis=1, keepdims=True)
    placer = (
        lax.broadcasted_iota(jnp.int32, (rows, packed), 1) == spread(recv_place)
    ).astype(low)

    if near_weights:
        line_pass(0)
    pack(1, cotangent_ref)
    if near_weights:
        line_pass(1)
    rows_start(1)

    ids = lax.broadcasted_iota(jnp.int32, (rows, 1), 0)
    end = jnp.int32(0)
    document = jnp.zeros((rows, 1), jnp.int32)
    begin = jnp.zeros((rows, 1), jnp.int32)
    for member in range(lengths_ref.shape[1]):
        end = end + lengths_ref[0, member]
        passed = ids >= end
        document = document + passed.astype(jnp.int32)
        begin = jnp.where(passed, end, begin)
    doc_col_ref[...] = document
    doc_row_ref[...] = to_row(document)
    angles = (ids - begin).astype(full) * frequency_ref[...]
    cosine_ref[...] = jnp.cos(angles)
    sine_ref[...] = jnp.sin(angles)
    cast(0, tile_count)
    if near_weights:
        rep_pass(0)
    sibling_copy(0).start()
    cast(tile_count, 2 * tile_count)
    sibling_copy(1).start()
    if near_weights:
        rep_pass(1)
    cast(2 * tile_count, 3 * tile_count)
    sibling_copy(2).start()
    near_stores = [
        pltpu.make_async_copy(
            weights.at[member, pl.ds(0, half)],
            weights_hbm.at[member, pl.ds(0, half)],
            store_sems.at[2 + member],
        )
        for member in range(3)
    ]
    for store in near_stores:
        store.start()

    def placed(kind):
        stacked = arrived[kind].astype(full).reshape(packed, width).astype(low)
        return jnp.dot(placer, stacked, preferred_element_type=full)

    if near_weights:
        for hop in range(1, shards):
            gain_copy(hop, lax.rem(shard + shards - hop, shards)).wait_recv()
        span = gains_in.shape[1]
        line_ids = lax.broadcasted_iota(jnp.int32, (gain_blocks.shape[2], width), 0)
        lane_ids = lax.broadcasted_iota(jnp.int32, (gain_blocks.shape[2], width), 1)
        joined = jnp.zeros((gain_blocks.shape[1], width), full)
        for member in range(shards):
            move = ((lane_ids - member * span == line_ids) & (line_ids < span)).astype(low)
            joined = joined + jnp.dot(gain_blocks[member], move, preferred_element_type=full)
        gains_ref[...] = joined[: gains_ref.shape[0]]
    else:
        gains_ref[...] = gains_in[...]
    rows_arrive(0)
    inputs = placed(0)
    inputs_ref[...] = inputs.astype(low)
    normed_ref[...] = (inputs * rms_scale(inputs) * gains_ref[0:1, :]).astype(low)
    if near_weights:
        pair_arrive(0)
        qkv_matrix = w_qkv[...].reshape(width, w_qkv.shape[2])
    else:
        qkv_matrix = qkv_in[...]
    projected[...] = jnp.dot(normed_ref[...], qkv_matrix, preferred_element_type=full)
    def turned(start):
        front = projected[:, pl.ds(start, half_key)]
        back = projected[:, pl.ds(start + half_key, half_key)]
        cosine, sine = cosine_ref[...], sine_ref[...]
        return (
            (front * cosine - back * sine).astype(low),
            (back * cosine + front * sine).astype(low),
        )

    keys_ref[:, :half_key], keys_ref[:, half_key:] = turned(query_width)
    values_ref[...] = projected[:, query_width + key_width :].astype(low)

    for head in range(heads):
        start = head * key_width
        cols = pl.ds(start, key_width)
        front, back = turned(start)
        queries_ref[:, pl.ds(start, half_key)] = front
        queries_ref[:, pl.ds(start + half_key, half_key)] = back
        allowed = (doc_col_ref[...] == doc_row_ref[...]) & (
            lax.broadcasted_iota(jnp.int32, (rows, rows), 0)
            >= lax.broadcasted_iota(jnp.int32, (rows, rows), 1)
        )
        scores = against_cols(queries_ref[:, cols], keys_ref[...]) * (HD ** (-0.5) / CAP_LIMIT)
        capped = jnp.where(allowed, CAP_LIMIT * jnp.tanh(scores), MASKED_SCORE)
        powers = jnp.exp(capped - jnp.max(capped, axis=-1, keepdims=True))
        probs = powers / jnp.sum(powers, axis=-1, keepdims=True)
        attended_ref[:, cols] = jnp.dot(
            probs.astype(low), values_ref[...], preferred_element_type=full
        ).astype(low)

    if near_weights:
        pair_arrive(1)
        out_matrix = w_out[...].reshape(query_width, width)
    else:
        out_matrix = out_in[...]
    stores = []
    if near_weights:
        stores.append(pltpu.make_async_copy(w_qkv, qkv_hbm, store_sems.at[0]))
        stores.append(pltpu.make_async_copy(w_out, outw_hbm, store_sems.at[1]))
    else:
        stores.append(pltpu.make_async_copy(qkv_in, qkv_hbm, store_sems.at[0]))
        stores.append(pltpu.make_async_copy(out_in, outw_hbm, store_sems.at[1]))
    for store in stores:
        store.start()
    for member in range(3):
        sibling_copy(member).wait_recv()
        store = pltpu.make_async_copy(
            weights.at[member, pl.ds(half, half)],
            weights_hbm.at[member, pl.ds(half, half)],
            store_sems.at[5 + member],
        )
        store.start()
        stores.append(store)
    branch = jnp.dot(attended_ref[...], out_matrix, preferred_element_type=full)
    branch_ref[...] = branch
    middle = inputs_ref[...].astype(full) + branch * rms_scale(branch) * gains_ref[1:2, :]
    middle_ref[...] = middle
    normed_two_ref[...] = (middle * rms_scale(middle) * gains_ref[2:3, :]).astype(low)
    rows_arrive(1)
    upstream_ref[...] = placed(1).astype(low)
    stores.extend(near_stores)

    for kind in range(2):

        @pl.loop(1, devices)
        def _(hop, kind=kind):
            row_copy(kind, hop, lax.rem(me + hop, devices), me).wait_send()

        if near_weights:
            for block in others():
                line_copy(kind, block, place).wait_send()
                for hop in range(1, share):
                    rep_copy(kind, block, hop, quarter).wait_send()
            for block in range(line):
                pair_copy(kind, block, core).wait_send()
    if near_weights:
        for hop in range(1, shards):
            gain_copy(hop, shard).wait_send()
    for member in range(3):
        sibling_copy(member).wait_send()
    for store in stores:
        store.wait()


def bring_and_attend(
    line, replicas, near_weights, tokens, cotangent, deal, small, gu, down, key_width
):
    gains_in, qkv_in, out_in = small[:3]
    rows, width = tokens.shape
    shards = 2 * line
    devices = replicas * shards
    share = min(4, replicas)
    block_rows = round_up(rows // devices, 8)
    units = down.shape[0]
    half = round_up(units, LANES)
    low = jnp.bfloat16
    full = jnp.float32
    vmem = pl.BlockSpec(memory_space=pltpu.VMEM)
    hbm = pl.BlockSpec(memory_space=pl.ANY)
    dma = pltpu.SemaphoreType.DMA
    qkv_width = qkv_in.shape[1]
    query_width = qkv_width - 2 * key_width
    if near_weights:
        qkv_shape = (shards, *qkv_in.shape)
        out_shape = (shards, *out_in.shape)
    else:
        qkv_shape = qkv_in.shape
        out_shape = out_in.shape
    tile_rows = max(size for size in range(16, 145, 16) if units % size == 0)
    hold = near_weights
    qkv_scratch = qkv_shape if hold else (shards, 16, LANES)
    out_scratch = out_shape if hold else (shards, 16, LANES)
    gain_lanes = round_up(width // shards, LANES) if hold else LANES

    def array(shape, dtype):
        return jax.ShapeDtypeStruct(shape, dtype)

    return pl.pallas_call(
        functools.partial(bring_kernel, line, replicas, near_weights),
        out_shape=(
            array((rows, width), low),
            array((rows, width), low),
            array((rows, width), low),
            array((rows, query_width), low),
            array((rows, key_width), low),
            array((rows, key_width), low),
            array((rows, query_width), low),
            array((rows, width), full),
            array((rows, width), full),
            array((rows, width), low),
            array((4, width), full),
            array((rows, key_width // 2), full),
            array((rows, key_width // 2), full),
            array((rows, 1), jnp.int32),
            array((1, rows), jnp.int32),
            array(qkv_shape, low),
            array(out_shape, low),
            array((3, 2 * half, width), low),
        ),
        in_specs=[vmem] * 6
        + [pl.BlockSpec(memory_space=pltpu.SMEM), vmem]
        + [hbm] * 2,
        out_specs=(vmem,) * 15 + (hbm,) * 3,
        scratch_shapes=[
            pltpu.VMEM(qkv_scratch, low),
            pltpu.VMEM(out_scratch, low),
            pltpu.VMEM((shards, 16, gain_lanes), low),
            pltpu.VMEM((3, 2 * half, width), low),
            pltpu.VMEM((4, tile_rows, width), full),
            pltpu.VMEM((2, devices, block_rows, width), low),
            pltpu.VMEM((2, devices, block_rows, width), low),
            pltpu.VMEM((rows, qkv_width), full),
            dma((4,)),
            dma((8,)),
            dma((2, devices)),
            dma((2, devices)),
            dma((2, line)),
            dma((2, line)),
            dma((2, line, share)),
            dma((2, line, share)),
            dma((2, line)),
            dma((2, line)),
            dma((shards,)),
            dma((shards,)),
            dma((3,)),
            dma((3,)),
        ],
        compiler_params=pltpu.CompilerParams(
            collective_id=2, has_side_effects=True, vmem_limit_bytes=63 * 1024 * 1024
        ),
        cost_estimate=pl.CostEstimate(
            flops=6 * rows * width * qkv_width,
            bytes_accessed=3 * units * width * 8,
            transcendentals=2 * rows * rows * 4,
        ),
    )(tokens, cotangent, deal, *small, gu, down)


def adam_half_kernel(which, first_half, second_half, *refs):
    del which
    inputs, results = refs[:6], refs[-10:]
    part, member = pl.program_id(0), pl.program_id(1)
    gradient = jnp.where(part == 0, first_half[0], second_half[0]).astype(jnp.float32)

    def step(rows_in, rows_out, rate, decay):
        master, first, second = (ref[...].reshape(gradient.shape) for ref in rows_in)
        moment = BETA_FIRST * first + (1.0 - BETA_FIRST) * gradient
        square = BETA_SECOND * second + (1.0 - BETA_SECOND) * gradient * gradient
        moment_hat = moment * (1.0 / (1.0 - BETA_FIRST**STEP))
        square_hat = square * (1.0 / (1.0 - BETA_SECOND**STEP))
        updated = master - rate * (moment_hat / (jnp.sqrt(square_hat) + ADAM_EPS) + decay * master)
        for ref, value in zip(rows_out, (updated, moment, square, gradient, updated)):
            ref[...] = value.astype(ref.dtype).reshape(ref.shape)

    @pl.when(member == 0)
    def _():
        step(inputs[:3], results[:5], LEARN_RATES[3], DECAY_RATES[3])

    @pl.when(member > 0)
    def _():
        step(inputs[3:], results[5:], LEARN_RATES[2], DECAY_RATES[2])


def adam_half(which, halves, arrays, begun=()):
    members, half_rows, width = halves[0].shape
    tile = half_rows // 2
    down, gu = arrays[0], arrays[3]

    def down_at(part, member, sub, chosen):
        return (part * 4 + chosen[part] * 2 + jnp.where(member == 0, sub, 1), 0)

    def gu_at(part, member, sub, chosen):
        row = part * 4 + chosen[part] * 2 + jnp.where(member == 0, 0, sub)
        return (jnp.maximum(member - 1, 0), row, 0)

    def first_at(part, member, sub, chosen):
        return (jnp.where(part == 0, member, members - 1), jnp.where(part == 0, sub, 1), 0)

    def second_at(part, member, sub, chosen):
        return (jnp.where(part == 0, 0, member), jnp.where(part == 0, 0, sub), 0)

    down_block = pl.BlockSpec((tile, width), down_at)
    gu_block = pl.BlockSpec((1, tile, width), gu_at)
    half_block = (1, tile, width)
    hbm = pl.BlockSpec(memory_space=pl.ANY)
    shapes = []
    for like in (down, gu):
        shapes.extend([jax.ShapeDtypeStruct(like.shape, jnp.float32)] * 4)
        shapes.append(jax.ShapeDtypeStruct(like.shape, jnp.bfloat16))
    count = members * half_rows * width * 2
    return pl.pallas_call(
        adam_half_kernel,
        out_shape=tuple(shapes),
        grid_spec=pltpu.PrefetchScalarGridSpec(
            num_scalar_prefetch=1,
            grid=(2, members, 2),
            in_specs=[
                pl.BlockSpec(half_block, first_at),
                pl.BlockSpec(half_block, second_at),
                *[down_block] * 3,
                *[gu_block] * 3,
                *[hbm] * len(begun),
            ],
            out_specs=(*[down_block] * 5, *[gu_block] * 5),
        ),
        input_output_aliases={9 + at: at for at in range(len(begun))},
        compiler_params=pltpu.CompilerParams(vmem_limit_bytes=60 * 1024 * 1024),
        cost_estimate=pl.CostEstimate(
            flops=16 * count, bytes_accessed=32 * count, transcendentals=2 * count
        ),
    )(which, *halves, *arrays, *begun)


def local(
    tokens,
    cotangent,
    lengths,
    deal,
    w_qkv,
    w_out,
    w_gu,
    w_down,
    gains,
    first_qkv,
    first_out,
    first_gu,
    first_down,
    first_gains,
    second_qkv,
    second_out,
    second_gu,
    second_down,
    second_gains,
):
    row_count, width = tokens.shape
    shards = lax.axis_size("shard")
    replicas = lax.axis_size("rep")
    line = shards // 2
    devices = replicas * shards
    deal_blocks = deal.reshape(deal.shape[0] // LANES, LANES)
    exponent = np.arange(HD // 2, dtype=np.float32) * np.float32(-2.0 / HD)
    frequency = jnp.asarray((np.float32(ROPE_BASE) ** exponent)[None, :])
    near_weights = w_qkv.shape[0] % 16 == 0
    if near_weights:
        first_weights = (gains, w_qkv, w_out)
    else:
        first_weights = (
            lax.all_gather(gains.astype(jnp.bfloat16), "shard", axis=1, tiled=True).astype(
                jnp.float32
            ),
            lax.all_gather(w_qkv.astype(jnp.bfloat16), "shard", axis=0, tiled=True),
            lax.all_gather(w_out.astype(jnp.bfloat16), "shard", axis=0, tiled=True),
        )
    (
        inputs,
        upstream,
        normed_one,
        queries,
        key_rows,
        value_rows,
        attended,
        branch,
        middle,
        normed_two,
        gain_values,
        cosine_table,
        sine_table,
        doc_col,
        doc_row,
        full_qkv,
        full_out,
        ff_weights,
    ) = bring_and_attend(
        line,
        replicas,
        near_weights,
        tokens,
        cotangent,
        deal_blocks,
        (*first_weights, lengths, frequency),
        w_gu,
        w_down,
        HD,
    )
    full_qkv = full_qkv.reshape(width, w_qkv.shape[1])
    full_out = full_out.reshape(H * HD, width)
    output_rows, last_gain_grad, grad_normed_two, ff_grads = feed_forward(
        line,
        replicas,
        normed_two,
        middle,
        upstream,
        gain_values,
        ff_weights,
    )
    first_half, second_half, qkv_sums, out_sums, output, input_grad = back_and_reduce(
        line,
        replicas,
        (
            grad_normed_two,
            middle,
            upstream,
            branch,
            inputs,
            normed_one,
            attended,
            queries,
            key_rows,
            value_rows,
            cosine_table,
            sine_table,
            doc_col,
            doc_row,
            gain_values,
            last_gain_grad,
            output_rows,
            deal_blocks,
        ),
        full_qkv,
        full_out,
        ff_grads,
    )
    bits = replicas.bit_length() - 1
    flips = (1, 1 << (bits - 1))
    other_halves = tuple(
        lax.ppermute(half, "rep", [(member, member ^ flip) for member in range(replicas)])
        for half, flip in zip((first_half, second_half), flips)
    )
    rep = lax.axis_index("rep")
    held = jnp.stack([lax.rem(lax.div(rep, flip), 2) for flip in flips]).astype(jnp.int32)
    ff_arrays = (w_down, first_down, second_down, w_gu, first_gu, second_gu)
    begun = adam_half(held, (first_half, second_half), ff_arrays)
    (
        new_down,
        moment_down,
        square_down,
        summed_down,
        copy_down,
        new_gu,
        moment_gu,
        square_gu,
        summed_gu,
        copy_gu,
    ) = adam_half(1 - held, other_halves, ff_arrays, begun)
    summed_qkv = qkv_sums[: w_qkv.shape[0]].astype(jnp.float32)
    summed_out = out_sums[: w_out.shape[0]].astype(jnp.float32)
    gain_span = gains.shape[1]
    summed_gains = lax.dynamic_slice(
        qkv_sums,
        (qkv_sums.shape[0] - 16, lax.axis_index("shard") * gain_span),
        (gains.shape[0], gain_span),
    ).astype(jnp.float32)
    new_qkv, moment_qkv, square_qkv = adamw_step(
        w_qkv, summed_qkv, first_qkv, second_qkv, LEARN_RATES[0], DECAY_RATES[0]
    )
    new_out, moment_out, square_out = adamw_step(
        w_out, summed_out, first_out, second_out, LEARN_RATES[1], DECAY_RATES[1]
    )
    new_gains, moment_gains, square_gains = adamw_step(
        gains, summed_gains, first_gains, second_gains, LEARN_RATES[4], DECAY_RATES[4]
    )
    return (
        output,
        input_grad,
        new_qkv,
        new_out,
        new_gu,
        new_down,
        new_gains,
        moment_qkv,
        moment_out,
        moment_gu,
        moment_down,
        moment_gains,
        square_qkv,
        square_out,
        square_gu,
        square_down,
        square_gains,
        summed_qkv,
        summed_out,
        summed_gu,
        summed_down,
        summed_gains,
        new_qkv.astype(jnp.bfloat16),
        new_out.astype(jnp.bfloat16),
        copy_gu,
        copy_down,
        new_gains.astype(jnp.bfloat16),
    )


def solution(mesh):
    placed = (
        P(("rep", "shard"), None),
        P(("rep", "shard"), None),
        P(("rep", "shard"), None),
        P(),
        P("shard", None),
        P("shard", None),
        P(None, "shard", None),
        P("shard", None),
        P(None, "shard"),
        P("shard", None),
        P("shard", None),
        P(None, "shard", None),
        P("shard", None),
        P(None, "shard"),
        P("shard", None),
        P("shard", None),
        P(None, "shard", None),
        P("shard", None),
        P(None, "shard"),
    )
    return jax.shard_map(
        local,
        mesh=mesh,
        in_specs=placed,
        out_specs=(
            P(("rep", "shard"), None),
            P(("rep", "shard"), None),
            P("shard", None),
            P("shard", None),
            P(None, "shard", None),
            P("shard", None),
            P(None, "shard"),
            P("shard", None),
            P("shard", None),
            P(None, "shard", None),
            P("shard", None),
            P(None, "shard"),
            P("shard", None),
            P("shard", None),
            P(None, "shard", None),
            P("shard", None),
            P(None, "shard"),
            P("shard", None),
            P("shard", None),
            P(None, "shard", None),
            P("shard", None),
            P(None, "shard"),
            P("shard", None),
            P("shard", None),
            P(None, "shard", None),
            P("shard", None),
            P(None, "shard"),
        ),
        check_vma=False,
    )
```

```python
import functools

import jax
import jax.numpy as jnp
import numpy as np
from jax import lax
from jax.experimental import pallas as pl
from jax.experimental.pallas import tpu as pltpu
from jax.sharding import PartitionSpec as P

H = 4
KV = 1
HD = 256
STEP = 10


CAP_LIMIT = 50.0
NORM_EPS = 1e-06
ROPE_BASE = 10000.0
MASKED_SCORE = -1e30
BETA_FIRST = 0.5
BETA_SECOND = 0.5
ADAM_EPS = 1e-08
LEARN_RATES = (0.05, 0.1, 0.03, 0.012, 0.4)
DECAY_RATES = (0.1, 0.1, 0.1, 0.1, 0.0)
GELU_COEF = 0.7978845608028654
GELU_CUBIC = 0.044715


def rms_scale(values):
    return lax.rsqrt(jnp.mean(values * values, axis=-1, keepdims=True) + NORM_EPS)


def norm_backward(grad_out, values, inverse_rms, gain_row):
    scaled = grad_out * gain_row
    inner = jnp.mean(scaled * values, axis=-1, keepdims=True)
    grad_in = inverse_rms * scaled - values * inverse_rms * inverse_rms * inverse_rms * inner
    grad_gain = jnp.sum(grad_out * values * inverse_rms, axis=0)
    return (grad_in, grad_gain)


def cross_rows(leading, trailing):
    return lax.dot_general(
        leading, trailing, (((0,), (0,)), ((), ())), preferred_element_type=jnp.float32
    )


def against_cols(leading, trailing):
    return lax.dot_general(
        leading, trailing, (((1,), (1,)), ((), ())), preferred_element_type=jnp.float32
    )


def adamw_step(master, gradient, first_moment, second_moment, rate, decay):
    moment = BETA_FIRST * first_moment + (1.0 - BETA_FIRST) * gradient
    square = BETA_SECOND * second_moment + (1.0 - BETA_SECOND) * gradient * gradient
    moment_hat = moment / (1.0 - BETA_FIRST**STEP)
    square_hat = square / (1.0 - BETA_SECOND**STEP)
    updated = master - rate * (moment_hat / (jnp.sqrt(square_hat) + ADAM_EPS) + decay * master)
    return (updated, moment, square)


LANES = 128
UNIT_TILE = 256
MESH = pl.DeviceIdType.MESH


def round_up(count, step):
    return -(-count // step) * step


def partner_of(index, bit):
    value = lax.rem(lax.div(index, 1 << bit), 2)
    return index + (1 - 2 * value) * (1 << bit), value


EARLY = 1


def deal_row(deal_ref, device, rows):
    lines = rows // LANES
    return jnp.concatenate(
        [deal_ref[pl.ds(device * lines + at, 1), :] for at in range(lines)], axis=1
    )


def halving_spans(rep, bits, part, part_rows):
    spans = []
    first = part * part_rows
    size = part_rows
    for bit in range(bits) if part == 0 else range(bits - 1, -1, -1):
        size //= 2
        partner, value = partner_of(rep, bit)
        spans.append((partner, first + value * size, first + (1 - value) * size, size))
        first = first + value * size
    return spans


def at_rows(first, size):
    return pl.ds(pl.multiple_of(first, 16), size)


def feed_kernel(
    line,
    replicas,
    own_rows,
    middle_ref,
    upstream_ref,
    gain_ref,
    weights_hbm,
    out_ref,
    gain_grad_ref,
    back_ref,
    grads_ref,
    weights,
    blocks,
    acts,
    partial,
    chain,
    sibling_out,
    sibling_in,
    landing,
    load_sems,
    store_sems,
    gather_send,
    gather_recv,
    chain_send,
    chain_recv,
    sibling_send,
    sibling_recv,
    half_send,
    half_recv,
):
    rep = lax.axis_index("rep")
    shard = lax.axis_index("shard")
    core = lax.rem(shard, 2)
    place = lax.div(shard, 2)
    sibling = (rep, shard + 1 - 2 * core)
    left = (rep, shard - 2)
    right = (rep, shard + 2)
    has_left = place > 0
    has_right = place < line - 1
    rows = own_rows.shape[0] // 2
    width = own_rows.shape[1]
    half = weights.shape[1] // 2
    tiles = 2 * half // UNIT_TILE

    load = pltpu.make_async_copy(weights_hbm, weights, load_sems.at[0])
    load.start()

    barrier = pltpu.get_barrier_semaphore()
    pl.semaphore_signal(barrier, inc=1, device_id=sibling, device_id_type=MESH)

    @pl.when(has_left)
    def _():
        pl.semaphore_signal(barrier, inc=1, device_id=left, device_id_type=MESH)

    @pl.when(has_right)
    def _():
        pl.semaphore_signal(barrier, inc=1, device_id=right, device_id_type=MESH)

    bits = replicas.bit_length() - 1
    greeted = sorted({0, bits - 1})
    for bit in greeted:
        partner, _ = partner_of(rep, bit)
        pl.semaphore_signal(barrier, inc=1, device_id=(partner, shard), device_id_type=MESH)

    def block_span(block):
        return pl.ds(pl.multiple_of(block * rows, rows), rows)

    for part in range(2):
        blocks[0, part, block_span(place), :] = own_rows[part * rows : (part + 1) * rows, :]

    pl.semaphore_wait(
        barrier,
        1 + len(greeted) + has_left.astype(jnp.int32) + has_right.astype(jnp.int32),
    )

    def gather_copy(phase, part, way, step, block):
        return pltpu.make_async_remote_copy(
            src_ref=blocks.at[phase, part, block_span(block)],
            dst_ref=blocks.at[phase, part, block_span(block)],
            send_sem=gather_send.at[phase, part, way, step],
            recv_sem=gather_recv.at[phase, part, way, step],
            device_id=left if way else right,
            device_id_type=MESH,
        )

    def gather_start(phase, part, step):
        @pl.when(has_right & (place - step >= 0))
        def _():
            gather_copy(phase, part, 0, step, place - step).start()

        @pl.when(has_left & (place + step <= line - 1))
        def _():
            gather_copy(phase, part, 1, step, place + step).start()

    def gather_arrive(phase, part, step):
        @pl.when(place - 1 - step >= 0)
        def _():
            gather_copy(phase, part, 0, step, place - 1 - step).wait_recv()

        @pl.when(place + 1 + step <= line - 1)
        def _():
            gather_copy(phase, part, 1, step, place + 1 + step).wait_recv()

    def gather_drain(phase, part):
        @pl.loop(0, line - 1)
        def _(step):
            @pl.when(has_right & (place - step >= 0))
            def _():
                gather_copy(phase, part, 0, step, place - step).wait_send()

            @pl.when(has_left & (place + step <= line - 1))
            def _():
                gather_copy(phase, part, 1, step, place + step).wait_send()

    def chain_copy(phase, part, way, packet, block):
        return pltpu.make_async_remote_copy(
            src_ref=partial.at[part, block_span(block)],
            dst_ref=chain.at[part, way, packet],
            send_sem=chain_send.at[phase, part, way, packet],
            recv_sem=chain_recv.at[phase, part, way, packet],
            device_id=left if way else right,
            device_id_type=MESH,
        )

    def chain_add(phase, part, way, packet, block):
        chain_copy(phase, part, way, packet, block).wait_recv()
        span = block_span(block)
        partial[part, span, :] = (
            partial[part, span, :].astype(jnp.float32) + chain[part, way, packet].astype(jnp.float32)
        ).astype(partial.dtype)

    def chain_turn(phase, part, turn):
        outward = turn - place

        @pl.when(outward >= 0)
        def _():
            @pl.when(has_left)
            def _():
                chain_add(phase, part, 0, outward, line - 1 - outward)

            chain_copy(phase, part, 0, outward, line - 1 - outward).start()

        inward = turn - (line - 1 - place)

        @pl.when(inward >= 0)
        def _():
            @pl.when(has_right)
            def _():
                chain_add(phase, part, 1, inward, inward)

            chain_copy(phase, part, 1, inward, inward).start()

    def chain_finish(phase, part):
        out = slice(part * rows, (part + 1) * rows)
        back_ref[out, :] = partial[part, block_span(place), :].astype(jnp.float32)

        @pl.when(has_left)
        def _():
            last = line - 1 - place
            chain_copy(phase, part, 0, last, place).wait_recv()
            back_ref[out, :] += chain[part, 0, last].astype(jnp.float32)

        @pl.when(has_right)
        def _():
            chain_copy(phase, part, 1, place, place).wait_recv()
            back_ref[out, :] += chain[part, 1, place].astype(jnp.float32)

    def chain_drain(phase, part):
        @pl.loop(0, line - 1)
        def _(packet):
            @pl.when(line - 1 - packet > place)
            def _():
                chain_copy(phase, part, 0, packet, line - 1 - packet).wait_send()

            @pl.when(packet < place)
            def _():
                chain_copy(phase, part, 1, packet, packet).wait_send()

    def sweep(phase, part, work, reduce=None, last=None, beside=None):
        @pl.loop(1, line)
        def _(turn):
            gather_arrive(phase, part, turn - 1)

            @pl.when(turn < line - 1)
            def _():
                gather_start(phase, part, turn)
                if reduce is not None:
                    chain_turn(*reduce, turn)

            if last is not None:

                @pl.when(turn == line - 1)
                def _():
                    last()

            @pl.loop(0, line // 2)
            def _(pair):
                ready = jnp.maximum(jnp.abs(2 * pair - place), jnp.abs(2 * pair + 1 - place))

                @pl.when(ready == turn)
                def _():
                    work(part, pair)

            if beside is not None:
                beside(turn)

    def pair_span(pair):
        return pl.ds(pl.multiple_of(pair * 2 * rows, 2 * rows), 2 * rows)

    def token_span(part, pair):
        first = part * line * rows
        return pl.ds(pl.multiple_of(first + pair * 2 * rows, 2 * rows), 2 * rows)

    def unit_span(tile):
        return pl.ds(pl.multiple_of(tile * UNIT_TILE, UNIT_TILE), UNIT_TILE)

    def forward(part, pair):
        span = token_span(part, pair)

        @pl.loop(0, tiles)
        def _(tile):
            cols = unit_span(tile)
            rows_in = blocks[0, part, pair_span(pair), :]
            gate = against_cols(rows_in, weights[1, cols, :])
            upper = against_cols(rows_in, weights[2, cols, :])
            tanh_inner = jnp.tanh(GELU_COEF * (gate + GELU_CUBIC * gate * gate * gate))
            lifted = 0.5 * (1.0 + tanh_inner)
            activated = gate * lifted
            slope = lifted + 0.5 * gate * (1.0 - tanh_inner * tanh_inner) * GELU_COEF * (
                1.0 + 3.0 * GELU_CUBIC * gate * gate
            )
            acts[0, span, cols] = (activated * upper).astype(acts.dtype)
            acts[1, span, cols] = (upper * slope).astype(acts.dtype)
            acts[2, span, cols] = activated.astype(acts.dtype)

        partial[part, pair_span(pair), :] = jnp.dot(
            acts[0, span, :], weights[0], preferred_element_type=jnp.float32
        ).astype(partial.dtype)

    def backward(part, pair):
        span = token_span(part, pair)

        @pl.loop(0, tiles)
        def _(tile):
            cols = unit_span(tile)
            grad_hidden = against_cols(blocks[1, part, pair_span(pair), :], weights[0, cols, :])
            for member in (1, 2):
                acts[member, span, cols] = (
                    grad_hidden * acts[member, span, cols].astype(jnp.float32)
                ).astype(acts.dtype)

        partial[part, pair_span(pair), :] = (
            jnp.dot(acts[1, span, :], weights[1], preferred_element_type=jnp.float32)
            + jnp.dot(acts[2, span, :], weights[2], preferred_element_type=jnp.float32)
        ).astype(partial.dtype)

    def output_half(part):
        out = slice(part * rows, (part + 1) * rows)
        feed = back_ref[out, :]
        upstream = upstream_ref[out, :].astype(jnp.float32)
        gain = gain_ref[3:4, :]
        inverse = lax.rsqrt(jnp.mean(feed * feed, axis=-1, keepdims=True) + NORM_EPS)
        scaled = upstream * gain
        inner = jnp.mean(scaled * feed, axis=-1, keepdims=True)
        blocks[1, part, block_span(place), :] = (
            inverse * scaled - feed * inverse * inverse * inverse * inner
        ).astype(blocks.dtype)
        gather_start(1, part, 0)
        gain_grad = jnp.sum(upstream * feed * inverse, axis=0, keepdims=True)
        if part == 0:
            gain_grad_ref[...] = gain_grad
        else:
            gain_grad_ref[...] += gain_grad
        out_ref[out, :] = (middle_ref[out, :] + feed * inverse * gain).astype(out_ref.dtype)

    def sibling_copy(member):
        return pltpu.make_async_remote_copy(
            src_ref=sibling_out.at[member],
            dst_ref=sibling_in.at[member],
            send_sem=sibling_send.at[member],
            recv_sem=sibling_recv.at[member],
            device_id=sibling,
            device_id_type=MESH,
        )

    def store_copy(member):
        return pltpu.make_async_copy(
            sibling_in.at[member], grads_ref.at[member], store_sems.at[member]
        )

    cuts = [(start, min(512, half - start)) for start in range(0, half, 512)]

    def far_grad(part, member):
        tokens = line * rows
        trailing = jnp.where(member == 0, 1, 0)
        for start, size in cuts:
            span = slice(start, start + size)
            piece = cross_rows(
                acts[member, part * tokens : (part + 1) * tokens, half + start : half + start + size],
                blocks[trailing, part],
            )
            if part == 1:
                piece = piece + sibling_out[member, span, :].astype(jnp.float32)
            sibling_out[member, span, :] = piece.astype(sibling_out.dtype)
        if part == 1:
            sibling_copy(member).start()

    first_spans = [halving_spans(rep, bits, part, half // 2)[0] for part in range(2)]

    def halve(member, part):
        partner, keep, give, size = first_spans[part]
        return pltpu.make_async_remote_copy(
            src_ref=sibling_in.at[member, at_rows(give, size)],
            dst_ref=landing.at[member, part],
            send_sem=half_send.at[member, part],
            recv_sem=half_recv.at[member, part],
            device_id=(partner, shard),
            device_id_type=MESH,
        )

    def near_grad(member):
        trailing = jnp.where(member == 0, 1, 0)
        sibling_copy(member).wait_recv()
        for start, size in cuts:
            span = slice(start, start + size)
            piece = cross_rows(
                acts[member, :, span], blocks[trailing].reshape(2 * line * rows, width)
            )
            sibling_in[member, span, :] = (
                sibling_in[member, span, :].astype(jnp.float32) + piece
            ).astype(sibling_in.dtype)

        @pl.when(member < EARLY)
        def _():
            for part in range(2):
                halve(member, part).start()

        @pl.when(member >= EARLY)
        def _():
            store_copy(member).start()

    def share(turn, count, turns):
        return lax.div(turn * count, turns), lax.div((turn + 1) * count, turns)

    def first_grads(turn):
        @pl.when(turn < line - 1)
        def _():
            @pl.loop(*share(turn - 1, 3, line - 2))
            def _(member):
                far_grad(0, member)

    def last_grads(turn):
        @pl.loop(*share(turn, 6, line - 1))
        def _(unit):
            @pl.when(unit < 3)
            def _():
                far_grad(1, unit)

            @pl.when(unit >= 3)
            def _():
                near_grad(unit - 3)

    def turn_around(part):
        chain_finish(0, part)
        output_half(part)

    gather_start(0, 0, 0)
    load.wait()
    sweep(0, 0, forward, last=lambda: gather_start(0, 1, 0))
    chain_turn(0, 0, 0)
    sweep(0, 1, forward, reduce=(0, 0), last=lambda: turn_around(0))
    chain_turn(0, 1, 0)
    chain_drain(0, 0)
    sweep(1, 0, backward, reduce=(0, 1), last=lambda: turn_around(1))
    chain_turn(1, 0, 0)
    chain_drain(0, 1)
    sweep(1, 1, backward, reduce=(1, 0), beside=first_grads)
    chain_turn(1, 1, 0)
    chain_finish(1, 0)

    @pl.loop(0, line - 1)
    def _(turn):
        @pl.when(turn > 0)
        def _():
            chain_turn(1, 1, turn)

        last_grads(turn)

    chain_finish(1, 1)
    for member in range(EARLY):
        for part in range(2):
            halve(member, part).wait_recv()
            partner, keep, give, size = first_spans[part]
            kept = at_rows(keep, size)
            sibling_in[member, kept, :] = (
                sibling_in[member, kept, :].astype(jnp.float32)
                + landing[member, part].astype(jnp.float32)
            ).astype(sibling_in.dtype)
        store_copy(member).start()
    for part in range(2):
        for phase in range(2):
            gather_drain(phase, part)
        chain_drain(1, part)
        for member in range(EARLY):
            halve(member, part).wait_send()
    for member in range(3):
        sibling_copy(member).wait_send()
        store_copy(member).wait()


def feed_forward(line, replicas, normed, middle, upstream, gains, weights):
    rows, width = normed.shape
    half = weights.shape[1] // 2
    low = jnp.bfloat16
    full = jnp.float32
    vmem = pl.BlockSpec(memory_space=pltpu.VMEM)
    hbm = pl.BlockSpec(memory_space=pl.ANY)
    tokens = line * rows
    return pl.pallas_call(
        functools.partial(feed_kernel, line, replicas),
        out_shape=(
            jax.ShapeDtypeStruct((rows, width), low),
            jax.ShapeDtypeStruct((1, width), full),
            jax.ShapeDtypeStruct((rows, width), full),
            jax.ShapeDtypeStruct((3, half, width), low),
        ),
        in_specs=[vmem, vmem, vmem, vmem, hbm],
        out_specs=(vmem, vmem, vmem, hbm),
        scratch_shapes=[
            pltpu.VMEM((3, 2 * half, width), low),
            pltpu.VMEM((2, 2, tokens // 2, width), low),
            pltpu.VMEM((3, tokens, 2 * half), low),
            pltpu.VMEM((2, tokens // 2, width), low),
            pltpu.VMEM((2, 2, line - 1, rows // 2, width), low),
            pltpu.VMEM((3, half, width), low),
            pltpu.VMEM((3, half, width), low),
            pltpu.VMEM((EARLY, 2, half // 4, width), low),
            pltpu.SemaphoreType.DMA((1,)),
            pltpu.SemaphoreType.DMA((3,)),
            pltpu.SemaphoreType.DMA((2, 2, 2, line - 1)),
            pltpu.SemaphoreType.DMA((2, 2, 2, line - 1)),
            pltpu.SemaphoreType.DMA((2, 2, 2, line - 1)),
            pltpu.SemaphoreType.DMA((2, 2, 2, line - 1)),
            pltpu.SemaphoreType.DMA((3,)),
            pltpu.SemaphoreType.DMA((3,)),
            pltpu.SemaphoreType.DMA((EARLY, 2)),
            pltpu.SemaphoreType.DMA((EARLY, 2)),
        ],
        compiler_params=pltpu.CompilerParams(
            collective_id=0, has_side_effects=True, vmem_limit_bytes=63 * 1024 * 1024
        ),
        cost_estimate=pl.CostEstimate(
            flops=18 * tokens * 2 * half * width,
            bytes_accessed=9 * half * width * 2,
            transcendentals=tokens * 2 * half,
        ),
    )(normed, middle, upstream, gains, weights)


def back_kernel(
    line,
    replicas,
    back_hbm,
    middle_hbm,
    upstream_hbm,
    branch_hbm,
    inputs_hbm,
    normed_hbm,
    attended_hbm,
    queries_hbm,
    keys_hbm,
    values_hbm,
    cosine_hbm,
    sine_hbm,
    doc_col_ref,
    doc_row_ref,
    gains_ref,
    last_gain_ref,
    out_rows_ref,
    deal_ref,
    first_hbm,
    out_hbm,
    grads_hbm,
    first_half_hbm,
    second_half_hbm,
    qkv_hbm,
    outw_hbm,
    output_ref,
    input_grad_ref,
    w_qkv,
    w_out,
    acc,
    total,
    landing,
    late_landing,
    query_parts,
    query_pair,
    query_chain,
    query_steps,
    query_land,
    key_parts,
    key_pair,
    key_chain,
    key_steps,
    key_land,
    out_parts,
    out_pair,
    out_chain,
    out_steps,
    out_land,
    grad_rows,
    grad_keys,
    grad_values,
    pack_rows,
    send_rows,
    recv_rows,
    held,
    operand_sems,
    load_sems,
    store_sems,
    half_send,
    half_recv,
    pair_send,
    pair_recv,
    chain_send,
    chain_recv,
    step_send,
    step_recv,
    row_send,
    row_recv,
):
    rep = lax.axis_index("rep")
    shard = lax.axis_index("shard")
    shards = 2 * line
    devices = replicas * shards
    me = rep * shards + shard
    core = lax.rem(shard, 2)
    place = lax.div(shard, 2)
    sibling = (rep, shard + 1 - 2 * core)
    left = (rep, shard - 2)
    right = (rep, shard + 2)
    has_left = place > 0
    has_right = place < line - 1
    bits = replicas.bit_length() - 1
    full = jnp.float32
    rows, width = inputs_hbm.shape
    key_width = keys_hbm.shape[1]
    query_width = queries_hbm.shape[1]
    heads = query_width // key_width
    members, half_rows = acc.shape[0], acc.shape[1]
    part_rows = half_rows // 2
    peer_rows = rows // devices
    block_rows = send_rows.shape[2]
    packed = devices * block_rows
    qkv_rows = first_hbm.shape[0] // shards
    out_rows = out_hbm.shape[0] // shards

    load_qkv = pltpu.make_async_copy(first_hbm, w_qkv, load_sems.at[0])
    load_out = pltpu.make_async_copy(out_hbm, w_out, load_sems.at[1])
    load_acc = pltpu.make_async_copy(grads_hbm, acc, load_sems.at[2])
    operands = (
        back_hbm,
        middle_hbm,
        upstream_hbm,
        branch_hbm,
        inputs_hbm,
        normed_hbm,
        attended_hbm,
        queries_hbm,
        keys_hbm,
        values_hbm,
        cosine_hbm,
        sine_hbm,
    )
    operand_loads = [
        pltpu.make_async_copy(source, target, operand_sems.at[at])
        for at, (source, target) in enumerate(zip(operands, held))
    ]
    (
        back_ref,
        middle_ref,
        upstream_ref,
        branch_ref,
        inputs_ref,
        normed_ref,
        attended_ref,
        queries_ref,
        keys_ref,
        values_ref,
        cosine_ref,
        sine_ref,
    ) = held
    load_acc.start()
    for load in operand_loads:
        load.start()
    load_out.start()
    load_qkv.start()

    barrier = pltpu.get_barrier_semaphore()

    @pl.loop(1, devices)
    def _(hop):
        peer = lax.rem(me + hop, devices)
        pl.semaphore_signal(
            barrier,
            inc=1,
            device_id=(lax.div(peer, shards), lax.rem(peer, shards)),
            device_id_type=MESH,
        )

    pl.semaphore_wait(barrier, devices - 1)

    spans = [halving_spans(rep, bits, part, part_rows) for part in range(2)]

    def first_stage(member):
        return 1 if member < EARLY else 0

    def landed(member, part, stage):
        if stage == 0:
            return landing.at[member - EARLY, part]
        size = part_rows >> (stage + 1)
        return late_landing.at[member, part, pl.ds(part_rows // 2 - 2 * size, size)]

    def halve(member, part, stage):
        partner, keep, give, size = spans[part][stage]
        source = grads_hbm if stage == first_stage(member) else acc
        return pltpu.make_async_remote_copy(
            src_ref=source.at[member, at_rows(give, size)],
            dst_ref=landed(member, part, stage),
            send_sem=half_send.at[0, member, part, stage],
            recv_sem=half_recv.at[0, member, part, stage],
            device_id=(partner, shard),
            device_id_type=MESH,
        )

    def halve_add(member, part, stage):
        partner, keep, give, size = spans[part][stage]
        halve(member, part, stage).wait_recv()
        target = total if stage == bits - 1 else acc
        target[member, at_rows(keep, size), :] = (
            acc[member, at_rows(keep, size), :].astype(full)
            + landed(member, part, stage)[...].astype(full)
        ).astype(acc.dtype)

    def double(member, part, stage):
        partner, keep, give, size = spans[part][stage]
        return pltpu.make_async_remote_copy(
            src_ref=total.at[member, at_rows(keep, size)],
            dst_ref=total.at[member, at_rows(keep, size)],
            send_sem=half_send.at[1, member, part, stage],
            recv_sem=half_recv.at[1, member, part, stage],
            device_id=(partner, shard),
            device_id_type=MESH,
        )

    def double_arrive(member, part, stage):
        partner, keep, give, size = spans[part][stage]
        pltpu.make_async_remote_copy(
            src_ref=total.at[member, at_rows(give, size)],
            dst_ref=total.at[member, at_rows(give, size)],
            send_sem=half_send.at[1, member, part, stage],
            recv_sem=half_recv.at[1, member, part, stage],
            device_id=(partner, shard),
            device_id_type=MESH,
        ).wait_recv()

    def each(work):
        for member in range(members):
            for part in range(2):
                work(member, part)

    for part in range(2):
        halve(members - 1, part, first_stage(members - 1)).start()
    for member in range(members - 1):
        for part in range(2):
            halve(member, part, first_stage(member)).start()
    load_acc.wait()

    def pair_copy(kind, parts, pair):
        return pltpu.make_async_remote_copy(
            src_ref=parts.at[1 - core],
            dst_ref=pair,
            send_sem=pair_send.at[kind],
            recv_sem=pair_recv.at[kind],
            device_id=sibling,
            device_id_type=MESH,
        )

    kinds = (
        (out_parts, out_pair, out_chain, out_steps, out_land),
        (query_parts, query_pair, query_chain, query_steps, query_land),
        (key_parts, key_pair, key_chain, key_steps, key_land),
    )

    def pair_add(kind):
        parts, pair = kinds[kind][:2]
        pair_copy(kind, parts, pair).wait_recv()

        @pl.loop(0, line)
        def _(block):
            parts[core, block] = (
                parts[core, block].astype(full) + pair[block].astype(full)
            ).astype(parts.dtype)

    def chain_copy(kind, way, step, block):
        parts, _, chain = kinds[kind][:3]
        return pltpu.make_async_remote_copy(
            src_ref=parts.at[core, block],
            dst_ref=chain.at[way, step],
            send_sem=chain_send.at[kind, way, step],
            recv_sem=chain_recv.at[kind, way, step],
            device_id=left if way else right,
            device_id_type=MESH,
        )

    def chain_add(kind, way, step, block):
        parts, _, chain = kinds[kind][:3]
        chain_copy(kind, way, step, block).wait_recv()
        parts[core, block] = (
            parts[core, block].astype(full) + chain[way, step].astype(full)
        ).astype(parts.dtype)

    def chain_step(kind, turn):
        outward = turn - place

        @pl.when(outward >= 0)
        def _():
            @pl.when(has_left)
            def _():
                chain_add(kind, 0, outward, line - 1 - outward)

            chain_copy(kind, 0, outward, line - 1 - outward).start()

        inward = turn - (line - 1 - place)

        @pl.when(inward >= 0)
        def _():
            @pl.when(has_right)
            def _():
                chain_add(kind, 1, inward, inward)

            chain_copy(kind, 1, inward, inward).start()

    def chain_finish(kind):
        parts, _, _, steps, _ = kinds[kind]

        @pl.when(has_left)
        def _():
            chain_add(kind, 0, line - 1 - place, place)

        @pl.when(has_right)
        def _():
            chain_add(kind, 1, place, place)

        steps[0] = parts[core, place]

    lanes = {0: ((0, None),), 1: ((1, 0), (2, 1)), 2: ((3, None),)}

    def columns(ref, piece):
        if piece is None:
            return ref
        size = ref.shape[1] // 2
        return ref.at[:, pl.ds(piece * size, size)]

    def step_copy(kind, stage, lane, piece):
        steps, land = kinds[kind][3:]
        partner, _ = partner_of(rep, stage if lane in (1, 3) else bits - 1 - stage)
        return pltpu.make_async_remote_copy(
            src_ref=columns(steps.at[stage], piece),
            dst_ref=columns(land.at[stage], piece),
            send_sem=step_send.at[lane, stage],
            recv_sem=step_recv.at[lane, stage],
            device_id=(partner, shard),
            device_id_type=MESH,
        )

    def step_start(kind, stage):
        for lane, piece in lanes[kind]:
            step_copy(kind, stage, lane, piece).start()

    def step_add(kind, stage):
        steps, land = kinds[kind][3:]
        for lane, piece in lanes[kind]:
            step_copy(kind, stage, lane, piece).wait_recv()
            columns(steps.at[stage + 1], piece)[...] = (
                columns(steps.at[stage], piece)[...].astype(full)
                + columns(land.at[stage], piece)[...].astype(full)
            ).astype(steps.dtype)
            if stage + 1 < bits:
                step_copy(kind, stage + 1, lane, piece).start()

    served = {0: 0}

    def chain_to(kind, end):
        for step in range(served[kind], end):
            chain_step(kind, step)
        served[kind] = max(end, served[kind])

    def advance(member, stage):
        for part in range(2):
            halve_add(member, part, stage)
            if stage + 1 < bits:
                halve(member, part, stage + 1).start()
            else:
                double(member, part, stage).start()

    def redouble(member, stage):
        for part in range(2):
            double_arrive(member, part, stage)
            if stage > 1:
                double(member, part, stage - 1).start()
            else:
                store_half(member, part).start()

    def store_half(member, part):
        _, keep, _, size = spans[part][0]
        return pltpu.make_async_copy(
            total.at[member, at_rows(keep, size)],
            (first_half_hbm, second_half_hbm)[part].at[member],
            store_sems.at[3 + 2 * member + part],
        )

    todo = [
        [functools.partial(advance, member, stage) for stage in range(first_stage(member), bits)]
        + [functools.partial(redouble, member, stage) for stage in range(bits - 1, 0, -1)]
        for member in range(members)
    ]

    def serve(*chosen):
        for member in chosen:
            if todo[member]:
                todo[member].pop(0)()

    for load in operand_loads:
        load.wait()
    middle = middle_ref[...]
    upstream = upstream_ref[...].astype(full)
    scale_two = rms_scale(middle)
    grad_middle_norm, gain_two = norm_backward(
        back_ref[...], middle, scale_two, gains_ref[2:3, :]
    )
    back_ref[...] = upstream + grad_middle_norm
    branch = branch_ref[...]
    grad_branch, gain_one = norm_backward(
        back_ref[...], branch, rms_scale(branch), gains_ref[1:2, :]
    )
    grad_branch = grad_branch.astype(jnp.bfloat16)
    half_query = query_width // 2
    half_shards = shards // 2
    for group in range(2):
        grad_out = cross_rows(
            attended_ref[:, group * half_query : (group + 1) * half_query], grad_branch
        )
        for offset in range(half_shards):
            member = group * half_shards + offset
            out_parts[member % 2, member // 2, 0:out_rows, :] = grad_out[
                offset * out_rows : (offset + 1) * out_rows
            ].astype(out_parts.dtype)

    pair_copy(0, out_parts, out_pair).start()
    load_out.wait()
    grad_rows[:, 0:query_width] = against_cols(grad_branch, w_out[...]).astype(grad_rows.dtype)
    grad_keys[...] = jnp.zeros_like(grad_keys)
    grad_values[...] = jnp.zeros_like(grad_values)
    half_key = key_width // 2

    down_ids = lax.broadcasted_iota(jnp.int32, (rows, rows), 0)
    along_ids = lax.broadcasted_iota(jnp.int32, (rows, rows), 1)
    own_slots = down_ids + me * rows

    def find(source, found):
        return found + jnp.where(deal_row(deal_ref, source, rows) == own_slots, source, 0)

    found = lax.fori_loop(0, devices, find, jnp.zeros((rows, rows), jnp.int32))
    origin = jnp.sum(found, axis=1, keepdims=True)
    origin_row = jnp.sum(jnp.where(down_ids == along_ids, origin, 0), axis=0, keepdims=True)
    before = (origin_row == origin) & (down_ids < along_ids)
    back_place = origin_row * block_rows + jnp.sum(
        before.astype(jnp.int32), axis=0, keepdims=True
    )
    pack_rows[...] = (
        lax.broadcasted_iota(jnp.int32, (packed, rows), 0) == back_place
    ).astype(pack_rows.dtype)

    def row_copy(kind, hop, peer, source):
        return pltpu.make_async_remote_copy(
            src_ref=send_rows.at[kind, peer],
            dst_ref=recv_rows.at[kind, source],
            send_sem=row_send.at[kind, hop],
            recv_sem=row_recv.at[kind, hop],
            device_id=(lax.div(peer, shards), lax.rem(peer, shards)),
            device_id_type=MESH,
        )

    def send_back(kind, values):
        send_rows[kind] = (
            jnp.dot(pack_rows[...], values, preferred_element_type=full)
            .reshape(devices, block_rows, width)
            .astype(send_rows.dtype)
        )
        recv_rows[kind, me] = send_rows[kind, me]

        @pl.loop(1, devices)
        def _(hop):
            row_copy(kind, hop, lax.rem(me + hop, devices), me).start()

    send_back(0, out_rows_ref[...])
    pair_add(0)
    chain_to(0, 1)

    for head in range(heads):
        start = head * key_width
        cols = pl.ds(start, key_width)
        query = queries_ref[:, cols]
        key = keys_ref[...]
        allowed = (doc_col_ref[...] == doc_row_ref[...]) & (
            lax.broadcasted_iota(jnp.int32, (rows, rows), 0)
            >= lax.broadcasted_iota(jnp.int32, (rows, rows), 1)
        )
        tanh_scores = jnp.tanh(against_cols(query, key) * (HD ** (-0.5) / CAP_LIMIT))
        capped = jnp.where(allowed, CAP_LIMIT * tanh_scores, MASKED_SCORE)
        powers = jnp.exp(capped - jnp.max(capped, axis=-1, keepdims=True))
        probs = powers / jnp.sum(powers, axis=-1, keepdims=True)
        grad_att = grad_rows[:, cols]
        grad_values[...] += cross_rows(probs.astype(jnp.bfloat16), grad_att)
        grad_probs = against_cols(grad_att, values_ref[...])
        grad_capped = probs * (grad_probs - jnp.sum(probs * grad_probs, axis=-1, keepdims=True))
        grad_raw = (
            grad_capped * (1.0 - tanh_scores * tanh_scores) * HD ** (-0.5)
        ).astype(jnp.bfloat16)
        grad_keys[...] += cross_rows(grad_raw, query)
        grad_query = jnp.dot(grad_raw, key, preferred_element_type=full)
        front = grad_query[:, :half_key]
        back = grad_query[:, half_key:]
        cosine, sine = cosine_ref[...], sine_ref[...]
        grad_rows[:, pl.ds(start, half_key)] = (front * cosine + back * sine).astype(
            grad_rows.dtype
        )
        grad_rows[:, pl.ds(start + half_key, half_key)] = (
            back * cosine - front * sine
        ).astype(grad_rows.dtype)

    def weight_parts(parts, first, size):
        for begin in range(0, size, 512):
            grad_cols = cross_rows(
                normed_ref[...], grad_rows[:, first + begin : first + begin + 512]
            )
            for member in range(shards):
                parts[member % 2, member // 2, 0:qkv_rows, begin : begin + 512] = grad_cols[
                    member * qkv_rows : (member + 1) * qkv_rows
                ].astype(parts.dtype)

    weight_parts(query_parts, 0, query_width)
    pair_copy(1, query_parts, query_pair).start()
    serve(members - 1, 0)
    chain_to(0, min(2, line - 1))
    front = grad_keys[:, :half_key]
    back = grad_keys[:, half_key:]
    cosine, sine = cosine_ref[...], sine_ref[...]
    grad_rows[:, query_width : query_width + half_key] = (
        front * cosine + back * sine
    ).astype(grad_rows.dtype)
    grad_rows[:, query_width + half_key : query_width + key_width] = (
        back * cosine - front * sine
    ).astype(grad_rows.dtype)
    grad_rows[:, query_width + key_width :] = grad_values[...].astype(grad_rows.dtype)
    pair_add(1)
    chain_step(1, 0)

    load_qkv.wait()
    grad_normed = against_cols(grad_rows[...], w_qkv[...])
    inputs = inputs_ref[...].astype(full)
    grad_norm, gain_zero = norm_backward(
        grad_normed, inputs, rms_scale(inputs), gains_ref[0:1, :]
    )
    grad_inputs = (back_ref[...] + grad_norm).astype(jnp.bfloat16)
    weight_parts(key_parts, query_width, 2 * key_width)
    gain_stack = jnp.stack([gain_zero, gain_one, gain_two, last_gain_ref[0]])
    third = width // 3
    gain_rows = jnp.concatenate(
        [gain_stack[:, at * third : (at + 1) * third] for at in range(3)]
        + [jnp.zeros((4, third), full)]
    ).astype(jnp.bfloat16)
    for member in range(shards):
        gain_at = key_parts.shape[2] - 16
        key_parts[member % 2, member // 2, gain_at:, 0:third] = gain_rows
        key_parts[member % 2, member // 2, gain_at:, third:] = jnp.zeros(
            (16, key_parts.shape[3] - third), key_parts.dtype
        )
    pair_copy(2, key_parts, key_pair).start()
    serve(1)

    if line > 2:
        chain_step(1, 1)
    pair_add(2)
    chain_step(2, 0)
    chain_to(0, line - 1)
    chain_finish(0)
    step_start(0, 0)
    serve(members - 1, 0)
    for step in range(2, line - 1):
        chain_step(1, step)
        chain_step(2, step - 1)
    if line > 2:
        chain_step(2, line - 2)
    chain_finish(1)
    step_start(1, 0)
    send_back(1, grad_inputs)
    serve(1, members - 1)
    step_add(0, 0)
    serve(0)
    chain_finish(2)
    step_start(2, 0)
    for stage in range(1, bits):
        step_add(0, stage)
    for stage in range(bits):
        serve(*range(members))
        for kind in (1, 2):
            step_add(kind, stage)
    while any(todo):
        serve(*range(members))
    store_small = (
        pltpu.make_async_copy(out_steps.at[bits], outw_hbm, store_sems.at[0]),
        pltpu.make_async_copy(
            query_steps.at[bits],
            qkv_hbm.at[pl.ds(0, query_steps.shape[1]), pl.ds(0, query_width)],
            store_sems.at[1],
        ),
        pltpu.make_async_copy(
            key_steps.at[bits], qkv_hbm.at[:, pl.ds(query_width, 2 * key_width)], store_sems.at[2]
        ),
    )
    for store in store_small:
        store.start()
    own_deal = deal_row(deal_ref, me, rows)
    own_column = jnp.sum(jnp.where(down_ids == along_ids, own_deal, 0), axis=1, keepdims=True)
    send_place = jnp.sum((own_deal < own_column).astype(jnp.int32), axis=1, keepdims=True)
    target = lax.div(send_place, peer_rows) * block_rows + lax.rem(send_place, peer_rows)
    placer = (
        lax.broadcasted_iota(jnp.int32, (rows, packed), 1) == target
    ).astype(jnp.bfloat16)
    for kind, result in enumerate((output_ref, input_grad_ref)):

        @pl.loop(1, devices)
        def _(hop, kind=kind):
            source = lax.rem(me + devices - hop, devices)
            row_copy(kind, hop, source, source).wait_recv()

        stacked = recv_rows[kind].astype(full).reshape(packed, width).astype(jnp.bfloat16)
        result[...] = jnp.dot(placer, stacked, preferred_element_type=full).astype(result.dtype)

    for kind in range(2):

        @pl.loop(1, devices)
        def _(hop, kind=kind):
            row_copy(kind, hop, lax.rem(me + hop, devices), me).wait_send()

    def sent(member, part):
        for stage in range(bits):
            if stage >= first_stage(member):
                halve(member, part, stage).wait_send()
            if stage > 0:
                double(member, part, stage).wait_send()

    each(sent)
    for kind in range(3):
        parts, pair = kinds[kind][:2]
        pair_copy(kind, parts, pair).wait_send()
        for stage in range(bits):
            for lane, piece in lanes[kind]:
                step_copy(kind, stage, lane, piece).wait_send()

        @pl.loop(0, line - 1)
        def _(step, kind=kind):
            far = line - 1 - step

            @pl.when(far > place)
            def _():
                chain_copy(kind, 0, step, far).wait_send()

            @pl.when(step < place)
            def _():
                chain_copy(kind, 1, step, step).wait_send()

    for store in store_small:
        store.wait()
    each(lambda member, part: store_half(member, part).wait())


def back_and_reduce(line, replicas, small, first_full, out_full, ff_grads):
    inputs, normed, queries, keys = small[4], small[5], small[7], small[8]
    held = 12
    rows, width = inputs.shape
    shards = 2 * line
    devices = replicas * shards
    vmem_limit = 63 * 1024 * 1024
    block_rows = round_up(rows // devices, 8)
    bits = replicas.bit_length() - 1
    qkv_width = queries.shape[1] + 2 * keys.shape[1]
    qkv_rows = round_up(width // shards, 16) + 16
    out_rows = round_up(out_full.shape[0] // shards, 16)
    members, half_rows = ff_grads.shape[:2]
    low = jnp.bfloat16
    full = jnp.float32
    vmem = pl.BlockSpec(memory_space=pltpu.VMEM)
    hbm = pl.BlockSpec(memory_space=pl.ANY)
    dma = pltpu.SemaphoreType.DMA

    def chain_scratch(count, cols):
        return [
            pltpu.VMEM((2, line, count, cols), low),
            pltpu.VMEM((line, count, cols), low),
            pltpu.VMEM((2, line - 1, count, cols), low),
            pltpu.VMEM((bits + 1, count, cols), low),
            pltpu.VMEM((bits, count, cols), low),
        ]

    return pl.pallas_call(
        functools.partial(back_kernel, line, replicas),
        out_shape=(
            jax.ShapeDtypeStruct((members, half_rows // 4, width), low),
            jax.ShapeDtypeStruct((members, half_rows // 4, width), low),
            jax.ShapeDtypeStruct((qkv_rows, qkv_width), low),
            jax.ShapeDtypeStruct((out_rows, width), low),
            jax.ShapeDtypeStruct((rows, width), full),
            jax.ShapeDtypeStruct((rows, width), full),
        ),
        in_specs=[hbm] * held + [vmem] * (len(small) - held) + [hbm] * 3,
        out_specs=(hbm,) * 4 + (vmem,) * 2,
        scratch_shapes=[
            pltpu.VMEM((width, qkv_width), low),
            pltpu.VMEM(out_full.shape, low),
            pltpu.VMEM(ff_grads.shape, low),
            pltpu.VMEM(ff_grads.shape, low),
            pltpu.VMEM((members - EARLY, 2, half_rows // 4, width), low),
            pltpu.VMEM(
                (members, 2, half_rows // 4 - half_rows // (2 * replicas), width), low
            ),
            *chain_scratch(qkv_rows - 16, queries.shape[1]),
            *chain_scratch(qkv_rows, 2 * keys.shape[1]),
            *chain_scratch(out_rows, width),
            pltpu.VMEM((rows, qkv_width), low),
            pltpu.VMEM((rows, keys.shape[1]), full),
            pltpu.VMEM((rows, keys.shape[1]), full),
            pltpu.VMEM((devices * block_rows, rows), low),
            pltpu.VMEM((2, devices, block_rows, width), low),
            pltpu.VMEM((2, devices, block_rows, width), low),
            [pltpu.VMEM(operand.shape, operand.dtype) for operand in small[:held]],
            dma((held,)),
            dma((3,)),
            dma((3 + 2 * members,)),
            dma((2, members, 2, bits)),
            dma((2, members, 2, bits)),
            dma((3,)),
            dma((3,)),
            dma((3, 2, line - 1)),
            dma((3, 2, line - 1)),
            dma((4, bits)),
            dma((4, bits)),
            dma((2, devices)),
            dma((2, devices)),
        ],
        compiler_params=pltpu.CompilerParams(
            collective_id=1, has_side_effects=True, vmem_limit_bytes=vmem_limit
        ),
        cost_estimate=pl.CostEstimate(
            flops=16 * rows * width * qkv_width,
            bytes_accessed=4 * members * half_rows * width,
            transcendentals=2 * rows * rows * 4,
        ),
    )(*small, first_full, out_full, ff_grads)


def bring_kernel(
    line,
    replicas,
    near_weights,
    tokens_ref,
    cotangent_ref,
    deal_ref,
    gains_in,
    qkv_in,
    out_in,
    lengths_ref,
    frequency_ref,
    gu_hbm,
    down_hbm,
    inputs_ref,
    upstream_ref,
    normed_ref,
    queries_ref,
    keys_ref,
    values_ref,
    attended_ref,
    branch_ref,
    middle_ref,
    normed_two_ref,
    gains_ref,
    cosine_ref,
    sine_ref,
    doc_col_ref,
    doc_row_ref,
    qkv_hbm,
    outw_hbm,
    weights_hbm,
    w_qkv,
    w_out,
    gain_blocks,
    weights,
    tiles,
    sent,
    arrived,
    projected,
    load_sems,
    store_sems,
    row_send,
    row_recv,
    line_send,
    line_recv,
    rep_send,
    rep_recv,
    pair_send,
    pair_recv,
    gain_send,
    gain_recv,
    sibling_send,
    sibling_recv,
):
    rep = lax.axis_index("rep")
    shard = lax.axis_index("shard")
    shards = 2 * line
    devices = replicas * shards
    me = rep * shards + shard
    core = lax.rem(shard, 2)
    place = lax.div(shard, 2)
    sibling = (rep, shard + 1 - 2 * core)
    share = min(4, replicas)
    quarter = lax.rem(rep, share)
    full = jnp.float32
    low = jnp.bfloat16
    rows, width = tokens_ref.shape
    peer_rows = rows // devices
    block_rows = sent.shape[2]
    units = gu_hbm.shape[1]
    half = weights.shape[1] // 2
    tile_rows = tiles.shape[1]
    tile_count = units // tile_rows
    depth = tiles.shape[0]
    key_width = keys_ref.shape[1]
    query_width = queries_ref.shape[1]
    heads = query_width // key_width
    half_key = key_width // 2

    def tile_load(turn):
        member, at = turn // tile_count, turn % tile_count * tile_rows
        source = down_hbm if member == 0 else gu_hbm.at[member - 1]
        return pltpu.make_async_copy(
            source.at[pl.ds(at, tile_rows)], tiles.at[turn % depth], load_sems.at[turn % depth]
        )

    for turn in range(min(depth, 3 * tile_count)):
        tile_load(turn).start()

    barrier = pltpu.get_barrier_semaphore()

    @pl.loop(1, devices)
    def _(hop):
        peer = lax.rem(me + hop, devices)
        pl.semaphore_signal(
            barrier,
            inc=1,
            device_id=(lax.div(peer, shards), lax.rem(peer, shards)),
            device_id_type=MESH,
        )

    if near_weights:
        w_qkv[shard] = qkv_in[...].astype(low)

    down_ids = lax.broadcasted_iota(jnp.int32, (rows, rows), 0)
    along_ids = lax.broadcasted_iota(jnp.int32, (rows, rows), 1)
    eye = down_ids == along_ids

    def to_column(row):
        return jnp.sum(jnp.where(eye, row, 0), axis=1, keepdims=True)

    def to_row(column):
        return jnp.sum(jnp.where(eye, column, 0), axis=0, keepdims=True)

    def spread(places):
        return lax.div(places, peer_rows) * block_rows + lax.rem(places, peer_rows)

    own_deal = deal_row(deal_ref, me, rows)
    send_place = jnp.sum((to_column(own_deal) < own_deal).astype(jnp.int32), axis=0, keepdims=True)
    packed = devices * block_rows
    picker = (
        lax.broadcasted_iota(jnp.int32, (packed, rows), 0) == spread(send_place)
    ).astype(low)

    def pack(kind, source):
        sent[kind] = (
            jnp.dot(picker, source[...], preferred_element_type=full)
            .reshape(devices, block_rows, width)
            .astype(low)
        )
        arrived[kind, me] = sent[kind, me]

    pack(0, tokens_ref)
    pl.semaphore_wait(barrier, devices - 1)

    def row_copy(kind, hop, peer, source):
        return pltpu.make_async_remote_copy(
            src_ref=sent.at[kind, peer],
            dst_ref=arrived.at[kind, source],
            send_sem=row_send.at[kind, hop],
            recv_sem=row_recv.at[kind, hop],
            device_id=(lax.div(peer, shards), lax.rem(peer, shards)),
            device_id_type=MESH,
        )

    def rows_start(kind):
        @pl.loop(1, devices)
        def _(hop):
            row_copy(kind, hop, lax.rem(me + hop, devices), me).start()

    def rows_arrive(kind):
        @pl.loop(1, devices)
        def _(hop):
            source = lax.rem(me + devices - hop, devices)
            row_copy(kind, hop, source, source).wait_recv()

    gathered = (w_qkv, w_out)

    def part_of(kind, member, portion):
        buffer = gathered[kind]
        if kind == 0:
            size = buffer.shape[2] // share
            return buffer.at[member, :, pl.ds(pl.multiple_of(portion * size, LANES), size)]
        size = buffer.shape[1] // share
        return buffer.at[member, pl.ds(pl.multiple_of(portion * size, 16), size)]

    def line_copy(kind, target, source):
        part = part_of(kind, 2 * source + core, quarter)
        return pltpu.make_async_remote_copy(
            src_ref=part,
            dst_ref=part,
            send_sem=line_send.at[kind, target],
            recv_sem=line_recv.at[kind, source],
            device_id=(rep, 2 * target + core),
            device_id_type=MESH,
        )

    def rep_copy(kind, block, hop, portion):
        part = part_of(kind, 2 * block + core, portion)
        return pltpu.make_async_remote_copy(
            src_ref=part,
            dst_ref=part,
            send_sem=rep_send.at[kind, block, hop],
            recv_sem=rep_recv.at[kind, block, portion],
            device_id=(rep - quarter + lax.rem(quarter + hop, share), shard),
            device_id_type=MESH,
        )

    def pair_copy(kind, block, side):
        buffer = gathered[kind]
        return pltpu.make_async_remote_copy(
            src_ref=buffer.at[2 * block + side],
            dst_ref=buffer.at[2 * block + side],
            send_sem=pair_send.at[kind, block],
            recv_sem=pair_recv.at[kind, block],
            device_id=sibling,
            device_id_type=MESH,
        )

    def gain_copy(hop, source):
        return pltpu.make_async_remote_copy(
            src_ref=gain_blocks.at[source],
            dst_ref=gain_blocks.at[source],
            send_sem=gain_send.at[hop],
            recv_sem=gain_recv.at[hop],
            device_id=(rep, lax.rem(shard + hop, shards)),
            device_id_type=MESH,
        )

    def others():
        return [lax.rem(place + hop, line) for hop in range(1, line)]

    def line_start(kind):
        for target in others():
            line_copy(kind, target, place).start()
        pair_copy(kind, place, core).start()

    def line_pass(kind):
        for source in others():
            line_copy(kind, source, source).wait_recv()
            for hop in range(1, share):
                rep_copy(kind, source, hop, quarter).start()

    def rep_pass(kind):
        for block in others():
            for hop in range(1, share):
                rep_copy(kind, block, hop, lax.rem(quarter + hop, share)).wait_recv()
            pair_copy(kind, block, core).start()

    def pair_arrive(kind):
        for block in range(line):
            pair_copy(kind, block, 1 - core).wait_recv()

    if near_weights:
        line_start(0)
        line_pass(0)
    rows_start(0)
    if near_weights:
        w_out[shard] = out_in[...].astype(low)
        line_start(1)
        gain_blocks[shard] = jnp.zeros(gain_blocks.shape[1:], low)
        gain_blocks[shard, : gains_in.shape[0], : gains_in.shape[1]] = gains_in[...].astype(low)
        for hop in range(1, shards):
            gain_copy(hop, shard).start()

    def sibling_copy(member):
        return pltpu.make_async_remote_copy(
            src_ref=weights.at[member, pl.ds(0, half)],
            dst_ref=weights.at[member, pl.ds(half, half)],
            send_sem=sibling_send.at[member],
            recv_sem=sibling_recv.at[member],
            device_id=sibling,
            device_id_type=MESH,
        )

    def cast(begin, end):
        for turn in range(begin, end):
            member, at = turn // tile_count, turn % tile_count * tile_rows
            tile_load(turn).wait()
            weights[member, at : at + tile_rows, :] = tiles[turn % depth].astype(low)
            if turn + depth < 3 * tile_count:
                tile_load(turn + depth).start()

    if half > units:
        for member in range(3):
            weights[member, units:half, :] = jnp.zeros((half - units, width), low)

    own_slots = lax.broadcasted_iota(jnp.int32, (rows, rows), 0) + me * rows

    def find(source, total):
        return total + jnp.where(deal_row(deal_ref, source, rows) == own_slots, source, 0)

    found = lax.fori_loop(0, devices, find, jnp.zeros((rows, rows), jnp.int32))
    source = jnp.sum(found, axis=1, keepdims=True)
    earlier = (to_row(source) == source) & (along_ids < down_ids)
    recv_place = source * peer_rows + jnp.sum(earlier.astype(jnp.int32), axis=1, keepdims=True)
    placer = (
        lax.broadcasted_iota(jnp.int32, (rows, packed), 1) == spread(recv_place)
    ).astype(low)

    pack(1, cotangent_ref)
    if near_weights:
        line_pass(1)
    rows_start(1)

    ids = lax.broadcasted_iota(jnp.int32, (rows, 1), 0)
    end = jnp.int32(0)
    document = jnp.zeros((rows, 1), jnp.int32)
    begin = jnp.zeros((rows, 1), jnp.int32)
    for member in range(lengths_ref.shape[1]):
        end = end + lengths_ref[0, member]
        passed = ids >= end
        document = document + passed.astype(jnp.int32)
        begin = jnp.where(passed, end, begin)
    doc_col_ref[...] = document
    doc_row_ref[...] = to_row(document)
    angles = (ids - begin).astype(full) * frequency_ref[...]
    cosine_ref[...] = jnp.cos(angles)
    sine_ref[...] = jnp.sin(angles)
    cast(0, tile_count)
    if near_weights:
        rep_pass(0)
    sibling_copy(0).start()
    cast(tile_count, 2 * tile_count)
    sibling_copy(1).start()
    if near_weights:
        rep_pass(1)
    cast(2 * tile_count, 3 * tile_count)
    sibling_copy(2).start()
    near_stores = [
        pltpu.make_async_copy(
            weights.at[member, pl.ds(0, half)],
            weights_hbm.at[member, pl.ds(0, half)],
            store_sems.at[2 + member],
        )
        for member in range(3)
    ]
    for store in near_stores:
        store.start()

    def placed(kind):
        stacked = arrived[kind].astype(full).reshape(packed, width).astype(low)
        return jnp.dot(placer, stacked, preferred_element_type=full)

    if near_weights:
        for hop in range(1, shards):
            gain_copy(hop, lax.rem(shard + shards - hop, shards)).wait_recv()
        span = gains_in.shape[1]
        line_ids = lax.broadcasted_iota(jnp.int32, (gain_blocks.shape[2], width), 0)
        lane_ids = lax.broadcasted_iota(jnp.int32, (gain_blocks.shape[2], width), 1)
        joined = jnp.zeros((gain_blocks.shape[1], width), full)
        for member in range(shards):
            move = ((lane_ids - member * span == line_ids) & (line_ids < span)).astype(low)
            joined = joined + jnp.dot(gain_blocks[member], move, preferred_element_type=full)
        gains_ref[...] = joined[: gains_ref.shape[0]]
    else:
        gains_ref[...] = gains_in[...]
    rows_arrive(0)
    inputs = placed(0)
    inputs_ref[...] = inputs.astype(low)
    normed_ref[...] = (inputs * rms_scale(inputs) * gains_ref[0:1, :]).astype(low)
    if near_weights:
        pair_arrive(0)
        qkv_matrix = w_qkv[...].reshape(width, w_qkv.shape[2])
    else:
        qkv_matrix = qkv_in[...]
    projected[...] = jnp.dot(normed_ref[...], qkv_matrix, preferred_element_type=full)
    def turned(start):
        front = projected[:, pl.ds(start, half_key)]
        back = projected[:, pl.ds(start + half_key, half_key)]
        cosine, sine = cosine_ref[...], sine_ref[...]
        return (
            (front * cosine - back * sine).astype(low),
            (back * cosine + front * sine).astype(low),
        )

    keys_ref[:, :half_key], keys_ref[:, half_key:] = turned(query_width)
    values_ref[...] = projected[:, query_width + key_width :].astype(low)

    for head in range(heads):
        start = head * key_width
        cols = pl.ds(start, key_width)
        front, back = turned(start)
        queries_ref[:, pl.ds(start, half_key)] = front
        queries_ref[:, pl.ds(start + half_key, half_key)] = back
        allowed = (doc_col_ref[...] == doc_row_ref[...]) & (
            lax.broadcasted_iota(jnp.int32, (rows, rows), 0)
            >= lax.broadcasted_iota(jnp.int32, (rows, rows), 1)
        )
        scores = against_cols(queries_ref[:, cols], keys_ref[...]) * (HD ** (-0.5) / CAP_LIMIT)
        capped = jnp.where(allowed, CAP_LIMIT * jnp.tanh(scores), MASKED_SCORE)
        powers = jnp.exp(capped - jnp.max(capped, axis=-1, keepdims=True))
        probs = powers / jnp.sum(powers, axis=-1, keepdims=True)
        attended_ref[:, cols] = jnp.dot(
            probs.astype(low), values_ref[...], preferred_element_type=full
        ).astype(low)

    if near_weights:
        pair_arrive(1)
        out_matrix = w_out[...].reshape(query_width, width)
    else:
        out_matrix = out_in[...]
    stores = []
    if near_weights:
        stores.append(pltpu.make_async_copy(w_qkv, qkv_hbm, store_sems.at[0]))
        stores.append(pltpu.make_async_copy(w_out, outw_hbm, store_sems.at[1]))
    else:
        stores.append(pltpu.make_async_copy(qkv_in, qkv_hbm, store_sems.at[0]))
        stores.append(pltpu.make_async_copy(out_in, outw_hbm, store_sems.at[1]))
    for store in stores:
        store.start()
    for member in range(3):
        sibling_copy(member).wait_recv()
        store = pltpu.make_async_copy(
            weights.at[member, pl.ds(half, half)],
            weights_hbm.at[member, pl.ds(half, half)],
            store_sems.at[5 + member],
        )
        store.start()
        stores.append(store)
    branch = jnp.dot(attended_ref[...], out_matrix, preferred_element_type=full)
    branch_ref[...] = branch
    middle = inputs_ref[...].astype(full) + branch * rms_scale(branch) * gains_ref[1:2, :]
    middle_ref[...] = middle
    normed_two_ref[...] = (middle * rms_scale(middle) * gains_ref[2:3, :]).astype(low)
    rows_arrive(1)
    upstream_ref[...] = placed(1).astype(low)
    stores.extend(near_stores)

    for kind in range(2):

        @pl.loop(1, devices)
        def _(hop, kind=kind):
            row_copy(kind, hop, lax.rem(me + hop, devices), me).wait_send()

        if near_weights:
            for block in others():
                line_copy(kind, block, place).wait_send()
                for hop in range(1, share):
                    rep_copy(kind, block, hop, quarter).wait_send()
            for block in range(line):
                pair_copy(kind, block, core).wait_send()
    if near_weights:
        for hop in range(1, shards):
            gain_copy(hop, shard).wait_send()
    for member in range(3):
        sibling_copy(member).wait_send()
    for store in stores:
        store.wait()


def bring_and_attend(
    line, replicas, near_weights, tokens, cotangent, deal, small, gu, down, key_width
):
    gains_in, qkv_in, out_in = small[:3]
    rows, width = tokens.shape
    shards = 2 * line
    devices = replicas * shards
    share = min(4, replicas)
    block_rows = round_up(rows // devices, 8)
    units = down.shape[0]
    half = round_up(units, LANES)
    low = jnp.bfloat16
    full = jnp.float32
    vmem = pl.BlockSpec(memory_space=pltpu.VMEM)
    hbm = pl.BlockSpec(memory_space=pl.ANY)
    dma = pltpu.SemaphoreType.DMA
    qkv_width = qkv_in.shape[1]
    query_width = qkv_width - 2 * key_width
    if near_weights:
        qkv_shape = (shards, *qkv_in.shape)
        out_shape = (shards, *out_in.shape)
    else:
        qkv_shape = qkv_in.shape
        out_shape = out_in.shape
    tile_rows = max(size for size in range(16, 145, 16) if units % size == 0)
    hold = near_weights
    qkv_scratch = qkv_shape if hold else (shards, 16, LANES)
    out_scratch = out_shape if hold else (shards, 16, LANES)
    gain_lanes = round_up(width // shards, LANES) if hold else LANES

    def array(shape, dtype):
        return jax.ShapeDtypeStruct(shape, dtype)

    return pl.pallas_call(
        functools.partial(bring_kernel, line, replicas, near_weights),
        out_shape=(
            array((rows, width), low),
            array((rows, width), low),
            array((rows, width), low),
            array((rows, query_width), low),
            array((rows, key_width), low),
            array((rows, key_width), low),
            array((rows, query_width), low),
            array((rows, width), full),
            array((rows, width), full),
            array((rows, width), low),
            array((4, width), full),
            array((rows, key_width // 2), full),
            array((rows, key_width // 2), full),
            array((rows, 1), jnp.int32),
            array((1, rows), jnp.int32),
            array(qkv_shape, low),
            array(out_shape, low),
            array((3, 2 * half, width), low),
        ),
        in_specs=[vmem] * 6
        + [pl.BlockSpec(memory_space=pltpu.SMEM), vmem]
        + [hbm] * 2,
        out_specs=(vmem,) * 15 + (hbm,) * 3,
        scratch_shapes=[
            pltpu.VMEM(qkv_scratch, low),
            pltpu.VMEM(out_scratch, low),
            pltpu.VMEM((shards, 16, gain_lanes), low),
            pltpu.VMEM((3, 2 * half, width), low),
            pltpu.VMEM((4, tile_rows, width), full),
            pltpu.VMEM((2, devices, block_rows, width), low),
            pltpu.VMEM((2, devices, block_rows, width), low),
            pltpu.VMEM((rows, qkv_width), full),
            dma((4,)),
            dma((8,)),
            dma((2, devices)),
            dma((2, devices)),
            dma((2, line)),
            dma((2, line)),
            dma((2, line, share)),
            dma((2, line, share)),
            dma((2, line)),
            dma((2, line)),
            dma((shards,)),
            dma((shards,)),
            dma((3,)),
            dma((3,)),
        ],
        compiler_params=pltpu.CompilerParams(
            collective_id=2, has_side_effects=True, vmem_limit_bytes=63 * 1024 * 1024
        ),
        cost_estimate=pl.CostEstimate(
            flops=6 * rows * width * qkv_width,
            bytes_accessed=3 * units * width * 8,
            transcendentals=2 * rows * rows * 4,
        ),
    )(tokens, cotangent, deal, *small, gu, down)


def adam_half_kernel(which, first_half, second_half, *refs):
    del which
    inputs, results = refs[:6], refs[-10:]
    part, member = pl.program_id(0), pl.program_id(1)
    gradient = jnp.where(part == 0, first_half[0], second_half[0]).astype(jnp.float32)

    def step(rows_in, rows_out, rate, decay):
        master, first, second = (ref[...].reshape(gradient.shape) for ref in rows_in)
        moment = BETA_FIRST * first + (1.0 - BETA_FIRST) * gradient
        square = BETA_SECOND * second + (1.0 - BETA_SECOND) * gradient * gradient
        moment_hat = moment * (1.0 / (1.0 - BETA_FIRST**STEP))
        square_hat = square * (1.0 / (1.0 - BETA_SECOND**STEP))
        updated = master - rate * (moment_hat / (jnp.sqrt(square_hat) + ADAM_EPS) + decay * master)
        for ref, value in zip(rows_out, (updated, moment, square, gradient, updated)):
            ref[...] = value.astype(ref.dtype).reshape(ref.shape)

    @pl.when(member == 0)
    def _():
        step(inputs[:3], results[:5], LEARN_RATES[3], DECAY_RATES[3])

    @pl.when(member > 0)
    def _():
        step(inputs[3:], results[5:], LEARN_RATES[2], DECAY_RATES[2])


def adam_half(which, halves, arrays, begun=()):
    members, half_rows, width = halves[0].shape
    tile = half_rows // 2
    down, gu = arrays[0], arrays[3]

    def down_at(part, member, sub, chosen):
        return (part * 4 + chosen[part] * 2 + jnp.where(member == 0, sub, 1), 0)

    def gu_at(part, member, sub, chosen):
        row = part * 4 + chosen[part] * 2 + jnp.where(member == 0, 0, sub)
        return (jnp.maximum(member - 1, 0), row, 0)

    def first_at(part, member, sub, chosen):
        return (jnp.where(part == 0, member, members - 1), jnp.where(part == 0, sub, 1), 0)

    def second_at(part, member, sub, chosen):
        return (jnp.where(part == 0, 0, member), jnp.where(part == 0, 0, sub), 0)

    down_block = pl.BlockSpec((tile, width), down_at)
    gu_block = pl.BlockSpec((1, tile, width), gu_at)
    half_block = (1, tile, width)
    hbm = pl.BlockSpec(memory_space=pl.ANY)
    shapes = []
    for like in (down, gu):
        shapes.extend([jax.ShapeDtypeStruct(like.shape, jnp.float32)] * 4)
        shapes.append(jax.ShapeDtypeStruct(like.shape, jnp.bfloat16))
    count = members * half_rows * width * 2
    return pl.pallas_call(
        adam_half_kernel,
        out_shape=tuple(shapes),
        grid_spec=pltpu.PrefetchScalarGridSpec(
            num_scalar_prefetch=1,
            grid=(2, members, 2),
            in_specs=[
                pl.BlockSpec(half_block, first_at),
                pl.BlockSpec(half_block, second_at),
                *[down_block] * 3,
                *[gu_block] * 3,
                *[hbm] * len(begun),
            ],
            out_specs=(*[down_block] * 5, *[gu_block] * 5),
        ),
        input_output_aliases={9 + at: at for at in range(len(begun))},
        compiler_params=pltpu.CompilerParams(vmem_limit_bytes=60 * 1024 * 1024),
        cost_estimate=pl.CostEstimate(
            flops=16 * count, bytes_accessed=32 * count, transcendentals=2 * count
        ),
    )(which, *halves, *arrays, *begun)


def local(
    tokens,
    cotangent,
    lengths,
    deal,
    w_qkv,
    w_out,
    w_gu,
    w_down,
    gains,
    first_qkv,
    first_out,
    first_gu,
    first_down,
    first_gains,
    second_qkv,
    second_out,
    second_gu,
    second_down,
    second_gains,
):
    row_count, width = tokens.shape
    shards = lax.axis_size("shard")
    replicas = lax.axis_size("rep")
    line = shards // 2
    devices = replicas * shards
    deal_blocks = deal.reshape(deal.shape[0] // LANES, LANES)
    exponent = np.arange(HD // 2, dtype=np.float32) * np.float32(-2.0 / HD)
    frequency = jnp.asarray((np.float32(ROPE_BASE) ** exponent)[None, :])
    near_weights = w_qkv.shape[0] % 16 == 0
    if near_weights:
        first_weights = (gains, w_qkv, w_out)
    else:
        first_weights = (
            lax.all_gather(gains.astype(jnp.bfloat16), "shard", axis=1, tiled=True).astype(
                jnp.float32
            ),
            lax.all_gather(w_qkv.astype(jnp.bfloat16), "shard", axis=0, tiled=True),
            lax.all_gather(w_out.astype(jnp.bfloat16), "shard", axis=0, tiled=True),
        )
    (
        inputs,
        upstream,
        normed_one,
        queries,
        key_rows,
        value_rows,
        attended,
        branch,
        middle,
        normed_two,
        gain_values,
        cosine_table,
        sine_table,
        doc_col,
        doc_row,
        full_qkv,
        full_out,
        ff_weights,
    ) = bring_and_attend(
        line,
        replicas,
        near_weights,
        tokens,
        cotangent,
        deal_blocks,
        (*first_weights, lengths, frequency),
        w_gu,
        w_down,
        HD,
    )
    full_qkv = full_qkv.reshape(width, w_qkv.shape[1])
    full_out = full_out.reshape(H * HD, width)
    output_rows, last_gain_grad, grad_normed_two, ff_grads = feed_forward(
        line,
        replicas,
        normed_two,
        middle,
        upstream,
        gain_values,
        ff_weights,
    )
    first_half, second_half, qkv_sums, out_sums, output, input_grad = back_and_reduce(
        line,
        replicas,
        (
            grad_normed_two,
            middle,
            upstream,
            branch,
            inputs,
            normed_one,
            attended,
            queries,
            key_rows,
            value_rows,
            cosine_table,
            sine_table,
            doc_col,
            doc_row,
            gain_values,
            last_gain_grad,
            output_rows,
            deal_blocks,
        ),
        full_qkv,
        full_out,
        ff_grads,
    )
    output = output.astype(jnp.bfloat16)
    input_grad = input_grad.astype(jnp.bfloat16)

    bits = replicas.bit_length() - 1
    flips = (1, 1 << (bits - 1))
    other_halves = tuple(
        lax.ppermute(half, "rep", [(member, member ^ flip) for member in range(replicas)])
        for half, flip in zip((first_half, second_half), flips)
    )
    rep = lax.axis_index("rep")
    held = jnp.stack([lax.rem(lax.div(rep, flip), 2) for flip in flips]).astype(jnp.int32)
    ff_arrays = (w_down, first_down, second_down, w_gu, first_gu, second_gu)
    begun = adam_half(held, (first_half, second_half), ff_arrays)
    (
        new_down,
        moment_down,
        square_down,
        summed_down,
        copy_down,
        new_gu,
        moment_gu,
        square_gu,
        summed_gu,
        copy_gu,
    ) = adam_half(1 - held, other_halves, ff_arrays, begun)
    summed_qkv = qkv_sums[: w_qkv.shape[0]].astype(jnp.float32)
    summed_out = out_sums[: w_out.shape[0]].astype(jnp.float32)
    gain_span = gains.shape[1]
    gain_rows = qkv_sums[-16:-4, H * HD : H * HD + width // 3]
    summed_gains = lax.dynamic_slice(
        gain_rows.reshape(3, gains.shape[0], width // 3)
        .transpose(1, 0, 2)
        .reshape(gains.shape[0], width),
        (0, lax.axis_index("shard") * gain_span),
        (gains.shape[0], gain_span),
    ).astype(jnp.float32)
    new_qkv, moment_qkv, square_qkv = adamw_step(
        w_qkv, summed_qkv, first_qkv, second_qkv, LEARN_RATES[0], DECAY_RATES[0]
    )
    new_out, moment_out, square_out = adamw_step(
        w_out, summed_out, first_out, second_out, LEARN_RATES[1], DECAY_RATES[1]
    )
    new_gains, moment_gains, square_gains = adamw_step(
        gains, summed_gains, first_gains, second_gains, LEARN_RATES[4], DECAY_RATES[4]
    )
    return (
        output,
        input_grad,
        new_qkv,
        new_out,
        new_gu,
        new_down,
        new_gains,
        moment_qkv,
        moment_out,
        moment_gu,
        moment_down,
        moment_gains,
        square_qkv,
        square_out,
        square_gu,
        square_down,
        square_gains,
        summed_qkv,
        summed_out,
        summed_gu,
        summed_down,
        summed_gains,
        new_qkv.astype(jnp.bfloat16),
        new_out.astype(jnp.bfloat16),
        copy_gu,
        copy_down,
        new_gains.astype(jnp.bfloat16),
    )


def solution(mesh):
    placed = (
        P(("rep", "shard"), None),
        P(("rep", "shard"), None),
        P(("rep", "shard"), None),
        P(),
        P("shard", None),
        P("shard", None),
        P(None, "shard", None),
        P("shard", None),
        P(None, "shard"),
        P("shard", None),
        P("shard", None),
        P(None, "shard", None),
        P("shard", None),
        P(None, "shard"),
        P("shard", None),
        P("shard", None),
        P(None, "shard", None),
        P("shard", None),
        P(None, "shard"),
    )
    return jax.shard_map(
        local,
        mesh=mesh,
        in_specs=placed,
        out_specs=(
            P(("rep", "shard"), None),
            P(("rep", "shard"), None),
            P("shard", None),
            P("shard", None),
            P(None, "shard", None),
            P("shard", None),
            P(None, "shard"),
            P("shard", None),
            P("shard", None),
            P(None, "shard", None),
            P("shard", None),
            P(None, "shard"),
            P("shard", None),
            P("shard", None),
            P(None, "shard", None),
            P("shard", None),
            P(None, "shard"),
            P("shard", None),
            P("shard", None),
            P(None, "shard", None),
            P("shard", None),
            P(None, "shard"),
            P("shard", None),
            P("shard", None),
            P(None, "shard", None),
            P("shard", None),
            P(None, "shard"),
        ),
        check_vma=False,
    )
```

```python
import functools

import jax
import jax.numpy as jnp
import numpy as np
from jax import lax
from jax.experimental import pallas as pl
from jax.experimental.pallas import tpu as pltpu
from jax.sharding import PartitionSpec as P

H = 4
KV = 1
HD = 256
STEP = 10


CAP_LIMIT = 50.0
NORM_EPS = 1e-06
ROPE_BASE = 10000.0
MASKED_SCORE = -1e30
BETA_FIRST = 0.5
BETA_SECOND = 0.5
ADAM_EPS = 1e-08
LEARN_RATES = (0.05, 0.1, 0.03, 0.012, 0.4)
DECAY_RATES = (0.1, 0.1, 0.1, 0.1, 0.0)
GELU_COEF = 0.7978845608028654
GELU_CUBIC = 0.044715


def rms_scale(values):
    return lax.rsqrt(jnp.mean(values * values, axis=-1, keepdims=True) + NORM_EPS)


def norm_backward(grad_out, values, inverse_rms, gain_row):
    scaled = grad_out * gain_row
    inner = jnp.mean(scaled * values, axis=-1, keepdims=True)
    grad_in = inverse_rms * scaled - values * inverse_rms * inverse_rms * inverse_rms * inner
    grad_gain = jnp.sum(grad_out * values * inverse_rms, axis=0)
    return (grad_in, grad_gain)


def cross_rows(leading, trailing):
    return lax.dot_general(
        leading, trailing, (((0,), (0,)), ((), ())), preferred_element_type=jnp.float32
    )


def against_cols(leading, trailing):
    return lax.dot_general(
        leading, trailing, (((1,), (1,)), ((), ())), preferred_element_type=jnp.float32
    )


def adamw_step(master, gradient, first_moment, second_moment, rate, decay):
    moment = BETA_FIRST * first_moment + (1.0 - BETA_FIRST) * gradient
    square = BETA_SECOND * second_moment + (1.0 - BETA_SECOND) * gradient * gradient
    moment_hat = moment / (1.0 - BETA_FIRST**STEP)
    square_hat = square / (1.0 - BETA_SECOND**STEP)
    updated = master - rate * (moment_hat / (jnp.sqrt(square_hat) + ADAM_EPS) + decay * master)
    return (updated, moment, square)


LANES = 128
UNIT_TILE = 256
MESH = pl.DeviceIdType.MESH


def round_up(count, step):
    return -(-count // step) * step


def partner_of(index, bit):
    value = lax.rem(lax.div(index, 1 << bit), 2)
    return index + (1 - 2 * value) * (1 << bit), value


EARLY = 1


def deal_row(deal_ref, device, rows):
    lines = rows // LANES
    return jnp.concatenate(
        [deal_ref[pl.ds(device * lines + at, 1), :] for at in range(lines)], axis=1
    )


def halving_spans(rep, bits, part, part_rows):
    spans = []
    first = part * part_rows
    size = part_rows
    for bit in range(bits) if part == 0 else range(bits - 1, -1, -1):
        size //= 2
        partner, value = partner_of(rep, bit)
        spans.append((partner, first + value * size, first + (1 - value) * size, size))
        first = first + value * size
    return spans


def at_rows(first, size):
    return pl.ds(pl.multiple_of(first, 16), size)


def feed_kernel(
    line,
    replicas,
    own_rows,
    middle_ref,
    upstream_ref,
    gain_ref,
    weights_hbm,
    out_ref,
    gain_grad_ref,
    back_ref,
    grads_ref,
    weights,
    blocks,
    acts,
    partial,
    chain,
    sibling_out,
    sibling_in,
    landing,
    load_sems,
    store_sems,
    gather_send,
    gather_recv,
    chain_send,
    chain_recv,
    sibling_send,
    sibling_recv,
    half_send,
    half_recv,
):
    rep = lax.axis_index("rep")
    shard = lax.axis_index("shard")
    core = lax.rem(shard, 2)
    place = lax.div(shard, 2)
    sibling = (rep, shard + 1 - 2 * core)
    left = (rep, shard - 2)
    right = (rep, shard + 2)
    has_left = place > 0
    has_right = place < line - 1
    rows = own_rows.shape[0] // 2
    width = own_rows.shape[1]
    half = weights.shape[1] // 2
    tiles = 2 * half // UNIT_TILE

    load = pltpu.make_async_copy(weights_hbm, weights, load_sems.at[0])
    load.start()

    barrier = pltpu.get_barrier_semaphore()
    pl.semaphore_signal(barrier, inc=1, device_id=sibling, device_id_type=MESH)

    @pl.when(has_left)
    def _():
        pl.semaphore_signal(barrier, inc=1, device_id=left, device_id_type=MESH)

    @pl.when(has_right)
    def _():
        pl.semaphore_signal(barrier, inc=1, device_id=right, device_id_type=MESH)

    bits = replicas.bit_length() - 1
    greeted = sorted({0, bits - 1})
    for bit in greeted:
        partner, _ = partner_of(rep, bit)
        pl.semaphore_signal(barrier, inc=1, device_id=(partner, shard), device_id_type=MESH)

    def block_span(block):
        return pl.ds(pl.multiple_of(block * rows, rows), rows)

    for part in range(2):
        blocks[0, part, block_span(place), :] = own_rows[part * rows : (part + 1) * rows, :]

    pl.semaphore_wait(
        barrier,
        1 + len(greeted) + has_left.astype(jnp.int32) + has_right.astype(jnp.int32),
    )

    def gather_copy(phase, part, way, step, block):
        return pltpu.make_async_remote_copy(
            src_ref=blocks.at[phase, part, block_span(block)],
            dst_ref=blocks.at[phase, part, block_span(block)],
            send_sem=gather_send.at[phase, part, way, step],
            recv_sem=gather_recv.at[phase, part, way, step],
            device_id=left if way else right,
            device_id_type=MESH,
        )

    def gather_start(phase, part, step):
        @pl.when(has_right & (place - step >= 0))
        def _():
            gather_copy(phase, part, 0, step, place - step).start()

        @pl.when(has_left & (place + step <= line - 1))
        def _():
            gather_copy(phase, part, 1, step, place + step).start()

    def gather_arrive(phase, part, step):
        @pl.when(place - 1 - step >= 0)
        def _():
            gather_copy(phase, part, 0, step, place - 1 - step).wait_recv()

        @pl.when(place + 1 + step <= line - 1)
        def _():
            gather_copy(phase, part, 1, step, place + 1 + step).wait_recv()

    def gather_drain(phase, part):
        @pl.loop(0, line - 1)
        def _(step):
            @pl.when(has_right & (place - step >= 0))
            def _():
                gather_copy(phase, part, 0, step, place - step).wait_send()

            @pl.when(has_left & (place + step <= line - 1))
            def _():
                gather_copy(phase, part, 1, step, place + step).wait_send()

    def chain_copy(phase, part, way, packet, block):
        return pltpu.make_async_remote_copy(
            src_ref=partial.at[part, block_span(block)],
            dst_ref=chain.at[part, way, packet],
            send_sem=chain_send.at[phase, part, way, packet],
            recv_sem=chain_recv.at[phase, part, way, packet],
            device_id=left if way else right,
            device_id_type=MESH,
        )

    def chain_add(phase, part, way, packet, block):
        chain_copy(phase, part, way, packet, block).wait_recv()
        span = block_span(block)
        partial[part, span, :] = (
            partial[part, span, :].astype(jnp.float32) + chain[part, way, packet].astype(jnp.float32)
        ).astype(partial.dtype)

    def chain_turn(phase, part, turn):
        outward = turn - place

        @pl.when(outward >= 0)
        def _():
            @pl.when(has_left)
            def _():
                chain_add(phase, part, 0, outward, line - 1 - outward)

            chain_copy(phase, part, 0, outward, line - 1 - outward).start()

        inward = turn - (line - 1 - place)

        @pl.when(inward >= 0)
        def _():
            @pl.when(has_right)
            def _():
                chain_add(phase, part, 1, inward, inward)

            chain_copy(phase, part, 1, inward, inward).start()

    def chain_finish(phase, part):
        out = slice(part * rows, (part + 1) * rows)
        back_ref[out, :] = partial[part, block_span(place), :].astype(jnp.float32)

        @pl.when(has_left)
        def _():
            last = line - 1 - place
            chain_copy(phase, part, 0, last, place).wait_recv()
            back_ref[out, :] += chain[part, 0, last].astype(jnp.float32)

        @pl.when(has_right)
        def _():
            chain_copy(phase, part, 1, place, place).wait_recv()
            back_ref[out, :] += chain[part, 1, place].astype(jnp.float32)

    def chain_drain(phase, part):
        @pl.loop(0, line - 1)
        def _(packet):
            @pl.when(line - 1 - packet > place)
            def _():
                chain_copy(phase, part, 0, packet, line - 1 - packet).wait_send()

            @pl.when(packet < place)
            def _():
                chain_copy(phase, part, 1, packet, packet).wait_send()

    def sweep(phase, part, work, reduce=None, last=None, beside=None):
        @pl.loop(1, line)
        def _(turn):
            gather_arrive(phase, part, turn - 1)

            @pl.when(turn < line - 1)
            def _():
                gather_start(phase, part, turn)
                if reduce is not None:
                    chain_turn(*reduce, turn)

            if last is not None:

                @pl.when(turn == line - 1)
                def _():
                    last()

            @pl.loop(0, line // 2)
            def _(pair):
                ready = jnp.maximum(jnp.abs(2 * pair - place), jnp.abs(2 * pair + 1 - place))

                @pl.when(ready == turn)
                def _():
                    work(part, pair)

            if beside is not None:
                beside(turn)

    def pair_span(pair):
        return pl.ds(pl.multiple_of(pair * 2 * rows, 2 * rows), 2 * rows)

    def token_span(part, pair):
        first = part * line * rows
        return pl.ds(pl.multiple_of(first + pair * 2 * rows, 2 * rows), 2 * rows)

    def unit_span(tile):
        return pl.ds(pl.multiple_of(tile * UNIT_TILE, UNIT_TILE), UNIT_TILE)

    def forward(part, pair):
        span = token_span(part, pair)

        @pl.loop(0, tiles)
        def _(tile):
            cols = unit_span(tile)
            rows_in = blocks[0, part, pair_span(pair), :]
            gate = against_cols(rows_in, weights[1, cols, :])
            upper = against_cols(rows_in, weights[2, cols, :])
            tanh_inner = jnp.tanh(GELU_COEF * (gate + GELU_CUBIC * gate * gate * gate))
            lifted = 0.5 * (1.0 + tanh_inner)
            activated = gate * lifted
            slope = lifted + 0.5 * gate * (1.0 - tanh_inner * tanh_inner) * GELU_COEF * (
                1.0 + 3.0 * GELU_CUBIC * gate * gate
            )
            acts[0, span, cols] = (activated * upper).astype(acts.dtype)
            acts[1, span, cols] = (upper * slope).astype(acts.dtype)
            acts[2, span, cols] = activated.astype(acts.dtype)

        partial[part, pair_span(pair), :] = jnp.dot(
            acts[0, span, :], weights[0], preferred_element_type=jnp.float32
        ).astype(partial.dtype)

    def backward(part, pair):
        span = token_span(part, pair)

        @pl.loop(0, tiles)
        def _(tile):
            cols = unit_span(tile)
            grad_hidden = against_cols(blocks[1, part, pair_span(pair), :], weights[0, cols, :])
            for member in (1, 2):
                acts[member, span, cols] = (
                    grad_hidden * acts[member, span, cols].astype(jnp.float32)
                ).astype(acts.dtype)

        partial[part, pair_span(pair), :] = (
            jnp.dot(acts[1, span, :], weights[1], preferred_element_type=jnp.float32)
            + jnp.dot(acts[2, span, :], weights[2], preferred_element_type=jnp.float32)
        ).astype(partial.dtype)

    def output_half(part):
        out = slice(part * rows, (part + 1) * rows)
        feed = back_ref[out, :]
        upstream = upstream_ref[out, :].astype(jnp.float32)
        gain = gain_ref[3:4, :]
        inverse = lax.rsqrt(jnp.mean(feed * feed, axis=-1, keepdims=True) + NORM_EPS)
        scaled = upstream * gain
        inner = jnp.mean(scaled * feed, axis=-1, keepdims=True)
        blocks[1, part, block_span(place), :] = (
            inverse * scaled - feed * inverse * inverse * inverse * inner
        ).astype(blocks.dtype)
        gather_start(1, part, 0)
        gain_grad = jnp.sum(upstream * feed * inverse, axis=0, keepdims=True)
        if part == 0:
            gain_grad_ref[...] = gain_grad
        else:
            gain_grad_ref[...] += gain_grad
        out_ref[out, :] = (middle_ref[out, :] + feed * inverse * gain).astype(out_ref.dtype)

    def sibling_copy(member):
        return pltpu.make_async_remote_copy(
            src_ref=sibling_out.at[member],
            dst_ref=sibling_in.at[member],
            send_sem=sibling_send.at[member],
            recv_sem=sibling_recv.at[member],
            device_id=sibling,
            device_id_type=MESH,
        )

    def store_copy(member):
        return pltpu.make_async_copy(
            sibling_in.at[member], grads_ref.at[member], store_sems.at[member]
        )

    cuts = [(start, min(512, half - start)) for start in range(0, half, 512)]

    def far_grad(part, member):
        tokens = line * rows
        trailing = jnp.where(member == 0, 1, 0)
        for start, size in cuts:
            span = slice(start, start + size)
            piece = cross_rows(
                acts[member, part * tokens : (part + 1) * tokens, half + start : half + start + size],
                blocks[trailing, part],
            )
            if part == 1:
                piece = piece + sibling_out[member, span, :].astype(jnp.float32)
            sibling_out[member, span, :] = piece.astype(sibling_out.dtype)
        if part == 1:
            sibling_copy(member).start()

    first_spans = [halving_spans(rep, bits, part, half // 2)[0] for part in range(2)]

    def halve(member, part):
        partner, keep, give, size = first_spans[part]
        return pltpu.make_async_remote_copy(
            src_ref=sibling_in.at[member, at_rows(give, size)],
            dst_ref=landing.at[member, part],
            send_sem=half_send.at[member, part],
            recv_sem=half_recv.at[member, part],
            device_id=(partner, shard),
            device_id_type=MESH,
        )

    def near_grad(member):
        trailing = jnp.where(member == 0, 1, 0)
        sibling_copy(member).wait_recv()
        for start, size in cuts:
            span = slice(start, start + size)
            piece = cross_rows(
                acts[member, :, span], blocks[trailing].reshape(2 * line * rows, width)
            )
            sibling_in[member, span, :] = (
                sibling_in[member, span, :].astype(jnp.float32) + piece
            ).astype(sibling_in.dtype)

        @pl.when(member < EARLY)
        def _():
            for part in range(2):
                halve(member, part).start()

        @pl.when(member >= EARLY)
        def _():
            store_copy(member).start()

    def share(turn, count, turns):
        return lax.div(turn * count, turns), lax.div((turn + 1) * count, turns)

    def first_grads(turn):
        @pl.when(turn < line - 1)
        def _():
            @pl.loop(*share(turn - 1, 3, line - 2))
            def _(member):
                far_grad(0, member)

    def last_grads(turn):
        @pl.loop(*share(turn, 6, line - 1))
        def _(unit):
            @pl.when(unit < 3)
            def _():
                far_grad(1, unit)

            @pl.when(unit >= 3)
            def _():
                near_grad(unit - 3)

    def turn_around(part):
        chain_finish(0, part)
        output_half(part)

    gather_start(0, 0, 0)
    load.wait()
    sweep(0, 0, forward, last=lambda: gather_start(0, 1, 0))
    chain_turn(0, 0, 0)
    sweep(0, 1, forward, reduce=(0, 0), last=lambda: turn_around(0))
    chain_turn(0, 1, 0)
    chain_drain(0, 0)
    sweep(1, 0, backward, reduce=(0, 1), last=lambda: turn_around(1))
    chain_turn(1, 0, 0)
    chain_drain(0, 1)
    sweep(1, 1, backward, reduce=(1, 0), beside=first_grads)
    chain_turn(1, 1, 0)
    chain_finish(1, 0)

    @pl.loop(0, line - 1)
    def _(turn):
        @pl.when(turn > 0)
        def _():
            chain_turn(1, 1, turn)

        last_grads(turn)

    chain_finish(1, 1)
    for member in range(EARLY):
        for part in range(2):
            halve(member, part).wait_recv()
            partner, keep, give, size = first_spans[part]
            kept = at_rows(keep, size)
            sibling_in[member, kept, :] = (
                sibling_in[member, kept, :].astype(jnp.float32)
                + landing[member, part].astype(jnp.float32)
            ).astype(sibling_in.dtype)
        store_copy(member).start()
    for part in range(2):
        for phase in range(2):
            gather_drain(phase, part)
        chain_drain(1, part)
        for member in range(EARLY):
            halve(member, part).wait_send()
    for member in range(3):
        sibling_copy(member).wait_send()
        store_copy(member).wait()


def feed_forward(line, replicas, normed, middle, upstream, gains, weights):
    rows, width = normed.shape
    half = weights.shape[1] // 2
    low = jnp.bfloat16
    full = jnp.float32
    vmem = pl.BlockSpec(memory_space=pltpu.VMEM)
    hbm = pl.BlockSpec(memory_space=pl.ANY)
    tokens = line * rows
    return pl.pallas_call(
        functools.partial(feed_kernel, line, replicas),
        out_shape=(
            jax.ShapeDtypeStruct((rows, width), low),
            jax.ShapeDtypeStruct((1, width), full),
            jax.ShapeDtypeStruct((rows, width), full),
            jax.ShapeDtypeStruct((3, half, width), low),
        ),
        in_specs=[vmem, vmem, vmem, vmem, hbm],
        out_specs=(vmem, vmem, vmem, hbm),
        scratch_shapes=[
            pltpu.VMEM((3, 2 * half, width), low),
            pltpu.VMEM((2, 2, tokens // 2, width), low),
            pltpu.VMEM((3, tokens, 2 * half), low),
            pltpu.VMEM((2, tokens // 2, width), low),
            pltpu.VMEM((2, 2, line - 1, rows // 2, width), low),
            pltpu.VMEM((3, half, width), low),
            pltpu.VMEM((3, half, width), low),
            pltpu.VMEM((EARLY, 2, half // 4, width), low),
            pltpu.SemaphoreType.DMA((1,)),
            pltpu.SemaphoreType.DMA((3,)),
            pltpu.SemaphoreType.DMA((2, 2, 2, line - 1)),
            pltpu.SemaphoreType.DMA((2, 2, 2, line - 1)),
            pltpu.SemaphoreType.DMA((2, 2, 2, line - 1)),
            pltpu.SemaphoreType.DMA((2, 2, 2, line - 1)),
            pltpu.SemaphoreType.DMA((3,)),
            pltpu.SemaphoreType.DMA((3,)),
            pltpu.SemaphoreType.DMA((EARLY, 2)),
            pltpu.SemaphoreType.DMA((EARLY, 2)),
        ],
        compiler_params=pltpu.CompilerParams(
            collective_id=0, has_side_effects=True, vmem_limit_bytes=63 * 1024 * 1024
        ),
        cost_estimate=pl.CostEstimate(
            flops=18 * tokens * 2 * half * width,
            bytes_accessed=9 * half * width * 2,
            transcendentals=tokens * 2 * half,
        ),
    )(normed, middle, upstream, gains, weights)


def back_kernel(
    line,
    replicas,
    back_hbm,
    middle_hbm,
    upstream_hbm,
    branch_hbm,
    inputs_hbm,
    normed_hbm,
    attended_hbm,
    queries_hbm,
    keys_hbm,
    values_hbm,
    cosine_hbm,
    sine_hbm,
    doc_col_ref,
    doc_row_ref,
    gains_ref,
    last_gain_ref,
    out_rows_ref,
    deal_ref,
    first_hbm,
    out_hbm,
    grads_hbm,
    first_half_hbm,
    second_half_hbm,
    qkv_hbm,
    outw_hbm,
    output_ref,
    input_grad_ref,
    w_qkv,
    w_out,
    acc,
    total,
    landing,
    late_landing,
    query_parts,
    query_pair,
    query_chain,
    query_steps,
    query_land,
    key_parts,
    key_pair,
    key_chain,
    key_steps,
    key_land,
    out_parts,
    out_pair,
    out_chain,
    out_steps,
    out_land,
    grad_rows,
    grad_keys,
    grad_values,
    pack_rows,
    send_rows,
    recv_rows,
    held,
    operand_sems,
    load_sems,
    store_sems,
    half_send,
    half_recv,
    pair_send,
    pair_recv,
    chain_send,
    chain_recv,
    step_send,
    step_recv,
    row_send,
    row_recv,
):
    rep = lax.axis_index("rep")
    shard = lax.axis_index("shard")
    shards = 2 * line
    devices = replicas * shards
    me = rep * shards + shard
    core = lax.rem(shard, 2)
    place = lax.div(shard, 2)
    sibling = (rep, shard + 1 - 2 * core)
    left = (rep, shard - 2)
    right = (rep, shard + 2)
    has_left = place > 0
    has_right = place < line - 1
    bits = replicas.bit_length() - 1
    full = jnp.float32
    rows, width = inputs_hbm.shape
    key_width = keys_hbm.shape[1]
    query_width = queries_hbm.shape[1]
    heads = query_width // key_width
    members, half_rows = acc.shape[0], acc.shape[1]
    part_rows = half_rows // 2
    peer_rows = rows // devices
    block_rows = send_rows.shape[2]
    packed = devices * block_rows
    qkv_rows = first_hbm.shape[0] // shards
    out_rows = out_hbm.shape[0] // shards

    load_qkv = pltpu.make_async_copy(first_hbm, w_qkv, load_sems.at[0])
    load_out = pltpu.make_async_copy(out_hbm, w_out, load_sems.at[1])
    load_acc = pltpu.make_async_copy(grads_hbm, acc, load_sems.at[2])
    operands = (
        back_hbm,
        middle_hbm,
        upstream_hbm,
        branch_hbm,
        inputs_hbm,
        normed_hbm,
        attended_hbm,
        queries_hbm,
        keys_hbm,
        values_hbm,
        cosine_hbm,
        sine_hbm,
    )
    operand_loads = [
        pltpu.make_async_copy(source, target, operand_sems.at[at])
        for at, (source, target) in enumerate(zip(operands, held))
    ]
    (
        back_ref,
        middle_ref,
        upstream_ref,
        branch_ref,
        inputs_ref,
        normed_ref,
        attended_ref,
        queries_ref,
        keys_ref,
        values_ref,
        cosine_ref,
        sine_ref,
    ) = held
    load_acc.start()
    for load in operand_loads:
        load.start()
    load_out.start()
    load_qkv.start()

    barrier = pltpu.get_barrier_semaphore()

    @pl.loop(1, devices)
    def _(hop):
        peer = lax.rem(me + hop, devices)
        pl.semaphore_signal(
            barrier,
            inc=1,
            device_id=(lax.div(peer, shards), lax.rem(peer, shards)),
            device_id_type=MESH,
        )

    pl.semaphore_wait(barrier, devices - 1)

    spans = [halving_spans(rep, bits, part, part_rows) for part in range(2)]

    def first_stage(member):
        return 1 if member < EARLY else 0

    def landed(member, part, stage):
        if stage == 0:
            return landing.at[member - EARLY, part]
        size = part_rows >> (stage + 1)
        return late_landing.at[member, part, pl.ds(part_rows // 2 - 2 * size, size)]

    def halve(member, part, stage):
        partner, keep, give, size = spans[part][stage]
        source = grads_hbm if stage == first_stage(member) else acc
        return pltpu.make_async_remote_copy(
            src_ref=source.at[member, at_rows(give, size)],
            dst_ref=landed(member, part, stage),
            send_sem=half_send.at[0, member, part, stage],
            recv_sem=half_recv.at[0, member, part, stage],
            device_id=(partner, shard),
            device_id_type=MESH,
        )

    def halve_add(member, part, stage):
        partner, keep, give, size = spans[part][stage]
        halve(member, part, stage).wait_recv()
        target = total if stage == bits - 1 else acc
        target[member, at_rows(keep, size), :] = (
            acc[member, at_rows(keep, size), :].astype(full)
            + landed(member, part, stage)[...].astype(full)
        ).astype(acc.dtype)

    def double(member, part, stage):
        partner, keep, give, size = spans[part][stage]
        return pltpu.make_async_remote_copy(
            src_ref=total.at[member, at_rows(keep, size)],
            dst_ref=total.at[member, at_rows(keep, size)],
            send_sem=half_send.at[1, member, part, stage],
            recv_sem=half_recv.at[1, member, part, stage],
            device_id=(partner, shard),
            device_id_type=MESH,
        )

    def double_arrive(member, part, stage):
        partner, keep, give, size = spans[part][stage]
        pltpu.make_async_remote_copy(
            src_ref=total.at[member, at_rows(give, size)],
            dst_ref=total.at[member, at_rows(give, size)],
            send_sem=half_send.at[1, member, part, stage],
            recv_sem=half_recv.at[1, member, part, stage],
            device_id=(partner, shard),
            device_id_type=MESH,
        ).wait_recv()

    def each(work):
        for member in range(members):
            for part in range(2):
                work(member, part)

    for part in range(2):
        halve(members - 1, part, first_stage(members - 1)).start()
    for member in range(members - 1):
        for part in range(2):
            halve(member, part, first_stage(member)).start()
    load_acc.wait()

    def pair_copy(kind, parts, pair):
        return pltpu.make_async_remote_copy(
            src_ref=parts.at[1 - core],
            dst_ref=pair,
            send_sem=pair_send.at[kind],
            recv_sem=pair_recv.at[kind],
            device_id=sibling,
            device_id_type=MESH,
        )

    kinds = (
        (out_parts, out_pair, out_chain, out_steps, out_land),
        (query_parts, query_pair, query_chain, query_steps, query_land),
        (key_parts, key_pair, key_chain, key_steps, key_land),
    )

    def pair_add(kind):
        parts, pair = kinds[kind][:2]
        pair_copy(kind, parts, pair).wait_recv()

        @pl.loop(0, line)
        def _(block):
            parts[core, block] = (
                parts[core, block].astype(full) + pair[block].astype(full)
            ).astype(parts.dtype)

    def chain_copy(kind, way, step, block):
        parts, _, chain = kinds[kind][:3]
        return pltpu.make_async_remote_copy(
            src_ref=parts.at[core, block],
            dst_ref=chain.at[way, step],
            send_sem=chain_send.at[kind, way, step],
            recv_sem=chain_recv.at[kind, way, step],
            device_id=left if way else right,
            device_id_type=MESH,
        )

    def chain_add(kind, way, step, block):
        parts, _, chain = kinds[kind][:3]
        chain_copy(kind, way, step, block).wait_recv()
        parts[core, block] = (
            parts[core, block].astype(full) + chain[way, step].astype(full)
        ).astype(parts.dtype)

    def chain_step(kind, turn):
        outward = turn - place

        @pl.when(outward >= 0)
        def _():
            @pl.when(has_left)
            def _():
                chain_add(kind, 0, outward, line - 1 - outward)

            chain_copy(kind, 0, outward, line - 1 - outward).start()

        inward = turn - (line - 1 - place)

        @pl.when(inward >= 0)
        def _():
            @pl.when(has_right)
            def _():
                chain_add(kind, 1, inward, inward)

            chain_copy(kind, 1, inward, inward).start()

    def chain_finish(kind):
        parts, _, _, steps, _ = kinds[kind]

        @pl.when(has_left)
        def _():
            chain_add(kind, 0, line - 1 - place, place)

        @pl.when(has_right)
        def _():
            chain_add(kind, 1, place, place)

        steps[0] = parts[core, place]

    lanes = {0: ((0, None),), 1: ((1, 0), (2, 1)), 2: ((3, None),)}

    def columns(ref, piece):
        if piece is None:
            return ref
        size = ref.shape[1] // 2
        return ref.at[:, pl.ds(piece * size, size)]

    def step_copy(kind, stage, lane, piece):
        steps, land = kinds[kind][3:]
        partner, _ = partner_of(rep, stage if lane in (1, 3) else bits - 1 - stage)
        return pltpu.make_async_remote_copy(
            src_ref=columns(steps.at[stage], piece),
            dst_ref=columns(land.at[stage], piece),
            send_sem=step_send.at[lane, stage],
            recv_sem=step_recv.at[lane, stage],
            device_id=(partner, shard),
            device_id_type=MESH,
        )

    def step_start(kind, stage):
        for lane, piece in lanes[kind]:
            step_copy(kind, stage, lane, piece).start()

    def step_add(kind, stage):
        steps, land = kinds[kind][3:]
        for lane, piece in lanes[kind]:
            step_copy(kind, stage, lane, piece).wait_recv()
            columns(steps.at[stage + 1], piece)[...] = (
                columns(steps.at[stage], piece)[...].astype(full)
                + columns(land.at[stage], piece)[...].astype(full)
            ).astype(steps.dtype)
            if stage + 1 < bits:
                step_copy(kind, stage + 1, lane, piece).start()

    served = {0: 0}

    def chain_to(kind, end):
        for step in range(served[kind], end):
            chain_step(kind, step)
        served[kind] = max(end, served[kind])

    def advance(member, stage):
        for part in range(2):
            halve_add(member, part, stage)
            if stage + 1 < bits:
                halve(member, part, stage + 1).start()
            else:
                double(member, part, stage).start()

    def redouble(member, stage):
        for part in range(2):
            double_arrive(member, part, stage)
            if stage > 1:
                double(member, part, stage - 1).start()
            else:
                store_half(member, part).start()

    def store_half(member, part):
        _, keep, _, size = spans[part][0]
        return pltpu.make_async_copy(
            total.at[member, at_rows(keep, size)],
            (first_half_hbm, second_half_hbm)[part].at[member],
            store_sems.at[3 + 2 * member + part],
        )

    todo = [
        [functools.partial(advance, member, stage) for stage in range(first_stage(member), bits)]
        + [functools.partial(redouble, member, stage) for stage in range(bits - 1, 0, -1)]
        for member in range(members)
    ]

    def serve(*chosen):
        for member in chosen:
            if todo[member]:
                todo[member].pop(0)()

    for load in operand_loads:
        load.wait()
    middle = middle_ref[...]
    upstream = upstream_ref[...].astype(full)
    scale_two = rms_scale(middle)
    grad_middle_norm, gain_two = norm_backward(
        back_ref[...], middle, scale_two, gains_ref[2:3, :]
    )
    back_ref[...] = upstream + grad_middle_norm
    branch = branch_ref[...]
    grad_branch, gain_one = norm_backward(
        back_ref[...], branch, rms_scale(branch), gains_ref[1:2, :]
    )
    grad_branch = grad_branch.astype(jnp.bfloat16)
    half_query = query_width // 2
    half_shards = shards // 2
    for group in range(2):
        grad_out = cross_rows(
            attended_ref[:, group * half_query : (group + 1) * half_query], grad_branch
        )
        for offset in range(half_shards):
            member = group * half_shards + offset
            out_parts[member % 2, member // 2, 0:out_rows, :] = grad_out[
                offset * out_rows : (offset + 1) * out_rows
            ].astype(out_parts.dtype)

    pair_copy(0, out_parts, out_pair).start()
    load_out.wait()
    grad_rows[:, 0:query_width] = against_cols(grad_branch, w_out[...]).astype(grad_rows.dtype)
    grad_keys[...] = jnp.zeros_like(grad_keys)
    grad_values[...] = jnp.zeros_like(grad_values)
    half_key = key_width // 2

    down_ids = lax.broadcasted_iota(jnp.int32, (rows, rows), 0)
    along_ids = lax.broadcasted_iota(jnp.int32, (rows, rows), 1)
    own_slots = down_ids + me * rows

    def find(source, found):
        return found + jnp.where(deal_row(deal_ref, source, rows) == own_slots, source, 0)

    found = lax.fori_loop(0, devices, find, jnp.zeros((rows, rows), jnp.int32))
    origin = jnp.sum(found, axis=1, keepdims=True)
    origin_row = jnp.sum(jnp.where(down_ids == along_ids, origin, 0), axis=0, keepdims=True)
    before = (origin_row == origin) & (down_ids < along_ids)
    back_place = origin_row * block_rows + jnp.sum(
        before.astype(jnp.int32), axis=0, keepdims=True
    )
    pack_rows[...] = (
        lax.broadcasted_iota(jnp.int32, (packed, rows), 0) == back_place
    ).astype(pack_rows.dtype)

    def row_copy(kind, hop, peer, source):
        return pltpu.make_async_remote_copy(
            src_ref=send_rows.at[kind, peer],
            dst_ref=recv_rows.at[kind, source],
            send_sem=row_send.at[kind, hop],
            recv_sem=row_recv.at[kind, hop],
            device_id=(lax.div(peer, shards), lax.rem(peer, shards)),
            device_id_type=MESH,
        )

    def send_back(kind, values):
        send_rows[kind] = (
            jnp.dot(pack_rows[...], values, preferred_element_type=full)
            .reshape(devices, block_rows, width)
            .astype(send_rows.dtype)
        )
        recv_rows[kind, me] = send_rows[kind, me]

        @pl.loop(1, devices)
        def _(hop):
            row_copy(kind, hop, lax.rem(me + hop, devices), me).start()

    send_back(0, out_rows_ref[...])
    pair_add(0)
    chain_to(0, 1)

    for head in range(heads):
        start = head * key_width
        cols = pl.ds(start, key_width)
        query = queries_ref[:, cols]
        key = keys_ref[...]
        allowed = (doc_col_ref[...] == doc_row_ref[...]) & (
            lax.broadcasted_iota(jnp.int32, (rows, rows), 0)
            >= lax.broadcasted_iota(jnp.int32, (rows, rows), 1)
        )
        tanh_scores = jnp.tanh(against_cols(query, key) * (HD ** (-0.5) / CAP_LIMIT))
        capped = jnp.where(allowed, CAP_LIMIT * tanh_scores, MASKED_SCORE)
        powers = jnp.exp(capped - jnp.max(capped, axis=-1, keepdims=True))
        probs = powers / jnp.sum(powers, axis=-1, keepdims=True)
        grad_att = grad_rows[:, cols]
        grad_values[...] += cross_rows(probs.astype(jnp.bfloat16), grad_att)
        grad_probs = against_cols(grad_att, values_ref[...])
        grad_capped = probs * (grad_probs - jnp.sum(probs * grad_probs, axis=-1, keepdims=True))
        grad_raw = (
            grad_capped * (1.0 - tanh_scores * tanh_scores) * HD ** (-0.5)
        ).astype(jnp.bfloat16)
        grad_keys[...] += cross_rows(grad_raw, query)
        grad_query = jnp.dot(grad_raw, key, preferred_element_type=full)
        front = grad_query[:, :half_key]
        back = grad_query[:, half_key:]
        cosine, sine = cosine_ref[...], sine_ref[...]
        grad_rows[:, pl.ds(start, half_key)] = (front * cosine + back * sine).astype(
            grad_rows.dtype
        )
        grad_rows[:, pl.ds(start + half_key, half_key)] = (
            back * cosine - front * sine
        ).astype(grad_rows.dtype)

    def weight_parts(parts, first, size):
        for begin in range(0, size, 512):
            grad_cols = cross_rows(
                normed_ref[...], grad_rows[:, first + begin : first + begin + 512]
            )
            for member in range(shards):
                parts[member % 2, member // 2, 0:qkv_rows, begin : begin + 512] = grad_cols[
                    member * qkv_rows : (member + 1) * qkv_rows
                ].astype(parts.dtype)

    weight_parts(query_parts, 0, query_width)
    pair_copy(1, query_parts, query_pair).start()
    serve(members - 1, 0)
    chain_to(0, min(2, line - 1))
    front = grad_keys[:, :half_key]
    back = grad_keys[:, half_key:]
    cosine, sine = cosine_ref[...], sine_ref[...]
    grad_rows[:, query_width : query_width + half_key] = (
        front * cosine + back * sine
    ).astype(grad_rows.dtype)
    grad_rows[:, query_width + half_key : query_width + key_width] = (
        back * cosine - front * sine
    ).astype(grad_rows.dtype)
    grad_rows[:, query_width + key_width :] = grad_values[...].astype(grad_rows.dtype)
    pair_add(1)
    chain_step(1, 0)

    load_qkv.wait()
    grad_normed = against_cols(grad_rows[...], w_qkv[...])
    inputs = inputs_ref[...].astype(full)
    grad_norm, gain_zero = norm_backward(
        grad_normed, inputs, rms_scale(inputs), gains_ref[0:1, :]
    )
    grad_inputs = (back_ref[...] + grad_norm).astype(jnp.bfloat16)
    weight_parts(key_parts, query_width, 2 * key_width)
    gain_stack = jnp.stack([gain_zero, gain_one, gain_two, last_gain_ref[0]])
    third = width // 3
    gain_rows = jnp.concatenate(
        [gain_stack[:, at * third : (at + 1) * third] for at in range(3)]
        + [jnp.zeros((4, third), full)]
    ).astype(jnp.bfloat16)
    for member in range(shards):
        gain_at = key_parts.shape[2] - 16
        key_parts[member % 2, member // 2, gain_at:, 0:third] = gain_rows
        key_parts[member % 2, member // 2, gain_at:, third:] = jnp.zeros(
            (16, key_parts.shape[3] - third), key_parts.dtype
        )
    pair_copy(2, key_parts, key_pair).start()
    serve(1)

    if line > 2:
        chain_step(1, 1)
    pair_add(2)
    chain_step(2, 0)
    chain_to(0, line - 1)
    chain_finish(0)
    step_start(0, 0)
    serve(members - 1, 0)
    for step in range(2, line - 1):
        chain_step(1, step)
        chain_step(2, step - 1)
    if line > 2:
        chain_step(2, line - 2)
    chain_finish(1)
    step_start(1, 0)
    send_back(1, grad_inputs)
    serve(1, members - 1)
    step_add(0, 0)
    serve(0)
    chain_finish(2)
    step_start(2, 0)
    for stage in range(1, bits):
        step_add(0, stage)
    for stage in range(bits):
        serve(*range(members))
        for kind in (1, 2):
            step_add(kind, stage)
    while any(todo):
        serve(*range(members))
    store_small = (
        pltpu.make_async_copy(out_steps.at[bits], outw_hbm, store_sems.at[0]),
        pltpu.make_async_copy(
            query_steps.at[bits],
            qkv_hbm.at[pl.ds(0, query_steps.shape[1]), pl.ds(0, query_width)],
            store_sems.at[1],
        ),
        pltpu.make_async_copy(
            key_steps.at[bits], qkv_hbm.at[:, pl.ds(query_width, 2 * key_width)], store_sems.at[2]
        ),
    )
    for store in store_small:
        store.start()
    own_deal = deal_row(deal_ref, me, rows)
    own_column = jnp.sum(jnp.where(down_ids == along_ids, own_deal, 0), axis=1, keepdims=True)
    send_place = jnp.sum((own_deal < own_column).astype(jnp.int32), axis=1, keepdims=True)
    target = lax.div(send_place, peer_rows) * block_rows + lax.rem(send_place, peer_rows)
    placer = (
        lax.broadcasted_iota(jnp.int32, (rows, packed), 1) == target
    ).astype(jnp.bfloat16)
    for kind, result in enumerate((output_ref, input_grad_ref)):

        @pl.loop(1, devices)
        def _(hop, kind=kind):
            source = lax.rem(me + devices - hop, devices)
            row_copy(kind, hop, source, source).wait_recv()

        stacked = recv_rows[kind].astype(full).reshape(packed, width).astype(jnp.bfloat16)
        result[...] = jnp.dot(placer, stacked, preferred_element_type=full).astype(result.dtype)

    for kind in range(2):

        @pl.loop(1, devices)
        def _(hop, kind=kind):
            row_copy(kind, hop, lax.rem(me + hop, devices), me).wait_send()

    def sent(member, part):
        for stage in range(bits):
            if stage >= first_stage(member):
                halve(member, part, stage).wait_send()
            if stage > 0:
                double(member, part, stage).wait_send()

    each(sent)
    for kind in range(3):
        parts, pair = kinds[kind][:2]
        pair_copy(kind, parts, pair).wait_send()
        for stage in range(bits):
            for lane, piece in lanes[kind]:
                step_copy(kind, stage, lane, piece).wait_send()

        @pl.loop(0, line - 1)
        def _(step, kind=kind):
            far = line - 1 - step

            @pl.when(far > place)
            def _():
                chain_copy(kind, 0, step, far).wait_send()

            @pl.when(step < place)
            def _():
                chain_copy(kind, 1, step, step).wait_send()

    for store in store_small:
        store.wait()
    each(lambda member, part: store_half(member, part).wait())


def back_and_reduce(line, replicas, small, first_full, out_full, ff_grads):
    inputs, normed, queries, keys = small[4], small[5], small[7], small[8]
    held = 12
    rows, width = inputs.shape
    shards = 2 * line
    devices = replicas * shards
    vmem_limit = 63 * 1024 * 1024
    block_rows = round_up(rows // devices, 8)
    bits = replicas.bit_length() - 1
    qkv_width = queries.shape[1] + 2 * keys.shape[1]
    qkv_rows = round_up(width // shards, 16) + 16
    out_rows = round_up(out_full.shape[0] // shards, 16)
    members, half_rows = ff_grads.shape[:2]
    low = jnp.bfloat16
    full = jnp.float32
    vmem = pl.BlockSpec(memory_space=pltpu.VMEM)
    hbm = pl.BlockSpec(memory_space=pl.ANY)
    dma = pltpu.SemaphoreType.DMA

    def chain_scratch(count, cols):
        return [
            pltpu.VMEM((2, line, count, cols), low),
            pltpu.VMEM((line, count, cols), low),
            pltpu.VMEM((2, line - 1, count, cols), low),
            pltpu.VMEM((bits + 1, count, cols), low),
            pltpu.VMEM((bits, count, cols), low),
        ]

    return pl.pallas_call(
        functools.partial(back_kernel, line, replicas),
        out_shape=(
            jax.ShapeDtypeStruct((members, half_rows // 4, width), low),
            jax.ShapeDtypeStruct((members, half_rows // 4, width), low),
            jax.ShapeDtypeStruct((qkv_rows, qkv_width), low),
            jax.ShapeDtypeStruct((out_rows, width), low),
            jax.ShapeDtypeStruct((rows, width), full),
            jax.ShapeDtypeStruct((rows, width), full),
        ),
        in_specs=[hbm] * held + [vmem] * (len(small) - held) + [hbm] * 3,
        out_specs=(hbm,) * 4 + (vmem,) * 2,
        scratch_shapes=[
            pltpu.VMEM((width, qkv_width), low),
            pltpu.VMEM(out_full.shape, low),
            pltpu.VMEM(ff_grads.shape, low),
            pltpu.VMEM(ff_grads.shape, low),
            pltpu.VMEM((members - EARLY, 2, half_rows // 4, width), low),
            pltpu.VMEM(
                (members, 2, half_rows // 4 - half_rows // (2 * replicas), width), low
            ),
            *chain_scratch(qkv_rows - 16, queries.shape[1]),
            *chain_scratch(qkv_rows, 2 * keys.shape[1]),
            *chain_scratch(out_rows, width),
            pltpu.VMEM((rows, qkv_width), low),
            pltpu.VMEM((rows, keys.shape[1]), full),
            pltpu.VMEM((rows, keys.shape[1]), full),
            pltpu.VMEM((devices * block_rows, rows), low),
            pltpu.VMEM((2, devices, block_rows, width), low),
            pltpu.VMEM((2, devices, block_rows, width), low),
            [pltpu.VMEM(operand.shape, operand.dtype) for operand in small[:held]],
            dma((held,)),
            dma((3,)),
            dma((3 + 2 * members,)),
            dma((2, members, 2, bits)),
            dma((2, members, 2, bits)),
            dma((3,)),
            dma((3,)),
            dma((3, 2, line - 1)),
            dma((3, 2, line - 1)),
            dma((4, bits)),
            dma((4, bits)),
            dma((2, devices)),
            dma((2, devices)),
        ],
        compiler_params=pltpu.CompilerParams(
            collective_id=1, has_side_effects=True, vmem_limit_bytes=vmem_limit
        ),
        cost_estimate=pl.CostEstimate(
            flops=16 * rows * width * qkv_width,
            bytes_accessed=4 * members * half_rows * width,
            transcendentals=2 * rows * rows * 4,
        ),
    )(*small, first_full, out_full, ff_grads)


def bring_kernel(
    line,
    replicas,
    near_weights,
    tokens_ref,
    cotangent_ref,
    deal_ref,
    gains_in,
    qkv_in,
    out_in,
    lengths_ref,
    frequency_ref,
    gu_hbm,
    down_hbm,
    inputs_ref,
    upstream_ref,
    normed_ref,
    queries_ref,
    keys_ref,
    values_ref,
    attended_ref,
    branch_ref,
    middle_ref,
    normed_two_ref,
    gains_ref,
    cosine_ref,
    sine_ref,
    doc_col_ref,
    doc_row_ref,
    qkv_hbm,
    outw_hbm,
    weights_hbm,
    w_qkv,
    w_out,
    gain_blocks,
    weights,
    tiles,
    sent,
    arrived,
    projected,
    load_sems,
    store_sems,
    row_send,
    row_recv,
    line_send,
    line_recv,
    rep_send,
    rep_recv,
    pair_send,
    pair_recv,
    gain_send,
    gain_recv,
    sibling_send,
    sibling_recv,
):
    rep = lax.axis_index("rep")
    shard = lax.axis_index("shard")
    shards = 2 * line
    devices = replicas * shards
    me = rep * shards + shard
    core = lax.rem(shard, 2)
    place = lax.div(shard, 2)
    sibling = (rep, shard + 1 - 2 * core)
    share = min(4, replicas)
    quarter = lax.rem(rep, share)
    full = jnp.float32
    low = jnp.bfloat16
    rows, width = tokens_ref.shape
    peer_rows = rows // devices
    block_rows = sent.shape[2]
    units = gu_hbm.shape[1]
    half = weights.shape[1] // 2
    tile_rows = tiles.shape[1]
    tile_count = units // tile_rows
    depth = tiles.shape[0]
    key_width = keys_ref.shape[1]
    query_width = queries_ref.shape[1]
    heads = query_width // key_width
    half_key = key_width // 2

    def tile_load(turn):
        member, at = turn // tile_count, turn % tile_count * tile_rows
        source = down_hbm if member == 0 else gu_hbm.at[member - 1]
        return pltpu.make_async_copy(
            source.at[pl.ds(at, tile_rows)], tiles.at[turn % depth], load_sems.at[turn % depth]
        )

    for turn in range(min(depth, 3 * tile_count)):
        tile_load(turn).start()

    barrier = pltpu.get_barrier_semaphore()

    @pl.loop(1, devices)
    def _(hop):
        peer = lax.rem(me + hop, devices)
        pl.semaphore_signal(
            barrier,
            inc=1,
            device_id=(lax.div(peer, shards), lax.rem(peer, shards)),
            device_id_type=MESH,
        )

    if near_weights:
        w_qkv[shard] = qkv_in[...].astype(low)

    down_ids = lax.broadcasted_iota(jnp.int32, (rows, rows), 0)
    along_ids = lax.broadcasted_iota(jnp.int32, (rows, rows), 1)
    eye = down_ids == along_ids

    def to_column(row):
        return jnp.sum(jnp.where(eye, row, 0), axis=1, keepdims=True)

    def to_row(column):
        return jnp.sum(jnp.where(eye, column, 0), axis=0, keepdims=True)

    def spread(places):
        return lax.div(places, peer_rows) * block_rows + lax.rem(places, peer_rows)

    own_deal = deal_row(deal_ref, me, rows)
    send_place = jnp.sum((to_column(own_deal) < own_deal).astype(jnp.int32), axis=0, keepdims=True)
    packed = devices * block_rows
    picker = (
        lax.broadcasted_iota(jnp.int32, (packed, rows), 0) == spread(send_place)
    ).astype(low)

    def pack(kind, source):
        sent[kind] = (
            jnp.dot(picker, source[...], preferred_element_type=full)
            .reshape(devices, block_rows, width)
            .astype(low)
        )
        arrived[kind, me] = sent[kind, me]

    pack(0, tokens_ref)
    pl.semaphore_wait(barrier, devices - 1)

    def row_copy(kind, hop, peer, source):
        return pltpu.make_async_remote_copy(
            src_ref=sent.at[kind, peer],
            dst_ref=arrived.at[kind, source],
            send_sem=row_send.at[kind, hop],
            recv_sem=row_recv.at[kind, hop],
            device_id=(lax.div(peer, shards), lax.rem(peer, shards)),
            device_id_type=MESH,
        )

    def rows_start(kind):
        @pl.loop(1, devices)
        def _(hop):
            row_copy(kind, hop, lax.rem(me + hop, devices), me).start()

    def rows_arrive(kind):
        @pl.loop(1, devices)
        def _(hop):
            source = lax.rem(me + devices - hop, devices)
            row_copy(kind, hop, source, source).wait_recv()

    gathered = (w_qkv, w_out)

    def part_of(kind, member, portion):
        buffer = gathered[kind]
        if kind == 0:
            size = buffer.shape[2] // share
            return buffer.at[member, :, pl.ds(pl.multiple_of(portion * size, LANES), size)]
        size = buffer.shape[1] // share
        return buffer.at[member, pl.ds(pl.multiple_of(portion * size, 16), size)]

    def line_copy(kind, target, source):
        part = part_of(kind, 2 * source + core, quarter)
        return pltpu.make_async_remote_copy(
            src_ref=part,
            dst_ref=part,
            send_sem=line_send.at[kind, target],
            recv_sem=line_recv.at[kind, source],
            device_id=(rep, 2 * target + core),
            device_id_type=MESH,
        )

    def rep_copy(kind, block, hop, portion):
        part = part_of(kind, 2 * block + core, portion)
        return pltpu.make_async_remote_copy(
            src_ref=part,
            dst_ref=part,
            send_sem=rep_send.at[kind, block, hop],
            recv_sem=rep_recv.at[kind, block, portion],
            device_id=(rep - quarter + lax.rem(quarter + hop, share), shard),
            device_id_type=MESH,
        )

    def pair_copy(kind, block, side):
        buffer = gathered[kind]
        return pltpu.make_async_remote_copy(
            src_ref=buffer.at[2 * block + side],
            dst_ref=buffer.at[2 * block + side],
            send_sem=pair_send.at[kind, block],
            recv_sem=pair_recv.at[kind, block],
            device_id=sibling,
            device_id_type=MESH,
        )

    def gain_copy(hop, source):
        return pltpu.make_async_remote_copy(
            src_ref=gain_blocks.at[source],
            dst_ref=gain_blocks.at[source],
            send_sem=gain_send.at[hop],
            recv_sem=gain_recv.at[hop],
            device_id=(rep, lax.rem(shard + hop, shards)),
            device_id_type=MESH,
        )

    def others():
        return [lax.rem(place + hop, line) for hop in range(1, line)]

    def line_start(kind):
        for target in others():
            line_copy(kind, target, place).start()
        pair_copy(kind, place, core).start()

    def line_pass(kind):
        for source in others():
            line_copy(kind, source, source).wait_recv()
            for hop in range(1, share):
                rep_copy(kind, source, hop, quarter).start()

    def rep_pass(kind):
        for block in others():
            for hop in range(1, share):
                rep_copy(kind, block, hop, lax.rem(quarter + hop, share)).wait_recv()
            pair_copy(kind, block, core).start()

    def pair_arrive(kind):
        for block in range(line):
            pair_copy(kind, block, 1 - core).wait_recv()

    if near_weights:
        line_start(0)
    rows_start(0)
    if near_weights:
        w_out[shard] = out_in[...].astype(low)
        line_start(1)
        gain_blocks[shard] = jnp.zeros(gain_blocks.shape[1:], low)
        gain_blocks[shard, : gains_in.shape[0], : gains_in.shape[1]] = gains_in[...].astype(low)
        for hop in range(1, shards):
            gain_copy(hop, shard).start()

    def sibling_copy(member):
        return pltpu.make_async_remote_copy(
            src_ref=weights.at[member, pl.ds(0, half)],
            dst_ref=weights.at[member, pl.ds(half, half)],
            send_sem=sibling_send.at[member],
            recv_sem=sibling_recv.at[member],
            device_id=sibling,
            device_id_type=MESH,
        )

    def cast(begin, end):
        for turn in range(begin, end):
            member, at = turn // tile_count, turn % tile_count * tile_rows
            tile_load(turn).wait()
            weights[member, at : at + tile_rows, :] = tiles[turn % depth].astype(low)
            if turn + depth < 3 * tile_count:
                tile_load(turn + depth).start()

    if half > units:
        for member in range(3):
            weights[member, units:half, :] = jnp.zeros((half - units, width), low)

    own_slots = lax.broadcasted_iota(jnp.int32, (rows, rows), 0) + me * rows

    def find(source, total):
        return total + jnp.where(deal_row(deal_ref, source, rows) == own_slots, source, 0)

    found = lax.fori_loop(0, devices, find, jnp.zeros((rows, rows), jnp.int32))
    source = jnp.sum(found, axis=1, keepdims=True)
    earlier = (to_row(source) == source) & (along_ids < down_ids)
    recv_place = source * peer_rows + jnp.sum(earlier.astype(jnp.int32), axis=1, keepdims=True)
    placer = (
        lax.broadcasted_iota(jnp.int32, (rows, packed), 1) == spread(recv_place)
    ).astype(low)

    ids = lax.broadcasted_iota(jnp.int32, (rows, 1), 0)
    end = jnp.int32(0)
    document = jnp.zeros((rows, 1), jnp.int32)
    begin = jnp.zeros((rows, 1), jnp.int32)
    for member in range(lengths_ref.shape[1]):
        end = end + lengths_ref[0, member]
        passed = ids >= end
        document = document + passed.astype(jnp.int32)
        begin = jnp.where(passed, end, begin)
    doc_col_ref[...] = document
    doc_row_ref[...] = to_row(document)
    angles = (ids - begin).astype(full) * frequency_ref[...]
    cosine_ref[...] = jnp.cos(angles)
    sine_ref[...] = jnp.sin(angles)
    if near_weights:
        line_pass(0)
    pack(1, cotangent_ref)
    for member in range(3):
        cast(member * tile_count, (member + 1) * tile_count)
        sibling_copy(member).start()
    near_stores = [
        pltpu.make_async_copy(
            weights.at[member, pl.ds(0, half)],
            weights_hbm.at[member, pl.ds(0, half)],
            store_sems.at[2 + member],
        )
        for member in range(3)
    ]
    for store in near_stores:
        store.start()

    def placed(kind):
        stacked = arrived[kind].astype(full).reshape(packed, width).astype(low)
        return jnp.dot(placer, stacked, preferred_element_type=full)

    if near_weights:
        for hop in range(1, shards):
            gain_copy(hop, lax.rem(shard + shards - hop, shards)).wait_recv()
        span = gains_in.shape[1]
        line_ids = lax.broadcasted_iota(jnp.int32, (gain_blocks.shape[2], width), 0)
        lane_ids = lax.broadcasted_iota(jnp.int32, (gain_blocks.shape[2], width), 1)
        joined = jnp.zeros((gain_blocks.shape[1], width), full)
        for member in range(shards):
            move = ((lane_ids - member * span == line_ids) & (line_ids < span)).astype(low)
            joined = joined + jnp.dot(gain_blocks[member], move, preferred_element_type=full)
        gains_ref[...] = joined[: gains_ref.shape[0]]
        rep_pass(0)
    else:
        gains_ref[...] = gains_in[...]
    rows_arrive(0)
    inputs = placed(0)
    inputs_ref[...] = inputs.astype(low)
    normed_ref[...] = (inputs * rms_scale(inputs) * gains_ref[0:1, :]).astype(low)
    if near_weights:
        line_pass(1)
    rows_start(1)
    if near_weights:
        pair_arrive(0)
        qkv_matrix = w_qkv[...].reshape(width, w_qkv.shape[2])
    else:
        qkv_matrix = qkv_in[...]
    projected[...] = jnp.dot(normed_ref[...], qkv_matrix, preferred_element_type=full)

    def turned(start):
        front = projected[:, pl.ds(start, half_key)]
        back = projected[:, pl.ds(start + half_key, half_key)]
        cosine, sine = cosine_ref[...], sine_ref[...]
        return (
            (front * cosine - back * sine).astype(low),
            (back * cosine + front * sine).astype(low),
        )

    keys_ref[:, :half_key], keys_ref[:, half_key:] = turned(query_width)
    values_ref[...] = projected[:, query_width + key_width :].astype(low)

    for head in range(heads):
        if near_weights and head == heads // 2:
            rep_pass(1)
        start = head * key_width
        cols = pl.ds(start, key_width)
        front, back = turned(start)
        queries_ref[:, pl.ds(start, half_key)] = front
        queries_ref[:, pl.ds(start + half_key, half_key)] = back
        allowed = (doc_col_ref[...] == doc_row_ref[...]) & (
            lax.broadcasted_iota(jnp.int32, (rows, rows), 0)
            >= lax.broadcasted_iota(jnp.int32, (rows, rows), 1)
        )
        scores = against_cols(queries_ref[:, cols], keys_ref[...]) * (HD ** (-0.5) / CAP_LIMIT)
        capped = jnp.where(allowed, CAP_LIMIT * jnp.tanh(scores), MASKED_SCORE)
        powers = jnp.exp(capped - jnp.max(capped, axis=-1, keepdims=True))
        probs = powers / jnp.sum(powers, axis=-1, keepdims=True)
        attended_ref[:, cols] = jnp.dot(
            probs.astype(low), values_ref[...], preferred_element_type=full
        ).astype(low)

    if near_weights:
        pair_arrive(1)
        out_matrix = w_out[...].reshape(query_width, width)
    else:
        out_matrix = out_in[...]
    stores = []
    if near_weights:
        stores.append(pltpu.make_async_copy(w_qkv, qkv_hbm, store_sems.at[0]))
        stores.append(pltpu.make_async_copy(w_out, outw_hbm, store_sems.at[1]))
    else:
        stores.append(pltpu.make_async_copy(qkv_in, qkv_hbm, store_sems.at[0]))
        stores.append(pltpu.make_async_copy(out_in, outw_hbm, store_sems.at[1]))
    for store in stores:
        store.start()
    for member in range(3):
        sibling_copy(member).wait_recv()
        store = pltpu.make_async_copy(
            weights.at[member, pl.ds(half, half)],
            weights_hbm.at[member, pl.ds(half, half)],
            store_sems.at[5 + member],
        )
        store.start()
        stores.append(store)
    branch = jnp.dot(attended_ref[...], out_matrix, preferred_element_type=full)
    branch_ref[...] = branch
    middle = inputs_ref[...].astype(full) + branch * rms_scale(branch) * gains_ref[1:2, :]
    middle_ref[...] = middle
    normed_two_ref[...] = (middle * rms_scale(middle) * gains_ref[2:3, :]).astype(low)
    rows_arrive(1)
    upstream_ref[...] = placed(1).astype(low)
    stores.extend(near_stores)

    for kind in range(2):

        @pl.loop(1, devices)
        def _(hop, kind=kind):
            row_copy(kind, hop, lax.rem(me + hop, devices), me).wait_send()

        if near_weights:
            for block in others():
                line_copy(kind, block, place).wait_send()
                for hop in range(1, share):
                    rep_copy(kind, block, hop, quarter).wait_send()
            for block in range(line):
                pair_copy(kind, block, core).wait_send()
    if near_weights:
        for hop in range(1, shards):
            gain_copy(hop, shard).wait_send()
    for member in range(3):
        sibling_copy(member).wait_send()
    for store in stores:
        store.wait()


def bring_and_attend(
    line, replicas, near_weights, tokens, cotangent, deal, small, gu, down, key_width
):
    gains_in, qkv_in, out_in = small[:3]
    rows, width = tokens.shape
    shards = 2 * line
    devices = replicas * shards
    share = min(4, replicas)
    block_rows = round_up(rows // devices, 8)
    units = down.shape[0]
    half = round_up(units, LANES)
    low = jnp.bfloat16
    full = jnp.float32
    vmem = pl.BlockSpec(memory_space=pltpu.VMEM)
    hbm = pl.BlockSpec(memory_space=pl.ANY)
    dma = pltpu.SemaphoreType.DMA
    qkv_width = qkv_in.shape[1]
    query_width = qkv_width - 2 * key_width
    if near_weights:
        qkv_shape = (shards, *qkv_in.shape)
        out_shape = (shards, *out_in.shape)
    else:
        qkv_shape = qkv_in.shape
        out_shape = out_in.shape
    tile_rows = max(size for size in range(16, 145, 16) if units % size == 0)
    hold = near_weights
    qkv_scratch = qkv_shape if hold else (shards, 16, LANES)
    out_scratch = out_shape if hold else (shards, 16, LANES)
    gain_lanes = round_up(width // shards, LANES) if hold else LANES

    def array(shape, dtype):
        return jax.ShapeDtypeStruct(shape, dtype)

    return pl.pallas_call(
        functools.partial(bring_kernel, line, replicas, near_weights),
        out_shape=(
            array((rows, width), low),
            array((rows, width), low),
            array((rows, width), low),
            array((rows, query_width), low),
            array((rows, key_width), low),
            array((rows, key_width), low),
            array((rows, query_width), low),
            array((rows, width), full),
            array((rows, width), full),
            array((rows, width), low),
            array((4, width), full),
            array((rows, key_width // 2), full),
            array((rows, key_width // 2), full),
            array((rows, 1), jnp.int32),
            array((1, rows), jnp.int32),
            array(qkv_shape, low),
            array(out_shape, low),
            array((3, 2 * half, width), low),
        ),
        in_specs=[vmem] * 6
        + [pl.BlockSpec(memory_space=pltpu.SMEM), vmem]
        + [hbm] * 2,
        out_specs=(vmem,) * 15 + (hbm,) * 3,
        scratch_shapes=[
            pltpu.VMEM(qkv_scratch, low),
            pltpu.VMEM(out_scratch, low),
            pltpu.VMEM((shards, 16, gain_lanes), low),
            pltpu.VMEM((3, 2 * half, width), low),
            pltpu.VMEM((4, tile_rows, width), full),
            pltpu.VMEM((2, devices, block_rows, width), low),
            pltpu.VMEM((2, devices, block_rows, width), low),
            pltpu.VMEM((rows, qkv_width), full),
            dma((4,)),
            dma((8,)),
            dma((2, devices)),
            dma((2, devices)),
            dma((2, line)),
            dma((2, line)),
            dma((2, line, share)),
            dma((2, line, share)),
            dma((2, line)),
            dma((2, line)),
            dma((shards,)),
            dma((shards,)),
            dma((3,)),
            dma((3,)),
        ],
        compiler_params=pltpu.CompilerParams(
            collective_id=2, has_side_effects=True, vmem_limit_bytes=63 * 1024 * 1024
        ),
        cost_estimate=pl.CostEstimate(
            flops=6 * rows * width * qkv_width,
            bytes_accessed=3 * units * width * 8,
            transcendentals=2 * rows * rows * 4,
        ),
    )(tokens, cotangent, deal, *small, gu, down)


def adam_half_kernel(which, first_half, second_half, *refs):
    del which
    inputs, results = refs[:6], refs[-10:]
    part, member = pl.program_id(0), pl.program_id(1)
    gradient = jnp.where(part == 0, first_half[0], second_half[0]).astype(jnp.float32)

    def step(rows_in, rows_out, rate, decay):
        master, first, second = (ref[...].reshape(gradient.shape) for ref in rows_in)
        moment = BETA_FIRST * first + (1.0 - BETA_FIRST) * gradient
        square = BETA_SECOND * second + (1.0 - BETA_SECOND) * gradient * gradient
        moment_hat = moment * (1.0 / (1.0 - BETA_FIRST**STEP))
        square_hat = square * (1.0 / (1.0 - BETA_SECOND**STEP))
        updated = master - rate * (moment_hat / (jnp.sqrt(square_hat) + ADAM_EPS) + decay * master)
        for ref, value in zip(rows_out, (updated, moment, square, gradient, updated)):
            ref[...] = value.astype(ref.dtype).reshape(ref.shape)

    @pl.when(member == 0)
    def _():
        step(inputs[:3], results[:5], LEARN_RATES[3], DECAY_RATES[3])

    @pl.when(member > 0)
    def _():
        step(inputs[3:], results[5:], LEARN_RATES[2], DECAY_RATES[2])


def adam_half(which, halves, arrays, begun=()):
    members, half_rows, width = halves[0].shape
    tile = half_rows // 2
    down, gu = arrays[0], arrays[3]

    def down_at(part, member, sub, chosen):
        return (part * 4 + chosen[part] * 2 + jnp.where(member == 0, sub, 1), 0)

    def gu_at(part, member, sub, chosen):
        row = part * 4 + chosen[part] * 2 + jnp.where(member == 0, 0, sub)
        return (jnp.maximum(member - 1, 0), row, 0)

    def first_at(part, member, sub, chosen):
        return (jnp.where(part == 0, member, members - 1), jnp.where(part == 0, sub, 1), 0)

    def second_at(part, member, sub, chosen):
        return (jnp.where(part == 0, 0, member), jnp.where(part == 0, 0, sub), 0)

    down_block = pl.BlockSpec((tile, width), down_at)
    gu_block = pl.BlockSpec((1, tile, width), gu_at)
    half_block = (1, tile, width)
    hbm = pl.BlockSpec(memory_space=pl.ANY)
    shapes = []
    for like in (down, gu):
        shapes.extend([jax.ShapeDtypeStruct(like.shape, jnp.float32)] * 4)
        shapes.append(jax.ShapeDtypeStruct(like.shape, jnp.bfloat16))
    count = members * half_rows * width * 2
    return pl.pallas_call(
        adam_half_kernel,
        out_shape=tuple(shapes),
        grid_spec=pltpu.PrefetchScalarGridSpec(
            num_scalar_prefetch=1,
            grid=(2, members, 2),
            in_specs=[
                pl.BlockSpec(half_block, first_at),
                pl.BlockSpec(half_block, second_at),
                *[down_block] * 3,
                *[gu_block] * 3,
                *[hbm] * len(begun),
            ],
            out_specs=(*[down_block] * 5, *[gu_block] * 5),
        ),
        input_output_aliases={9 + at: at for at in range(len(begun))},
        compiler_params=pltpu.CompilerParams(vmem_limit_bytes=60 * 1024 * 1024),
        cost_estimate=pl.CostEstimate(
            flops=16 * count, bytes_accessed=32 * count, transcendentals=2 * count
        ),
    )(which, *halves, *arrays, *begun)


def local(
    tokens,
    cotangent,
    lengths,
    deal,
    w_qkv,
    w_out,
    w_gu,
    w_down,
    gains,
    first_qkv,
    first_out,
    first_gu,
    first_down,
    first_gains,
    second_qkv,
    second_out,
    second_gu,
    second_down,
    second_gains,
):
    row_count, width = tokens.shape
    shards = lax.axis_size("shard")
    replicas = lax.axis_size("rep")
    line = shards // 2
    devices = replicas * shards
    deal_blocks = deal.reshape(deal.shape[0] // LANES, LANES)
    exponent = np.arange(HD // 2, dtype=np.float32) * np.float32(-2.0 / HD)
    frequency = jnp.asarray((np.float32(ROPE_BASE) ** exponent)[None, :])
    near_weights = w_qkv.shape[0] % 16 == 0
    if near_weights:
        first_weights = (gains, w_qkv, w_out)
    else:
        first_weights = (
            lax.all_gather(gains.astype(jnp.bfloat16), "shard", axis=1, tiled=True).astype(
                jnp.float32
            ),
            lax.all_gather(w_qkv.astype(jnp.bfloat16), "shard", axis=0, tiled=True),
            lax.all_gather(w_out.astype(jnp.bfloat16), "shard", axis=0, tiled=True),
        )
    (
        inputs,
        upstream,
        normed_one,
        queries,
        key_rows,
        value_rows,
        attended,
        branch,
        middle,
        normed_two,
        gain_values,
        cosine_table,
        sine_table,
        doc_col,
        doc_row,
        full_qkv,
        full_out,
        ff_weights,
    ) = bring_and_attend(
        line,
        replicas,
        near_weights,
        tokens,
        cotangent,
        deal_blocks,
        (*first_weights, lengths, frequency),
        w_gu,
        w_down,
        HD,
    )
    full_qkv = full_qkv.reshape(width, w_qkv.shape[1])
    full_out = full_out.reshape(H * HD, width)
    output_rows, last_gain_grad, grad_normed_two, ff_grads = feed_forward(
        line,
        replicas,
        normed_two,
        middle,
        upstream,
        gain_values,
        ff_weights,
    )
    first_half, second_half, qkv_sums, out_sums, output, input_grad = back_and_reduce(
        line,
        replicas,
        (
            grad_normed_two,
            middle,
            upstream,
            branch,
            inputs,
            normed_one,
            attended,
            queries,
            key_rows,
            value_rows,
            cosine_table,
            sine_table,
            doc_col,
            doc_row,
            gain_values,
            last_gain_grad,
            output_rows,
            deal_blocks,
        ),
        full_qkv,
        full_out,
        ff_grads,
    )
    output = output.astype(jnp.bfloat16)
    input_grad = input_grad.astype(jnp.bfloat16)

    bits = replicas.bit_length() - 1
    flips = (1, 1 << (bits - 1))
    other_halves = tuple(
        lax.ppermute(half, "rep", [(member, member ^ flip) for member in range(replicas)])
        for half, flip in zip((first_half, second_half), flips)
    )
    rep = lax.axis_index("rep")
    held = jnp.stack([lax.rem(lax.div(rep, flip), 2) for flip in flips]).astype(jnp.int32)
    ff_arrays = (w_down, first_down, second_down, w_gu, first_gu, second_gu)
    begun = adam_half(held, (first_half, second_half), ff_arrays)
    (
        new_down,
        moment_down,
        square_down,
        summed_down,
        copy_down,
        new_gu,
        moment_gu,
        square_gu,
        summed_gu,
        copy_gu,
    ) = adam_half(1 - held, other_halves, ff_arrays, begun)
    summed_qkv = qkv_sums[: w_qkv.shape[0]].astype(jnp.float32)
    summed_out = out_sums[: w_out.shape[0]].astype(jnp.float32)
    gain_span = gains.shape[1]
    gain_rows = qkv_sums[-16:-4, H * HD : H * HD + width // 3]
    summed_gains = lax.dynamic_slice(
        gain_rows.reshape(3, gains.shape[0], width // 3)
        .transpose(1, 0, 2)
        .reshape(gains.shape[0], width),
        (0, lax.axis_index("shard") * gain_span),
        (gains.shape[0], gain_span),
    ).astype(jnp.float32)
    new_qkv, moment_qkv, square_qkv = adamw_step(
        w_qkv, summed_qkv, first_qkv, second_qkv, LEARN_RATES[0], DECAY_RATES[0]
    )
    new_out, moment_out, square_out = adamw_step(
        w_out, summed_out, first_out, second_out, LEARN_RATES[1], DECAY_RATES[1]
    )
    new_gains, moment_gains, square_gains = adamw_step(
        gains, summed_gains, first_gains, second_gains, LEARN_RATES[4], DECAY_RATES[4]
    )
    return (
        output,
        input_grad,
        new_qkv,
        new_out,
        new_gu,
        new_down,
        new_gains,
        moment_qkv,
        moment_out,
        moment_gu,
        moment_down,
        moment_gains,
        square_qkv,
        square_out,
        square_gu,
        square_down,
        square_gains,
        summed_qkv,
        summed_out,
        summed_gu,
        summed_down,
        summed_gains,
        new_qkv.astype(jnp.bfloat16),
        new_out.astype(jnp.bfloat16),
        copy_gu,
        copy_down,
        new_gains.astype(jnp.bfloat16),
    )


def solution(mesh):
    placed = (
        P(("rep", "shard"), None),
        P(("rep", "shard"), None),
        P(("rep", "shard"), None),
        P(),
        P("shard", None),
        P("shard", None),
        P(None, "shard", None),
        P("shard", None),
        P(None, "shard"),
        P("shard", None),
        P("shard", None),
        P(None, "shard", None),
        P("shard", None),
        P(None, "shard"),
        P("shard", None),
        P("shard", None),
        P(None, "shard", None),
        P("shard", None),
        P(None, "shard"),
    )
    return jax.shard_map(
        local,
        mesh=mesh,
        in_specs=placed,
        out_specs=(
            P(("rep", "shard"), None),
            P(("rep", "shard"), None),
            P("shard", None),
            P("shard", None),
            P(None, "shard", None),
            P("shard", None),
            P(None, "shard"),
            P("shard", None),
            P("shard", None),
            P(None, "shard", None),
            P("shard", None),
            P(None, "shard"),
            P("shard", None),
            P("shard", None),
            P(None, "shard", None),
            P("shard", None),
            P(None, "shard"),
            P("shard", None),
            P("shard", None),
            P(None, "shard", None),
            P("shard", None),
            P(None, "shard"),
            P("shard", None),
            P("shard", None),
            P(None, "shard", None),
            P("shard", None),
            P(None, "shard"),
        ),
        check_vma=False,
    )
```

```python
import functools

import jax
import jax.numpy as jnp
import numpy as np
from jax import lax
from jax.experimental import pallas as pl
from jax.experimental.pallas import tpu as pltpu
from jax.sharding import PartitionSpec as P

H = 4
KV = 1
HD = 256
STEP = 10


CAP_LIMIT = 50.0
NORM_EPS = 1e-06
ROPE_BASE = 10000.0
MASKED_SCORE = -1e30
BETA_FIRST = 0.5
BETA_SECOND = 0.5
ADAM_EPS = 1e-08
LEARN_RATES = (0.05, 0.1, 0.03, 0.012, 0.4)
DECAY_RATES = (0.1, 0.1, 0.1, 0.1, 0.0)
GELU_COEF = 0.7978845608028654
GELU_CUBIC = 0.044715


def rms_scale(values):
    return lax.rsqrt(jnp.mean(values * values, axis=-1, keepdims=True) + NORM_EPS)


def norm_backward(grad_out, values, inverse_rms, gain_row):
    scaled = grad_out * gain_row
    inner = jnp.mean(scaled * values, axis=-1, keepdims=True)
    grad_in = inverse_rms * scaled - values * inverse_rms * inverse_rms * inverse_rms * inner
    grad_gain = jnp.sum(grad_out * values * inverse_rms, axis=0)
    return (grad_in, grad_gain)


def cross_rows(leading, trailing):
    return lax.dot_general(
        leading, trailing, (((0,), (0,)), ((), ())), preferred_element_type=jnp.float32
    )


def against_cols(leading, trailing):
    return lax.dot_general(
        leading, trailing, (((1,), (1,)), ((), ())), preferred_element_type=jnp.float32
    )


def adamw_step(master, gradient, first_moment, second_moment, rate, decay):
    moment = BETA_FIRST * first_moment + (1.0 - BETA_FIRST) * gradient
    square = BETA_SECOND * second_moment + (1.0 - BETA_SECOND) * gradient * gradient
    moment_hat = moment / (1.0 - BETA_FIRST**STEP)
    square_hat = square / (1.0 - BETA_SECOND**STEP)
    updated = master - rate * (moment_hat / (jnp.sqrt(square_hat) + ADAM_EPS) + decay * master)
    return (updated, moment, square)


LANES = 128
UNIT_TILE = 256
MESH = pl.DeviceIdType.MESH


def round_up(count, step):
    return -(-count // step) * step


def partner_of(index, bit):
    value = lax.rem(lax.div(index, 1 << bit), 2)
    return index + (1 - 2 * value) * (1 << bit), value


EARLY = 1


def deal_row(deal_ref, device, rows):
    lines = rows // LANES
    return jnp.concatenate(
        [deal_ref[pl.ds(device * lines + at, 1), :] for at in range(lines)], axis=1
    )


def halving_spans(rep, bits, part, part_rows):
    spans = []
    first = part * part_rows
    size = part_rows
    for bit in range(bits) if part == 0 else range(bits - 1, -1, -1):
        size //= 2
        partner, value = partner_of(rep, bit)
        spans.append((partner, first + value * size, first + (1 - value) * size, size))
        first = first + value * size
    return spans


def at_rows(first, size):
    return pl.ds(pl.multiple_of(first, 16), size)


def feed_kernel(
    line,
    replicas,
    own_rows,
    middle_ref,
    upstream_ref,
    gain_ref,
    weights_hbm,
    out_ref,
    gain_grad_ref,
    back_ref,
    grads_ref,
    weights,
    blocks,
    acts,
    partial,
    chain,
    sibling_out,
    sibling_in,
    landing,
    load_sems,
    store_sems,
    gather_send,
    gather_recv,
    chain_send,
    chain_recv,
    sibling_send,
    sibling_recv,
    half_send,
    half_recv,
):
    rep = lax.axis_index("rep")
    shard = lax.axis_index("shard")
    core = lax.rem(shard, 2)
    place = lax.div(shard, 2)
    sibling = (rep, shard + 1 - 2 * core)
    left = (rep, shard - 2)
    right = (rep, shard + 2)
    has_left = place > 0
    has_right = place < line - 1
    rows = own_rows.shape[0] // 2
    width = own_rows.shape[1]
    half = weights.shape[1] // 2
    tiles = 2 * half // UNIT_TILE

    load = pltpu.make_async_copy(weights_hbm, weights, load_sems.at[0])
    load.start()

    barrier = pltpu.get_barrier_semaphore()
    pl.semaphore_signal(barrier, inc=1, device_id=sibling, device_id_type=MESH)

    @pl.when(has_left)
    def _():
        pl.semaphore_signal(barrier, inc=1, device_id=left, device_id_type=MESH)

    @pl.when(has_right)
    def _():
        pl.semaphore_signal(barrier, inc=1, device_id=right, device_id_type=MESH)

    bits = replicas.bit_length() - 1
    greeted = sorted({0, bits - 1})
    for bit in greeted:
        partner, _ = partner_of(rep, bit)
        pl.semaphore_signal(barrier, inc=1, device_id=(partner, shard), device_id_type=MESH)

    def block_span(block):
        return pl.ds(pl.multiple_of(block * rows, rows), rows)

    for part in range(2):
        blocks[0, part, block_span(place), :] = own_rows[part * rows : (part + 1) * rows, :]

    pl.semaphore_wait(
        barrier,
        1 + len(greeted) + has_left.astype(jnp.int32) + has_right.astype(jnp.int32),
    )

    def gather_copy(phase, part, way, step, block):
        return pltpu.make_async_remote_copy(
            src_ref=blocks.at[phase, part, block_span(block)],
            dst_ref=blocks.at[phase, part, block_span(block)],
            send_sem=gather_send.at[phase, part, way, step],
            recv_sem=gather_recv.at[phase, part, way, step],
            device_id=left if way else right,
            device_id_type=MESH,
        )

    def gather_start(phase, part, step):
        @pl.when(has_right & (place - step >= 0))
        def _():
            gather_copy(phase, part, 0, step, place - step).start()

        @pl.when(has_left & (place + step <= line - 1))
        def _():
            gather_copy(phase, part, 1, step, place + step).start()

    def gather_arrive(phase, part, step):
        @pl.when(place - 1 - step >= 0)
        def _():
            gather_copy(phase, part, 0, step, place - 1 - step).wait_recv()

        @pl.when(place + 1 + step <= line - 1)
        def _():
            gather_copy(phase, part, 1, step, place + 1 + step).wait_recv()

    def gather_drain(phase, part):
        @pl.loop(0, line - 1)
        def _(step):
            @pl.when(has_right & (place - step >= 0))
            def _():
                gather_copy(phase, part, 0, step, place - step).wait_send()

            @pl.when(has_left & (place + step <= line - 1))
            def _():
                gather_copy(phase, part, 1, step, place + step).wait_send()

    def chain_copy(phase, part, way, packet, block):
        return pltpu.make_async_remote_copy(
            src_ref=partial.at[part, block_span(block)],
            dst_ref=chain.at[part, way, packet],
            send_sem=chain_send.at[phase, part, way, packet],
            recv_sem=chain_recv.at[phase, part, way, packet],
            device_id=left if way else right,
            device_id_type=MESH,
        )

    def chain_add(phase, part, way, packet, block):
        chain_copy(phase, part, way, packet, block).wait_recv()
        span = block_span(block)
        partial[part, span, :] = (
            partial[part, span, :].astype(jnp.float32) + chain[part, way, packet].astype(jnp.float32)
        ).astype(partial.dtype)

    def chain_turn(phase, part, turn):
        outward = turn - place

        @pl.when(outward >= 0)
        def _():
            @pl.when(has_left)
            def _():
                chain_add(phase, part, 0, outward, line - 1 - outward)

            chain_copy(phase, part, 0, outward, line - 1 - outward).start()

        inward = turn - (line - 1 - place)

        @pl.when(inward >= 0)
        def _():
            @pl.when(has_right)
            def _():
                chain_add(phase, part, 1, inward, inward)

            chain_copy(phase, part, 1, inward, inward).start()

    def chain_finish(phase, part):
        out = slice(part * rows, (part + 1) * rows)
        back_ref[out, :] = partial[part, block_span(place), :].astype(jnp.float32)

        @pl.when(has_left)
        def _():
            last = line - 1 - place
            chain_copy(phase, part, 0, last, place).wait_recv()
            back_ref[out, :] += chain[part, 0, last].astype(jnp.float32)

        @pl.when(has_right)
        def _():
            chain_copy(phase, part, 1, place, place).wait_recv()
            back_ref[out, :] += chain[part, 1, place].astype(jnp.float32)

    def chain_drain(phase, part):
        @pl.loop(0, line - 1)
        def _(packet):
            @pl.when(line - 1 - packet > place)
            def _():
                chain_copy(phase, part, 0, packet, line - 1 - packet).wait_send()

            @pl.when(packet < place)
            def _():
                chain_copy(phase, part, 1, packet, packet).wait_send()

    def sweep(phase, part, work, reduce=None, last=None, beside=None):
        @pl.loop(1, line)
        def _(turn):
            gather_arrive(phase, part, turn - 1)

            @pl.when(turn < line - 1)
            def _():
                gather_start(phase, part, turn)
                if reduce is not None:
                    chain_turn(*reduce, turn)

            if last is not None:

                @pl.when(turn == line - 1)
                def _():
                    last()

            @pl.loop(0, line // 2)
            def _(pair):
                ready = jnp.maximum(jnp.abs(2 * pair - place), jnp.abs(2 * pair + 1 - place))

                @pl.when(ready == turn)
                def _():
                    work(part, pair)

            if beside is not None:
                beside(turn)

    def pair_span(pair):
        return pl.ds(pl.multiple_of(pair * 2 * rows, 2 * rows), 2 * rows)

    def token_span(part, pair):
        first = part * line * rows
        return pl.ds(pl.multiple_of(first + pair * 2 * rows, 2 * rows), 2 * rows)

    def unit_span(tile):
        return pl.ds(pl.multiple_of(tile * UNIT_TILE, UNIT_TILE), UNIT_TILE)

    def forward(part, pair):
        span = token_span(part, pair)

        @pl.loop(0, tiles)
        def _(tile):
            cols = unit_span(tile)
            rows_in = blocks[0, part, pair_span(pair), :]
            gate = against_cols(rows_in, weights[1, cols, :])
            upper = against_cols(rows_in, weights[2, cols, :])
            tanh_inner = jnp.tanh(GELU_COEF * (gate + GELU_CUBIC * gate * gate * gate))
            lifted = 0.5 * (1.0 + tanh_inner)
            activated = gate * lifted
            slope = lifted + 0.5 * gate * (1.0 - tanh_inner * tanh_inner) * GELU_COEF * (
                1.0 + 3.0 * GELU_CUBIC * gate * gate
            )
            acts[0, span, cols] = (activated * upper).astype(acts.dtype)
            acts[1, span, cols] = (upper * slope).astype(acts.dtype)
            acts[2, span, cols] = activated.astype(acts.dtype)

        partial[part, pair_span(pair), :] = jnp.dot(
            acts[0, span, :], weights[0], preferred_element_type=jnp.float32
        ).astype(partial.dtype)

    def backward(part, pair):
        span = token_span(part, pair)

        @pl.loop(0, tiles)
        def _(tile):
            cols = unit_span(tile)
            grad_hidden = against_cols(blocks[1, part, pair_span(pair), :], weights[0, cols, :])
            for member in (1, 2):
                acts[member, span, cols] = (
                    grad_hidden * acts[member, span, cols].astype(jnp.float32)
                ).astype(acts.dtype)

        partial[part, pair_span(pair), :] = (
            jnp.dot(acts[1, span, :], weights[1], preferred_element_type=jnp.float32)
            + jnp.dot(acts[2, span, :], weights[2], preferred_element_type=jnp.float32)
        ).astype(partial.dtype)

    def output_half(part):
        out = slice(part * rows, (part + 1) * rows)
        feed = back_ref[out, :]
        upstream = upstream_ref[out, :].astype(jnp.float32)
        gain = gain_ref[3:4, :]
        inverse = lax.rsqrt(jnp.mean(feed * feed, axis=-1, keepdims=True) + NORM_EPS)
        scaled = upstream * gain
        inner = jnp.mean(scaled * feed, axis=-1, keepdims=True)
        blocks[1, part, block_span(place), :] = (
            inverse * scaled - feed * inverse * inverse * inverse * inner
        ).astype(blocks.dtype)
        gather_start(1, part, 0)
        gain_grad = jnp.sum(upstream * feed * inverse, axis=0, keepdims=True)
        if part == 0:
            gain_grad_ref[...] = gain_grad
        else:
            gain_grad_ref[...] += gain_grad
        out_ref[out, :] = (middle_ref[out, :] + feed * inverse * gain).astype(out_ref.dtype)

    def sibling_copy(member):
        return pltpu.make_async_remote_copy(
            src_ref=sibling_out.at[member],
            dst_ref=sibling_in.at[member],
            send_sem=sibling_send.at[member],
            recv_sem=sibling_recv.at[member],
            device_id=sibling,
            device_id_type=MESH,
        )

    def store_copy(member):
        return pltpu.make_async_copy(
            sibling_in.at[member], grads_ref.at[member], store_sems.at[member]
        )

    cuts = [(start, min(512, half - start)) for start in range(0, half, 512)]

    def far_grad(part, member):
        tokens = line * rows
        trailing = jnp.where(member == 0, 1, 0)
        for start, size in cuts:
            span = slice(start, start + size)
            piece = cross_rows(
                acts[member, part * tokens : (part + 1) * tokens, half + start : half + start + size],
                blocks[trailing, part],
            )
            if part == 1:
                piece = piece + sibling_out[member, span, :].astype(jnp.float32)
            sibling_out[member, span, :] = piece.astype(sibling_out.dtype)
        if part == 1:
            sibling_copy(member).start()

    first_spans = [halving_spans(rep, bits, part, half // 2)[0] for part in range(2)]

    def halve(member, part):
        partner, keep, give, size = first_spans[part]
        return pltpu.make_async_remote_copy(
            src_ref=sibling_in.at[member, at_rows(give, size)],
            dst_ref=landing.at[member, part],
            send_sem=half_send.at[member, part],
            recv_sem=half_recv.at[member, part],
            device_id=(partner, shard),
            device_id_type=MESH,
        )

    def near_grad(member):
        trailing = jnp.where(member == 0, 1, 0)
        sibling_copy(member).wait_recv()
        for start, size in cuts:
            span = slice(start, start + size)
            piece = cross_rows(
                acts[member, :, span], blocks[trailing].reshape(2 * line * rows, width)
            )
            sibling_in[member, span, :] = (
                sibling_in[member, span, :].astype(jnp.float32) + piece
            ).astype(sibling_in.dtype)

        @pl.when(member < EARLY)
        def _():
            for part in range(2):
                halve(member, part).start()

        @pl.when(member >= EARLY)
        def _():
            store_copy(member).start()

    def share(turn, count, turns):
        return lax.div(turn * count, turns), lax.div((turn + 1) * count, turns)

    def first_grads(turn):
        @pl.when(turn < line - 1)
        def _():
            @pl.loop(*share(turn - 1, 3, line - 2))
            def _(member):
                far_grad(0, member)

    def last_grads(turn):
        @pl.loop(*share(turn, 6, line - 1))
        def _(unit):
            @pl.when(unit < 3)
            def _():
                far_grad(1, unit)

            @pl.when(unit >= 3)
            def _():
                near_grad(unit - 3)

    def turn_around(part):
        chain_finish(0, part)
        output_half(part)

    gather_start(0, 0, 0)
    load.wait()
    sweep(0, 0, forward, last=lambda: gather_start(0, 1, 0))
    chain_turn(0, 0, 0)
    sweep(0, 1, forward, reduce=(0, 0), last=lambda: turn_around(0))
    chain_turn(0, 1, 0)
    chain_drain(0, 0)
    sweep(1, 0, backward, reduce=(0, 1), last=lambda: turn_around(1))
    chain_turn(1, 0, 0)
    chain_drain(0, 1)
    sweep(1, 1, backward, reduce=(1, 0), beside=first_grads)
    chain_turn(1, 1, 0)
    chain_finish(1, 0)

    @pl.loop(0, line - 1)
    def _(turn):
        @pl.when(turn > 0)
        def _():
            chain_turn(1, 1, turn)

        last_grads(turn)

    chain_finish(1, 1)
    for member in range(EARLY):
        for part in range(2):
            halve(member, part).wait_recv()
            partner, keep, give, size = first_spans[part]
            kept = at_rows(keep, size)
            sibling_in[member, kept, :] = (
                sibling_in[member, kept, :].astype(jnp.float32)
                + landing[member, part].astype(jnp.float32)
            ).astype(sibling_in.dtype)
        store_copy(member).start()
    for part in range(2):
        for phase in range(2):
            gather_drain(phase, part)
        chain_drain(1, part)
        for member in range(EARLY):
            halve(member, part).wait_send()
    for member in range(3):
        sibling_copy(member).wait_send()
        store_copy(member).wait()


def feed_forward(line, replicas, normed, middle, upstream, gains, weights):
    rows, width = normed.shape
    half = weights.shape[1] // 2
    low = jnp.bfloat16
    full = jnp.float32
    vmem = pl.BlockSpec(memory_space=pltpu.VMEM)
    hbm = pl.BlockSpec(memory_space=pl.ANY)
    tokens = line * rows
    return pl.pallas_call(
        functools.partial(feed_kernel, line, replicas),
        out_shape=(
            jax.ShapeDtypeStruct((rows, width), low),
            jax.ShapeDtypeStruct((1, width), full),
            jax.ShapeDtypeStruct((rows, width), full),
            jax.ShapeDtypeStruct((3, half, width), low),
        ),
        in_specs=[vmem, vmem, vmem, vmem, hbm],
        out_specs=(vmem, vmem, vmem, hbm),
        scratch_shapes=[
            pltpu.VMEM((3, 2 * half, width), low),
            pltpu.VMEM((2, 2, tokens // 2, width), low),
            pltpu.VMEM((3, tokens, 2 * half), low),
            pltpu.VMEM((2, tokens // 2, width), low),
            pltpu.VMEM((2, 2, line - 1, rows // 2, width), low),
            pltpu.VMEM((3, half, width), low),
            pltpu.VMEM((3, half, width), low),
            pltpu.VMEM((EARLY, 2, half // 4, width), low),
            pltpu.SemaphoreType.DMA((1,)),
            pltpu.SemaphoreType.DMA((3,)),
            pltpu.SemaphoreType.DMA((2, 2, 2, line - 1)),
            pltpu.SemaphoreType.DMA((2, 2, 2, line - 1)),
            pltpu.SemaphoreType.DMA((2, 2, 2, line - 1)),
            pltpu.SemaphoreType.DMA((2, 2, 2, line - 1)),
            pltpu.SemaphoreType.DMA((3,)),
            pltpu.SemaphoreType.DMA((3,)),
            pltpu.SemaphoreType.DMA((EARLY, 2)),
            pltpu.SemaphoreType.DMA((EARLY, 2)),
        ],
        compiler_params=pltpu.CompilerParams(
            collective_id=0, has_side_effects=True, vmem_limit_bytes=63 * 1024 * 1024
        ),
        cost_estimate=pl.CostEstimate(
            flops=18 * tokens * 2 * half * width,
            bytes_accessed=9 * half * width * 2,
            transcendentals=tokens * 2 * half,
        ),
    )(normed, middle, upstream, gains, weights)


def back_kernel(
    line,
    replicas,
    back_hbm,
    middle_hbm,
    upstream_hbm,
    branch_hbm,
    inputs_hbm,
    normed_hbm,
    attended_hbm,
    queries_hbm,
    keys_hbm,
    values_hbm,
    cosine_hbm,
    sine_hbm,
    doc_col_ref,
    doc_row_ref,
    gains_ref,
    last_gain_ref,
    out_rows_ref,
    deal_ref,
    first_hbm,
    out_hbm,
    grads_hbm,
    first_half_hbm,
    second_half_hbm,
    qkv_hbm,
    outw_hbm,
    output_ref,
    input_grad_ref,
    w_qkv,
    w_out,
    acc,
    total,
    landing,
    late_landing,
    query_parts,
    query_pair,
    query_chain,
    query_steps,
    query_land,
    key_parts,
    key_pair,
    key_chain,
    key_steps,
    key_land,
    out_parts,
    out_pair,
    out_chain,
    out_steps,
    out_land,
    grad_rows,
    grad_keys,
    grad_values,
    pack_rows,
    send_rows,
    recv_rows,
    held,
    operand_sems,
    load_sems,
    store_sems,
    half_send,
    half_recv,
    pair_send,
    pair_recv,
    chain_send,
    chain_recv,
    step_send,
    step_recv,
    row_send,
    row_recv,
):
    rep = lax.axis_index("rep")
    shard = lax.axis_index("shard")
    shards = 2 * line
    devices = replicas * shards
    me = rep * shards + shard
    core = lax.rem(shard, 2)
    place = lax.div(shard, 2)
    sibling = (rep, shard + 1 - 2 * core)
    left = (rep, shard - 2)
    right = (rep, shard + 2)
    has_left = place > 0
    has_right = place < line - 1
    bits = replicas.bit_length() - 1
    full = jnp.float32
    rows, width = inputs_hbm.shape
    key_width = keys_hbm.shape[1]
    query_width = queries_hbm.shape[1]
    heads = query_width // key_width
    members, half_rows = acc.shape[0], acc.shape[1]
    part_rows = half_rows // 2
    peer_rows = rows // devices
    block_rows = send_rows.shape[2]
    packed = devices * block_rows
    qkv_rows = first_hbm.shape[0] // shards
    out_rows = out_hbm.shape[0] // shards

    load_qkv = pltpu.make_async_copy(first_hbm, w_qkv, load_sems.at[0])
    load_out = pltpu.make_async_copy(out_hbm, w_out, load_sems.at[1])
    load_acc = pltpu.make_async_copy(grads_hbm, acc, load_sems.at[2])
    operands = (
        back_hbm,
        middle_hbm,
        upstream_hbm,
        branch_hbm,
        inputs_hbm,
        normed_hbm,
        attended_hbm,
        queries_hbm,
        keys_hbm,
        values_hbm,
        cosine_hbm,
        sine_hbm,
    )
    operand_loads = [
        pltpu.make_async_copy(source, target, operand_sems.at[at])
        for at, (source, target) in enumerate(zip(operands, held))
    ]
    (
        back_ref,
        middle_ref,
        upstream_ref,
        branch_ref,
        inputs_ref,
        normed_ref,
        attended_ref,
        queries_ref,
        keys_ref,
        values_ref,
        cosine_ref,
        sine_ref,
    ) = held
    load_acc.start()
    for load in operand_loads:
        load.start()
    load_out.start()
    load_qkv.start()

    barrier = pltpu.get_barrier_semaphore()

    @pl.loop(1, devices)
    def _(hop):
        peer = lax.rem(me + hop, devices)
        pl.semaphore_signal(
            barrier,
            inc=1,
            device_id=(lax.div(peer, shards), lax.rem(peer, shards)),
            device_id_type=MESH,
        )

    pl.semaphore_wait(barrier, devices - 1)

    spans = [halving_spans(rep, bits, part, part_rows) for part in range(2)]

    def first_stage(member):
        return 1 if member < EARLY else 0

    def landed(member, part, stage):
        if stage == 0:
            return landing.at[member - EARLY, part]
        size = part_rows >> (stage + 1)
        return late_landing.at[member, part, pl.ds(part_rows // 2 - 2 * size, size)]

    def halve(member, part, stage):
        partner, keep, give, size = spans[part][stage]
        source = grads_hbm if stage == first_stage(member) else acc
        return pltpu.make_async_remote_copy(
            src_ref=source.at[member, at_rows(give, size)],
            dst_ref=landed(member, part, stage),
            send_sem=half_send.at[0, member, part, stage],
            recv_sem=half_recv.at[0, member, part, stage],
            device_id=(partner, shard),
            device_id_type=MESH,
        )

    def halve_add(member, part, stage):
        partner, keep, give, size = spans[part][stage]
        halve(member, part, stage).wait_recv()
        target = total if stage == bits - 1 else acc
        target[member, at_rows(keep, size), :] = (
            acc[member, at_rows(keep, size), :].astype(full)
            + landed(member, part, stage)[...].astype(full)
        ).astype(acc.dtype)

    def double(member, part, stage):
        partner, keep, give, size = spans[part][stage]
        return pltpu.make_async_remote_copy(
            src_ref=total.at[member, at_rows(keep, size)],
            dst_ref=total.at[member, at_rows(keep, size)],
            send_sem=half_send.at[1, member, part, stage],
            recv_sem=half_recv.at[1, member, part, stage],
            device_id=(partner, shard),
            device_id_type=MESH,
        )

    def double_arrive(member, part, stage):
        partner, keep, give, size = spans[part][stage]
        pltpu.make_async_remote_copy(
            src_ref=total.at[member, at_rows(give, size)],
            dst_ref=total.at[member, at_rows(give, size)],
            send_sem=half_send.at[1, member, part, stage],
            recv_sem=half_recv.at[1, member, part, stage],
            device_id=(partner, shard),
            device_id_type=MESH,
        ).wait_recv()

    def each(work):
        for member in range(members):
            for part in range(2):
                work(member, part)

    for part in range(2):
        halve(members - 1, part, first_stage(members - 1)).start()
    for member in range(members - 1):
        for part in range(2):
            halve(member, part, first_stage(member)).start()
    load_acc.wait()

    def pair_copy(kind, parts, pair):
        return pltpu.make_async_remote_copy(
            src_ref=parts.at[1 - core],
            dst_ref=pair,
            send_sem=pair_send.at[kind],
            recv_sem=pair_recv.at[kind],
            device_id=sibling,
            device_id_type=MESH,
        )

    kinds = (
        (out_parts, out_pair, out_chain, out_steps, out_land),
        (query_parts, query_pair, query_chain, query_steps, query_land),
        (key_parts, key_pair, key_chain, key_steps, key_land),
    )

    def pair_add(kind):
        parts, pair = kinds[kind][:2]
        pair_copy(kind, parts, pair).wait_recv()

        @pl.loop(0, line)
        def _(block):
            parts[core, block] = (
                parts[core, block].astype(full) + pair[block].astype(full)
            ).astype(parts.dtype)

    def chain_copy(kind, way, step, block):
        parts, _, chain = kinds[kind][:3]
        return pltpu.make_async_remote_copy(
            src_ref=parts.at[core, block],
            dst_ref=chain.at[way, step],
            send_sem=chain_send.at[kind, way, step],
            recv_sem=chain_recv.at[kind, way, step],
            device_id=left if way else right,
            device_id_type=MESH,
        )

    def chain_add(kind, way, step, block):
        parts, _, chain = kinds[kind][:3]
        chain_copy(kind, way, step, block).wait_recv()
        parts[core, block] = (
            parts[core, block].astype(full) + chain[way, step].astype(full)
        ).astype(parts.dtype)

    def chain_step(kind, turn):
        outward = turn - place

        @pl.when(outward >= 0)
        def _():
            @pl.when(has_left)
            def _():
                chain_add(kind, 0, outward, line - 1 - outward)

            chain_copy(kind, 0, outward, line - 1 - outward).start()

        inward = turn - (line - 1 - place)

        @pl.when(inward >= 0)
        def _():
            @pl.when(has_right)
            def _():
                chain_add(kind, 1, inward, inward)

            chain_copy(kind, 1, inward, inward).start()

    def chain_finish(kind):
        parts, _, _, steps, _ = kinds[kind]

        @pl.when(has_left)
        def _():
            chain_add(kind, 0, line - 1 - place, place)

        @pl.when(has_right)
        def _():
            chain_add(kind, 1, place, place)

        steps[0] = parts[core, place]

    lanes = {0: ((0, None),), 1: ((1, 0), (2, 1)), 2: ((3, None),)}

    def columns(ref, piece):
        if piece is None:
            return ref
        size = ref.shape[1] // 2
        return ref.at[:, pl.ds(piece * size, size)]

    def step_copy(kind, stage, lane, piece):
        steps, land = kinds[kind][3:]
        partner, _ = partner_of(rep, stage if lane in (1, 3) else bits - 1 - stage)
        return pltpu.make_async_remote_copy(
            src_ref=columns(steps.at[stage], piece),
            dst_ref=columns(land.at[stage], piece),
            send_sem=step_send.at[lane, stage],
            recv_sem=step_recv.at[lane, stage],
            device_id=(partner, shard),
            device_id_type=MESH,
        )

    def step_start(kind, stage):
        for lane, piece in lanes[kind]:
            step_copy(kind, stage, lane, piece).start()

    def step_add(kind, stage):
        steps, land = kinds[kind][3:]
        for lane, piece in lanes[kind]:
            step_copy(kind, stage, lane, piece).wait_recv()
            columns(steps.at[stage + 1], piece)[...] = (
                columns(steps.at[stage], piece)[...].astype(full)
                + columns(land.at[stage], piece)[...].astype(full)
            ).astype(steps.dtype)
            if stage + 1 < bits:
                step_copy(kind, stage + 1, lane, piece).start()

    served = {0: 0}

    def chain_to(kind, end):
        for step in range(served[kind], end):
            chain_step(kind, step)
        served[kind] = max(end, served[kind])

    def advance(member, stage):
        for part in range(2):
            halve_add(member, part, stage)
            if stage + 1 < bits:
                halve(member, part, stage + 1).start()
            else:
                double(member, part, stage).start()

    def redouble(member, stage):
        for part in range(2):
            double_arrive(member, part, stage)
            if stage > 1:
                double(member, part, stage - 1).start()
            else:
                store_half(member, part).start()

    def store_half(member, part):
        _, keep, _, size = spans[part][0]
        return pltpu.make_async_copy(
            total.at[member, at_rows(keep, size)],
            (first_half_hbm, second_half_hbm)[part].at[member],
            store_sems.at[3 + 2 * member + part],
        )

    todo = [
        [functools.partial(advance, member, stage) for stage in range(first_stage(member), bits)]
        + [functools.partial(redouble, member, stage) for stage in range(bits - 1, 0, -1)]
        for member in range(members)
    ]

    def serve(*chosen):
        for member in chosen:
            if todo[member]:
                todo[member].pop(0)()

    for load in operand_loads:
        load.wait()
    middle = middle_ref[...]
    upstream = upstream_ref[...].astype(full)
    scale_two = rms_scale(middle)
    grad_middle_norm, gain_two = norm_backward(
        back_ref[...], middle, scale_two, gains_ref[2:3, :]
    )
    back_ref[...] = upstream + grad_middle_norm
    branch = branch_ref[...]
    grad_branch, gain_one = norm_backward(
        back_ref[...], branch, rms_scale(branch), gains_ref[1:2, :]
    )
    grad_branch = grad_branch.astype(jnp.bfloat16)
    half_query = query_width // 2
    half_shards = shards // 2
    for group in range(2):
        grad_out = cross_rows(
            attended_ref[:, group * half_query : (group + 1) * half_query], grad_branch
        )
        for offset in range(half_shards):
            member = group * half_shards + offset
            out_parts[member % 2, member // 2, 0:out_rows, :] = grad_out[
                offset * out_rows : (offset + 1) * out_rows
            ].astype(out_parts.dtype)

    pair_copy(0, out_parts, out_pair).start()
    load_out.wait()
    grad_rows[:, 0:query_width] = against_cols(grad_branch, w_out[...]).astype(grad_rows.dtype)
    grad_keys[...] = jnp.zeros_like(grad_keys)
    grad_values[...] = jnp.zeros_like(grad_values)
    half_key = key_width // 2

    down_ids = lax.broadcasted_iota(jnp.int32, (rows, rows), 0)
    along_ids = lax.broadcasted_iota(jnp.int32, (rows, rows), 1)
    own_slots = down_ids + me * rows

    def find(source, found):
        return found + jnp.where(deal_row(deal_ref, source, rows) == own_slots, source, 0)

    found = lax.fori_loop(0, devices, find, jnp.zeros((rows, rows), jnp.int32))
    origin = jnp.sum(found, axis=1, keepdims=True)
    origin_row = jnp.sum(jnp.where(down_ids == along_ids, origin, 0), axis=0, keepdims=True)
    before = (origin_row == origin) & (down_ids < along_ids)
    back_place = origin_row * block_rows + jnp.sum(
        before.astype(jnp.int32), axis=0, keepdims=True
    )
    pack_rows[...] = (
        lax.broadcasted_iota(jnp.int32, (packed, rows), 0) == back_place
    ).astype(pack_rows.dtype)

    def row_copy(kind, hop, peer, source):
        return pltpu.make_async_remote_copy(
            src_ref=send_rows.at[kind, peer],
            dst_ref=recv_rows.at[kind, source],
            send_sem=row_send.at[kind, hop],
            recv_sem=row_recv.at[kind, hop],
            device_id=(lax.div(peer, shards), lax.rem(peer, shards)),
            device_id_type=MESH,
        )

    def send_back(kind, values):
        send_rows[kind] = (
            jnp.dot(pack_rows[...], values, preferred_element_type=full)
            .reshape(devices, block_rows, width)
            .astype(send_rows.dtype)
        )
        recv_rows[kind, me] = send_rows[kind, me]

        @pl.loop(1, devices)
        def _(hop):
            row_copy(kind, hop, lax.rem(me + hop, devices), me).start()

    send_back(0, out_rows_ref[...])
    pair_add(0)
    chain_to(0, 1)

    for head in range(heads):
        start = head * key_width
        cols = pl.ds(start, key_width)
        query = queries_ref[:, cols]
        key = keys_ref[...]
        allowed = (doc_col_ref[...] == doc_row_ref[...]) & (
            lax.broadcasted_iota(jnp.int32, (rows, rows), 0)
            >= lax.broadcasted_iota(jnp.int32, (rows, rows), 1)
        )
        tanh_scores = jnp.tanh(against_cols(query, key) * (HD ** (-0.5) / CAP_LIMIT))
        capped = jnp.where(allowed, CAP_LIMIT * tanh_scores, MASKED_SCORE)
        powers = jnp.exp(capped - jnp.max(capped, axis=-1, keepdims=True))
        probs = powers / jnp.sum(powers, axis=-1, keepdims=True)
        grad_att = grad_rows[:, cols]
        grad_values[...] += cross_rows(probs.astype(jnp.bfloat16), grad_att)
        grad_probs = against_cols(grad_att, values_ref[...])
        grad_capped = probs * (grad_probs - jnp.sum(probs * grad_probs, axis=-1, keepdims=True))
        grad_raw = (
            grad_capped * (1.0 - tanh_scores * tanh_scores) * HD ** (-0.5)
        ).astype(jnp.bfloat16)
        grad_keys[...] += cross_rows(grad_raw, query)
        grad_query = jnp.dot(grad_raw, key, preferred_element_type=full)
        front = grad_query[:, :half_key]
        back = grad_query[:, half_key:]
        cosine, sine = cosine_ref[...], sine_ref[...]
        grad_rows[:, pl.ds(start, half_key)] = (front * cosine + back * sine).astype(
            grad_rows.dtype
        )
        grad_rows[:, pl.ds(start + half_key, half_key)] = (
            back * cosine - front * sine
        ).astype(grad_rows.dtype)

    def weight_parts(parts, first, size):
        for begin in range(0, size, 512):
            grad_cols = cross_rows(
                normed_ref[...], grad_rows[:, first + begin : first + begin + 512]
            )
            for member in range(shards):
                parts[member % 2, member // 2, 0:qkv_rows, begin : begin + 512] = grad_cols[
                    member * qkv_rows : (member + 1) * qkv_rows
                ].astype(parts.dtype)

    weight_parts(query_parts, 0, query_width)
    pair_copy(1, query_parts, query_pair).start()
    serve(members - 1, 0)
    chain_to(0, min(2, line - 1))
    front = grad_keys[:, :half_key]
    back = grad_keys[:, half_key:]
    cosine, sine = cosine_ref[...], sine_ref[...]
    grad_rows[:, query_width : query_width + half_key] = (
        front * cosine + back * sine
    ).astype(grad_rows.dtype)
    grad_rows[:, query_width + half_key : query_width + key_width] = (
        back * cosine - front * sine
    ).astype(grad_rows.dtype)
    grad_rows[:, query_width + key_width :] = grad_values[...].astype(grad_rows.dtype)
    pair_add(1)
    chain_step(1, 0)

    load_qkv.wait()
    grad_normed = against_cols(grad_rows[...], w_qkv[...])
    inputs = inputs_ref[...].astype(full)
    grad_norm, gain_zero = norm_backward(
        grad_normed, inputs, rms_scale(inputs), gains_ref[0:1, :]
    )
    grad_inputs = (back_ref[...] + grad_norm).astype(jnp.bfloat16)
    weight_parts(key_parts, query_width, 2 * key_width)
    gain_stack = jnp.stack([gain_zero, gain_one, gain_two, last_gain_ref[0]])
    third = width // 3
    gain_rows = jnp.concatenate(
        [gain_stack[:, at * third : (at + 1) * third] for at in range(3)]
        + [jnp.zeros((4, third), full)]
    ).astype(jnp.bfloat16)
    for member in range(shards):
        gain_at = key_parts.shape[2] - 16
        key_parts[member % 2, member // 2, gain_at:, 0:third] = gain_rows
        key_parts[member % 2, member // 2, gain_at:, third:] = jnp.zeros(
            (16, key_parts.shape[3] - third), key_parts.dtype
        )
    pair_copy(2, key_parts, key_pair).start()
    serve(1)

    if line > 2:
        chain_step(1, 1)
    pair_add(2)
    chain_step(2, 0)
    chain_to(0, line - 1)
    chain_finish(0)
    step_start(0, 0)
    serve(members - 1, 0)
    for step in range(2, line - 1):
        chain_step(1, step)
        chain_step(2, step - 1)
    if line > 2:
        chain_step(2, line - 2)
    chain_finish(1)
    step_start(1, 0)
    send_back(1, grad_inputs)
    serve(1, members - 1)
    step_add(0, 0)
    serve(0)
    chain_finish(2)
    step_start(2, 0)
    for stage in range(1, bits):
        step_add(0, stage)
    for stage in range(bits):
        serve(*range(members))
        for kind in (1, 2):
            step_add(kind, stage)
    while any(todo):
        serve(*range(members))
    store_small = (
        pltpu.make_async_copy(out_steps.at[bits], outw_hbm, store_sems.at[0]),
        pltpu.make_async_copy(
            query_steps.at[bits],
            qkv_hbm.at[pl.ds(0, query_steps.shape[1]), pl.ds(0, query_width)],
            store_sems.at[1],
        ),
        pltpu.make_async_copy(
            key_steps.at[bits], qkv_hbm.at[:, pl.ds(query_width, 2 * key_width)], store_sems.at[2]
        ),
    )
    for store in store_small:
        store.start()
    own_deal = deal_row(deal_ref, me, rows)
    own_column = jnp.sum(jnp.where(down_ids == along_ids, own_deal, 0), axis=1, keepdims=True)
    send_place = jnp.sum((own_deal < own_column).astype(jnp.int32), axis=1, keepdims=True)
    target = lax.div(send_place, peer_rows) * block_rows + lax.rem(send_place, peer_rows)
    placer = (
        lax.broadcasted_iota(jnp.int32, (rows, packed), 1) == target
    ).astype(jnp.bfloat16)
    for kind, result in enumerate((output_ref, input_grad_ref)):

        @pl.loop(1, devices)
        def _(hop, kind=kind):
            source = lax.rem(me + devices - hop, devices)
            row_copy(kind, hop, source, source).wait_recv()

        stacked = recv_rows[kind].astype(full).reshape(packed, width).astype(jnp.bfloat16)
        result[...] = jnp.dot(placer, stacked, preferred_element_type=full).astype(result.dtype)

    for kind in range(2):

        @pl.loop(1, devices)
        def _(hop, kind=kind):
            row_copy(kind, hop, lax.rem(me + hop, devices), me).wait_send()

    def sent(member, part):
        for stage in range(bits):
            if stage >= first_stage(member):
                halve(member, part, stage).wait_send()
            if stage > 0:
                double(member, part, stage).wait_send()

    each(sent)
    for kind in range(3):
        parts, pair = kinds[kind][:2]
        pair_copy(kind, parts, pair).wait_send()
        for stage in range(bits):
            for lane, piece in lanes[kind]:
                step_copy(kind, stage, lane, piece).wait_send()

        @pl.loop(0, line - 1)
        def _(step, kind=kind):
            far = line - 1 - step

            @pl.when(far > place)
            def _():
                chain_copy(kind, 0, step, far).wait_send()

            @pl.when(step < place)
            def _():
                chain_copy(kind, 1, step, step).wait_send()

    for store in store_small:
        store.wait()
    each(lambda member, part: store_half(member, part).wait())


def back_and_reduce(line, replicas, small, first_full, out_full, ff_grads):
    inputs, normed, queries, keys = small[4], small[5], small[7], small[8]
    held = 12
    rows, width = inputs.shape
    shards = 2 * line
    devices = replicas * shards
    vmem_limit = 63 * 1024 * 1024
    block_rows = round_up(rows // devices, 8)
    bits = replicas.bit_length() - 1
    qkv_width = queries.shape[1] + 2 * keys.shape[1]
    qkv_rows = round_up(width // shards, 16) + 16
    out_rows = round_up(out_full.shape[0] // shards, 16)
    members, half_rows = ff_grads.shape[:2]
    low = jnp.bfloat16
    full = jnp.float32
    vmem = pl.BlockSpec(memory_space=pltpu.VMEM)
    hbm = pl.BlockSpec(memory_space=pl.ANY)
    dma = pltpu.SemaphoreType.DMA

    def chain_scratch(count, cols):
        return [
            pltpu.VMEM((2, line, count, cols), low),
            pltpu.VMEM((line, count, cols), low),
            pltpu.VMEM((2, line - 1, count, cols), low),
            pltpu.VMEM((bits + 1, count, cols), low),
            pltpu.VMEM((bits, count, cols), low),
        ]

    return pl.pallas_call(
        functools.partial(back_kernel, line, replicas),
        out_shape=(
            jax.ShapeDtypeStruct((members, half_rows // 4, width), low),
            jax.ShapeDtypeStruct((members, half_rows // 4, width), low),
            jax.ShapeDtypeStruct((qkv_rows, qkv_width), low),
            jax.ShapeDtypeStruct((out_rows, width), low),
            jax.ShapeDtypeStruct((rows, width), full),
            jax.ShapeDtypeStruct((rows, width), full),
        ),
        in_specs=[hbm] * held + [vmem] * (len(small) - held) + [hbm] * 3,
        out_specs=(hbm,) * 4 + (vmem,) * 2,
        scratch_shapes=[
            pltpu.VMEM((width, qkv_width), low),
            pltpu.VMEM(out_full.shape, low),
            pltpu.VMEM(ff_grads.shape, low),
            pltpu.VMEM(ff_grads.shape, low),
            pltpu.VMEM((members - EARLY, 2, half_rows // 4, width), low),
            pltpu.VMEM(
                (members, 2, half_rows // 4 - half_rows // (2 * replicas), width), low
            ),
            *chain_scratch(qkv_rows - 16, queries.shape[1]),
            *chain_scratch(qkv_rows, 2 * keys.shape[1]),
            *chain_scratch(out_rows, width),
            pltpu.VMEM((rows, qkv_width), low),
            pltpu.VMEM((rows, keys.shape[1]), full),
            pltpu.VMEM((rows, keys.shape[1]), full),
            pltpu.VMEM((devices * block_rows, rows), low),
            pltpu.VMEM((2, devices, block_rows, width), low),
            pltpu.VMEM((2, devices, block_rows, width), low),
            [pltpu.VMEM(operand.shape, operand.dtype) for operand in small[:held]],
            dma((held,)),
            dma((3,)),
            dma((3 + 2 * members,)),
            dma((2, members, 2, bits)),
            dma((2, members, 2, bits)),
            dma((3,)),
            dma((3,)),
            dma((3, 2, line - 1)),
            dma((3, 2, line - 1)),
            dma((4, bits)),
            dma((4, bits)),
            dma((2, devices)),
            dma((2, devices)),
        ],
        compiler_params=pltpu.CompilerParams(
            collective_id=1, has_side_effects=True, vmem_limit_bytes=vmem_limit
        ),
        cost_estimate=pl.CostEstimate(
            flops=16 * rows * width * qkv_width,
            bytes_accessed=4 * members * half_rows * width,
            transcendentals=2 * rows * rows * 4,
        ),
    )(*small, first_full, out_full, ff_grads)


def bring_kernel(
    line,
    replicas,
    near_weights,
    tokens_ref,
    cotangent_ref,
    deal_ref,
    gains_in,
    qkv_in,
    out_in,
    lengths_ref,
    frequency_ref,
    gu_hbm,
    down_hbm,
    inputs_ref,
    upstream_ref,
    normed_ref,
    queries_ref,
    keys_ref,
    values_ref,
    attended_ref,
    branch_ref,
    middle_ref,
    normed_two_ref,
    gains_ref,
    cosine_ref,
    sine_ref,
    doc_col_ref,
    doc_row_ref,
    qkv_hbm,
    outw_hbm,
    weights_hbm,
    w_qkv,
    w_out,
    gain_blocks,
    weights,
    tiles,
    sent,
    arrived,
    projected,
    load_sems,
    store_sems,
    row_send,
    row_recv,
    line_send,
    line_recv,
    rep_send,
    rep_recv,
    pair_send,
    pair_recv,
    gain_send,
    gain_recv,
    sibling_send,
    sibling_recv,
):
    rep = lax.axis_index("rep")
    shard = lax.axis_index("shard")
    shards = 2 * line
    devices = replicas * shards
    me = rep * shards + shard
    core = lax.rem(shard, 2)
    place = lax.div(shard, 2)
    sibling = (rep, shard + 1 - 2 * core)
    share = min(4, replicas)
    quarter = lax.rem(rep, share)
    full = jnp.float32
    low = jnp.bfloat16
    rows, width = tokens_ref.shape
    peer_rows = rows // devices
    block_rows = sent.shape[2]
    units = gu_hbm.shape[1]
    half = weights.shape[1] // 2
    tile_rows = tiles.shape[1]
    tile_count = units // tile_rows
    depth = tiles.shape[0]
    key_width = keys_ref.shape[1]
    query_width = queries_ref.shape[1]
    heads = query_width // key_width
    half_key = key_width // 2

    def tile_load(turn):
        member, at = turn // tile_count, turn % tile_count * tile_rows
        source = down_hbm if member == 0 else gu_hbm.at[member - 1]
        return pltpu.make_async_copy(
            source.at[pl.ds(at, tile_rows)], tiles.at[turn % depth], load_sems.at[turn % depth]
        )

    for turn in range(min(depth, 3 * tile_count)):
        tile_load(turn).start()

    barrier = pltpu.get_barrier_semaphore()

    @pl.loop(1, devices)
    def _(hop):
        peer = lax.rem(me + hop, devices)
        pl.semaphore_signal(
            barrier,
            inc=1,
            device_id=(lax.div(peer, shards), lax.rem(peer, shards)),
            device_id_type=MESH,
        )

    if near_weights:
        w_qkv[shard] = qkv_in[...].astype(low)

    down_ids = lax.broadcasted_iota(jnp.int32, (rows, rows), 0)
    along_ids = lax.broadcasted_iota(jnp.int32, (rows, rows), 1)
    eye = down_ids == along_ids

    def to_column(row):
        return jnp.sum(jnp.where(eye, row, 0), axis=1, keepdims=True)

    def to_row(column):
        return jnp.sum(jnp.where(eye, column, 0), axis=0, keepdims=True)

    def spread(places):
        return lax.div(places, peer_rows) * block_rows + lax.rem(places, peer_rows)

    own_deal = deal_row(deal_ref, me, rows)
    send_place = jnp.sum((to_column(own_deal) < own_deal).astype(jnp.int32), axis=0, keepdims=True)
    packed = devices * block_rows
    picker = (
        lax.broadcasted_iota(jnp.int32, (packed, rows), 0) == spread(send_place)
    ).astype(low)

    def pack(kind, source):
        sent[kind] = (
            jnp.dot(picker, source[...], preferred_element_type=full)
            .reshape(devices, block_rows, width)
            .astype(low)
        )
        arrived[kind, me] = sent[kind, me]

    pack(0, tokens_ref)
    pl.semaphore_wait(barrier, devices - 1)

    def row_copy(kind, hop, peer, source):
        return pltpu.make_async_remote_copy(
            src_ref=sent.at[kind, peer],
            dst_ref=arrived.at[kind, source],
            send_sem=row_send.at[kind, hop],
            recv_sem=row_recv.at[kind, hop],
            device_id=(lax.div(peer, shards), lax.rem(peer, shards)),
            device_id_type=MESH,
        )

    def rows_start(kind):
        @pl.loop(1, devices)
        def _(hop):
            row_copy(kind, hop, lax.rem(me + hop, devices), me).start()

    def rows_arrive(kind):
        @pl.loop(1, devices)
        def _(hop):
            source = lax.rem(me + devices - hop, devices)
            row_copy(kind, hop, source, source).wait_recv()

    gathered = (w_qkv, w_out)

    def part_of(kind, member, portion):
        buffer = gathered[kind]
        if kind == 0:
            size = buffer.shape[2] // share
            return buffer.at[member, :, pl.ds(pl.multiple_of(portion * size, LANES), size)]
        size = buffer.shape[1] // share
        return buffer.at[member, pl.ds(pl.multiple_of(portion * size, 16), size)]

    def line_copy(kind, target, source):
        part = part_of(kind, 2 * source + core, quarter)
        return pltpu.make_async_remote_copy(
            src_ref=part,
            dst_ref=part,
            send_sem=line_send.at[kind, target],
            recv_sem=line_recv.at[kind, source],
            device_id=(rep, 2 * target + core),
            device_id_type=MESH,
        )

    def rep_copy(kind, block, hop, portion):
        part = part_of(kind, 2 * block + core, portion)
        return pltpu.make_async_remote_copy(
            src_ref=part,
            dst_ref=part,
            send_sem=rep_send.at[kind, block, hop],
            recv_sem=rep_recv.at[kind, block, portion],
            device_id=(rep - quarter + lax.rem(quarter + hop, share), shard),
            device_id_type=MESH,
        )

    def pair_copy(kind, block, side):
        buffer = gathered[kind]
        return pltpu.make_async_remote_copy(
            src_ref=buffer.at[2 * block + side],
            dst_ref=buffer.at[2 * block + side],
            send_sem=pair_send.at[kind, block],
            recv_sem=pair_recv.at[kind, block],
            device_id=sibling,
            device_id_type=MESH,
        )

    def gain_copy(hop, source):
        return pltpu.make_async_remote_copy(
            src_ref=gain_blocks.at[source],
            dst_ref=gain_blocks.at[source],
            send_sem=gain_send.at[hop],
            recv_sem=gain_recv.at[hop],
            device_id=(rep, lax.rem(shard + hop, shards)),
            device_id_type=MESH,
        )

    def others():
        return [lax.rem(place + hop, line) for hop in range(1, line)]

    def line_start(kind):
        for target in others():
            line_copy(kind, target, place).start()
        pair_copy(kind, place, core).start()

    def line_pass(kind):
        for source in others():
            line_copy(kind, source, source).wait_recv()
            for hop in range(1, share):
                rep_copy(kind, source, hop, quarter).start()

    def rep_pass(kind):
        for block in others():
            for hop in range(1, share):
                rep_copy(kind, block, hop, lax.rem(quarter + hop, share)).wait_recv()
            pair_copy(kind, block, core).start()

    def pair_arrive(kind):
        for block in range(line):
            pair_copy(kind, block, 1 - core).wait_recv()

    if near_weights:
        line_start(0)
    rows_start(0)
    if near_weights:
        w_out[shard] = out_in[...].astype(low)
        line_start(1)
        gain_blocks[shard] = jnp.zeros(gain_blocks.shape[1:], low)
        gain_blocks[shard, : gains_in.shape[0], : gains_in.shape[1]] = gains_in[...].astype(low)
        for hop in range(1, shards):
            gain_copy(hop, shard).start()

    def sibling_copy(member):
        return pltpu.make_async_remote_copy(
            src_ref=weights.at[member, pl.ds(0, half)],
            dst_ref=weights.at[member, pl.ds(half, half)],
            send_sem=sibling_send.at[member],
            recv_sem=sibling_recv.at[member],
            device_id=sibling,
            device_id_type=MESH,
        )

    def cast(begin, end):
        for turn in range(begin, end):
            member, at = turn // tile_count, turn % tile_count * tile_rows
            tile_load(turn).wait()
            weights[member, at : at + tile_rows, :] = tiles[turn % depth].astype(low)
            if turn + depth < 3 * tile_count:
                tile_load(turn + depth).start()

    if half > units:
        for member in range(3):
            weights[member, units:half, :] = jnp.zeros((half - units, width), low)

    own_slots = lax.broadcasted_iota(jnp.int32, (rows, rows), 0) + me * rows

    def find(source, total):
        return total + jnp.where(deal_row(deal_ref, source, rows) == own_slots, source, 0)

    found = lax.fori_loop(0, devices, find, jnp.zeros((rows, rows), jnp.int32))
    source = jnp.sum(found, axis=1, keepdims=True)
    earlier = (to_row(source) == source) & (along_ids < down_ids)
    recv_place = source * peer_rows + jnp.sum(earlier.astype(jnp.int32), axis=1, keepdims=True)
    placer = (
        lax.broadcasted_iota(jnp.int32, (rows, packed), 1) == spread(recv_place)
    ).astype(low)

    ids = lax.broadcasted_iota(jnp.int32, (rows, 1), 0)
    end = jnp.int32(0)
    document = jnp.zeros((rows, 1), jnp.int32)
    begin = jnp.zeros((rows, 1), jnp.int32)
    for member in range(lengths_ref.shape[1]):
        end = end + lengths_ref[0, member]
        passed = ids >= end
        document = document + passed.astype(jnp.int32)
        begin = jnp.where(passed, end, begin)
    doc_col_ref[...] = document
    doc_row_ref[...] = to_row(document)
    angles = (ids - begin).astype(full) * frequency_ref[...]
    cosine_ref[...] = jnp.cos(angles)
    sine_ref[...] = jnp.sin(angles)
    if near_weights:
        line_pass(0)
    pack(1, cotangent_ref)
    for member in range(3):
        cast(member * tile_count, (member + 1) * tile_count)
        sibling_copy(member).start()
    near_stores = [
        pltpu.make_async_copy(
            weights.at[member, pl.ds(0, half)],
            weights_hbm.at[member, pl.ds(0, half)],
            store_sems.at[2 + member],
        )
        for member in range(3)
    ]
    for store in near_stores:
        store.start()

    def placed(kind):
        stacked = arrived[kind].astype(full).reshape(packed, width).astype(low)
        return jnp.dot(placer, stacked, preferred_element_type=full)

    if near_weights:
        for hop in range(1, shards):
            gain_copy(hop, lax.rem(shard + shards - hop, shards)).wait_recv()
        span = gains_in.shape[1]
        line_ids = lax.broadcasted_iota(jnp.int32, (gain_blocks.shape[2], width), 0)
        lane_ids = lax.broadcasted_iota(jnp.int32, (gain_blocks.shape[2], width), 1)
        joined = jnp.zeros((gain_blocks.shape[1], width), full)
        for member in range(shards):
            move = ((lane_ids - member * span == line_ids) & (line_ids < span)).astype(low)
            joined = joined + jnp.dot(gain_blocks[member], move, preferred_element_type=full)
        gains_ref[...] = joined[: gains_ref.shape[0]]
        rep_pass(0)
    else:
        gains_ref[...] = gains_in[...]
    rows_arrive(0)
    inputs = placed(0)
    inputs_ref[...] = inputs.astype(low)
    normed_ref[...] = (inputs * rms_scale(inputs) * gains_ref[0:1, :]).astype(low)
    if near_weights:
        line_pass(1)
    rows_start(1)
    if near_weights:
        pair_arrive(0)
        qkv_matrix = w_qkv[...].reshape(width, w_qkv.shape[2])
    else:
        qkv_matrix = qkv_in[...]
    projected[...] = jnp.dot(normed_ref[...], qkv_matrix, preferred_element_type=full)

    def turned(start):
        front = projected[:, pl.ds(start, half_key)]
        back = projected[:, pl.ds(start + half_key, half_key)]
        cosine, sine = cosine_ref[...], sine_ref[...]
        return (
            (front * cosine - back * sine).astype(low),
            (back * cosine + front * sine).astype(low),
        )

    keys_ref[:, :half_key], keys_ref[:, half_key:] = turned(query_width)
    values_ref[...] = projected[:, query_width + key_width :].astype(low)

    for head in range(heads):
        if near_weights and head == heads // 2:
            rep_pass(1)
        start = head * key_width
        cols = pl.ds(start, key_width)
        front, back = turned(start)
        queries_ref[:, pl.ds(start, half_key)] = front
        queries_ref[:, pl.ds(start + half_key, half_key)] = back
        allowed = (doc_col_ref[...] == doc_row_ref[...]) & (
            lax.broadcasted_iota(jnp.int32, (rows, rows), 0)
            >= lax.broadcasted_iota(jnp.int32, (rows, rows), 1)
        )
        scores = against_cols(queries_ref[:, cols], keys_ref[...]) * (HD ** (-0.5) / CAP_LIMIT)
        capped = jnp.where(allowed, CAP_LIMIT * jnp.tanh(scores), MASKED_SCORE)
        powers = jnp.exp(capped - jnp.max(capped, axis=-1, keepdims=True))
        probs = powers / jnp.sum(powers, axis=-1, keepdims=True)
        attended_ref[:, cols] = jnp.dot(
            probs.astype(low), values_ref[...], preferred_element_type=full
        ).astype(low)

    if near_weights:
        pair_arrive(1)
        out_matrix = w_out[...].reshape(query_width, width)
    else:
        out_matrix = out_in[...]
    stores = []
    if near_weights:
        stores.append(pltpu.make_async_copy(w_qkv, qkv_hbm, store_sems.at[0]))
        stores.append(pltpu.make_async_copy(w_out, outw_hbm, store_sems.at[1]))
    else:
        stores.append(pltpu.make_async_copy(qkv_in, qkv_hbm, store_sems.at[0]))
        stores.append(pltpu.make_async_copy(out_in, outw_hbm, store_sems.at[1]))
    for store in stores:
        store.start()
    for member in range(3):
        sibling_copy(member).wait_recv()
        store = pltpu.make_async_copy(
            weights.at[member, pl.ds(half, half)],
            weights_hbm.at[member, pl.ds(half, half)],
            store_sems.at[5 + member],
        )
        store.start()
        stores.append(store)
    branch = jnp.dot(attended_ref[...], out_matrix, preferred_element_type=full)
    branch_ref[...] = branch
    middle = inputs_ref[...].astype(full) + branch * rms_scale(branch) * gains_ref[1:2, :]
    middle_ref[...] = middle
    normed_two_ref[...] = (middle * rms_scale(middle) * gains_ref[2:3, :]).astype(low)
    rows_arrive(1)
    upstream_ref[...] = placed(1).astype(low)
    stores.extend(near_stores)

    for kind in range(2):

        @pl.loop(1, devices)
        def _(hop, kind=kind):
            row_copy(kind, hop, lax.rem(me + hop, devices), me).wait_send()

        if near_weights:
            for block in others():
                line_copy(kind, block, place).wait_send()
                for hop in range(1, share):
                    rep_copy(kind, block, hop, quarter).wait_send()
            for block in range(line):
                pair_copy(kind, block, core).wait_send()
    if near_weights:
        for hop in range(1, shards):
            gain_copy(hop, shard).wait_send()
    for member in range(3):
        sibling_copy(member).wait_send()
    for store in stores:
        store.wait()


def bring_and_attend(
    line, replicas, near_weights, tokens, cotangent, deal, small, gu, down, key_width
):
    gains_in, qkv_in, out_in = small[:3]
    rows, width = tokens.shape
    shards = 2 * line
    devices = replicas * shards
    share = min(4, replicas)
    block_rows = round_up(rows // devices, 8)
    units = down.shape[0]
    half = round_up(units, LANES)
    low = jnp.bfloat16
    full = jnp.float32
    vmem = pl.BlockSpec(memory_space=pltpu.VMEM)
    hbm = pl.BlockSpec(memory_space=pl.ANY)
    dma = pltpu.SemaphoreType.DMA
    qkv_width = qkv_in.shape[1]
    query_width = qkv_width - 2 * key_width
    if near_weights:
        qkv_shape = (shards, *qkv_in.shape)
        out_shape = (shards, *out_in.shape)
    else:
        qkv_shape = qkv_in.shape
        out_shape = out_in.shape
    tile_rows = max(size for size in range(16, 145, 16) if units % size == 0)
    hold = near_weights
    qkv_scratch = qkv_shape if hold else (shards, 16, LANES)
    out_scratch = out_shape if hold else (shards, 16, LANES)
    gain_lanes = round_up(width // shards, LANES) if hold else LANES

    def array(shape, dtype):
        return jax.ShapeDtypeStruct(shape, dtype)

    return pl.pallas_call(
        functools.partial(bring_kernel, line, replicas, near_weights),
        out_shape=(
            array((rows, width), low),
            array((rows, width), low),
            array((rows, width), low),
            array((rows, query_width), low),
            array((rows, key_width), low),
            array((rows, key_width), low),
            array((rows, query_width), low),
            array((rows, width), full),
            array((rows, width), full),
            array((rows, width), low),
            array((4, width), full),
            array((rows, key_width // 2), full),
            array((rows, key_width // 2), full),
            array((rows, 1), jnp.int32),
            array((1, rows), jnp.int32),
            array(qkv_shape, low),
            array(out_shape, low),
            array((3, 2 * half, width), low),
        ),
        in_specs=[vmem] * 6
        + [pl.BlockSpec(memory_space=pltpu.SMEM), vmem]
        + [hbm] * 2,
        out_specs=(vmem,) * 15 + (hbm,) * 3,
        scratch_shapes=[
            pltpu.VMEM(qkv_scratch, low),
            pltpu.VMEM(out_scratch, low),
            pltpu.VMEM((shards, 16, gain_lanes), low),
            pltpu.VMEM((3, 2 * half, width), low),
            pltpu.VMEM((4, tile_rows, width), full),
            pltpu.VMEM((2, devices, block_rows, width), low),
            pltpu.VMEM((2, devices, block_rows, width), low),
            pltpu.VMEM((rows, qkv_width), full),
            dma((4,)),
            dma((8,)),
            dma((2, devices)),
            dma((2, devices)),
            dma((2, line)),
            dma((2, line)),
            dma((2, line, share)),
            dma((2, line, share)),
            dma((2, line)),
            dma((2, line)),
            dma((shards,)),
            dma((shards,)),
            dma((3,)),
            dma((3,)),
        ],
        compiler_params=pltpu.CompilerParams(
            collective_id=2, has_side_effects=True, vmem_limit_bytes=63 * 1024 * 1024
        ),
        cost_estimate=pl.CostEstimate(
            flops=6 * rows * width * qkv_width,
            bytes_accessed=3 * units * width * 8,
            transcendentals=2 * rows * rows * 4,
        ),
    )(tokens, cotangent, deal, *small, gu, down)


def adam_half_kernel(which, first_half, second_half, *refs):
    del which
    inputs, results = refs[:6], refs[-10:]
    part, member = pl.program_id(0), pl.program_id(1)
    gradient = jnp.where(part == 0, first_half[0], second_half[0]).astype(jnp.float32)

    def step(rows_in, rows_out, rate, decay):
        master, first, second = (ref[...].reshape(gradient.shape) for ref in rows_in)
        updated, moment, square = adam_values(master, gradient, first, second, rate, decay)
        for ref, value in zip(rows_out, (updated, moment, square, gradient, updated)):
            ref[...] = value.astype(ref.dtype).reshape(ref.shape)

    @pl.when(member == 0)
    def _():
        step(inputs[:3], results[:5], LEARN_RATES[3], DECAY_RATES[3])

    @pl.when(member > 0)
    def _():
        step(inputs[3:], results[5:], LEARN_RATES[2], DECAY_RATES[2])


def adam_values(master, gradient, first, second, rate, decay):
    moment = BETA_FIRST * first + (1.0 - BETA_FIRST) * gradient
    square = BETA_SECOND * second + (1.0 - BETA_SECOND) * gradient * gradient
    moment_hat = moment * (1.0 / (1.0 - BETA_FIRST**STEP))
    square_hat = square * (1.0 / (1.0 - BETA_SECOND**STEP))
    updated = master - rate * (moment_hat / (jnp.sqrt(square_hat) + ADAM_EPS) + decay * master)
    return updated, moment, square


def adam_stream_kernel(begun, which, first_half, second_half, *refs):
    sources, refs = refs[:6], refs[6 + begun :]
    results, (taken, grads, given, copies, in_sems, out_sems) = refs[:10], refs[10:]
    depth, tile = taken.shape[0], taken.shape[2]
    units = sources[0].shape[0]
    members = first_half.shape[0]
    order = [
        (part, sub, member) for part in range(2) for sub in range(2) for member in range(members)
    ]

    def rows_of(part, sub):
        begin = (part * 4 + which[part] * 2) * tile
        start = begin + sub * tile
        if part == 1 and sub == 1:
            start = jnp.minimum(start, units - tile)
        return at_rows(start, tile), at_rows(start - begin, tile)

    def view(ref, member, span):
        return ref.at[span] if member == 0 else ref.at[member - 1, span]

    def loads(turn):
        part, sub, member = order[turn]
        span, grad_span = rows_of(part, sub)
        slot = turn % depth
        group = sources[:3] if member == 0 else sources[3:]
        pairs = [(view(ref, member, span), taken.at[slot, at]) for at, ref in enumerate(group)]
        half = (first_half, second_half)[part]
        pairs.append((half.at[member, grad_span], grads.at[slot]))
        return [
            pltpu.make_async_copy(source, target, in_sems.at[slot, at])
            for at, (source, target) in enumerate(pairs)
        ]

    def stores(turn):
        part, sub, member = order[turn]
        span, _ = rows_of(part, sub)
        slot = turn % 2
        group = results[:5] if member == 0 else results[5:]
        held = [given.at[slot, at] for at in range(4)] + [copies.at[slot]]
        return [
            pltpu.make_async_copy(source, view(ref, member, span), out_sems.at[slot, at])
            for at, (source, ref) in enumerate(zip(held, group))
        ]

    for turn in range(depth):
        for load in loads(turn):
            load.start()
    for turn, (_, _, member) in enumerate(order):
        slot, out = turn % depth, turn % 2
        rate, decay = (LEARN_RATES[3], DECAY_RATES[3]) if member == 0 else (
            LEARN_RATES[2],
            DECAY_RATES[2],
        )
        for load in loads(turn):
            load.wait()
        if turn >= 2:
            for store in stores(turn - 2):
                store.wait()

        @pl.loop(0, tile // 16)
        def _(group, slot=slot, out=out, rate=rate, decay=decay):
            span = at_rows(group * 16, 16)
            gradient = grads[slot, span, :].astype(jnp.float32)
            updated, moment, square = adam_values(
                taken[slot, 0, span, :],
                gradient,
                taken[slot, 1, span, :],
                taken[slot, 2, span, :],
                rate,
                decay,
            )
            for at, value in enumerate((updated, moment, square, gradient)):
                given[out, at, span, :] = value
            copies[out, span, :] = updated.astype(copies.dtype)

        for store in stores(turn):
            store.start()
        if turn + depth < len(order):
            for load in loads(turn + depth):
                load.start()
    for turn in range(len(order) - 2, len(order)):
        for store in stores(turn):
            store.wait()


def adam_stream(which, halves, arrays, begun=()):
    members, half_rows, width = halves[0].shape
    tile = half_rows // 2
    hbm = pl.BlockSpec(memory_space=pl.ANY)
    full, low = jnp.float32, jnp.bfloat16
    shapes = []
    for like in (arrays[0], arrays[3]):
        shapes.extend([jax.ShapeDtypeStruct(like.shape, full)] * 4)
        shapes.append(jax.ShapeDtypeStruct(like.shape, low))
    count = members * half_rows * width * 2
    return pl.pallas_call(
        functools.partial(adam_stream_kernel, len(begun)),
        out_shape=tuple(shapes),
        in_specs=[pl.BlockSpec(memory_space=pltpu.SMEM)] + [hbm] * (8 + len(begun)),
        out_specs=(hbm,) * 10,
        scratch_shapes=[
            pltpu.VMEM((3, 3, tile, width), full),
            pltpu.VMEM((3, tile, width), low),
            pltpu.VMEM((2, 4, tile, width), full),
            pltpu.VMEM((2, tile, width), low),
            pltpu.SemaphoreType.DMA((3, 4)),
            pltpu.SemaphoreType.DMA((2, 5)),
        ],
        input_output_aliases={9 + at: at for at in range(len(begun))},
        compiler_params=pltpu.CompilerParams(vmem_limit_bytes=60 * 1024 * 1024),
        cost_estimate=pl.CostEstimate(
            flops=16 * count, bytes_accessed=32 * count, transcendentals=2 * count
        ),
    )(which, *halves, *arrays, *begun)


def adam_half(which, halves, arrays, begun=()):
    members, half_rows, width = halves[0].shape
    tile = half_rows // 2
    down, gu = arrays[0], arrays[3]
    if down.shape[0] - 3 * half_rows >= tile:
        return adam_stream(which, halves, arrays, begun)

    def down_at(part, member, sub, chosen):
        return (part * 4 + chosen[part] * 2 + jnp.where(member == 0, sub, 1), 0)

    def gu_at(part, member, sub, chosen):
        row = part * 4 + chosen[part] * 2 + jnp.where(member == 0, 0, sub)
        return (jnp.maximum(member - 1, 0), row, 0)

    def first_at(part, member, sub, chosen):
        return (jnp.where(part == 0, member, members - 1), jnp.where(part == 0, sub, 1), 0)

    def second_at(part, member, sub, chosen):
        return (jnp.where(part == 0, 0, member), jnp.where(part == 0, 0, sub), 0)

    down_block = pl.BlockSpec((tile, width), down_at)
    gu_block = pl.BlockSpec((1, tile, width), gu_at)
    half_block = (1, tile, width)
    hbm = pl.BlockSpec(memory_space=pl.ANY)
    shapes = []
    for like in (down, gu):
        shapes.extend([jax.ShapeDtypeStruct(like.shape, jnp.float32)] * 4)
        shapes.append(jax.ShapeDtypeStruct(like.shape, jnp.bfloat16))
    count = members * half_rows * width * 2
    return pl.pallas_call(
        adam_half_kernel,
        out_shape=tuple(shapes),
        grid_spec=pltpu.PrefetchScalarGridSpec(
            num_scalar_prefetch=1,
            grid=(2, members, 2),
            in_specs=[
                pl.BlockSpec(half_block, first_at),
                pl.BlockSpec(half_block, second_at),
                *[down_block] * 3,
                *[gu_block] * 3,
                *[hbm] * len(begun),
            ],
            out_specs=(*[down_block] * 5, *[gu_block] * 5),
        ),
        input_output_aliases={9 + at: at for at in range(len(begun))},
        compiler_params=pltpu.CompilerParams(vmem_limit_bytes=60 * 1024 * 1024),
        cost_estimate=pl.CostEstimate(
            flops=16 * count, bytes_accessed=32 * count, transcendentals=2 * count
        ),
    )(which, *halves, *arrays, *begun)


def local(
    tokens,
    cotangent,
    lengths,
    deal,
    w_qkv,
    w_out,
    w_gu,
    w_down,
    gains,
    first_qkv,
    first_out,
    first_gu,
    first_down,
    first_gains,
    second_qkv,
    second_out,
    second_gu,
    second_down,
    second_gains,
):
    row_count, width = tokens.shape
    shards = lax.axis_size("shard")
    replicas = lax.axis_size("rep")
    line = shards // 2
    devices = replicas * shards
    deal_blocks = deal.reshape(deal.shape[0] // LANES, LANES)
    exponent = np.arange(HD // 2, dtype=np.float32) * np.float32(-2.0 / HD)
    frequency = jnp.asarray((np.float32(ROPE_BASE) ** exponent)[None, :])
    near_weights = w_qkv.shape[0] % 16 == 0
    if near_weights:
        first_weights = (gains, w_qkv, w_out)
    else:
        first_weights = (
            lax.all_gather(gains.astype(jnp.bfloat16), "shard", axis=1, tiled=True).astype(
                jnp.float32
            ),
            lax.all_gather(w_qkv.astype(jnp.bfloat16), "shard", axis=0, tiled=True),
            lax.all_gather(w_out.astype(jnp.bfloat16), "shard", axis=0, tiled=True),
        )
    (
        inputs,
        upstream,
        normed_one,
        queries,
        key_rows,
        value_rows,
        attended,
        branch,
        middle,
        normed_two,
        gain_values,
        cosine_table,
        sine_table,
        doc_col,
        doc_row,
        full_qkv,
        full_out,
        ff_weights,
    ) = bring_and_attend(
        line,
        replicas,
        near_weights,
        tokens,
        cotangent,
        deal_blocks,
        (*first_weights, lengths, frequency),
        w_gu,
        w_down,
        HD,
    )
    full_qkv = full_qkv.reshape(width, w_qkv.shape[1])
    full_out = full_out.reshape(H * HD, width)
    output_rows, last_gain_grad, grad_normed_two, ff_grads = feed_forward(
        line,
        replicas,
        normed_two,
        middle,
        upstream,
        gain_values,
        ff_weights,
    )
    first_half, second_half, qkv_sums, out_sums, output, input_grad = back_and_reduce(
        line,
        replicas,
        (
            grad_normed_two,
            middle,
            upstream,
            branch,
            inputs,
            normed_one,
            attended,
            queries,
            key_rows,
            value_rows,
            cosine_table,
            sine_table,
            doc_col,
            doc_row,
            gain_values,
            last_gain_grad,
            output_rows,
            deal_blocks,
        ),
        full_qkv,
        full_out,
        ff_grads,
    )
    output = output.astype(jnp.bfloat16)
    input_grad = input_grad.astype(jnp.bfloat16)

    bits = replicas.bit_length() - 1
    flips = (1, 1 << (bits - 1))
    other_halves = tuple(
        lax.ppermute(half, "rep", [(member, member ^ flip) for member in range(replicas)])
        for half, flip in zip((first_half, second_half), flips)
    )
    rep = lax.axis_index("rep")
    held = jnp.stack([lax.rem(lax.div(rep, flip), 2) for flip in flips]).astype(jnp.int32)
    ff_arrays = (w_down, first_down, second_down, w_gu, first_gu, second_gu)
    begun = adam_half(held, (first_half, second_half), ff_arrays)
    (
        new_down,
        moment_down,
        square_down,
        summed_down,
        copy_down,
        new_gu,
        moment_gu,
        square_gu,
        summed_gu,
        copy_gu,
    ) = adam_half(1 - held, other_halves, ff_arrays, begun)
    summed_qkv = qkv_sums[: w_qkv.shape[0]].astype(jnp.float32)
    summed_out = out_sums[: w_out.shape[0]].astype(jnp.float32)
    gain_span = gains.shape[1]
    gain_rows = qkv_sums[-16:-4, H * HD : H * HD + width // 3]
    summed_gains = lax.dynamic_slice(
        gain_rows.reshape(3, gains.shape[0], width // 3)
        .transpose(1, 0, 2)
        .reshape(gains.shape[0], width),
        (0, lax.axis_index("shard") * gain_span),
        (gains.shape[0], gain_span),
    ).astype(jnp.float32)
    new_qkv, moment_qkv, square_qkv = adamw_step(
        w_qkv, summed_qkv, first_qkv, second_qkv, LEARN_RATES[0], DECAY_RATES[0]
    )
    new_out, moment_out, square_out = adamw_step(
        w_out, summed_out, first_out, second_out, LEARN_RATES[1], DECAY_RATES[1]
    )
    new_gains, moment_gains, square_gains = adamw_step(
        gains, summed_gains, first_gains, second_gains, LEARN_RATES[4], DECAY_RATES[4]
    )
    return (
        output,
        input_grad,
        new_qkv,
        new_out,
        new_gu,
        new_down,
        new_gains,
        moment_qkv,
        moment_out,
        moment_gu,
        moment_down,
        moment_gains,
        square_qkv,
        square_out,
        square_gu,
        square_down,
        square_gains,
        summed_qkv,
        summed_out,
        summed_gu,
        summed_down,
        summed_gains,
        new_qkv.astype(jnp.bfloat16),
        new_out.astype(jnp.bfloat16),
        copy_gu,
        copy_down,
        new_gains.astype(jnp.bfloat16),
    )


def solution(mesh):
    placed = (
        P(("rep", "shard"), None),
        P(("rep", "shard"), None),
        P(("rep", "shard"), None),
        P(),
        P("shard", None),
        P("shard", None),
        P(None, "shard", None),
        P("shard", None),
        P(None, "shard"),
        P("shard", None),
        P("shard", None),
        P(None, "shard", None),
        P("shard", None),
        P(None, "shard"),
        P("shard", None),
        P("shard", None),
        P(None, "shard", None),
        P("shard", None),
        P(None, "shard"),
    )
    return jax.shard_map(
        local,
        mesh=mesh,
        in_specs=placed,
        out_specs=(
            P(("rep", "shard"), None),
            P(("rep", "shard"), None),
            P("shard", None),
            P("shard", None),
            P(None, "shard", None),
            P("shard", None),
            P(None, "shard"),
            P("shard", None),
            P("shard", None),
            P(None, "shard", None),
            P("shard", None),
            P(None, "shard"),
            P("shard", None),
            P("shard", None),
            P(None, "shard", None),
            P("shard", None),
            P(None, "shard"),
            P("shard", None),
            P("shard", None),
            P(None, "shard", None),
            P("shard", None),
            P(None, "shard"),
            P("shard", None),
            P("shard", None),
            P(None, "shard", None),
            P("shard", None),
            P(None, "shard"),
        ),
        check_vma=False,
    )
```

```python
import functools

import jax
import jax.numpy as jnp
import numpy as np
from jax import lax
from jax.experimental import pallas as pl
from jax.experimental.pallas import tpu as pltpu
from jax.sharding import PartitionSpec as P

H = 4
KV = 1
HD = 256
STEP = 10


CAP_LIMIT = 50.0
NORM_EPS = 1e-06
ROPE_BASE = 10000.0
MASKED_SCORE = -1e30
BETA_FIRST = 0.5
BETA_SECOND = 0.5
ADAM_EPS = 1e-08
LEARN_RATES = (0.05, 0.1, 0.03, 0.012, 0.4)
DECAY_RATES = (0.1, 0.1, 0.1, 0.1, 0.0)
GELU_COEF = 0.7978845608028654
GELU_CUBIC = 0.044715


def rms_scale(values):
    return lax.rsqrt(jnp.mean(values * values, axis=-1, keepdims=True) + NORM_EPS)


def norm_backward(grad_out, values, inverse_rms, gain_row):
    scaled = grad_out * gain_row
    inner = jnp.mean(scaled * values, axis=-1, keepdims=True)
    grad_in = inverse_rms * scaled - values * inverse_rms * inverse_rms * inverse_rms * inner
    grad_gain = jnp.sum(grad_out * values * inverse_rms, axis=0)
    return (grad_in, grad_gain)


def cross_rows(leading, trailing):
    return lax.dot_general(
        leading, trailing, (((0,), (0,)), ((), ())), preferred_element_type=jnp.float32
    )


def against_cols(leading, trailing):
    return lax.dot_general(
        leading, trailing, (((1,), (1,)), ((), ())), preferred_element_type=jnp.float32
    )


def adamw_step(master, gradient, first_moment, second_moment, rate, decay):
    moment = BETA_FIRST * first_moment + (1.0 - BETA_FIRST) * gradient
    square = BETA_SECOND * second_moment + (1.0 - BETA_SECOND) * gradient * gradient
    moment_hat = moment / (1.0 - BETA_FIRST**STEP)
    square_hat = square / (1.0 - BETA_SECOND**STEP)
    updated = master - rate * (moment_hat / (jnp.sqrt(square_hat) + ADAM_EPS) + decay * master)
    return (updated, moment, square)


LANES = 128
UNIT_TILE = 256
MESH = pl.DeviceIdType.MESH


def round_up(count, step):
    return -(-count // step) * step


def partner_of(index, bit):
    value = lax.rem(lax.div(index, 1 << bit), 2)
    return index + (1 - 2 * value) * (1 << bit), value


EARLY = 1


def deal_row(deal_ref, device, rows):
    lines = rows // LANES
    return jnp.concatenate(
        [deal_ref[pl.ds(device * lines + at, 1), :] for at in range(lines)], axis=1
    )


def halving_spans(rep, bits, part, part_rows):
    spans = []
    first = part * part_rows
    size = part_rows
    for bit in range(bits) if part == 0 else range(bits - 1, -1, -1):
        size //= 2
        partner, value = partner_of(rep, bit)
        spans.append((partner, first + value * size, first + (1 - value) * size, size))
        first = first + value * size
    return spans


def at_rows(first, size):
    return pl.ds(pl.multiple_of(first, 16), size)


def feed_kernel(
    line,
    replicas,
    own_rows,
    middle_ref,
    upstream_ref,
    gain_ref,
    weights_hbm,
    out_ref,
    gain_grad_ref,
    back_ref,
    grads_ref,
    weights,
    blocks,
    acts,
    partial,
    chain,
    sibling_out,
    sibling_in,
    landing,
    load_sems,
    store_sems,
    gather_send,
    gather_recv,
    chain_send,
    chain_recv,
    sibling_send,
    sibling_recv,
    half_send,
    half_recv,
):
    rep = lax.axis_index("rep")
    shard = lax.axis_index("shard")
    core = lax.rem(shard, 2)
    place = lax.div(shard, 2)
    sibling = (rep, shard + 1 - 2 * core)
    left = (rep, shard - 2)
    right = (rep, shard + 2)
    has_left = place > 0
    has_right = place < line - 1
    rows = own_rows.shape[0] // 2
    width = own_rows.shape[1]
    half = weights.shape[1] // 2
    tiles = 2 * half // UNIT_TILE

    load = pltpu.make_async_copy(weights_hbm, weights, load_sems.at[0])
    load.start()

    barrier = pltpu.get_barrier_semaphore()
    pl.semaphore_signal(barrier, inc=1, device_id=sibling, device_id_type=MESH)

    @pl.when(has_left)
    def _():
        pl.semaphore_signal(barrier, inc=1, device_id=left, device_id_type=MESH)

    @pl.when(has_right)
    def _():
        pl.semaphore_signal(barrier, inc=1, device_id=right, device_id_type=MESH)

    bits = replicas.bit_length() - 1
    greeted = sorted({0, bits - 1})
    for bit in greeted:
        partner, _ = partner_of(rep, bit)
        pl.semaphore_signal(barrier, inc=1, device_id=(partner, shard), device_id_type=MESH)

    def block_span(block):
        return pl.ds(pl.multiple_of(block * rows, rows), rows)

    for part in range(2):
        blocks[0, part, block_span(place), :] = own_rows[part * rows : (part + 1) * rows, :]

    pl.semaphore_wait(
        barrier,
        1 + len(greeted) + has_left.astype(jnp.int32) + has_right.astype(jnp.int32),
    )

    def gather_copy(phase, part, way, step, block):
        return pltpu.make_async_remote_copy(
            src_ref=blocks.at[phase, part, block_span(block)],
            dst_ref=blocks.at[phase, part, block_span(block)],
            send_sem=gather_send.at[phase, part, way, step],
            recv_sem=gather_recv.at[phase, part, way, step],
            device_id=left if way else right,
            device_id_type=MESH,
        )

    def gather_start(phase, part, step):
        @pl.when(has_right & (place - step >= 0))
        def _():
            gather_copy(phase, part, 0, step, place - step).start()

        @pl.when(has_left & (place + step <= line - 1))
        def _():
            gather_copy(phase, part, 1, step, place + step).start()

    def gather_arrive(phase, part, step):
        @pl.when(place - 1 - step >= 0)
        def _():
            gather_copy(phase, part, 0, step, place - 1 - step).wait_recv()

        @pl.when(place + 1 + step <= line - 1)
        def _():
            gather_copy(phase, part, 1, step, place + 1 + step).wait_recv()

    def gather_drain(phase, part):
        @pl.loop(0, line - 1)
        def _(step):
            @pl.when(has_right & (place - step >= 0))
            def _():
                gather_copy(phase, part, 0, step, place - step).wait_send()

            @pl.when(has_left & (place + step <= line - 1))
            def _():
                gather_copy(phase, part, 1, step, place + step).wait_send()

    def chain_copy(phase, part, way, packet, block):
        return pltpu.make_async_remote_copy(
            src_ref=partial.at[part, block_span(block)],
            dst_ref=chain.at[part, way, packet],
            send_sem=chain_send.at[phase, part, way, packet],
            recv_sem=chain_recv.at[phase, part, way, packet],
            device_id=left if way else right,
            device_id_type=MESH,
        )

    def chain_add(phase, part, way, packet, block):
        chain_copy(phase, part, way, packet, block).wait_recv()
        span = block_span(block)
        partial[part, span, :] = (
            partial[part, span, :].astype(jnp.float32) + chain[part, way, packet].astype(jnp.float32)
        ).astype(partial.dtype)

    def chain_turn(phase, part, turn):
        outward = turn - place

        @pl.when(outward >= 0)
        def _():
            @pl.when(has_left)
            def _():
                chain_add(phase, part, 0, outward, line - 1 - outward)

            chain_copy(phase, part, 0, outward, line - 1 - outward).start()

        inward = turn - (line - 1 - place)

        @pl.when(inward >= 0)
        def _():
            @pl.when(has_right)
            def _():
                chain_add(phase, part, 1, inward, inward)

            chain_copy(phase, part, 1, inward, inward).start()

    def chain_finish(phase, part):
        out = slice(part * rows, (part + 1) * rows)
        back_ref[out, :] = partial[part, block_span(place), :].astype(jnp.float32)

        @pl.when(has_left)
        def _():
            last = line - 1 - place
            chain_copy(phase, part, 0, last, place).wait_recv()
            back_ref[out, :] += chain[part, 0, last].astype(jnp.float32)

        @pl.when(has_right)
        def _():
            chain_copy(phase, part, 1, place, place).wait_recv()
            back_ref[out, :] += chain[part, 1, place].astype(jnp.float32)

    def chain_drain(phase, part):
        @pl.loop(0, line - 1)
        def _(packet):
            @pl.when(line - 1 - packet > place)
            def _():
                chain_copy(phase, part, 0, packet, line - 1 - packet).wait_send()

            @pl.when(packet < place)
            def _():
                chain_copy(phase, part, 1, packet, packet).wait_send()

    def sweep(phase, part, work, reduce=None, last=None, beside=None):
        @pl.loop(1, line)
        def _(turn):
            gather_arrive(phase, part, turn - 1)

            @pl.when(turn < line - 1)
            def _():
                gather_start(phase, part, turn)
                if reduce is not None:
                    chain_turn(*reduce, turn)

            if last is not None:

                @pl.when(turn == line - 1)
                def _():
                    last()

            @pl.loop(0, line // 2)
            def _(pair):
                ready = jnp.maximum(jnp.abs(2 * pair - place), jnp.abs(2 * pair + 1 - place))

                @pl.when(ready == turn)
                def _():
                    work(part, pair)

            if beside is not None:
                beside(turn)

    def pair_span(pair):
        return pl.ds(pl.multiple_of(pair * 2 * rows, 2 * rows), 2 * rows)

    def token_span(part, pair):
        first = part * line * rows
        return pl.ds(pl.multiple_of(first + pair * 2 * rows, 2 * rows), 2 * rows)

    def unit_span(tile):
        return pl.ds(pl.multiple_of(tile * UNIT_TILE, UNIT_TILE), UNIT_TILE)

    def forward(part, pair):
        span = token_span(part, pair)

        @pl.loop(0, tiles)
        def _(tile):
            cols = unit_span(tile)
            rows_in = blocks[0, part, pair_span(pair), :]
            gate = against_cols(rows_in, weights[1, cols, :])
            upper = against_cols(rows_in, weights[2, cols, :])
            tanh_inner = jnp.tanh(GELU_COEF * (gate + GELU_CUBIC * gate * gate * gate))
            lifted = 0.5 * (1.0 + tanh_inner)
            activated = gate * lifted
            slope = lifted + 0.5 * gate * (1.0 - tanh_inner * tanh_inner) * GELU_COEF * (
                1.0 + 3.0 * GELU_CUBIC * gate * gate
            )
            acts[0, span, cols] = (activated * upper).astype(acts.dtype)
            acts[1, span, cols] = (upper * slope).astype(acts.dtype)
            acts[2, span, cols] = activated.astype(acts.dtype)

        partial[part, pair_span(pair), :] = jnp.dot(
            acts[0, span, :], weights[0], preferred_element_type=jnp.float32
        ).astype(partial.dtype)

    def backward(part, pair):
        span = token_span(part, pair)

        @pl.loop(0, tiles)
        def _(tile):
            cols = unit_span(tile)
            grad_hidden = against_cols(blocks[1, part, pair_span(pair), :], weights[0, cols, :])
            for member in (1, 2):
                acts[member, span, cols] = (
                    grad_hidden * acts[member, span, cols].astype(jnp.float32)
                ).astype(acts.dtype)

        partial[part, pair_span(pair), :] = (
            jnp.dot(acts[1, span, :], weights[1], preferred_element_type=jnp.float32)
            + jnp.dot(acts[2, span, :], weights[2], preferred_element_type=jnp.float32)
        ).astype(partial.dtype)

    def output_half(part):
        out = slice(part * rows, (part + 1) * rows)
        feed = back_ref[out, :]
        upstream = upstream_ref[out, :].astype(jnp.float32)
        gain = gain_ref[3:4, :]
        inverse = lax.rsqrt(jnp.mean(feed * feed, axis=-1, keepdims=True) + NORM_EPS)
        scaled = upstream * gain
        inner = jnp.mean(scaled * feed, axis=-1, keepdims=True)
        blocks[1, part, block_span(place), :] = (
            inverse * scaled - feed * inverse * inverse * inverse * inner
        ).astype(blocks.dtype)
        gather_start(1, part, 0)
        gain_grad = jnp.sum(upstream * feed * inverse, axis=0, keepdims=True)
        if part == 0:
            gain_grad_ref[...] = gain_grad
        else:
            gain_grad_ref[...] += gain_grad
        out_ref[out, :] = (middle_ref[out, :] + feed * inverse * gain).astype(out_ref.dtype)

    def sibling_copy(member):
        return pltpu.make_async_remote_copy(
            src_ref=sibling_out.at[member],
            dst_ref=sibling_in.at[member],
            send_sem=sibling_send.at[member],
            recv_sem=sibling_recv.at[member],
            device_id=sibling,
            device_id_type=MESH,
        )

    def store_copy(member):
        return pltpu.make_async_copy(
            sibling_in.at[member], grads_ref.at[member], store_sems.at[member]
        )

    cuts = [(start, min(512, half - start)) for start in range(0, half, 512)]

    def far_grad(part, member):
        tokens = line * rows
        trailing = jnp.where(member == 0, 1, 0)
        for start, size in cuts:
            span = slice(start, start + size)
            piece = cross_rows(
                acts[member, part * tokens : (part + 1) * tokens, half + start : half + start + size],
                blocks[trailing, part],
            )
            if part == 1:
                piece = piece + sibling_out[member, span, :].astype(jnp.float32)
            sibling_out[member, span, :] = piece.astype(sibling_out.dtype)
        if part == 1:
            sibling_copy(member).start()

    first_spans = [halving_spans(rep, bits, part, half // 2)[0] for part in range(2)]

    def halve(member, part):
        partner, keep, give, size = first_spans[part]
        return pltpu.make_async_remote_copy(
            src_ref=sibling_in.at[member, at_rows(give, size)],
            dst_ref=landing.at[member, part],
            send_sem=half_send.at[member, part],
            recv_sem=half_recv.at[member, part],
            device_id=(partner, shard),
            device_id_type=MESH,
        )

    def near_grad(member):
        trailing = jnp.where(member == 0, 1, 0)
        sibling_copy(member).wait_recv()
        for start, size in cuts:
            span = slice(start, start + size)
            piece = cross_rows(
                acts[member, :, span], blocks[trailing].reshape(2 * line * rows, width)
            )
            sibling_in[member, span, :] = (
                sibling_in[member, span, :].astype(jnp.float32) + piece
            ).astype(sibling_in.dtype)

        @pl.when(member < EARLY)
        def _():
            for part in range(2):
                halve(member, part).start()

        @pl.when(member >= EARLY)
        def _():
            store_copy(member).start()

    def share(turn, count, turns):
        return lax.div(turn * count, turns), lax.div((turn + 1) * count, turns)

    def first_grads(turn):
        @pl.when(turn < line - 1)
        def _():
            @pl.loop(*share(turn - 1, 3, line - 2))
            def _(member):
                far_grad(0, member)

    def last_grads(turn):
        @pl.loop(*share(turn, 6, line - 1))
        def _(unit):
            @pl.when((unit < 2) | (unit == 3))
            def _():
                far_grad(1, jnp.minimum(unit, 2))

            @pl.when((unit == 2) | (unit > 3))
            def _():
                near_grad(jnp.where(unit == 2, 0, unit - 3))

    def turn_around(part):
        chain_finish(0, part)
        output_half(part)

    gather_start(0, 0, 0)
    load.wait()
    sweep(0, 0, forward, last=lambda: gather_start(0, 1, 0))
    chain_turn(0, 0, 0)
    sweep(0, 1, forward, reduce=(0, 0), last=lambda: turn_around(0))
    chain_turn(0, 1, 0)
    chain_drain(0, 0)
    sweep(1, 0, backward, reduce=(0, 1), last=lambda: turn_around(1))
    chain_turn(1, 0, 0)
    chain_drain(0, 1)
    sweep(1, 1, backward, reduce=(1, 0), beside=first_grads)
    chain_turn(1, 1, 0)
    chain_finish(1, 0)

    @pl.loop(0, line - 1)
    def _(turn):
        @pl.when(turn > 0)
        def _():
            chain_turn(1, 1, turn)

        last_grads(turn)

    chain_finish(1, 1)
    for member in range(EARLY):
        for part in range(2):
            halve(member, part).wait_recv()
            partner, keep, give, size = first_spans[part]
            kept = at_rows(keep, size)
            sibling_in[member, kept, :] = (
                sibling_in[member, kept, :].astype(jnp.float32)
                + landing[member, part].astype(jnp.float32)
            ).astype(sibling_in.dtype)
        store_copy(member).start()
    for part in range(2):
        for phase in range(2):
            gather_drain(phase, part)
        chain_drain(1, part)
        for member in range(EARLY):
            halve(member, part).wait_send()
    for member in range(3):
        sibling_copy(member).wait_send()
        store_copy(member).wait()


def feed_forward(line, replicas, normed, middle, upstream, gains, weights):
    rows, width = normed.shape
    half = weights.shape[1] // 2
    low = jnp.bfloat16
    full = jnp.float32
    vmem = pl.BlockSpec(memory_space=pltpu.VMEM)
    hbm = pl.BlockSpec(memory_space=pl.ANY)
    tokens = line * rows
    return pl.pallas_call(
        functools.partial(feed_kernel, line, replicas),
        out_shape=(
            jax.ShapeDtypeStruct((rows, width), low),
            jax.ShapeDtypeStruct((1, width), full),
            jax.ShapeDtypeStruct((rows, width), full),
            jax.ShapeDtypeStruct((3, half, width), low),
        ),
        in_specs=[vmem, vmem, vmem, vmem, hbm],
        out_specs=(vmem, vmem, vmem, hbm),
        scratch_shapes=[
            pltpu.VMEM((3, 2 * half, width), low),
            pltpu.VMEM((2, 2, tokens // 2, width), low),
            pltpu.VMEM((3, tokens, 2 * half), low),
            pltpu.VMEM((2, tokens // 2, width), low),
            pltpu.VMEM((2, 2, line - 1, rows // 2, width), low),
            pltpu.VMEM((3, half, width), low),
            pltpu.VMEM((3, half, width), low),
            pltpu.VMEM((EARLY, 2, half // 4, width), low),
            pltpu.SemaphoreType.DMA((1,)),
            pltpu.SemaphoreType.DMA((3,)),
            pltpu.SemaphoreType.DMA((2, 2, 2, line - 1)),
            pltpu.SemaphoreType.DMA((2, 2, 2, line - 1)),
            pltpu.SemaphoreType.DMA((2, 2, 2, line - 1)),
            pltpu.SemaphoreType.DMA((2, 2, 2, line - 1)),
            pltpu.SemaphoreType.DMA((3,)),
            pltpu.SemaphoreType.DMA((3,)),
            pltpu.SemaphoreType.DMA((EARLY, 2)),
            pltpu.SemaphoreType.DMA((EARLY, 2)),
        ],
        compiler_params=pltpu.CompilerParams(
            collective_id=0, has_side_effects=True, vmem_limit_bytes=63 * 1024 * 1024
        ),
        cost_estimate=pl.CostEstimate(
            flops=18 * tokens * 2 * half * width,
            bytes_accessed=9 * half * width * 2,
            transcendentals=tokens * 2 * half,
        ),
    )(normed, middle, upstream, gains, weights)


def back_kernel(
    line,
    replicas,
    back_hbm,
    middle_hbm,
    upstream_hbm,
    branch_hbm,
    inputs_hbm,
    normed_hbm,
    attended_hbm,
    queries_hbm,
    keys_hbm,
    values_hbm,
    cosine_hbm,
    sine_hbm,
    doc_col_ref,
    doc_row_ref,
    gains_ref,
    last_gain_ref,
    out_rows_ref,
    deal_ref,
    first_hbm,
    out_hbm,
    grads_hbm,
    first_half_hbm,
    second_half_hbm,
    qkv_hbm,
    outw_hbm,
    output_ref,
    input_grad_ref,
    w_qkv,
    w_out,
    acc,
    total,
    landing,
    late_landing,
    query_parts,
    query_pair,
    query_chain,
    query_steps,
    query_land,
    key_parts,
    key_pair,
    key_chain,
    key_steps,
    key_land,
    out_parts,
    out_pair,
    out_chain,
    out_steps,
    out_land,
    grad_rows,
    grad_keys,
    grad_values,
    pack_rows,
    send_rows,
    recv_rows,
    held,
    operand_sems,
    load_sems,
    store_sems,
    half_send,
    half_recv,
    pair_send,
    pair_recv,
    chain_send,
    chain_recv,
    step_send,
    step_recv,
    row_send,
    row_recv,
):
    rep = lax.axis_index("rep")
    shard = lax.axis_index("shard")
    shards = 2 * line
    devices = replicas * shards
    me = rep * shards + shard
    core = lax.rem(shard, 2)
    place = lax.div(shard, 2)
    sibling = (rep, shard + 1 - 2 * core)
    left = (rep, shard - 2)
    right = (rep, shard + 2)
    has_left = place > 0
    has_right = place < line - 1
    bits = replicas.bit_length() - 1
    full = jnp.float32
    rows, width = inputs_hbm.shape
    key_width = keys_hbm.shape[1]
    query_width = queries_hbm.shape[1]
    heads = query_width // key_width
    members, half_rows = acc.shape[0], acc.shape[1]
    part_rows = half_rows // 2
    peer_rows = rows // devices
    block_rows = send_rows.shape[2]
    packed = devices * block_rows
    qkv_rows = first_hbm.shape[0] // shards
    out_rows = out_hbm.shape[0] // shards

    load_qkv = pltpu.make_async_copy(first_hbm, w_qkv, load_sems.at[0])
    load_out = pltpu.make_async_copy(out_hbm, w_out, load_sems.at[1])
    load_acc = pltpu.make_async_copy(grads_hbm, acc, load_sems.at[2])
    operands = (
        back_hbm,
        middle_hbm,
        upstream_hbm,
        branch_hbm,
        inputs_hbm,
        normed_hbm,
        attended_hbm,
        queries_hbm,
        keys_hbm,
        values_hbm,
        cosine_hbm,
        sine_hbm,
    )
    operand_loads = [
        pltpu.make_async_copy(source, target, operand_sems.at[at])
        for at, (source, target) in enumerate(zip(operands, held))
    ]
    (
        back_ref,
        middle_ref,
        upstream_ref,
        branch_ref,
        inputs_ref,
        normed_ref,
        attended_ref,
        queries_ref,
        keys_ref,
        values_ref,
        cosine_ref,
        sine_ref,
    ) = held
    load_acc.start()
    for load in operand_loads:
        load.start()
    load_out.start()
    load_qkv.start()

    barrier = pltpu.get_barrier_semaphore()

    @pl.loop(1, devices)
    def _(hop):
        peer = lax.rem(me + hop, devices)
        pl.semaphore_signal(
            barrier,
            inc=1,
            device_id=(lax.div(peer, shards), lax.rem(peer, shards)),
            device_id_type=MESH,
        )

    pl.semaphore_wait(barrier, devices - 1)

    spans = [halving_spans(rep, bits, part, part_rows) for part in range(2)]

    def first_stage(member):
        return 1 if member < EARLY else 0

    def landed(member, part, stage):
        if stage == 0:
            return landing.at[member - EARLY, part]
        size = part_rows >> (stage + 1)
        return late_landing.at[member, part, pl.ds(part_rows // 2 - 2 * size, size)]

    def halve(member, part, stage):
        partner, keep, give, size = spans[part][stage]
        source = grads_hbm if stage == first_stage(member) else acc
        return pltpu.make_async_remote_copy(
            src_ref=source.at[member, at_rows(give, size)],
            dst_ref=landed(member, part, stage),
            send_sem=half_send.at[0, member, part, stage],
            recv_sem=half_recv.at[0, member, part, stage],
            device_id=(partner, shard),
            device_id_type=MESH,
        )

    def halve_add(member, part, stage):
        partner, keep, give, size = spans[part][stage]
        halve(member, part, stage).wait_recv()
        target = total if stage == bits - 1 else acc
        target[member, at_rows(keep, size), :] = (
            acc[member, at_rows(keep, size), :].astype(full)
            + landed(member, part, stage)[...].astype(full)
        ).astype(acc.dtype)

    def double(member, part, stage):
        partner, keep, give, size = spans[part][stage]
        return pltpu.make_async_remote_copy(
            src_ref=total.at[member, at_rows(keep, size)],
            dst_ref=total.at[member, at_rows(keep, size)],
            send_sem=half_send.at[1, member, part, stage],
            recv_sem=half_recv.at[1, member, part, stage],
            device_id=(partner, shard),
            device_id_type=MESH,
        )

    def double_arrive(member, part, stage):
        partner, keep, give, size = spans[part][stage]
        pltpu.make_async_remote_copy(
            src_ref=total.at[member, at_rows(give, size)],
            dst_ref=total.at[member, at_rows(give, size)],
            send_sem=half_send.at[1, member, part, stage],
            recv_sem=half_recv.at[1, member, part, stage],
            device_id=(partner, shard),
            device_id_type=MESH,
        ).wait_recv()

    def each(work):
        for member in range(members):
            for part in range(2):
                work(member, part)

    for part in range(2):
        halve(members - 1, part, first_stage(members - 1)).start()
    for member in range(members - 1):
        for part in range(2):
            halve(member, part, first_stage(member)).start()
    load_acc.wait()

    def pair_copy(kind, parts, pair):
        return pltpu.make_async_remote_copy(
            src_ref=parts.at[1 - core],
            dst_ref=pair,
            send_sem=pair_send.at[kind],
            recv_sem=pair_recv.at[kind],
            device_id=sibling,
            device_id_type=MESH,
        )

    kinds = (
        (out_parts, out_pair, out_chain, out_steps, out_land),
        (query_parts, query_pair, query_chain, query_steps, query_land),
        (key_parts, key_pair, key_chain, key_steps, key_land),
    )

    def pair_add(kind):
        parts, pair = kinds[kind][:2]
        pair_copy(kind, parts, pair).wait_recv()

        @pl.loop(0, line)
        def _(block):
            parts[core, block] = (
                parts[core, block].astype(full) + pair[block].astype(full)
            ).astype(parts.dtype)

    def chain_copy(kind, way, step, block):
        parts, _, chain = kinds[kind][:3]
        return pltpu.make_async_remote_copy(
            src_ref=parts.at[core, block],
            dst_ref=chain.at[way, step],
            send_sem=chain_send.at[kind, way, step],
            recv_sem=chain_recv.at[kind, way, step],
            device_id=left if way else right,
            device_id_type=MESH,
        )

    def chain_add(kind, way, step, block):
        parts, _, chain = kinds[kind][:3]
        chain_copy(kind, way, step, block).wait_recv()
        parts[core, block] = (
            parts[core, block].astype(full) + chain[way, step].astype(full)
        ).astype(parts.dtype)

    def chain_step(kind, turn):
        outward = turn - place

        @pl.when(outward >= 0)
        def _():
            @pl.when(has_left)
            def _():
                chain_add(kind, 0, outward, line - 1 - outward)

            chain_copy(kind, 0, outward, line - 1 - outward).start()

        inward = turn - (line - 1 - place)

        @pl.when(inward >= 0)
        def _():
            @pl.when(has_right)
            def _():
                chain_add(kind, 1, inward, inward)

            chain_copy(kind, 1, inward, inward).start()

    def chain_finish(kind):
        parts, _, _, steps, _ = kinds[kind]

        @pl.when(has_left)
        def _():
            chain_add(kind, 0, line - 1 - place, place)

        @pl.when(has_right)
        def _():
            chain_add(kind, 1, place, place)

        steps[0] = parts[core, place]

    lanes = {0: ((0, None),), 1: ((1, 0), (2, 1)), 2: ((3, None),)}

    def columns(ref, piece):
        if piece is None:
            return ref
        size = ref.shape[1] // 2
        return ref.at[:, pl.ds(piece * size, size)]

    def step_copy(kind, stage, lane, piece):
        steps, land = kinds[kind][3:]
        partner, _ = partner_of(rep, stage if lane in (1, 3) else bits - 1 - stage)
        return pltpu.make_async_remote_copy(
            src_ref=columns(steps.at[stage], piece),
            dst_ref=columns(land.at[stage], piece),
            send_sem=step_send.at[lane, stage],
            recv_sem=step_recv.at[lane, stage],
            device_id=(partner, shard),
            device_id_type=MESH,
        )

    def step_start(kind, stage):
        for lane, piece in lanes[kind]:
            step_copy(kind, stage, lane, piece).start()

    def step_add(kind, stage):
        steps, land = kinds[kind][3:]
        for lane, piece in lanes[kind]:
            step_copy(kind, stage, lane, piece).wait_recv()
            columns(steps.at[stage + 1], piece)[...] = (
                columns(steps.at[stage], piece)[...].astype(full)
                + columns(land.at[stage], piece)[...].astype(full)
            ).astype(steps.dtype)
            if stage + 1 < bits:
                step_copy(kind, stage + 1, lane, piece).start()

    served = {0: 0}

    def chain_to(kind, end):
        for step in range(served[kind], end):
            chain_step(kind, step)
        served[kind] = max(end, served[kind])

    def advance(member, stage):
        for part in range(2):
            halve_add(member, part, stage)
            if stage + 1 < bits:
                halve(member, part, stage + 1).start()
            else:
                double(member, part, stage).start()

    def redouble(member, stage):
        for part in range(2):
            double_arrive(member, part, stage)
            if stage > 1:
                double(member, part, stage - 1).start()
            else:
                store_half(member, part).start()

    def store_half(member, part):
        _, keep, _, size = spans[part][0]
        return pltpu.make_async_copy(
            total.at[member, at_rows(keep, size)],
            (first_half_hbm, second_half_hbm)[part].at[member],
            store_sems.at[3 + 2 * member + part],
        )

    todo = [
        [functools.partial(advance, member, stage) for stage in range(first_stage(member), bits)]
        + [functools.partial(redouble, member, stage) for stage in range(bits - 1, 0, -1)]
        for member in range(members)
    ]

    def serve(*chosen):
        for member in chosen:
            if todo[member]:
                todo[member].pop(0)()

    for load in operand_loads:
        load.wait()
    middle = middle_ref[...]
    upstream = upstream_ref[...].astype(full)
    scale_two = rms_scale(middle)
    grad_middle_norm, gain_two = norm_backward(
        back_ref[...], middle, scale_two, gains_ref[2:3, :]
    )
    back_ref[...] = upstream + grad_middle_norm
    branch = branch_ref[...]
    grad_branch, gain_one = norm_backward(
        back_ref[...], branch, rms_scale(branch), gains_ref[1:2, :]
    )
    grad_branch = grad_branch.astype(jnp.bfloat16)
    half_query = query_width // 2
    half_shards = shards // 2
    for group in range(2):
        grad_out = cross_rows(
            attended_ref[:, group * half_query : (group + 1) * half_query], grad_branch
        )
        for offset in range(half_shards):
            member = group * half_shards + offset
            out_parts[member % 2, member // 2, 0:out_rows, :] = grad_out[
                offset * out_rows : (offset + 1) * out_rows
            ].astype(out_parts.dtype)

    pair_copy(0, out_parts, out_pair).start()
    load_out.wait()
    grad_rows[:, 0:query_width] = against_cols(grad_branch, w_out[...]).astype(grad_rows.dtype)
    grad_keys[...] = jnp.zeros_like(grad_keys)
    grad_values[...] = jnp.zeros_like(grad_values)
    half_key = key_width // 2

    down_ids = lax.broadcasted_iota(jnp.int32, (rows, rows), 0)
    along_ids = lax.broadcasted_iota(jnp.int32, (rows, rows), 1)
    own_slots = down_ids + me * rows

    def find(source, found):
        return found + jnp.where(deal_row(deal_ref, source, rows) == own_slots, source, 0)

    found = lax.fori_loop(0, devices, find, jnp.zeros((rows, rows), jnp.int32))
    origin = jnp.sum(found, axis=1, keepdims=True)
    origin_row = jnp.sum(jnp.where(down_ids == along_ids, origin, 0), axis=0, keepdims=True)
    before = (origin_row == origin) & (down_ids < along_ids)
    back_place = origin_row * block_rows + jnp.sum(
        before.astype(jnp.int32), axis=0, keepdims=True
    )
    pack_rows[...] = (
        lax.broadcasted_iota(jnp.int32, (packed, rows), 0) == back_place
    ).astype(pack_rows.dtype)

    def row_copy(kind, hop, peer, source):
        return pltpu.make_async_remote_copy(
            src_ref=send_rows.at[kind, peer],
            dst_ref=recv_rows.at[kind, source],
            send_sem=row_send.at[kind, hop],
            recv_sem=row_recv.at[kind, hop],
            device_id=(lax.div(peer, shards), lax.rem(peer, shards)),
            device_id_type=MESH,
        )

    def send_back(kind, values):
        send_rows[kind] = (
            jnp.dot(pack_rows[...], values, preferred_element_type=full)
            .reshape(devices, block_rows, width)
            .astype(send_rows.dtype)
        )
        recv_rows[kind, me] = send_rows[kind, me]

        @pl.loop(1, devices)
        def _(hop):
            row_copy(kind, hop, lax.rem(me + hop, devices), me).start()

    send_back(0, out_rows_ref[...])
    pair_add(0)
    chain_to(0, 1)

    for head in range(heads):
        start = head * key_width
        cols = pl.ds(start, key_width)
        query = queries_ref[:, cols]
        key = keys_ref[...]
        allowed = (doc_col_ref[...] == doc_row_ref[...]) & (
            lax.broadcasted_iota(jnp.int32, (rows, rows), 0)
            >= lax.broadcasted_iota(jnp.int32, (rows, rows), 1)
        )
        tanh_scores = jnp.tanh(against_cols(query, key) * (HD ** (-0.5) / CAP_LIMIT))
        capped = jnp.where(allowed, CAP_LIMIT * tanh_scores, MASKED_SCORE)
        powers = jnp.exp(capped - jnp.max(capped, axis=-1, keepdims=True))
        probs = powers / jnp.sum(powers, axis=-1, keepdims=True)
        grad_att = grad_rows[:, cols]
        grad_values[...] += cross_rows(probs.astype(jnp.bfloat16), grad_att)
        grad_probs = against_cols(grad_att, values_ref[...])
        grad_capped = probs * (grad_probs - jnp.sum(probs * grad_probs, axis=-1, keepdims=True))
        grad_raw = (
            grad_capped * (1.0 - tanh_scores * tanh_scores) * HD ** (-0.5)
        ).astype(jnp.bfloat16)
        grad_keys[...] += cross_rows(grad_raw, query)
        grad_query = jnp.dot(grad_raw, key, preferred_element_type=full)
        front = grad_query[:, :half_key]
        back = grad_query[:, half_key:]
        cosine, sine = cosine_ref[...], sine_ref[...]
        grad_rows[:, pl.ds(start, half_key)] = (front * cosine + back * sine).astype(
            grad_rows.dtype
        )
        grad_rows[:, pl.ds(start + half_key, half_key)] = (
            back * cosine - front * sine
        ).astype(grad_rows.dtype)

    def weight_parts(parts, first, size):
        for begin in range(0, size, 512):
            grad_cols = cross_rows(
                normed_ref[...], grad_rows[:, first + begin : first + begin + 512]
            )
            for member in range(shards):
                parts[member % 2, member // 2, 0:qkv_rows, begin : begin + 512] = grad_cols[
                    member * qkv_rows : (member + 1) * qkv_rows
                ].astype(parts.dtype)

    weight_parts(query_parts, 0, query_width)
    pair_copy(1, query_parts, query_pair).start()
    serve(members - 1, 0)
    chain_to(0, min(2, line - 1))
    front = grad_keys[:, :half_key]
    back = grad_keys[:, half_key:]
    cosine, sine = cosine_ref[...], sine_ref[...]
    grad_rows[:, query_width : query_width + half_key] = (
        front * cosine + back * sine
    ).astype(grad_rows.dtype)
    grad_rows[:, query_width + half_key : query_width + key_width] = (
        back * cosine - front * sine
    ).astype(grad_rows.dtype)
    grad_rows[:, query_width + key_width :] = grad_values[...].astype(grad_rows.dtype)
    pair_add(1)
    chain_step(1, 0)

    load_qkv.wait()
    grad_normed = against_cols(grad_rows[...], w_qkv[...])
    inputs = inputs_ref[...].astype(full)
    grad_norm, gain_zero = norm_backward(
        grad_normed, inputs, rms_scale(inputs), gains_ref[0:1, :]
    )
    grad_inputs = (back_ref[...] + grad_norm).astype(jnp.bfloat16)
    weight_parts(key_parts, query_width, 2 * key_width)
    gain_stack = jnp.stack([gain_zero, gain_one, gain_two, last_gain_ref[0]])
    third = width // 3
    gain_rows = jnp.concatenate(
        [gain_stack[:, at * third : (at + 1) * third] for at in range(3)]
        + [jnp.zeros((4, third), full)]
    ).astype(jnp.bfloat16)
    for member in range(shards):
        gain_at = key_parts.shape[2] - 16
        key_parts[member % 2, member // 2, gain_at:, 0:third] = gain_rows
        key_parts[member % 2, member // 2, gain_at:, third:] = jnp.zeros(
            (16, key_parts.shape[3] - third), key_parts.dtype
        )
    pair_copy(2, key_parts, key_pair).start()
    serve(1)

    if line > 2:
        chain_step(1, 1)
    pair_add(2)
    chain_step(2, 0)
    chain_to(0, line - 1)
    chain_finish(0)
    step_start(0, 0)
    serve(members - 1, 0)
    for step in range(2, line - 1):
        chain_step(1, step)
        chain_step(2, step - 1)
    if line > 2:
        chain_step(2, line - 2)
    chain_finish(1)
    step_start(1, 0)
    send_back(1, grad_inputs)
    serve(1, members - 1)
    step_add(0, 0)
    serve(0)
    chain_finish(2)
    step_start(2, 0)
    for stage in range(1, bits):
        step_add(0, stage)
    for stage in range(bits):
        serve(*range(members))
        for kind in (1, 2):
            step_add(kind, stage)
    while any(todo):
        serve(*range(members))
    store_small = (
        pltpu.make_async_copy(out_steps.at[bits], outw_hbm, store_sems.at[0]),
        pltpu.make_async_copy(
            query_steps.at[bits],
            qkv_hbm.at[pl.ds(0, query_steps.shape[1]), pl.ds(0, query_width)],
            store_sems.at[1],
        ),
        pltpu.make_async_copy(
            key_steps.at[bits], qkv_hbm.at[:, pl.ds(query_width, 2 * key_width)], store_sems.at[2]
        ),
    )
    for store in store_small:
        store.start()
    own_deal = deal_row(deal_ref, me, rows)
    own_column = jnp.sum(jnp.where(down_ids == along_ids, own_deal, 0), axis=1, keepdims=True)
    send_place = jnp.sum((own_deal < own_column).astype(jnp.int32), axis=1, keepdims=True)
    target = lax.div(send_place, peer_rows) * block_rows + lax.rem(send_place, peer_rows)
    placer = (
        lax.broadcasted_iota(jnp.int32, (rows, packed), 1) == target
    ).astype(jnp.bfloat16)
    for kind, result in enumerate((output_ref, input_grad_ref)):

        @pl.loop(1, devices)
        def _(hop, kind=kind):
            source = lax.rem(me + devices - hop, devices)
            row_copy(kind, hop, source, source).wait_recv()

        stacked = recv_rows[kind].astype(full).reshape(packed, width).astype(jnp.bfloat16)
        result[...] = jnp.dot(placer, stacked, preferred_element_type=full).astype(result.dtype)

    for kind in range(2):

        @pl.loop(1, devices)
        def _(hop, kind=kind):
            row_copy(kind, hop, lax.rem(me + hop, devices), me).wait_send()

    def sent(member, part):
        for stage in range(bits):
            if stage >= first_stage(member):
                halve(member, part, stage).wait_send()
            if stage > 0:
                double(member, part, stage).wait_send()

    each(sent)
    for kind in range(3):
        parts, pair = kinds[kind][:2]
        pair_copy(kind, parts, pair).wait_send()
        for stage in range(bits):
            for lane, piece in lanes[kind]:
                step_copy(kind, stage, lane, piece).wait_send()

        @pl.loop(0, line - 1)
        def _(step, kind=kind):
            far = line - 1 - step

            @pl.when(far > place)
            def _():
                chain_copy(kind, 0, step, far).wait_send()

            @pl.when(step < place)
            def _():
                chain_copy(kind, 1, step, step).wait_send()

    for store in store_small:
        store.wait()
    each(lambda member, part: store_half(member, part).wait())


def back_and_reduce(line, replicas, small, first_full, out_full, ff_grads):
    inputs, normed, queries, keys = small[4], small[5], small[7], small[8]
    held = 12
    rows, width = inputs.shape
    shards = 2 * line
    devices = replicas * shards
    vmem_limit = 63 * 1024 * 1024
    block_rows = round_up(rows // devices, 8)
    bits = replicas.bit_length() - 1
    qkv_width = queries.shape[1] + 2 * keys.shape[1]
    qkv_rows = round_up(width // shards, 16) + 16
    out_rows = round_up(out_full.shape[0] // shards, 16)
    members, half_rows = ff_grads.shape[:2]
    low = jnp.bfloat16
    full = jnp.float32
    vmem = pl.BlockSpec(memory_space=pltpu.VMEM)
    hbm = pl.BlockSpec(memory_space=pl.ANY)
    dma = pltpu.SemaphoreType.DMA

    def chain_scratch(count, cols):
        return [
            pltpu.VMEM((2, line, count, cols), low),
            pltpu.VMEM((line, count, cols), low),
            pltpu.VMEM((2, line - 1, count, cols), low),
            pltpu.VMEM((bits + 1, count, cols), low),
            pltpu.VMEM((bits, count, cols), low),
        ]

    return pl.pallas_call(
        functools.partial(back_kernel, line, replicas),
        out_shape=(
            jax.ShapeDtypeStruct((members, half_rows // 4, width), low),
            jax.ShapeDtypeStruct((members, half_rows // 4, width), low),
            jax.ShapeDtypeStruct((qkv_rows, qkv_width), low),
            jax.ShapeDtypeStruct((out_rows, width), low),
            jax.ShapeDtypeStruct((rows, width), low),
            jax.ShapeDtypeStruct((rows, width), low),
        ),
        in_specs=[hbm] * held + [vmem] * (len(small) - held) + [hbm] * 3,
        out_specs=(hbm,) * 4 + (vmem,) * 2,
        scratch_shapes=[
            pltpu.VMEM((width, qkv_width), low),
            pltpu.VMEM(out_full.shape, low),
            pltpu.VMEM(ff_grads.shape, low),
            pltpu.VMEM(ff_grads.shape, low),
            pltpu.VMEM((members - EARLY, 2, half_rows // 4, width), low),
            pltpu.VMEM(
                (members, 2, half_rows // 4 - half_rows // (2 * replicas), width), low
            ),
            *chain_scratch(qkv_rows - 16, queries.shape[1]),
            *chain_scratch(qkv_rows, 2 * keys.shape[1]),
            *chain_scratch(out_rows, width),
            pltpu.VMEM((rows, qkv_width), low),
            pltpu.VMEM((rows, keys.shape[1]), full),
            pltpu.VMEM((rows, keys.shape[1]), full),
            pltpu.VMEM((devices * block_rows, rows), low),
            pltpu.VMEM((2, devices, block_rows, width), low),
            pltpu.VMEM((2, devices, block_rows, width), low),
            [pltpu.VMEM(operand.shape, operand.dtype) for operand in small[:held]],
            dma((held,)),
            dma((3,)),
            dma((3 + 2 * members,)),
            dma((2, members, 2, bits)),
            dma((2, members, 2, bits)),
            dma((3,)),
            dma((3,)),
            dma((3, 2, line - 1)),
            dma((3, 2, line - 1)),
            dma((4, bits)),
            dma((4, bits)),
            dma((2, devices)),
            dma((2, devices)),
        ],
        compiler_params=pltpu.CompilerParams(
            collective_id=1, has_side_effects=True, vmem_limit_bytes=vmem_limit
        ),
        cost_estimate=pl.CostEstimate(
            flops=16 * rows * width * qkv_width,
            bytes_accessed=4 * members * half_rows * width,
            transcendentals=2 * rows * rows * 4,
        ),
    )(*small, first_full, out_full, ff_grads)


def bring_kernel(
    line,
    replicas,
    near_weights,
    tokens_ref,
    cotangent_ref,
    deal_ref,
    gains_in,
    qkv_in,
    out_in,
    lengths_ref,
    frequency_ref,
    gu_hbm,
    down_hbm,
    inputs_ref,
    upstream_ref,
    normed_ref,
    queries_ref,
    keys_ref,
    values_ref,
    attended_ref,
    branch_ref,
    middle_ref,
    normed_two_ref,
    gains_ref,
    cosine_ref,
    sine_ref,
    doc_col_ref,
    doc_row_ref,
    qkv_hbm,
    outw_hbm,
    weights_hbm,
    w_qkv,
    w_out,
    gain_blocks,
    weights,
    tiles,
    sent,
    arrived,
    projected,
    load_sems,
    store_sems,
    row_send,
    row_recv,
    line_send,
    line_recv,
    rep_send,
    rep_recv,
    pair_send,
    pair_recv,
    gain_send,
    gain_recv,
    sibling_send,
    sibling_recv,
):
    rep = lax.axis_index("rep")
    shard = lax.axis_index("shard")
    shards = 2 * line
    devices = replicas * shards
    me = rep * shards + shard
    core = lax.rem(shard, 2)
    place = lax.div(shard, 2)
    sibling = (rep, shard + 1 - 2 * core)
    share = min(4, replicas)
    quarter = lax.rem(rep, share)
    full = jnp.float32
    low = jnp.bfloat16
    rows, width = tokens_ref.shape
    peer_rows = rows // devices
    block_rows = sent.shape[2]
    units = gu_hbm.shape[1]
    half = weights.shape[1] // 2
    tile_rows = tiles.shape[1]
    tile_count = units // tile_rows
    depth = tiles.shape[0]
    key_width = keys_ref.shape[1]
    query_width = queries_ref.shape[1]
    heads = query_width // key_width
    half_key = key_width // 2

    def tile_load(turn):
        member, at = turn // tile_count, turn % tile_count * tile_rows
        source = down_hbm if member == 0 else gu_hbm.at[member - 1]
        return pltpu.make_async_copy(
            source.at[pl.ds(at, tile_rows)], tiles.at[turn % depth], load_sems.at[turn % depth]
        )

    for turn in range(min(depth, 3 * tile_count)):
        tile_load(turn).start()

    barrier = pltpu.get_barrier_semaphore()

    @pl.loop(1, devices)
    def _(hop):
        peer = lax.rem(me + hop, devices)
        pl.semaphore_signal(
            barrier,
            inc=1,
            device_id=(lax.div(peer, shards), lax.rem(peer, shards)),
            device_id_type=MESH,
        )

    if near_weights:
        w_qkv[shard] = qkv_in[...].astype(low)

    down_ids = lax.broadcasted_iota(jnp.int32, (rows, rows), 0)
    along_ids = lax.broadcasted_iota(jnp.int32, (rows, rows), 1)
    eye = down_ids == along_ids

    def to_column(row):
        return jnp.sum(jnp.where(eye, row, 0), axis=1, keepdims=True)

    def to_row(column):
        return jnp.sum(jnp.where(eye, column, 0), axis=0, keepdims=True)

    def spread(places):
        return lax.div(places, peer_rows) * block_rows + lax.rem(places, peer_rows)

    own_deal = deal_row(deal_ref, me, rows)
    send_place = jnp.sum((to_column(own_deal) < own_deal).astype(jnp.int32), axis=0, keepdims=True)
    packed = devices * block_rows
    picker = (
        lax.broadcasted_iota(jnp.int32, (packed, rows), 0) == spread(send_place)
    ).astype(low)

    def pack(kind, source):
        sent[kind] = (
            jnp.dot(picker, source[...], preferred_element_type=full)
            .reshape(devices, block_rows, width)
            .astype(low)
        )
        arrived[kind, me] = sent[kind, me]

    pack(0, tokens_ref)
    pl.semaphore_wait(barrier, devices - 1)

    def row_copy(kind, hop, peer, source):
        return pltpu.make_async_remote_copy(
            src_ref=sent.at[kind, peer],
            dst_ref=arrived.at[kind, source],
            send_sem=row_send.at[kind, hop],
            recv_sem=row_recv.at[kind, hop],
            device_id=(lax.div(peer, shards), lax.rem(peer, shards)),
            device_id_type=MESH,
        )

    def rows_start(kind):
        @pl.loop(1, devices)
        def _(hop):
            row_copy(kind, hop, lax.rem(me + hop, devices), me).start()

    def rows_arrive(kind):
        @pl.loop(1, devices)
        def _(hop):
            source = lax.rem(me + devices - hop, devices)
            row_copy(kind, hop, source, source).wait_recv()

    gathered = (w_qkv, w_out)

    def part_of(kind, member, portion):
        buffer = gathered[kind]
        if kind == 0:
            size = buffer.shape[2] // share
            return buffer.at[member, :, pl.ds(pl.multiple_of(portion * size, LANES), size)]
        size = buffer.shape[1] // share
        return buffer.at[member, pl.ds(pl.multiple_of(portion * size, 16), size)]

    def line_copy(kind, target, source):
        part = part_of(kind, 2 * source + core, quarter)
        return pltpu.make_async_remote_copy(
            src_ref=part,
            dst_ref=part,
            send_sem=line_send.at[kind, target],
            recv_sem=line_recv.at[kind, source],
            device_id=(rep, 2 * target + core),
            device_id_type=MESH,
        )

    def rep_copy(kind, block, hop, portion):
        part = part_of(kind, 2 * block + core, portion)
        return pltpu.make_async_remote_copy(
            src_ref=part,
            dst_ref=part,
            send_sem=rep_send.at[kind, block, hop],
            recv_sem=rep_recv.at[kind, block, portion],
            device_id=(rep - quarter + lax.rem(quarter + hop, share), shard),
            device_id_type=MESH,
        )

    def pair_copy(kind, block, side):
        buffer = gathered[kind]
        return pltpu.make_async_remote_copy(
            src_ref=buffer.at[2 * block + side],
            dst_ref=buffer.at[2 * block + side],
            send_sem=pair_send.at[kind, block],
            recv_sem=pair_recv.at[kind, block],
            device_id=sibling,
            device_id_type=MESH,
        )

    def gain_copy(hop, source):
        return pltpu.make_async_remote_copy(
            src_ref=gain_blocks.at[source],
            dst_ref=gain_blocks.at[source],
            send_sem=gain_send.at[hop],
            recv_sem=gain_recv.at[hop],
            device_id=(rep, lax.rem(shard + hop, shards)),
            device_id_type=MESH,
        )

    def others():
        return [lax.rem(place + hop, line) for hop in range(1, line)]

    def line_start(kind):
        for target in others():
            line_copy(kind, target, place).start()
        pair_copy(kind, place, core).start()

    def line_pass(kind):
        for source in others():
            line_copy(kind, source, source).wait_recv()
            for hop in range(1, share):
                rep_copy(kind, source, hop, quarter).start()

    def rep_pass(kind):
        for block in others():
            for hop in range(1, share):
                rep_copy(kind, block, hop, lax.rem(quarter + hop, share)).wait_recv()
            pair_copy(kind, block, core).start()

    def pair_arrive(kind):
        for block in range(line):
            pair_copy(kind, block, 1 - core).wait_recv()

    if near_weights:
        line_start(0)
    rows_start(0)
    if near_weights:
        w_out[shard] = out_in[...].astype(low)
        line_start(1)
        gain_blocks[shard] = jnp.zeros(gain_blocks.shape[1:], low)
        gain_blocks[shard, : gains_in.shape[0], : gains_in.shape[1]] = gains_in[...].astype(low)
        for hop in range(1, shards):
            gain_copy(hop, shard).start()

    def sibling_copy(member):
        return pltpu.make_async_remote_copy(
            src_ref=weights.at[member, pl.ds(0, half)],
            dst_ref=weights.at[member, pl.ds(half, half)],
            send_sem=sibling_send.at[member],
            recv_sem=sibling_recv.at[member],
            device_id=sibling,
            device_id_type=MESH,
        )

    def cast(begin, end):
        for turn in range(begin, end):
            member, at = turn // tile_count, turn % tile_count * tile_rows
            tile_load(turn).wait()
            weights[member, at : at + tile_rows, :] = tiles[turn % depth].astype(low)
            if turn + depth < 3 * tile_count:
                tile_load(turn + depth).start()

    if half > units:
        for member in range(3):
            weights[member, units:half, :] = jnp.zeros((half - units, width), low)

    own_slots = lax.broadcasted_iota(jnp.int32, (rows, rows), 0) + me * rows

    def find(source, total):
        return total + jnp.where(deal_row(deal_ref, source, rows) == own_slots, source, 0)

    found = lax.fori_loop(0, devices, find, jnp.zeros((rows, rows), jnp.int32))
    source = jnp.sum(found, axis=1, keepdims=True)
    earlier = (to_row(source) == source) & (along_ids < down_ids)
    recv_place = source * peer_rows + jnp.sum(earlier.astype(jnp.int32), axis=1, keepdims=True)
    placer = (
        lax.broadcasted_iota(jnp.int32, (rows, packed), 1) == spread(recv_place)
    ).astype(low)

    ids = lax.broadcasted_iota(jnp.int32, (rows, 1), 0)
    end = jnp.int32(0)
    document = jnp.zeros((rows, 1), jnp.int32)
    begin = jnp.zeros((rows, 1), jnp.int32)
    for member in range(lengths_ref.shape[1]):
        end = end + lengths_ref[0, member]
        passed = ids >= end
        document = document + passed.astype(jnp.int32)
        begin = jnp.where(passed, end, begin)
    doc_col_ref[...] = document
    doc_row_ref[...] = to_row(document)
    angles = (ids - begin).astype(full) * frequency_ref[...]
    cosine_ref[...] = jnp.cos(angles)
    sine_ref[...] = jnp.sin(angles)
    if near_weights:
        line_pass(0)
    pack(1, cotangent_ref)
    for member in range(3):
        cast(member * tile_count, (member + 1) * tile_count)
        sibling_copy(member).start()
    near_stores = [
        pltpu.make_async_copy(
            weights.at[member, pl.ds(0, half)],
            weights_hbm.at[member, pl.ds(0, half)],
            store_sems.at[2 + member],
        )
        for member in range(3)
    ]
    for store in near_stores:
        store.start()

    def placed(kind):
        stacked = arrived[kind].astype(full).reshape(packed, width).astype(low)
        return jnp.dot(placer, stacked, preferred_element_type=full)

    if near_weights:
        for hop in range(1, shards):
            gain_copy(hop, lax.rem(shard + shards - hop, shards)).wait_recv()
        span = gains_in.shape[1]
        line_ids = lax.broadcasted_iota(jnp.int32, (gain_blocks.shape[2], width), 0)
        lane_ids = lax.broadcasted_iota(jnp.int32, (gain_blocks.shape[2], width), 1)
        joined = jnp.zeros((gain_blocks.shape[1], width), full)
        for member in range(shards):
            move = ((lane_ids - member * span == line_ids) & (line_ids < span)).astype(low)
            joined = joined + jnp.dot(gain_blocks[member], move, preferred_element_type=full)
        gains_ref[...] = joined[: gains_ref.shape[0]]
        rep_pass(0)
    else:
        gains_ref[...] = gains_in[...]
    rows_arrive(0)
    inputs = placed(0)
    inputs_ref[...] = inputs.astype(low)
    normed_ref[...] = (inputs * rms_scale(inputs) * gains_ref[0:1, :]).astype(low)
    if near_weights:
        line_pass(1)
    rows_start(1)
    if near_weights:
        pair_arrive(0)
        qkv_matrix = w_qkv[...].reshape(width, w_qkv.shape[2])
    else:
        qkv_matrix = qkv_in[...]
    projected[...] = jnp.dot(normed_ref[...], qkv_matrix, preferred_element_type=full)

    def turned(start):
        front = projected[:, pl.ds(start, half_key)]
        back = projected[:, pl.ds(start + half_key, half_key)]
        cosine, sine = cosine_ref[...], sine_ref[...]
        return (
            (front * cosine - back * sine).astype(low),
            (back * cosine + front * sine).astype(low),
        )

    keys_ref[:, :half_key], keys_ref[:, half_key:] = turned(query_width)
    values_ref[...] = projected[:, query_width + key_width :].astype(low)

    for head in range(heads):
        if near_weights and head == heads // 2:
            rep_pass(1)
        start = head * key_width
        cols = pl.ds(start, key_width)
        front, back = turned(start)
        queries_ref[:, pl.ds(start, half_key)] = front
        queries_ref[:, pl.ds(start + half_key, half_key)] = back
        allowed = (doc_col_ref[...] == doc_row_ref[...]) & (
            lax.broadcasted_iota(jnp.int32, (rows, rows), 0)
            >= lax.broadcasted_iota(jnp.int32, (rows, rows), 1)
        )
        scores = against_cols(queries_ref[:, cols], keys_ref[...]) * (HD ** (-0.5) / CAP_LIMIT)
        capped = jnp.where(allowed, CAP_LIMIT * jnp.tanh(scores), MASKED_SCORE)
        powers = jnp.exp(capped - jnp.max(capped, axis=-1, keepdims=True))
        probs = powers / jnp.sum(powers, axis=-1, keepdims=True)
        attended_ref[:, cols] = jnp.dot(
            probs.astype(low), values_ref[...], preferred_element_type=full
        ).astype(low)

    if near_weights:
        pair_arrive(1)
        out_matrix = w_out[...].reshape(query_width, width)
    else:
        out_matrix = out_in[...]
    stores = []
    if near_weights:
        stores.append(pltpu.make_async_copy(w_qkv, qkv_hbm, store_sems.at[0]))
        stores.append(pltpu.make_async_copy(w_out, outw_hbm, store_sems.at[1]))
    else:
        stores.append(pltpu.make_async_copy(qkv_in, qkv_hbm, store_sems.at[0]))
        stores.append(pltpu.make_async_copy(out_in, outw_hbm, store_sems.at[1]))
    for store in stores:
        store.start()
    for member in range(3):
        sibling_copy(member).wait_recv()
        store = pltpu.make_async_copy(
            weights.at[member, pl.ds(half, half)],
            weights_hbm.at[member, pl.ds(half, half)],
            store_sems.at[5 + member],
        )
        store.start()
        stores.append(store)
    branch = jnp.dot(attended_ref[...], out_matrix, preferred_element_type=full)
    branch_ref[...] = branch
    middle = inputs_ref[...].astype(full) + branch * rms_scale(branch) * gains_ref[1:2, :]
    middle_ref[...] = middle
    normed_two_ref[...] = (middle * rms_scale(middle) * gains_ref[2:3, :]).astype(low)
    rows_arrive(1)
    upstream_ref[...] = placed(1).astype(low)
    stores.extend(near_stores)

    for kind in range(2):

        @pl.loop(1, devices)
        def _(hop, kind=kind):
            row_copy(kind, hop, lax.rem(me + hop, devices), me).wait_send()

        if near_weights:
            for block in others():
                line_copy(kind, block, place).wait_send()
                for hop in range(1, share):
                    rep_copy(kind, block, hop, quarter).wait_send()
            for block in range(line):
                pair_copy(kind, block, core).wait_send()
    if near_weights:
        for hop in range(1, shards):
            gain_copy(hop, shard).wait_send()
    for member in range(3):
        sibling_copy(member).wait_send()
    for store in stores:
        store.wait()


def bring_and_attend(
    line, replicas, near_weights, tokens, cotangent, deal, small, gu, down, key_width
):
    gains_in, qkv_in, out_in = small[:3]
    rows, width = tokens.shape
    shards = 2 * line
    devices = replicas * shards
    share = min(4, replicas)
    block_rows = round_up(rows // devices, 8)
    units = down.shape[0]
    half = round_up(units, LANES)
    low = jnp.bfloat16
    full = jnp.float32
    vmem = pl.BlockSpec(memory_space=pltpu.VMEM)
    hbm = pl.BlockSpec(memory_space=pl.ANY)
    dma = pltpu.SemaphoreType.DMA
    qkv_width = qkv_in.shape[1]
    query_width = qkv_width - 2 * key_width
    if near_weights:
        qkv_shape = (shards, *qkv_in.shape)
        out_shape = (shards, *out_in.shape)
    else:
        qkv_shape = qkv_in.shape
        out_shape = out_in.shape
    tile_rows = max(size for size in range(16, 145, 16) if units % size == 0)
    hold = near_weights
    qkv_scratch = qkv_shape if hold else (shards, 16, LANES)
    out_scratch = out_shape if hold else (shards, 16, LANES)
    gain_lanes = round_up(width // shards, LANES) if hold else LANES

    def array(shape, dtype):
        return jax.ShapeDtypeStruct(shape, dtype)

    return pl.pallas_call(
        functools.partial(bring_kernel, line, replicas, near_weights),
        out_shape=(
            array((rows, width), low),
            array((rows, width), low),
            array((rows, width), low),
            array((rows, query_width), low),
            array((rows, key_width), low),
            array((rows, key_width), low),
            array((rows, query_width), low),
            array((rows, width), full),
            array((rows, width), full),
            array((rows, width), low),
            array((4, width), full),
            array((rows, key_width // 2), full),
            array((rows, key_width // 2), full),
            array((rows, 1), jnp.int32),
            array((1, rows), jnp.int32),
            array(qkv_shape, low),
            array(out_shape, low),
            array((3, 2 * half, width), low),
        ),
        in_specs=[vmem] * 6
        + [pl.BlockSpec(memory_space=pltpu.SMEM), vmem]
        + [hbm] * 2,
        out_specs=(vmem,) * 15 + (hbm,) * 3,
        scratch_shapes=[
            pltpu.VMEM(qkv_scratch, low),
            pltpu.VMEM(out_scratch, low),
            pltpu.VMEM((shards, 16, gain_lanes), low),
            pltpu.VMEM((3, 2 * half, width), low),
            pltpu.VMEM((4, tile_rows, width), full),
            pltpu.VMEM((2, devices, block_rows, width), low),
            pltpu.VMEM((2, devices, block_rows, width), low),
            pltpu.VMEM((rows, qkv_width), full),
            dma((4,)),
            dma((8,)),
            dma((2, devices)),
            dma((2, devices)),
            dma((2, line)),
            dma((2, line)),
            dma((2, line, share)),
            dma((2, line, share)),
            dma((2, line)),
            dma((2, line)),
            dma((shards,)),
            dma((shards,)),
            dma((3,)),
            dma((3,)),
        ],
        compiler_params=pltpu.CompilerParams(
            collective_id=2, has_side_effects=True, vmem_limit_bytes=63 * 1024 * 1024
        ),
        cost_estimate=pl.CostEstimate(
            flops=6 * rows * width * qkv_width,
            bytes_accessed=3 * units * width * 8,
            transcendentals=2 * rows * rows * 4,
        ),
    )(tokens, cotangent, deal, *small, gu, down)


def adam_half_kernel(which, first_half, second_half, *refs):
    del which
    inputs, results = refs[:6], refs[-10:]
    part, member = pl.program_id(0), pl.program_id(1)
    gradient = jnp.where(part == 0, first_half[0], second_half[0]).astype(jnp.float32)

    def step(rows_in, rows_out, rate, decay):
        master, first, second = (ref[...].reshape(gradient.shape) for ref in rows_in)
        updated, moment, square = adam_values(master, gradient, first, second, rate, decay)
        for ref, value in zip(rows_out, (updated, moment, square, gradient, updated)):
            ref[...] = value.astype(ref.dtype).reshape(ref.shape)

    @pl.when(member == 0)
    def _():
        step(inputs[:3], results[:5], LEARN_RATES[3], DECAY_RATES[3])

    @pl.when(member > 0)
    def _():
        step(inputs[3:], results[5:], LEARN_RATES[2], DECAY_RATES[2])


def adam_values(master, gradient, first, second, rate, decay):
    moment = BETA_FIRST * first + (1.0 - BETA_FIRST) * gradient
    square = BETA_SECOND * second + (1.0 - BETA_SECOND) * gradient * gradient
    moment_hat = moment * (1.0 / (1.0 - BETA_FIRST**STEP))
    square_hat = square * (1.0 / (1.0 - BETA_SECOND**STEP))
    updated = master - rate * (moment_hat / (jnp.sqrt(square_hat) + ADAM_EPS) + decay * master)
    return updated, moment, square


def adam_stream_kernel(begun, carry, which, first_half, second_half, *refs):
    sources, refs = refs[:6], refs[6 + begun :]
    rows_in, refs = refs[:carry], refs[carry:]
    results, refs = refs[:10], refs[10:]
    rows_out, refs = refs[:carry], refs[carry:]
    taken, grads, given, copies, in_sems, out_sems, *passing = refs
    depth, tile = taken.shape[0], taken.shape[2]
    units = sources[0].shape[0]
    members = first_half.shape[0]
    order = [
        (part, sub, member) for part in range(2) for sub in range(2) for member in range(members)
    ]

    def rows_of(part, sub):
        begin = (part * 4 + which[part] * 2) * tile
        start = begin + sub * tile
        if part == 1 and sub == 1:
            start = jnp.minimum(start, units - tile)
        return at_rows(start, tile), at_rows(start - begin, tile)

    def view(ref, member, span):
        return ref.at[span] if member == 0 else ref.at[member - 1, span]

    def loads(turn):
        part, sub, member = order[turn]
        span, grad_span = rows_of(part, sub)
        slot = turn % depth
        group = sources[:3] if member == 0 else sources[3:]
        pairs = [(view(ref, member, span), taken.at[slot, at]) for at, ref in enumerate(group)]
        half = (first_half, second_half)[part]
        pairs.append((half.at[member, grad_span], grads.at[slot]))
        return [
            pltpu.make_async_copy(source, target, in_sems.at[slot, at])
            for at, (source, target) in enumerate(pairs)
        ]

    def stores(turn):
        part, sub, member = order[turn]
        span, _ = rows_of(part, sub)
        slot = turn % 2
        group = results[:5] if member == 0 else results[5:]
        held = [given.at[slot, at] for at in range(4)] + [copies.at[slot]]
        return [
            pltpu.make_async_copy(source, view(ref, member, span), out_sems.at[slot, at])
            for at, (source, ref) in enumerate(zip(held, group))
        ]

    def passes(outward):
        held, sems = passing
        return [
            pltpu.make_async_copy(held.at[at], rows_out[at], sems.at[1, at])
            if outward
            else pltpu.make_async_copy(rows_in[at], held.at[at], sems.at[0, at])
            for at in range(carry)
        ]

    for turn in range(depth):
        for load in loads(turn):
            load.start()
    if carry:
        for load in passes(False):
            load.start()
    for turn, (_, _, member) in enumerate(order):
        slot, out = turn % depth, turn % 2
        rate, decay = (LEARN_RATES[3], DECAY_RATES[3]) if member == 0 else (
            LEARN_RATES[2],
            DECAY_RATES[2],
        )
        for load in loads(turn):
            load.wait()
        if turn >= 2:
            for store in stores(turn - 2):
                store.wait()

        @pl.loop(0, tile // 16)
        def _(group, slot=slot, out=out, rate=rate, decay=decay):
            span = at_rows(group * 16, 16)
            gradient = grads[slot, span, :].astype(jnp.float32)
            updated, moment, square = adam_values(
                taken[slot, 0, span, :],
                gradient,
                taken[slot, 1, span, :],
                taken[slot, 2, span, :],
                rate,
                decay,
            )
            for at, value in enumerate((updated, moment, square, gradient)):
                given[out, at, span, :] = value
            copies[out, span, :] = updated.astype(copies.dtype)

        for store in stores(turn):
            store.start()
        if turn + depth < len(order):
            for load in loads(turn + depth):
                load.start()
        if carry and turn == depth:
            for load in passes(False):
                load.wait()
            for store in passes(True):
                store.start()
    for turn in range(len(order) - 2, len(order)):
        for store in stores(turn):
            store.wait()
    if carry:
        for store in passes(True):
            store.wait()


def adam_stream(which, halves, arrays, begun=(), carry=()):
    members, half_rows, width = halves[0].shape
    tile = half_rows // 2
    hbm = pl.BlockSpec(memory_space=pl.ANY)
    full, low = jnp.float32, jnp.bfloat16
    shapes = []
    for like in (arrays[0], arrays[3]):
        shapes.extend([jax.ShapeDtypeStruct(like.shape, full)] * 4)
        shapes.append(jax.ShapeDtypeStruct(like.shape, low))
    passing = []
    if carry:
        passing.append(pltpu.VMEM((len(carry), *carry[0].shape), carry[0].dtype))
        passing.append(pltpu.SemaphoreType.DMA((2, len(carry))))
    count = members * half_rows * width * 2
    return pl.pallas_call(
        functools.partial(adam_stream_kernel, len(begun), len(carry)),
        out_shape=(*shapes, *(jax.ShapeDtypeStruct(rows.shape, rows.dtype) for rows in carry)),
        in_specs=[pl.BlockSpec(memory_space=pltpu.SMEM)] + [hbm] * (8 + len((*begun, *carry))),
        out_specs=(hbm,) * (10 + len(carry)),
        scratch_shapes=[
            pltpu.VMEM((3, 3, tile, width), full),
            pltpu.VMEM((3, tile, width), low),
            pltpu.VMEM((2, 4, tile, width), full),
            pltpu.VMEM((2, tile, width), low),
            pltpu.SemaphoreType.DMA((3, 4)),
            pltpu.SemaphoreType.DMA((2, 5)),
            *passing,
        ],
        input_output_aliases={9 + at: at for at in range(len(begun))},
        compiler_params=pltpu.CompilerParams(vmem_limit_bytes=60 * 1024 * 1024),
        cost_estimate=pl.CostEstimate(
            flops=16 * count, bytes_accessed=32 * count, transcendentals=2 * count
        ),
    )(which, *halves, *arrays, *begun, *carry)


def adam_half(which, halves, arrays, begun=(), carry=()):
    members, half_rows, width = halves[0].shape
    tile = half_rows // 2
    down, gu = arrays[0], arrays[3]
    if down.shape[0] - 3 * half_rows >= tile:
        return adam_stream(which, halves, arrays, begun, carry)

    def down_at(part, member, sub, chosen):
        return (part * 4 + chosen[part] * 2 + jnp.where(member == 0, sub, 1), 0)

    def gu_at(part, member, sub, chosen):
        row = part * 4 + chosen[part] * 2 + jnp.where(member == 0, 0, sub)
        return (jnp.maximum(member - 1, 0), row, 0)

    def first_at(part, member, sub, chosen):
        return (jnp.where(part == 0, member, members - 1), jnp.where(part == 0, sub, 1), 0)

    def second_at(part, member, sub, chosen):
        return (jnp.where(part == 0, 0, member), jnp.where(part == 0, 0, sub), 0)

    down_block = pl.BlockSpec((tile, width), down_at)
    gu_block = pl.BlockSpec((1, tile, width), gu_at)
    half_block = (1, tile, width)
    hbm = pl.BlockSpec(memory_space=pl.ANY)
    shapes = []
    for like in (down, gu):
        shapes.extend([jax.ShapeDtypeStruct(like.shape, jnp.float32)] * 4)
        shapes.append(jax.ShapeDtypeStruct(like.shape, jnp.bfloat16))
    count = members * half_rows * width * 2
    done = pl.pallas_call(
        adam_half_kernel,
        out_shape=tuple(shapes),
        grid_spec=pltpu.PrefetchScalarGridSpec(
            num_scalar_prefetch=1,
            grid=(2, members, 2),
            in_specs=[
                pl.BlockSpec(half_block, first_at),
                pl.BlockSpec(half_block, second_at),
                *[down_block] * 3,
                *[gu_block] * 3,
                *[hbm] * len(begun),
            ],
            out_specs=(*[down_block] * 5, *[gu_block] * 5),
        ),
        input_output_aliases={9 + at: at for at in range(len(begun))},
        compiler_params=pltpu.CompilerParams(vmem_limit_bytes=60 * 1024 * 1024),
        cost_estimate=pl.CostEstimate(
            flops=16 * count, bytes_accessed=32 * count, transcendentals=2 * count
        ),
    )(which, *halves, *arrays, *begun)
    return (*done, *carry)


def local(
    tokens,
    cotangent,
    lengths,
    deal,
    w_qkv,
    w_out,
    w_gu,
    w_down,
    gains,
    first_qkv,
    first_out,
    first_gu,
    first_down,
    first_gains,
    second_qkv,
    second_out,
    second_gu,
    second_down,
    second_gains,
):
    row_count, width = tokens.shape
    shards = lax.axis_size("shard")
    replicas = lax.axis_size("rep")
    line = shards // 2
    devices = replicas * shards
    deal_blocks = deal.reshape(deal.shape[0] // LANES, LANES)
    exponent = np.arange(HD // 2, dtype=np.float32) * np.float32(-2.0 / HD)
    frequency = jnp.asarray((np.float32(ROPE_BASE) ** exponent)[None, :])
    near_weights = w_qkv.shape[0] % 16 == 0
    if near_weights:
        first_weights = (gains, w_qkv, w_out)
    else:
        first_weights = (
            lax.all_gather(gains.astype(jnp.bfloat16), "shard", axis=1, tiled=True).astype(
                jnp.float32
            ),
            lax.all_gather(w_qkv.astype(jnp.bfloat16), "shard", axis=0, tiled=True),
            lax.all_gather(w_out.astype(jnp.bfloat16), "shard", axis=0, tiled=True),
        )
    (
        inputs,
        upstream,
        normed_one,
        queries,
        key_rows,
        value_rows,
        attended,
        branch,
        middle,
        normed_two,
        gain_values,
        cosine_table,
        sine_table,
        doc_col,
        doc_row,
        full_qkv,
        full_out,
        ff_weights,
    ) = bring_and_attend(
        line,
        replicas,
        near_weights,
        tokens,
        cotangent,
        deal_blocks,
        (*first_weights, lengths, frequency),
        w_gu,
        w_down,
        HD,
    )
    full_qkv = full_qkv.reshape(width, w_qkv.shape[1])
    full_out = full_out.reshape(H * HD, width)
    output_rows, last_gain_grad, grad_normed_two, ff_grads = feed_forward(
        line,
        replicas,
        normed_two,
        middle,
        upstream,
        gain_values,
        ff_weights,
    )
    first_half, second_half, qkv_sums, out_sums, output, input_grad = back_and_reduce(
        line,
        replicas,
        (
            grad_normed_two,
            middle,
            upstream,
            branch,
            inputs,
            normed_one,
            attended,
            queries,
            key_rows,
            value_rows,
            cosine_table,
            sine_table,
            doc_col,
            doc_row,
            gain_values,
            last_gain_grad,
            output_rows,
            deal_blocks,
        ),
        full_qkv,
        full_out,
        ff_grads,
    )
    bits = replicas.bit_length() - 1
    flips = (1, 1 << (bits - 1))
    other_halves = tuple(
        lax.ppermute(half, "rep", [(member, member ^ flip) for member in range(replicas)])
        for half, flip in zip((first_half, second_half), flips)
    )
    rep = lax.axis_index("rep")
    held = jnp.stack([lax.rem(lax.div(rep, flip), 2) for flip in flips]).astype(jnp.int32)
    ff_arrays = (w_down, first_down, second_down, w_gu, first_gu, second_gu)
    *begun, output, input_grad = adam_half(
        held, (first_half, second_half), ff_arrays, carry=(output, input_grad)
    )
    (
        new_down,
        moment_down,
        square_down,
        summed_down,
        copy_down,
        new_gu,
        moment_gu,
        square_gu,
        summed_gu,
        copy_gu,
    ) = adam_half(1 - held, other_halves, ff_arrays, begun)
    summed_qkv = qkv_sums[: w_qkv.shape[0]].astype(jnp.float32)
    summed_out = out_sums[: w_out.shape[0]].astype(jnp.float32)
    gain_span = gains.shape[1]
    gain_rows = qkv_sums[-16:-4, H * HD : H * HD + width // 3]
    summed_gains = lax.dynamic_slice(
        gain_rows.reshape(3, gains.shape[0], width // 3)
        .transpose(1, 0, 2)
        .reshape(gains.shape[0], width),
        (0, lax.axis_index("shard") * gain_span),
        (gains.shape[0], gain_span),
    ).astype(jnp.float32)
    new_qkv, moment_qkv, square_qkv = adamw_step(
        w_qkv, summed_qkv, first_qkv, second_qkv, LEARN_RATES[0], DECAY_RATES[0]
    )
    new_out, moment_out, square_out = adamw_step(
        w_out, summed_out, first_out, second_out, LEARN_RATES[1], DECAY_RATES[1]
    )
    new_gains, moment_gains, square_gains = adamw_step(
        gains, summed_gains, first_gains, second_gains, LEARN_RATES[4], DECAY_RATES[4]
    )
    return (
        output,
        input_grad,
        new_qkv,
        new_out,
        new_gu,
        new_down,
        new_gains,
        moment_qkv,
        moment_out,
        moment_gu,
        moment_down,
        moment_gains,
        square_qkv,
        square_out,
        square_gu,
        square_down,
        square_gains,
        summed_qkv,
        summed_out,
        summed_gu,
        summed_down,
        summed_gains,
        new_qkv.astype(jnp.bfloat16),
        new_out.astype(jnp.bfloat16),
        copy_gu,
        copy_down,
        new_gains.astype(jnp.bfloat16),
    )


def solution(mesh):
    placed = (
        P(("rep", "shard"), None),
        P(("rep", "shard"), None),
        P(("rep", "shard"), None),
        P(),
        P("shard", None),
        P("shard", None),
        P(None, "shard", None),
        P("shard", None),
        P(None, "shard"),
        P("shard", None),
        P("shard", None),
        P(None, "shard", None),
        P("shard", None),
        P(None, "shard"),
        P("shard", None),
        P("shard", None),
        P(None, "shard", None),
        P("shard", None),
        P(None, "shard"),
    )
    return jax.shard_map(
        local,
        mesh=mesh,
        in_specs=placed,
        out_specs=(
            P(("rep", "shard"), None),
            P(("rep", "shard"), None),
            P("shard", None),
            P("shard", None),
            P(None, "shard", None),
            P("shard", None),
            P(None, "shard"),
            P("shard", None),
            P("shard", None),
            P(None, "shard", None),
            P("shard", None),
            P(None, "shard"),
            P("shard", None),
            P("shard", None),
            P(None, "shard", None),
            P("shard", None),
            P(None, "shard"),
            P("shard", None),
            P("shard", None),
            P(None, "shard", None),
            P("shard", None),
            P(None, "shard"),
            P("shard", None),
            P("shard", None),
            P(None, "shard", None),
            P("shard", None),
            P(None, "shard"),
        ),
        check_vma=False,
    )
```
